32 devices in a mesh: dp: 2 (over core), wide: 16 (over z, y, x).
Axes of the slice: x: 2, y: 2, z: 4, core: 2. Of those that a mesh axis runs over, the one named last changes fastest.
Arguments:
- feature_map: float32 [32, 6144], P(None, ('dp', 'wide')), may hold values from -6 to 6
- condition: float32 [12, 1024], P('dp'), may hold values from -6 to 6
- item_lengths: int32 [2, 6], P('dp'), may hold values from 0 to 2240, as said below
- cotangent: bfloat16 [6144, 1024], P(('dp', 'wide')), may hold values from -6 to 6
- code_book: bfloat16 [4096, 1024], replicated, may hold values from -0.5 to 0.5
- qkv_state: float32 [3, 1024, 3072], P(None, 'dp', 'wide'), as said below
- out_state: float32 [3, 1024, 1024], P(None, 'dp', 'wide'), as said below
- up_state: float32 [3, 1024, 4096], P(None, 'dp', 'wide'), as said below
- down_state: float32 [3, 4096, 1024], P(None, 'dp', 'wide'), as said below
- ada_state: float32 [3, 1024, 6144], P(None, 'dp', 'wide'), as said below
- embed_state: float32 [3, 32, 1024], replicated, as said below
- vector_state: float32 [3, 8, 1024], replicated, as said below
Outputs:
- block_out: bfloat16 [6144, 1024], P(('dp', 'wide'))
- map_grad: float32 [32, 6144], P(None, ('dp', 'wide'))
- histogram: float32 [4096], replicated
- qkv_new: float32 [3, 1024, 3072], P(None, 'dp', 'wide')
- qkv_copy: bfloat16 [1024, 3072], P('dp', 'wide')
- out_new: float32 [3, 1024, 1024], P(None, 'dp', 'wide')
- out_copy: bfloat16 [1024, 1024], P('dp', 'wide')
- up_new: float32 [3, 1024, 4096], P(None, 'dp', 'wide')
- up_copy: bfloat16 [1024, 4096], P('dp', 'wide')
- down_new: float32 [3, 4096, 1024], P(None, 'dp', 'wide')
- down_copy: bfloat16 [4096, 1024], P('dp', 'wide')
- ada_new: float32 [3, 1024, 6144], P(None, 'dp', 'wide')
- ada_copy: bfloat16 [1024, 6144], P('dp', 'wide')
- embed_new: float32 [3, 32, 1024], replicated
- vector_new: float32 [3, 8, 1024], replicated
- gain_grad: float32 [1024], replicated
The draws below stay inside these ranges and needn't reach their ends.
Inputs may be any that keep to these rules, and one draw needn't show every extreme that they name: `item_lengths`: each entry is 0, 680 or 2240; every row holds the same number of 2240 entries (at least one) and the same number of 680 entries, a row's entries sum to at most 3072 and to more than 2392. `qkv_state`: index 0 is the momentum, 1 the weight, 2 the running average. `out_state`: index 0 is the momentum, 1 the weight, 2 the running average. `up_state`: index 0 is the momentum, 1 the weight, 2 the running average. `down_state`: index 0 is the momentum, 1 the weight, 2 the running average. `ada_state`: index 0 is the momentum, 1 the weight, 2 the running average. `embed_state`: index 0 is the momentum, 1 the weight, 2 the running average. `vector_state`: index 0 is the momentum, 1 the value, 2 the running average; the query gain row of the value is positive.
All inputs are finite; a program needn't handle non-finite values.
Results may differ from the reference program's by a relative error of at most 0.019.
Values may be sent and summed in bfloat16 or wider, within the bound.
A program may use at most 320 MiB of HBM per device.

```python
import math
import jax
import jax.numpy as jnp
from jax import lax

D = 1024
HEADS = 16
FF = 4096
CODES = 4096
CODE_DIM = 32
TOK_DEV = 192
LEVELS = 10
STEP = 7
GROUPS = 2
GROUP_TOKENS = 3072
TOKENS = 6144
SHORT_LEN = 680
LONG_LEN = 2240
SLOTS = 6
CONDS = 12
N_WIDE = 16


def stacked_state(base_key, rows_count, cols_count, spread):
    first_key, second_key, third_key = jax.random.split(base_key, 3)
    weight = spread * jax.random.normal(first_key, (rows_count, cols_count), jnp.float32)
    moment = 0.37 * spread * jax.random.normal(second_key, (rows_count, cols_count), jnp.float32)
    average = 0.8 * weight + 0.6 * spread * jax.random.normal(third_key, (rows_count, cols_count), jnp.float32)
    return jnp.stack([moment, weight, average])


def draw_item_lengths(key, part):
    key = jax.random.fold_in(key, 11)
    best_long = 1
    best_short = (GROUP_TOKENS - LONG_LEN) // SHORT_LEN
    best_unused = GROUP_TOKENS - LONG_LEN - best_short * SHORT_LEN
    for long_try in range(2, GROUP_TOKENS // LONG_LEN + 1):
        short_try = (GROUP_TOKENS - long_try * LONG_LEN) // SHORT_LEN
        unused_try = GROUP_TOKENS - long_try * LONG_LEN - short_try * SHORT_LEN
        if unused_try < best_unused:
            best_long = long_try
            best_short = short_try
            best_unused = unused_try

    def per_group(group_key):
        places = jnp.arange(SLOTS, dtype=jnp.int32)
        kinds = jnp.where(places < best_long, LONG_LEN, jnp.where(places < best_long + best_short, SHORT_LEN, 0))
        return kinds[jax.random.permutation(group_key, SLOTS)].astype(jnp.int32)
    return jax.vmap(per_group)(jax.random.split(key, GROUPS))


def draw_qkv_state(key, part):
    key = jax.random.fold_in(key, 1)
    return stacked_state(key, D, 3 * D, D ** (-0.5))


def draw_out_state(key, part):
    key = jax.random.fold_in(key, 2)
    return stacked_state(key, D, D, (D // 16) ** (-0.5))


def draw_up_state(key, part):
    key = jax.random.fold_in(key, 3)
    return stacked_state(key, D, FF, D ** (-0.5))


def draw_down_state(key, part):
    key = jax.random.fold_in(key, 4)
    return stacked_state(key, FF, D, FF ** (-0.5))


def draw_ada_state(key, part):
    key = jax.random.fold_in(key, 5)
    return stacked_state(key, D, 6 * D, D ** (-0.5))


def draw_embed_state(key, part):
    key = jax.random.fold_in(key, 6)
    return stacked_state(key, CODE_DIM, D, CODE_DIM ** (-0.5))


def draw_vector_state(key, part):
    key = jax.random.fold_in(key, 7)
    bias_key, gain_key, moment_key, average_key = jax.random.split(key, 4)
    biases = 0.3 * jax.random.normal(bias_key, (7, D), jnp.float32)
    gains = jax.random.uniform(gain_key, (1, D), jnp.float32, 0.25, 1.5)
    weight = jnp.concatenate([biases, gains], axis=0)
    moment = 0.11 * jax.random.normal(moment_key, (8, D), jnp.float32)
    average = weight + 0.1 * jax.random.normal(average_key, (8, D), jnp.float32)
    return jnp.stack([moment, weight, average])


def level_of(key, dims, cuts, smallest, high):
    def one(position, parts):
        steps = jax.random.uniform(jax.random.fold_in(jax.random.fold_in(key, 6), position), (parts,), jnp.float32, smallest / len(cuts), high / len(cuts))
        return jnp.repeat(jnp.exp(steps), dims[position] // parts).reshape((-1,) + (1,) * (len(dims) - position - 1))

    gain = one(*cuts[0])
    for cut in cuts[1:]:
        gain = gain * one(*cut)
    return gain


def normal_values(stream_key, shape, scale, most, cuts=(), kind=jnp.bfloat16):
    values = scale * jax.random.normal(stream_key, shape, jnp.float32)
    if cuts:
        values = values * level_of(stream_key, shape, cuts, -0.22, 0.18)
    return jnp.clip(values, -most, most).astype(kind)


def setup_inputs(seed: int = 0) -> dict:
    splits = jax.random.split(jax.random.key(seed), 13)
    feature_map = normal_values(splits[0], (CODE_DIM, TOKENS), 1.0, 6.0, ((1, 32),), jnp.float32)
    condition = normal_values(splits[1], (CONDS, D), 1.0, 6.0, ((0, 2),), jnp.float32)
    item_lengths = draw_item_lengths(jax.random.fold_in(splits[12], 71), 0)
    cotangent = normal_values(splits[3], (TOKENS, D), 1.0, 6.0, ((0, 32),))
    code_book = normal_values(splits[4], (CODES, D), (D // 9) ** -0.5, 0.5)
    qkv_state = draw_qkv_state(jax.random.fold_in(splits[12], 71), 0)
    out_state = draw_out_state(jax.random.fold_in(splits[12], 71), 0)
    up_state = draw_up_state(jax.random.fold_in(splits[12], 71), 0)
    down_state = draw_down_state(jax.random.fold_in(splits[12], 71), 0)
    ada_state = draw_ada_state(jax.random.fold_in(splits[12], 71), 0)
    embed_state = draw_embed_state(jax.random.fold_in(splits[12], 71), 0)
    vector_state = draw_vector_state(jax.random.fold_in(splits[12], 71), 0)
    return {"feature_map": feature_map, "condition": condition, "item_lengths": item_lengths, "cotangent": cotangent, "code_book": code_book, "qkv_state": qkv_state, "out_state": out_state, "up_state": up_state, "down_state": down_state, "ada_state": ada_state, "embed_state": embed_state, "vector_state": vector_state}


@jax.custom_vjp
def low(v):
    return lax.optimization_barrier(v.astype(jnp.bfloat16)).astype(jnp.float32)

@jax.custom_vjp
def low_back(v):
    return v

def low_keep(v):
    return (low(v), None)

def low_pass(kept, grad):
    return (grad,)

def back_keep(v):
    return (v, None)

def back_low(kept, grad):
    return (low(grad),)
low.defvjp(low_keep, low_pass)
low_back.defvjp(back_keep, back_low)
SHORT_SIDES = (1, 2, 3, 4, 5, 6, 8, 10, 13, 16)
LONG_SIDES = (1, 2, 3, 4, 6, 9, 13, 18, 24, 32)
MASKED = -1e+30
NORM_EPS = 1e-06
MOMENTUM = 0.9
WEIGHT_DECAY = 0.05
BASE_RATE = 0.37
VECTOR_RATE = 0.22
GRAD_FACTORS = (0.15, 0.1, 0.3, 0.35, 0.3)
EMBED_FACTOR = 0.6
HIGHEST_PRECISION = lax.Precision.HIGHEST

def layout(lengths, positions, group_len):
    short_sq = jnp.array([side * side for side in SHORT_SIDES[:LEVELS]], jnp.int32)
    long_sq = jnp.array([side * side for side in LONG_SIDES[:LEVELS]], jnp.int32)
    short_total = sum((side * side for side in SHORT_SIDES[:LEVELS]))
    long_total = sum((side * side for side in LONG_SIDES[:LEVELS]))
    slot_count = lengths.shape[0]
    counts = jnp.where(lengths[None, :] == long_total, long_sq[:, None], jnp.where(lengths[None, :] == short_total, short_sq[:, None], 0)).astype(jnp.int32)
    unused = (group_len - jnp.sum(lengths)).astype(jnp.int32)
    ordered = jnp.concatenate([counts.reshape(-1), unused[None]])
    boundary = jnp.cumsum(ordered).astype(jnp.int32)
    segment = lax.optimization_barrier(jnp.sum((boundary[None, :] <= positions[:, None]).astype(jnp.int32), axis=1))
    segment = jnp.minimum(segment, ordered.shape[0] - 1).astype(jnp.int32)
    unused_id = slot_count * LEVELS
    tok_level = jnp.where(segment >= unused_id, 0, segment // slot_count).astype(jnp.int32)
    tok_slot = jnp.where(segment >= unused_id, slot_count, segment % slot_count).astype(jnp.int32)
    return (tok_slot, tok_level, segment)

def pre_norm(inputs, scaling, offset_add):
    row_mean = lax.optimization_barrier(jnp.mean(inputs, axis=-1, keepdims=True))
    centred = inputs - row_mean
    spread = lax.optimization_barrier(jnp.mean(centred * centred, axis=-1, keepdims=True))
    return centred * lax.rsqrt(spread + NORM_EPS) * (1.0 + scaling) + offset_add

def unit_heads(inputs):
    shaped = inputs.reshape(inputs.shape[0], HEADS, -1)
    shaped = shaped * lax.rsqrt(lax.optimization_barrier(jnp.sum(shaped * shaped, axis=-1, keepdims=True)) + NORM_EPS)
    return shaped.reshape(inputs.shape)

def split_heads(projected, q_gain):
    queries, key_part, value_part = jnp.split(projected, 3, axis=1)
    head_scale = math.sqrt(queries.shape[1] // HEADS)
    return (unit_heads(queries) * (head_scale * (1.0 + q_gain)), unit_heads(key_part), value_part)

def smooth_map(values, left_ok, right_ok, before, following):
    return (left_ok * before + 2.0 * values + right_ok * following) / (2.0 + left_ok + right_ok)

def nesterov(stacked, gradient, step_rate, decay_rate):
    moment, weight, average = (stacked[0], stacked[1], stacked[2])
    step_grad = gradient + decay_rate * weight
    new_moment = MOMENTUM * moment + step_rate * step_grad
    new_weight = weight - (step_rate * step_grad + MOMENTUM * new_moment)
    retain = min(0.999, (1.0 + STEP) / (10.0 + STEP))
    new_average = retain * average + (1.0 - retain) * new_weight
    return jnp.stack([new_moment, new_weight, new_average])

def attention(queries, keys_low, values_low, tok_slot, tok_level):
    group_len = queries.shape[0]
    block_size = math.gcd(group_len, 512)
    head_dim = queries.shape[1] // HEADS
    key_heads = keys_low.reshape(group_len, HEADS, head_dim)
    value_heads = values_low.reshape(group_len, HEADS, head_dim)

    def per_block(inputs):
        query_block, slot_block, level_block = inputs
        raw_scores = low_back(jnp.einsum('qhd,khd->hqk', query_block, key_heads, precision=HIGHEST_PRECISION))
        allowed = (slot_block[:, None] == tok_slot[None, :]) & (tok_level[None, :] <= level_block[:, None])
        scores = jnp.where(allowed[None], raw_scores, MASKED)
        attn_probs = low(jnp.exp(scores - jax.nn.logsumexp(scores, axis=-1, keepdims=True)))
        return jnp.einsum('hqk,khd->qhd', attn_probs, value_heads, precision=HIGHEST_PRECISION)
    blocks = group_len // block_size
    result = lax.map(jax.checkpoint(per_block), (queries.reshape(blocks, block_size, HEADS, head_dim), tok_slot.reshape(blocks, block_size), tok_level.reshape(blocks, block_size)))
    return result.reshape(group_len, HEADS * head_dim)

def block_forward(weights, embed_w, vectors, values, cond_rows, lengths):
    w_qkv, w_out, w_up, w_down, w_ada = weights
    group_len = values.shape[1]
    positions = jnp.arange(group_len, dtype=jnp.int32)
    tok_slot, tok_level, segment = layout(lengths, positions, group_len)
    live_rows = (tok_slot < lengths.shape[0]).astype(values.dtype)[:, None]
    left_ok = ((layout(lengths, positions - 1, group_len)[2] == segment) & (positions > 0)).astype(values.dtype)
    right_ok = ((layout(lengths, positions + 1, group_len)[2] == segment) & (positions < group_len - 1)).astype(values.dtype)
    padded = jnp.pad(values, ((0, 0), (1, 1)))
    smooth = smooth_map(values, left_ok, right_ok, padded[:, :-2], padded[:, 2:])
    x_zero = jnp.dot(smooth.T, embed_w, precision=HIGHEST_PRECISION) + vectors[6]
    silu_cond = low(jax.nn.silu(cond_rows))
    ada_all = jnp.dot(silu_cond, w_ada, precision=HIGHEST_PRECISION) + vectors[:6].reshape(-1)
    one_hot = (tok_slot[:, None] == jnp.arange(lengths.shape[0], dtype=jnp.int32)[None, :]).astype(values.dtype)
    token_ada = jnp.dot(one_hot, ada_all, precision=HIGHEST_PRECISION)
    gate_one, gate_two, scale_one, scale_two, shift_one, shift_two = jnp.split(token_ada, 6, axis=1)
    h_one = low(pre_norm(x_zero, scale_one, shift_one))
    projected = low_back(jnp.dot(h_one, w_qkv, precision=HIGHEST_PRECISION))
    q_unit, k_unit, v_full = split_heads(projected, vectors[7])
    attended = low(low_back(attention(low(q_unit), low(k_unit), low(v_full), tok_slot, tok_level)))
    attn_proj = low_back(jnp.dot(attended, w_out, precision=HIGHEST_PRECISION))
    x_one = x_zero + gate_one * attn_proj
    h_two = low(pre_norm(x_one, scale_two, shift_two))
    hidden_pre = low_back(jnp.dot(h_two, w_up, precision=HIGHEST_PRECISION))
    act_low = low(jax.nn.gelu(hidden_pre, approximate=True))
    mlp_out = low_back(jnp.dot(act_low, w_down, precision=HIGHEST_PRECISION))
    x_two = x_one + gate_two * mlp_out
    return x_two * live_rows

def reference(feature_map, condition, item_lengths, cotangent, code_book, qkv_state, out_state, up_state, down_state, ada_state, embed_state, vector_state):
    states = (qkv_state, out_state, up_state, down_state, ada_state)
    weights = tuple((stacked[1].astype(jnp.bfloat16).astype(jnp.float32) for stacked in states))
    embed_w = embed_state[1]
    vectors = vector_state[1]
    group_len = N_WIDE * TOK_DEV
    map_groups = feature_map.reshape(CODE_DIM, GROUPS, group_len).transpose(1, 0, 2)
    cond_groups = condition.reshape(GROUPS, SLOTS, D)
    cot_groups = cotangent.astype(jnp.float32).reshape(GROUPS, group_len, D)
    book_f32 = code_book.astype(jnp.float32)

    def per_group(totals, inputs):
        values, cond_rows, lengths, cot_rows = inputs

        def forward(weight_set, embed_in, vector_in, map_in):
            return block_forward(weight_set, embed_in, vector_in, map_in, cond_rows, lengths)
        output, pullback = jax.vjp(forward, weights, embed_w, vectors, values)
        gradients = pullback(cot_rows)
        out_low = output.astype(jnp.bfloat16)
        logits = jnp.dot(out_low.astype(jnp.float32), book_f32.T, precision=HIGHEST_PRECISION)
        positions = jnp.arange(group_len, dtype=jnp.int32)
        live_rows = (layout(lengths, positions, group_len)[0] < SLOTS).astype(jnp.float32)[:, None]
        code_mass = lax.optimization_barrier(jnp.sum(jax.nn.softmax(logits, axis=-1) * live_rows, axis=0))
        totals = jax.tree.map(jnp.add, totals, (gradients[0], gradients[1], gradients[2], code_mass))
        return (totals, (out_low, gradients[3]))
    start_totals = (jax.tree.map(jnp.zeros_like, weights), jnp.zeros_like(embed_w), jnp.zeros_like(vectors), jnp.zeros((CODES,), jnp.float32))
    totals, stacked_out = lax.scan(per_group, start_totals, (map_groups, cond_groups, item_lengths, cot_groups))
    weight_grads, embed_grad, vector_grad, code_mass = totals
    block_out = stacked_out[0].reshape(TOKENS, D)
    map_grad = stacked_out[1].transpose(1, 0, 2).reshape(CODE_DIM, TOKENS)
    histogram = code_mass * (CODES / TOKENS)
    root_tokens = math.sqrt(TOKENS)
    spreads = (D ** (-0.5), (D // 16) ** (-0.5), D ** (-0.5), FF ** (-0.5), D ** (-0.5))
    new_states = tuple((nesterov(stacked, gradient, BASE_RATE * spread_w / (factor_g * root_tokens), WEIGHT_DECAY) for stacked, gradient, spread_w, factor_g in zip(states, weight_grads, spreads, GRAD_FACTORS)))
    embed_new = nesterov(embed_state, embed_grad, BASE_RATE * CODE_DIM ** (-0.5) / (EMBED_FACTOR * root_tokens), 0.0)
    vector_new = nesterov(vector_state, vector_grad, VECTOR_RATE / root_tokens, 0.0)
    return (block_out, map_grad, histogram, new_states[0], new_states[0][1].astype(jnp.bfloat16), new_states[1], new_states[1][1].astype(jnp.bfloat16), new_states[2], new_states[2][1].astype(jnp.bfloat16), new_states[3], new_states[3][1].astype(jnp.bfloat16), new_states[4], new_states[4][1].astype(jnp.bfloat16), embed_new, vector_new, vector_grad[7])
```

```python
import functools
import math

import jax
import jax.numpy as jnp
import numpy as np
from jax import lax
from jax.experimental import pallas as pl
from jax.experimental.pallas import tpu as pltpu
from jax.sharding import PartitionSpec as P

HEADS = 16
LEVELS = 10
STEP = 7


SHORT_SIDES = (1, 2, 3, 4, 5, 6, 8, 10, 13, 16)
LONG_SIDES = (1, 2, 3, 4, 6, 9, 13, 18, 24, 32)
MASKED = -1e30
NORM_EPS = 1e-06
MOMENTUM = 0.9
WEIGHT_DECAY = 0.05
BASE_RATE = 0.37
VECTOR_RATE = 0.22
GRAD_FACTORS = (0.15, 0.1, 0.3, 0.35, 0.3)
EMBED_FACTOR = 0.6
HIGHEST_PRECISION = lax.Precision.HIGHEST


def padded(cells, sides, width):
    for axis, dim in sides:
        count = lax.axis_size(axis)
        ends = count - 1
        head = lax.slice_in_dim(cells, 0, width, axis=dim)
        tail = lax.slice_in_dim(cells, cells.shape[dim] - width, cells.shape[dim], axis=dim)
        cells = jnp.concatenate(
            [
                lax.ppermute(tail, axis, [(i, (i + 1) % count) for i in range(ends)]),
                cells,
                lax.ppermute(head, axis, [((i + 1) % count, i) for i in range(ends)]),
            ],
            axis=dim,
        )
    return cells


def layout(lengths, positions, group_len):
    short_sq = jnp.array([side * side for side in SHORT_SIDES[:LEVELS]], jnp.int32)
    long_sq = jnp.array([side * side for side in LONG_SIDES[:LEVELS]], jnp.int32)
    short_total = sum((side * side for side in SHORT_SIDES[:LEVELS]))
    long_total = sum((side * side for side in LONG_SIDES[:LEVELS]))
    slot_count = lengths.shape[0]
    counts = jnp.where(
        lengths[None, :] == long_total,
        long_sq[:, None],
        jnp.where(lengths[None, :] == short_total, short_sq[:, None], 0),
    )
    unused = group_len - jnp.sum(lengths)
    ordered = jnp.concatenate([counts.reshape(-1), unused[None]])
    boundary = jnp.cumsum(ordered)
    segment = jnp.sum((boundary[None, :] <= positions[:, None]).astype(jnp.int32), axis=1)
    segment = jnp.minimum(segment, ordered.shape[0] - 1)
    unused_id = slot_count * LEVELS
    tok_level = jnp.where(segment >= unused_id, 0, segment // slot_count)
    tok_slot = jnp.where(segment >= unused_id, slot_count, segment % slot_count)
    return (tok_slot, tok_level, segment)


def pre_norm(inputs, scaling, offset_add):
    row_mean = jnp.mean(inputs, axis=-1, keepdims=True)
    centred = inputs - row_mean
    spread = jnp.mean(centred * centred, axis=-1, keepdims=True)
    return centred * lax.rsqrt(spread + NORM_EPS) * (1.0 + scaling) + offset_add


def unit_heads(inputs):
    shaped = inputs.reshape(inputs.shape[0], HEADS, -1)
    shaped = shaped * lax.rsqrt(jnp.sum(shaped * shaped, axis=-1, keepdims=True) + NORM_EPS)
    return shaped.reshape(inputs.shape)


def split_heads(projected, q_gain):
    queries, key_part, value_part = jnp.split(projected, 3, axis=1)
    head_scale = math.sqrt(queries.shape[1] // HEADS)
    return (unit_heads(queries) * (head_scale * (1.0 + q_gain)), unit_heads(key_part), value_part)


def smooth_map(values, left_ok, right_ok, before, following):
    return (left_ok * before + 2.0 * values + right_ok * following) / (2.0 + left_ok + right_ok)


def nesterov(stacked, gradient, step_rate, decay_rate):
    moment, weight, average = (stacked[0], stacked[1], stacked[2])
    step_grad = gradient + decay_rate * weight
    new_moment = MOMENTUM * moment + step_rate * step_grad
    new_weight = weight - (step_rate * step_grad + MOMENTUM * new_moment)
    retain = min(0.999, (1.0 + STEP) / (10.0 + STEP))
    new_average = retain * average + (1.0 - retain) * new_weight
    return jnp.stack([new_moment, new_weight, new_average])


def contract_rows(left_side, right_side, precision=None):
    return lax.dot_general(
        left_side,
        right_side,
        (((0,), (0,)), ((), ())),
        precision=precision,
        preferred_element_type=jnp.float32,
    )


def against(left_side, right_side):
    return lax.dot_general(
        left_side, right_side, (((1,), (1,)), ((), ())), preferred_element_type=jnp.float32
    )


def shards(
    feature_map,
    condition,
    item_lengths,
    cotangent,
    code_book,
    qkv_state,
    out_state,
    up_state,
    down_state,
    ada_state,
    embed_state,
    vector_state,
):
    tok_rows = cotangent.shape[0]
    model_width = cotangent.shape[1]
    head_dim = model_width // HEADS
    wide_count = lax.axis_size("wide")
    group_len = tok_rows * wide_count
    tokens_all = lax.axis_size("dp") * group_len
    lengths = item_lengths[0]
    slot_count = lengths.shape[0]
    positions = lax.axis_index("wide") * tok_rows + jnp.arange(tok_rows, dtype=jnp.int32)
    tok_slot, tok_level, segment = layout(lengths, positions, group_len)
    live_rows = (tok_slot < slot_count).astype(jnp.float32)[:, None]
    left_ok = ((layout(lengths, positions - 1, group_len)[2] == segment) & (positions > 0)).astype(
        jnp.float32
    )
    right_ok = (
        (layout(lengths, positions + 1, group_len)[2] == segment) & (positions < group_len - 1)
    ).astype(jnp.float32)
    rimmed = padded(feature_map, (("wide", 1),), 1)
    smooth = smooth_map(feature_map, left_ok, right_ok, rimmed[:, :-2], rimmed[:, 2:])
    states = (qkv_state, out_state, up_state, down_state, ada_state)
    masters = tuple((stacked[1].astype(jnp.bfloat16) for stacked in states))
    columns = (
        lax.all_gather(masters[0], "wide", axis=1, tiled=True),
        lax.all_gather(masters[1], "wide", axis=1, tiled=True),
        lax.all_gather(masters[2], "wide", axis=1, tiled=True),
        lax.all_gather(masters[3], "wide", axis=1, tiled=True),
    )
    ada_piece = lax.all_gather(masters[4], "wide", axis=1, tiled=True)
    w_qkv, w_out, w_up, w_down, w_ada = (
        lax.all_gather(columns[0], "dp", axis=0, tiled=True),
        lax.all_gather(columns[1], "dp", axis=0, tiled=True),
        lax.all_gather(columns[2], "dp", axis=0, tiled=True),
        lax.all_gather(columns[3], "dp", axis=0, tiled=True),
        lax.all_gather(ada_piece, "dp", axis=0, tiled=True),
    )
    embed_w = embed_state[1]
    vectors = vector_state[1]
    x_zero = (
        lax.dot_general(smooth, embed_w, (((0,), (0,)), ((), ())), precision=HIGHEST_PRECISION)
        + vectors[6]
    )
    silu_cond = jax.nn.silu(condition).astype(jnp.bfloat16)
    ada_product = jnp.dot(silu_cond, w_ada, preferred_element_type=jnp.float32)
    ada_all = ada_product + vectors[:6].reshape(-1)
    one_hot = (tok_slot[:, None] == jnp.arange(slot_count, dtype=jnp.int32)[None, :]).astype(
        jnp.float32
    )
    token_ada = jnp.dot(one_hot, ada_all, precision=HIGHEST_PRECISION)
    gate_one, gate_two, scale_one, scale_two, shift_one, shift_two = jnp.split(token_ada, 6, axis=1)
    h_one_low = pre_norm(x_zero, scale_one, shift_one).astype(jnp.bfloat16)
    projected = jnp.dot(h_one_low, w_qkv, preferred_element_type=jnp.float32)
    (q_unit, k_unit, v_full), heads_back = jax.vjp(split_heads, projected, vectors[7])
    queries = q_unit.astype(jnp.bfloat16)
    keys_low = k_unit.astype(jnp.bfloat16)
    values_low = v_full.astype(jnp.bfloat16)
    query_heads = queries.reshape(tok_rows, HEADS, head_dim)

    def blockwise(advance, running, pieces, first_row):
        key_count = pieces[0].shape[0]
        block_size = math.gcd(key_count, 1024)

        def per_block(current, offset):
            key_part = tuple(
                (lax.dynamic_slice_in_dim(piece_arr, offset, block_size, 0) for piece_arr in pieces)
            )
            first_key = first_row + offset
            k_slot, k_level, _ = layout(
                lengths, first_key + jnp.arange(block_size, dtype=jnp.int32), group_len
            )
            allowed = (tok_slot[:, None] == k_slot[None, :]) & (
                k_level[None, :] <= tok_level[:, None]
            )
            current = advance(current, key_part, allowed, first_key)
            return (current, None)

        offsets = jnp.arange(key_count // block_size, dtype=jnp.int32) * block_size
        return lax.scan(per_block, running, offsets)[0]

    def scores_of(key_block, allowed):
        raw_scores = jnp.einsum(
            "qhd,khd->hqk",
            query_heads,
            key_block.reshape(-1, HEADS, head_dim),
            preferred_element_type=jnp.float32,
        )
        return jnp.where(allowed[None], raw_scores, MASKED)

    def stats_step(running, key_part, allowed, first_key):
        scores = scores_of(key_part[0], allowed)
        top_score, exp_total = running
        new_top = jnp.maximum(top_score, jnp.max(scores, axis=-1, keepdims=True))
        exp_total = exp_total * jnp.exp(top_score - new_top) + jnp.sum(
            jnp.exp(scores - new_top), axis=-1, keepdims=True
        )
        return (new_top, exp_total)

    kv_rows = (
        lax.all_gather(keys_low, "wide", axis=0, tiled=True),
        lax.all_gather(values_low, "wide", axis=0, tiled=True),
    )
    start_stats = (
        jnp.full((HEADS, tok_rows, 1), MASKED, jnp.float32),
        jnp.zeros((HEADS, tok_rows, 1), jnp.float32),
    )
    top_score, exp_total = blockwise(stats_step, start_stats, kv_rows, 0)
    log_total = top_score + jnp.log(exp_total)

    def value_step(running, key_part, allowed, first_key):
        attn_probs = jnp.exp(scores_of(key_part[0], allowed) - log_total).astype(jnp.bfloat16)
        return running + jnp.einsum(
            "hqk,khd->qhd",
            attn_probs,
            key_part[1].reshape(-1, HEADS, head_dim),
            preferred_element_type=jnp.float32,
        )

    attended = blockwise(
        value_step, jnp.zeros((tok_rows, HEADS, head_dim), jnp.float32), kv_rows, 0
    )
    attn_low = attended.reshape(tok_rows, model_width).astype(jnp.bfloat16)
    attn_proj = jnp.dot(attn_low, w_out, preferred_element_type=jnp.float32)
    x_one = x_zero + gate_one * attn_proj
    h_two_low = pre_norm(x_one, scale_two, shift_two).astype(jnp.bfloat16)
    hidden_pre = jnp.dot(h_two_low, w_up, preferred_element_type=jnp.float32)
    act_low = jax.nn.gelu(hidden_pre, approximate=True).astype(jnp.bfloat16)
    mlp_out = jnp.dot(act_low, w_down, preferred_element_type=jnp.float32)
    x_two = x_one + gate_two * mlp_out
    block_out = (x_two * live_rows).astype(jnp.bfloat16)
    logits = against(block_out, code_book)
    code_mass = jnp.sum(jax.nn.softmax(logits, axis=-1) * live_rows, axis=0)
    g_two = cotangent.astype(jnp.float32) * live_rows
    d_mlp = (gate_two * g_two).astype(jnp.bfloat16)
    d_gate_two = g_two * mlp_out
    dw_down = contract_rows(act_low, d_mlp)
    d_act = against(d_mlp, w_down)
    _, gelu_back = jax.vjp(lambda inputs: jax.nn.gelu(inputs, approximate=True), hidden_pre)
    d_hidden = gelu_back(d_act)[0].astype(jnp.bfloat16)
    dw_up = contract_rows(h_two_low, d_hidden)
    d_h_two = against(d_hidden, w_up)
    _, norm_back_two = jax.vjp(pre_norm, x_one, scale_two, shift_two)
    d_x_one, d_scale_two, d_shift_two = norm_back_two(d_h_two)
    d_x_one = d_x_one + g_two
    d_attn = (gate_one * d_x_one).astype(jnp.bfloat16)
    d_gate_one = d_x_one * attn_proj
    dw_out = contract_rows(attn_low, d_attn)
    grad_flat = against(d_attn, w_out).astype(jnp.bfloat16)
    grad_heads = grad_flat.reshape(tok_rows, HEADS, head_dim)

    def delta_step(running, key_part, allowed, first_key):
        attn_probs = jnp.exp(scores_of(key_part[0], allowed) - log_total)
        d_probs = jnp.einsum(
            "qhd,khd->hqk",
            grad_heads,
            key_part[1].reshape(-1, HEADS, head_dim),
            preferred_element_type=jnp.float32,
        )
        return running + jnp.sum(attn_probs * d_probs, axis=-1, keepdims=True)

    row_delta = blockwise(delta_step, jnp.zeros((HEADS, tok_rows, 1), jnp.float32), kv_rows, 0)

    def grad_step(running, key_part, allowed, first_key):
        d_query, d_keys, d_values = running
        key_heads = key_part[0].reshape(-1, HEADS, head_dim)
        value_heads = key_part[1].reshape(-1, HEADS, head_dim)
        block_rows = key_part[0].shape[0]
        attn_probs = jnp.exp(scores_of(key_part[0], allowed) - log_total)
        d_probs = jnp.einsum(
            "qhd,khd->hqk", grad_heads, value_heads, preferred_element_type=jnp.float32
        )
        d_scores = (attn_probs * (d_probs - row_delta)).astype(jnp.bfloat16)
        d_query = d_query + jnp.einsum(
            "hqk,khd->qhd", d_scores, key_heads, preferred_element_type=jnp.float32
        )
        key_grad = jnp.einsum(
            "hqk,qhd->khd", d_scores, query_heads, preferred_element_type=jnp.float32
        )
        value_grad = jnp.einsum(
            "hqk,qhd->khd",
            attn_probs.astype(jnp.bfloat16),
            grad_heads,
            preferred_element_type=jnp.float32,
        )
        key_sum = lax.dynamic_slice_in_dim(d_keys, first_key, block_rows, 0) + key_grad.reshape(
            block_rows, model_width
        )
        value_sum = lax.dynamic_slice_in_dim(
            d_values, first_key, block_rows, 0
        ) + value_grad.reshape(block_rows, model_width)
        d_keys = lax.dynamic_update_slice_in_dim(d_keys, key_sum, first_key, 0)
        d_values = lax.dynamic_update_slice_in_dim(d_values, value_sum, first_key, 0)
        return (d_query, d_keys, d_values)

    grad_init = (
        jnp.zeros((tok_rows, HEADS, head_dim), jnp.float32),
        jnp.zeros((group_len, model_width), jnp.float32),
        jnp.zeros((group_len, model_width), jnp.float32),
    )
    d_query, d_keys, d_values = blockwise(grad_step, grad_init, kv_rows, 0)
    d_keys_own, d_values_own = (
        lax.psum_scatter(
            d_keys.astype(jnp.bfloat16), "wide", scatter_dimension=0, tiled=True
        ).astype(jnp.float32),
        lax.psum_scatter(
            d_values.astype(jnp.bfloat16), "wide", scatter_dimension=0, tiled=True
        ).astype(jnp.float32),
    )
    d_projected, d_gain = heads_back(
        (d_query.reshape(tok_rows, model_width), d_keys_own, d_values_own)
    )
    d_projected_low = d_projected.astype(jnp.bfloat16)
    dw_qkv = contract_rows(h_one_low, d_projected_low)
    d_h_one = against(d_projected_low, w_qkv)
    _, norm_back_one = jax.vjp(pre_norm, x_zero, scale_one, shift_one)
    d_x_zero, d_scale_one, d_shift_one = norm_back_one(d_h_one)
    d_x_zero = d_x_zero + d_x_one
    d_token_ada = jnp.concatenate(
        [d_gate_one, d_gate_two, d_scale_one, d_scale_two, d_shift_one, d_shift_two], axis=1
    )
    d_ada_all = contract_rows(one_hot, d_token_ada, HIGHEST_PRECISION)
    d_smooth = lax.dot_general(
        embed_w, d_x_zero, (((1,), (1,)), ((), ())), precision=HIGHEST_PRECISION
    )
    d_embed = lax.dot_general(
        smooth, d_x_zero, (((1,), (0,)), ((), ())), precision=HIGHEST_PRECISION
    )
    d_vectors = jnp.concatenate(
        [
            jnp.sum(d_ada_all, axis=0).reshape(6, model_width),
            jnp.sum(d_x_zero, axis=0)[None],
            d_gain[None],
        ],
        axis=0,
    )
    grad_share = d_smooth / (2.0 + left_ok + right_ok)
    rim_share = padded(grad_share, (("wide", 1),), 1)
    map_grad = 2.0 * grad_share + left_ok * rim_share[:, :-2] + right_ok * rim_share[:, 2:]
    d_embed_all, d_vectors_all, mass_all = lax.psum((d_embed, d_vectors, code_mass), ("dp", "wide"))
    histogram = mass_all * (code_book.shape[0] / tokens_all)
    ada_term = contract_rows(silu_cond.astype(jnp.float32), d_ada_all, HIGHEST_PRECISION)
    split_cols = (
        lax.psum_scatter(
            dw_qkv.astype(jnp.bfloat16), "wide", scatter_dimension=1, tiled=True
        ).astype(jnp.float32),
        lax.psum_scatter(
            dw_out.astype(jnp.bfloat16), "wide", scatter_dimension=1, tiled=True
        ).astype(jnp.float32),
        lax.psum_scatter(
            dw_up.astype(jnp.bfloat16), "wide", scatter_dimension=1, tiled=True
        ).astype(jnp.float32),
        lax.psum_scatter(
            dw_down.astype(jnp.bfloat16), "wide", scatter_dimension=1, tiled=True
        ).astype(jnp.float32),
        lax.psum_scatter(
            ada_term.astype(jnp.bfloat16), "wide", scatter_dimension=1, tiled=True
        ).astype(jnp.float32),
    )
    ada_cols = split_cols[4]
    owned_grads = (
        lax.psum_scatter(
            split_cols[0].astype(jnp.bfloat16), "dp", scatter_dimension=0, tiled=True
        ).astype(jnp.float32),
        lax.psum_scatter(
            split_cols[1].astype(jnp.bfloat16), "dp", scatter_dimension=0, tiled=True
        ).astype(jnp.float32),
        lax.psum_scatter(
            split_cols[2].astype(jnp.bfloat16), "dp", scatter_dimension=0, tiled=True
        ).astype(jnp.float32),
        lax.psum_scatter(
            split_cols[3].astype(jnp.bfloat16), "dp", scatter_dimension=0, tiled=True
        ).astype(jnp.float32),
        lax.psum_scatter(
            ada_cols.astype(jnp.bfloat16), "dp", scatter_dimension=0, tiled=True
        ).astype(jnp.float32),
    )
    root_tokens = math.sqrt(tokens_all)
    spreads = (
        model_width ** (-0.5),
        (model_width // 16) ** (-0.5),
        model_width ** (-0.5),
        w_up.shape[1] ** (-0.5),
        model_width ** (-0.5),
    )
    new_states = tuple(
        (
            nesterov(
                stacked, gradient, BASE_RATE * spread_w / (factor_g * root_tokens), WEIGHT_DECAY
            )
            for stacked, gradient, spread_w, factor_g in zip(
                states, owned_grads, spreads, GRAD_FACTORS
            )
        )
    )
    embed_new = nesterov(
        embed_state,
        d_embed_all,
        BASE_RATE * embed_w.shape[0] ** (-0.5) / (EMBED_FACTOR * root_tokens),
        0.0,
    )
    vector_new = nesterov(vector_state, d_vectors_all, VECTOR_RATE / root_tokens, 0.0)
    return (
        block_out,
        map_grad,
        histogram,
        new_states[0],
        new_states[0][1].astype(jnp.bfloat16),
        new_states[1],
        new_states[1][1].astype(jnp.bfloat16),
        new_states[2],
        new_states[2][1].astype(jnp.bfloat16),
        new_states[3],
        new_states[3][1].astype(jnp.bfloat16),
        new_states[4],
        new_states[4][1].astype(jnp.bfloat16),
        embed_new,
        vector_new,
        d_vectors_all[7],
    )


MESH_ID = pl.DeviceIdType.MESH
ANY = pl.BlockSpec(memory_space=pl.ANY)
VM = pl.BlockSpec(memory_space=pltpu.VMEM)
VMEM_BYTES = 56 * 1024 * 1024
LANES = 128
HALF_LANES = 64
BIG = 1e30


def nt(left_side, right_side):
    return lax.dot_general(
        left_side, right_side, (((1,), (1,)), ((), ())), preferred_element_type=jnp.float32
    )


def nn(left_side, right_side):
    return lax.dot_general(
        left_side, right_side, (((1,), (0,)), ((), ())), preferred_element_type=jnp.float32
    )


def entry_barrier(peers):
    barrier = pltpu.get_barrier_semaphore()
    for peer in peers:
        pl.semaphore_signal(barrier, inc=1, device_id=peer, device_id_type=MESH_ID)
    pl.semaphore_wait(barrier, len(peers))


def place():
    core, wide = lax.axis_index("dp"), lax.axis_index("wide")
    return core, wide // 4, wide % 4


def at_dev(core, z, yx):
    return (core, z * 4 + yx)


def gather_kernel(count, has_small, *refs):
    shards = refs[:count]
    small = refs[count] if has_small else None
    base = count + has_small
    fulls = refs[base : base + count]
    small_out = refs[base + count] if has_small else None
    sems = refs[base + count + has_small :]
    send_x, send_y, send_z, send_s, recv_i, recv_s, local = sems[:7]
    core, z, yx = place()
    x_dev, y_dev = at_dev(core, z, yx ^ 1), at_dev(core, z, yx ^ 2)
    sib = at_dev(1 - core, z, yx)
    z_devs = [None] + [at_dev(core, lax.rem(z + r, 4), yx) for r in (1, 2, 3)]
    wide = z * 4 + yx
    if has_small:
        everyone = [(core, wide ^ r) for r in range(1, 16)]
        entry_barrier(everyone + [sib])
    else:
        entry_barrier([x_dev, y_dev, sib] + z_devs[1:])
    pending = []

    def spot(full, dz, d):
        return full.at[core, lax.rem(z + dz, 4), yx ^ d]

    def push(i, dz, d, src, sem, device, there):
        copy = pltpu.make_async_remote_copy(
            src_ref=src,
            dst_ref=spot(fulls[i], dz, d),
            send_sem=sem,
            recv_sem=there,
            device_id=device,
            device_id_type=MESH_ID,
        )
        copy.start()
        pending.append(copy)

    def to_x(i, dz, d, src):
        push(i, dz, d, src, send_x.at[i, dz, d], x_dev, recv_i.at[i, dz, d ^ 1])

    def to_y(i, dz, d, src):
        push(i, dz, d, src, send_y.at[i, dz, d], y_dev, recv_i.at[i, dz, d ^ 2])

    def to_s(i, dz, d, src):
        push(i, dz, d, src, send_s.at[i, dz, d], sib, recv_s.at[i, dz, d])

    def arrive(ref, sem):
        pltpu.make_async_copy(ref, ref, sem).wait()

    def got(i, dz, d):
        ref = spot(fulls[i], dz, d)
        arrive(ref, recv_i.at[i, dz, d])
        return ref

    small_copies = []
    if has_small:
        small_send, small_recv, small_local = sems[7:]
        own = pltpu.make_async_copy(small, small_out.at[wide], small_local)
        own.start()
        small_copies.append(own)
        for r in range(1, 16):
            copy = pltpu.make_async_remote_copy(
                src_ref=small,
                dst_ref=small_out.at[wide],
                send_sem=small_send.at[r],
                recv_sem=small_recv.at[r],
                device_id=(core, wide ^ r),
                device_id_type=MESH_ID,
            )
            copy.start()
            small_copies.append(copy)
    locals_ = []
    for i in range(count):
        src = shards[i]
        for r in (1, 3, 2):
            push(i, 0, 0, src, send_z.at[i, r], z_devs[r], recv_i.at[i, (4 - r) % 4, 0])
        to_x(i, 0, 0, src)
        to_y(i, 0, 0, src)
        to_s(i, 0, 0, src)
        copy = pltpu.make_async_copy(src, spot(fulls[i], 0, 0), local.at[i])
        copy.start()
        locals_.append(copy)
    for i in range(count):
        ref = got(i, 0, 1)
        to_y(i, 0, 1, ref)
        to_s(i, 0, 1, ref)
        ref = got(i, 0, 2)
        to_s(i, 0, 2, ref)
    for i in range(count):
        for dz in (1, 3, 2):
            ref = got(i, dz, 0)
            to_x(i, dz, 0, ref)
            to_y(i, dz, 0, ref)
            to_s(i, dz, 0, ref)
        for dz in (1, 3, 2):
            ref = got(i, dz, 1)
            if dz == 1:
                to_y(i, dz, 1, ref)
            to_s(i, dz, 1, ref)
            ref = got(i, dz, 2)
            if dz != 1:
                to_x(i, dz, 2, ref)
            to_s(i, dz, 2, ref)
    for i in range(count):
        for dz in (0, 1, 3, 2):
            to_s(i, dz, 3, got(i, dz, 3))
    for i in range(count):
        for dz in range(4):
            for d in range(4):
                ref = fulls[i].at[1 - core, lax.rem(z + dz, 4), yx ^ d]
                arrive(ref, recv_s.at[i, dz, d])
    for copy in pending:
        copy.wait_send()
    for copy in locals_ + small_copies:
        copy.wait()


def gather_weights(shards, small, call_id):
    count, has_small = len(shards), int(small is not None)
    dma = pltpu.SemaphoreType.DMA
    scratch = [
        dma((count, 4, 4)),
        dma((count, 4, 4)),
        dma((count, 4)),
        dma((count, 4, 4)),
        dma((count, 4, 4)),
        dma((count, 4, 4)),
        dma((count,)),
    ]
    outs = [jax.ShapeDtypeStruct((2, 4, 4) + s.shape, s.dtype) for s in shards]
    args = list(shards)
    if has_small:
        scratch += [dma((16,)), dma((16,)), dma]
        outs.append(jax.ShapeDtypeStruct((16,) + small.shape, small.dtype))
        args.append(small)
    return pl.pallas_call(
        functools.partial(gather_kernel, count, has_small),
        out_shape=outs,
        in_specs=[ANY] * len(args),
        out_specs=[ANY] * len(outs),
        scratch_shapes=scratch,
        compiler_params=pltpu.CompilerParams(
            collective_id=call_id, has_side_effects=True, vmem_limit_bytes=VMEM_BYTES
        ),
    )(*args)


def scatter_kernel(count, *refs):
    parts = refs[:count]
    outs = refs[count : 2 * count]
    bufs = refs[2 * count : 2 * count + 8 * count]
    sems = refs[2 * count + 8 * count :]
    send, recv = sems
    core, z, yx = place()
    x_dev, y_dev = at_dev(core, z, yx ^ 1), at_dev(core, z, yx ^ 2)
    z_devs = [None] + [at_dev(core, lax.rem(z + r, 4), yx) for r in (1, 2, 3)]
    entry_barrier([x_dev, y_dev] + z_devs[1:])
    pending = []

    def push(i, slot, src, dst, device):
        copy = pltpu.make_async_remote_copy(
            src_ref=src,
            dst_ref=dst,
            send_sem=send.at[i, slot],
            recv_sem=recv.at[i, slot],
            device_id=device,
            device_id_type=MESH_ID,
        )
        copy.start()
        pending.append(copy)
        return copy

    def part(i, dz, d):
        return parts[i].at[lax.rem(z + dz, 4), yx ^ d]

    def f32(ref):
        return ref[...].astype(jnp.float32)

    arrivals = []
    for i in range(count):
        a_x, a_y, r_x, r_y, t_x, t_y, s_z, r_z = bufs[8 * i : 8 * i + 8]
        here = {}
        for j, dz in enumerate((0, 1)):
            here["ax", dz] = push(i, j, part(i, dz, 3), a_x.at[j], x_dev)
        for j, dz in enumerate((2, 3)):
            here["ay", dz] = push(i, 2 + j, part(i, dz, 3), a_y.at[j], y_dev)
        for j, dz in enumerate((0, 1)):
            here["rx", dz] = push(i, 4 + dz, part(i, dz, 1), r_x.at[dz], x_dev)
        for j, dz in enumerate((2, 3)):
            here["ry", dz] = push(i, 8 + dz, part(i, dz, 2), r_y.at[dz], y_dev)
        arrivals.append(here)
    for i in range(count):
        a_x, a_y, r_x, r_y, t_x, t_y, s_z, r_z = bufs[8 * i : 8 * i + 8]
        here = arrivals[i]
        for j, (low, high) in enumerate(((1, 2), (0, 3))):
            here["ax", low].wait_recv()
            t_y[j] = (f32(part(i, low, 2)) + f32(a_x.at[low])).astype(jnp.bfloat16)
            here["ry", low] = push(i, 8 + low, t_y.at[j], r_y.at[low], y_dev)
            here["ay", high].wait_recv()
            t_x[j] = (f32(part(i, high, 1)) + f32(a_y.at[high - 2])).astype(jnp.bfloat16)
            here["rx", high] = push(i, 4 + high, t_x.at[j], r_x.at[high], x_dev)
    for i in range(count):
        a_x, a_y, r_x, r_y, t_x, t_y, s_z, r_z = bufs[8 * i : 8 * i + 8]
        here = arrivals[i]
        for dz in (1, 2, 3, 0):
            here["rx", dz].wait_recv()
            here["ry", dz].wait_recv()
            total = f32(part(i, dz, 0)) + f32(r_x.at[dz]) + f32(r_y.at[dz])
            if dz:
                s_z[dz - 1] = total.astype(jnp.bfloat16)
                here["rz", dz] = push(i, 12 + dz, s_z.at[dz - 1], r_z.at[dz - 1], z_devs[dz])
            else:
                outs[i][...] = total
    for i in range(count):
        r_z = bufs[8 * i + 7]
        for dz in (1, 2, 3):
            arrivals[i]["rz", dz].wait_recv()
        outs[i][...] += f32(r_z.at[0]) + f32(r_z.at[1]) + f32(r_z.at[2])
    for copy in pending:
        copy.wait_send()


def scatter_grads(parts, call_id):
    count = len(parts)
    scratch = []
    for part in parts:
        for depth in (2, 2, 4, 4, 2, 2, 3, 3):
            scratch.append(pltpu.VMEM((depth,) + part.shape[2:], jnp.bfloat16))
    dma = pltpu.SemaphoreType.DMA
    scratch += [dma((count, 16)), dma((count, 16))]
    return pl.pallas_call(
        functools.partial(scatter_kernel, count),
        out_shape=[jax.ShapeDtypeStruct(part.shape[2:], jnp.float32) for part in parts],
        in_specs=[VM] * count,
        out_specs=[VM] * count,
        scratch_shapes=scratch,
        compiler_params=pltpu.CompilerParams(
            collective_id=call_id, has_side_effects=True, vmem_limit_bytes=VMEM_BYTES
        ),
    )(*parts)


def small_kernel(ada_rows, slots, part_ref, ada_ref, all_ref, landed, summed, other, mine, *sems):
    send_a, recv_a, send_b, recv_b, send_s, recv_s = sems
    core, z, yx = place()
    wide = z * 4 + yx
    sib = (1 - core, wide)
    peers = [(core, wide ^ r) for r in range(1, 16)]
    entry_barrier(peers + [sib])
    first = []
    for r in range(1, 16):
        copy = pltpu.make_async_remote_copy(
            src_ref=part_ref.at[wide ^ r],
            dst_ref=landed.at[r],
            send_sem=send_a.at[r],
            recv_sem=recv_a.at[r],
            device_id=peers[r - 1],
            device_id_type=MESH_ID,
        )
        copy.start()
        first.append(copy)
    total = part_ref[wide]
    for r, copy in enumerate(first):
        copy.wait_recv()
        total = total + landed[r + 1]
    summed[...] = total
    swap = pltpu.make_async_remote_copy(
        src_ref=summed,
        dst_ref=other,
        send_sem=send_s,
        recv_sem=recv_s,
        device_id=sib,
        device_id_type=MESH_ID,
    )
    swap.start()
    swap.wait()
    ada_ref[core] = summed[0:ada_rows]
    ada_ref[1 - core] = other[0:ada_rows]
    both = summed[...] + other[...]
    rest = both.shape[0] - ada_rows
    width = ada_rows // slots
    bias = both[0:width]
    for j in range(1, slots):
        bias = bias + both[j * width : (j + 1) * width]
    mine[0:rest] = both[ada_rows:]
    mine[rest : rest + width] = bias
    all_ref[wide] = mine[...]
    second = []
    for r in range(1, 16):
        copy = pltpu.make_async_remote_copy(
            src_ref=mine,
            dst_ref=all_ref.at[wide],
            send_sem=send_b.at[r],
            recv_sem=recv_b.at[r],
            device_id=peers[r - 1],
            device_id_type=MESH_ID,
        )
        copy.start()
        second.append(copy)
    for copy in second:
        copy.wait_recv()
    for copy in first + second:
        copy.wait_send()


def small_sums(parts, ada_rows, slots, call_id):
    rows = parts.shape[1]
    out_rows = rows - ada_rows + ada_rows // slots
    dma = pltpu.SemaphoreType.DMA
    f32 = jnp.float32
    return pl.pallas_call(
        functools.partial(small_kernel, ada_rows, slots),
        out_shape=[
            jax.ShapeDtypeStruct((2, ada_rows, LANES), f32),
            jax.ShapeDtypeStruct((16, out_rows, LANES), f32),
        ],
        in_specs=[VM],
        out_specs=[VM, VM],
        scratch_shapes=[
            pltpu.VMEM((16, rows, LANES), f32),
            pltpu.VMEM((rows, LANES), f32),
            pltpu.VMEM((rows, LANES), f32),
            pltpu.VMEM((out_rows, LANES), f32),
            dma((16,)),
            dma((16,)),
            dma((16,)),
            dma((16,)),
            dma,
            dma,
        ],
        compiler_params=pltpu.CompilerParams(collective_id=call_id, has_side_effects=True),
    )(parts)


def lane_iota(shape):
    return lax.broadcasted_iota(jnp.int32, shape, len(shape) - 1)


def swap_halves(pair):
    return pltpu.roll(pair, HALF_LANES, 1)


def head_sums(values):
    width = values.shape[1]
    rows = lax.broadcasted_iota(jnp.int32, (width, width), 0) // HALF_LANES
    cols = lax.broadcasted_iota(jnp.int32, (width, width), 1) // HALF_LANES
    ones = (rows == cols).astype(jnp.float32)
    return lax.dot_general(
        values,
        ones,
        (((1,), (0,)), ((), ())),
        precision=HIGHEST_PRECISION,
        preferred_element_type=jnp.float32,
    )


def qkv_kernel(h_ref, w_ref, gain_ref, pack_ref, kept_ref):
    tokens, width = h_ref.shape
    half = width // 2
    mid = tokens // 2
    group = 256
    low = jnp.bfloat16
    lane = lane_iota((tokens, LANES))
    lane_mid = lane_iota((mid, LANES))

    def project(first):
        rows = pl.ds(first, group)
        return nt(h_ref[:, :half], w_ref[0, rows, :]) + nt(h_ref[:, half:], w_ref[1, rows, :])

    def step(g, carry):
        first = pl.multiple_of(g * group, group)
        q_all, k_all, v_all = (project(first + part * width) for part in range(3))
        kept_ref[:, pl.ds(first, group)] = q_all
        kept_ref[:, pl.ds(first + width, group)] = k_all
        q_all = q_all * lax.rsqrt(head_sums(q_all * q_all) + NORM_EPS)
        q_all = q_all * (8.0 * (1.0 + gain_ref[:, pl.ds(first, group)]))
        k_all = k_all * lax.rsqrt(head_sums(k_all * k_all) + NORM_EPS)
        for pair in range(group // LANES):
            cols = slice(pair * LANES, (pair + 1) * LANES)
            q, k, v = q_all[:, cols], k_all[:, cols], v_all[:, cols]
            head = g * (group // HALF_LANES) + 2 * pair
            pack_ref[head, 0:tokens, :] = jnp.where(lane < HALF_LANES, q, swap_halves(k)).astype(low)
            pack_ref[head + 1, 0:tokens, :] = jnp.where(lane < HALF_LANES, swap_halves(q), k).astype(low)
            v_a, v_b = v[:mid], v[mid:]
            pack_ref[head, tokens:, :] = jnp.where(lane_mid < HALF_LANES, v_a, swap_halves(v_b)).astype(low)
            pack_ref[head + 1, tokens:, :] = jnp.where(lane_mid < HALF_LANES, swap_halves(v_a), v_b).astype(low)
        return carry

    lax.fori_loop(0, width // group, step, 0)


def project_heads(h_low, w_all, gain):
    tokens, width = h_low.shape
    return pl.pallas_call(
        qkv_kernel,
        out_shape=[
            jax.ShapeDtypeStruct((HEADS, tokens + tokens // 2, LANES), jnp.bfloat16),
            jax.ShapeDtypeStruct((tokens, 2 * width), jnp.float32),
        ],
        in_specs=[VM] * 3,
        out_specs=[VM] * 2,
        compiler_params=pltpu.CompilerParams(vmem_limit_bytes=VMEM_BYTES),
    )(h_low, w_all, gain)


def heads_back_kernel(got_ref, kept_ref, gain_ref, out_ref, gain_grad_ref):
    tokens = kept_ref.shape[0]
    width = kept_ref.shape[1] // 2
    mid = tokens // 2
    f32, low = jnp.float32, jnp.bfloat16
    lane = lane_iota((tokens, LANES))
    lane_mid = lane_iota((mid, LANES))

    def unnormalize(values, grad):
        inverse = lax.rsqrt(head_sums(values * values) + NORM_EPS)
        unit = values * inverse
        return inverse * (grad - unit * head_sums(unit * grad)), unit

    def step(pair, carry):
        cols = pl.ds(pl.multiple_of(pair * LANES, LANES), LANES)
        key_cols = pl.ds(pl.multiple_of(pair * LANES + width, LANES), LANES)
        val_cols = pl.ds(pl.multiple_of(pair * LANES + 2 * width, LANES), LANES)
        even = got_ref[2 * pair].astype(f32)
        odd = got_ref[2 * pair + 1].astype(f32)
        even_qk, odd_qk = even[:tokens], odd[:tokens]
        d_query = jnp.where(lane < HALF_LANES, even_qk, swap_halves(odd_qk))
        d_key = jnp.where(lane < HALF_LANES, swap_halves(even_qk), odd_qk)
        even_v, odd_v = even[tokens:], odd[tokens:]
        out_ref[0:mid, val_cols] = jnp.where(lane_mid < HALF_LANES, even_v, swap_halves(odd_v)).astype(low)
        out_ref[mid:, val_cols] = jnp.where(lane_mid < HALF_LANES, swap_halves(even_v), odd_v).astype(low)
        scaled = d_query * (8.0 * (1.0 + gain_ref[:, cols]))
        d_q, unit = unnormalize(kept_ref[:, cols], scaled)
        gain_grad_ref[:, cols] = jnp.sum(d_query * unit, axis=0, keepdims=True) * 8.0
        out_ref[:, cols] = d_q.astype(low)
        out_ref[:, key_cols] = unnormalize(kept_ref[:, key_cols], d_key)[0].astype(low)
        return carry

    lax.fori_loop(0, width // LANES, step, 0)


def heads_backward(got, kept, gain):
    tokens, width = kept.shape[0], kept.shape[1] // 2
    return pl.pallas_call(
        heads_back_kernel,
        out_shape=[
            jax.ShapeDtypeStruct((tokens, 3 * width), jnp.bfloat16),
            jax.ShapeDtypeStruct((1, width), jnp.float32),
        ],
        in_specs=[VM] * 3,
        out_specs=[VM] * 2,
        compiler_params=pltpu.CompilerParams(vmem_limit_bytes=VMEM_BYTES),
    )(got, kept, gain)


ROWS = 256
CHUNK = 512


def key_limits(group_len, slots):
    short_total = sum(side * side for side in SHORT_SIDES)
    long_total = sum(side * side for side in LONG_SIDES)
    limits = [0] * (group_len // ROWS)
    for longs in range(1, slots + 1):
        for shorts in range(slots - longs + 1):
            total = longs * long_total + shorts * short_total
            if not group_len - short_total < total <= group_len:
                continue
            ends, position = [], 0
            for long_side, short_side in zip(LONG_SIDES, SHORT_SIDES):
                position += longs * long_side**2 + shorts * short_side**2
                ends.append(position)
            ends.append(group_len)
            for block in range(len(limits)):
                last = block * ROWS + ROWS - 1
                seen = min(end for end in ends if end > last)
                limits[block] = max(limits[block], -(-seen // LANES) * LANES)
    return limits


def same_limits(limits):
    groups = []
    for block, limit in enumerate(limits):
        if groups and groups[-1][2] == limit:
            groups[-1][1] = block + 1
        else:
            groups.append([block, block + 1, limit])
    return groups


def chunks_of(limit, step):
    whole = limit // CHUNK

    def body(c, carry):
        step(pl.multiple_of(c * CHUNK, CHUNK), CHUNK)
        return carry

    lax.fori_loop(0, whole, body, 0)
    if limit % CHUNK:
        step(whole * CHUNK, limit % CHUNK)


def fold_lanes(values, combine):
    total = values[:, :LANES]
    for j in range(1, values.shape[1] // LANES):
        total = combine(total, values[:, j * LANES : (j + 1) * LANES])
    return total


def split_three(values):
    high = values.astype(jnp.bfloat16).astype(jnp.float32)
    rest = values - high
    mid = rest.astype(jnp.bfloat16).astype(jnp.float32)
    return high, mid, rest - mid


def lanes_three(lane, first, values, otherwise):
    high, mid, rest = split_three(values)
    return jnp.where(
        lane == first, high, jnp.where(lane == first + 1, mid, jnp.where(lane == first + 2, rest, otherwise))
    )


def attend_kernel(
    groups, got_ref, starts_ref, ends_ref, rule_ref, out_ref, out32_ref, q_ref, k_ref, kt_ref, vt_ref, v_ref, s_ref
):
    owners = got_ref.shape[0]
    tokens = got_ref.shape[1] * 2 // 3
    mid = tokens // 2
    f32, low = jnp.float32, jnp.bfloat16
    two = 2 * tokens
    lane = lane_iota((two, LANES))
    lane_mid = lane_iota((mid, LANES))

    def unpack(pair, carry):
        first = pl.multiple_of(pair * two, two)
        qk = jnp.concatenate([got_ref[2 * pair + e, 0:tokens, :].astype(f32) for e in range(2)], axis=0)
        spot = first + lax.broadcasted_iota(jnp.int32, (two, LANES), 0)
        runs = ((spot >= starts_ref[...]) & (spot < ends_ref[...])).astype(f32)
        barred = nn(runs.astype(low), rule_ref[...])
        rows = pl.ds(first, two)
        q_ref[rows, :] = jnp.where(lane < HALF_LANES, qk, barred).astype(low)
        tail = jnp.where(lane >= LANES - 3, 1.0, runs)
        keys = jnp.where(lane < HALF_LANES, swap_halves(qk), tail)
        k_ref[rows, :] = keys.astype(low)
        kt_ref[:, rows] = keys.T.astype(low)
        ones = ((lane_mid >= HALF_LANES) & (lane_mid < HALF_LANES + 3)).astype(f32)
        pieces = []
        for e in range(2):
            v = got_ref[2 * pair + e, tokens:, :].astype(f32)
            pieces.append(jnp.where(lane_mid < HALF_LANES, v, ones))
            pieces.append(jnp.where(lane_mid < HALF_LANES, swap_halves(v), ones))
        values = jnp.concatenate(pieces, axis=0)
        v_ref[rows, :] = values.astype(low)
        vt_ref[:, rows] = values.T.astype(low)
        return carry

    lax.fori_loop(0, owners // 2, unpack, 0)
    lane_q = lane_iota((ROWS, LANES))

    def query_block(limit, b, carry):
        rows = pl.ds(pl.multiple_of(b * ROWS, ROWS), ROWS)
        q = q_ref[rows, :]

        def score(c, top):
            cols = pl.ds(pl.multiple_of(c * CHUNK, CHUNK), CHUNK)
            s = nn(q, kt_ref[:, cols])
            s_ref[:, cols] = s
            return jnp.maximum(top, fold_lanes(s, jnp.maximum))

        whole, left = limit // CHUNK, limit % CHUNK
        top = lax.fori_loop(0, whole, score, jnp.full((ROWS, LANES), -3e38, f32))
        if left:
            tail = slice(whole * CHUNK, limit)
            s = nn(q, kt_ref[:, tail])
            s_ref[:, tail] = s
            top = jnp.maximum(top, fold_lanes(s, jnp.maximum))
        peak = jnp.max(top, axis=1, keepdims=True)

        def weigh(cols, carry):
            total, acc = carry
            p = jnp.exp(s_ref[:, cols] - peak)
            return total + fold_lanes(p, jnp.add), acc + nn(p.astype(low), v_ref[cols, :])

        zero = jnp.zeros((ROWS, LANES), f32)
        total, acc = lax.fori_loop(
            0,
            whole,
            lambda c, carry: weigh(pl.ds(pl.multiple_of(c * CHUNK, CHUNK), CHUNK), carry),
            (zero, zero),
        )
        if left:
            total, acc = weigh(slice(whole * CHUNK, limit), (total, acc))
        total = jnp.sum(total, axis=1, keepdims=True)
        out32_ref[rows, :] = acc / total
        log_total = peak + jnp.log(total)
        q_ref[rows, :] = lanes_three(lane_q, LANES - 3, -log_total, q.astype(f32)).astype(low)
        return carry

    for first, last, limit in groups:
        lax.fori_loop(first, last, functools.partial(query_block, limit), 0)

    def send_out(w, carry):
        rows = pl.multiple_of(w * tokens, tokens)
        a = out32_ref[pl.ds(rows, mid), :]
        b = out32_ref[pl.ds(rows + mid, mid), :]
        out_ref[w] = jnp.where(lane_mid < HALF_LANES, a, swap_halves(b)).astype(low)
        return carry

    lax.fori_loop(0, owners, send_out, 0)


def attend(got, starts, ends, rule, groups):
    owners, packed, _ = got.shape
    tokens = packed * 2 // 3
    group_len = owners * tokens
    low = jnp.bfloat16
    whole = jax.ShapeDtypeStruct((group_len, LANES), low)
    flipped = jax.ShapeDtypeStruct((LANES, group_len), low)
    return pl.pallas_call(
        functools.partial(attend_kernel, groups),
        out_shape=[
            jax.ShapeDtypeStruct((owners, tokens // 2, LANES), low),
            jax.ShapeDtypeStruct((group_len, LANES), jnp.float32),
            whole,
            whole,
            flipped,
            flipped,
        ],
        in_specs=[VM] * 4,
        out_specs=[VM] * 6,
        scratch_shapes=[
            pltpu.VMEM((group_len, LANES), low),
            pltpu.VMEM((ROWS, group_len), jnp.float32),
        ],
        compiler_params=pltpu.CompilerParams(vmem_limit_bytes=VMEM_BYTES),
    )(got, starts, ends, rule)


def attend_back_kernel(
    groups, got_ref, out32_ref, q_ref, k_ref, kt_ref, vt_ref, pack_ref, g_ref, gt_ref, qt_ref, dq_ref, dkt_ref, dvt_ref
):
    owners = got_ref.shape[0]
    mid = got_ref.shape[1]
    tokens = 2 * mid
    two = 2 * tokens
    f32, low = jnp.float32, jnp.bfloat16
    lane = lane_iota((two, LANES))
    lane_mid = lane_iota((mid, LANES))

    def unpack(pair, carry):
        rows = pl.ds(pl.multiple_of(pair * two, two), two)
        pieces = []
        for e in range(2):
            g = got_ref[2 * pair + e].astype(f32)
            pieces += [g, swap_halves(g)]
        grad = jnp.where(lane < HALF_LANES, jnp.concatenate(pieces, axis=0), 0.0)
        delta = jnp.sum(grad * out32_ref[rows, :], axis=1, keepdims=True)
        grad = lanes_three(lane, HALF_LANES, -delta, grad)
        g_ref[rows, :] = grad.astype(low)
        gt_ref[:, rows] = grad.T[:HALF_LANES].astype(low)
        qt_ref[:, rows] = q_ref[rows, :].astype(f32).T[:HALF_LANES].astype(low)
        return carry

    lax.fori_loop(0, owners // 2, unpack, 0)
    dkt_ref[...] = jnp.zeros_like(dkt_ref)
    dvt_ref[...] = jnp.zeros_like(dvt_ref)

    def query_block(limit, b, carry):
        rows = pl.ds(pl.multiple_of(b * ROWS, ROWS), ROWS)
        q, g = q_ref[rows, :], g_ref[rows, :]
        qt, gt = qt_ref[:, rows], gt_ref[:, rows]

        def chunk(cols, acc):
            p = jnp.exp(nn(q, kt_ref[:, cols]))
            ds = (p * nn(g, vt_ref[:, cols])).astype(low)
            dvt_ref[:, cols] += nn(gt, p.astype(low))
            dkt_ref[:, cols] += nn(qt, ds)
            return acc + nn(ds, k_ref[cols, :])

        whole, left = limit // CHUNK, limit % CHUNK
        acc = lax.fori_loop(
            0,
            whole,
            lambda c, acc: chunk(pl.ds(pl.multiple_of(c * CHUNK, CHUNK), CHUNK), acc),
            jnp.zeros((ROWS, LANES), f32),
        )
        if left:
            acc = chunk(slice(whole * CHUNK, limit), acc)
        dq_ref[rows, :] = acc
        return carry

    for first, last, limit in groups:
        lax.fori_loop(first, last, functools.partial(query_block, limit), 0)

    def send_out(pair, carry):
        first = pl.multiple_of(pair * two, two)
        rows = pl.ds(first, two)
        dkv = jnp.concatenate([dkt_ref[:, rows], dvt_ref[:, rows]], axis=0).T
        dq = dq_ref[rows, :]
        qk = jnp.where(lane < HALF_LANES, dq, swap_halves(dkv)).astype(low)
        for e in range(2):
            pack_ref[2 * pair + e, 0:tokens, :] = qk[e * tokens : (e + 1) * tokens]
            a = dkv[e * tokens : e * tokens + mid]
            b = dkv[e * tokens + mid : (e + 1) * tokens]
            pack_ref[2 * pair + e, tokens:, :] = jnp.where(lane_mid < HALF_LANES, swap_halves(a), b).astype(low)
        return carry

    lax.fori_loop(0, owners // 2, send_out, 0)


def attend_back(got, kept, groups):
    owners, mid, _ = got.shape
    group_len = owners * mid * 2
    low = jnp.bfloat16
    return pl.pallas_call(
        functools.partial(attend_back_kernel, groups),
        out_shape=jax.ShapeDtypeStruct((owners, 3 * mid, LANES), low),
        in_specs=[VM] * 6,
        out_specs=VM,
        scratch_shapes=[
            pltpu.VMEM((group_len, LANES), low),
            pltpu.VMEM((HALF_LANES, group_len), low),
            pltpu.VMEM((HALF_LANES, group_len), low),
            pltpu.VMEM((group_len, LANES), jnp.float32),
            pltpu.VMEM((HALF_LANES, group_len), jnp.float32),
            pltpu.VMEM((HALF_LANES, group_len), jnp.float32),
        ],
        compiler_params=pltpu.CompilerParams(vmem_limit_bytes=VMEM_BYTES),
    )(got, *kept)


def run_bounds(lengths, group_len):
    short_sq = jnp.array([side * side for side in SHORT_SIDES], jnp.int32)
    long_sq = jnp.array([side * side for side in LONG_SIDES], jnp.int32)
    counts = jnp.where(
        lengths[None, :] == sum(side * side for side in LONG_SIDES),
        long_sq[:, None],
        jnp.where(lengths[None, :] == sum(side * side for side in SHORT_SIDES), short_sq[:, None], 0),
    ).reshape(-1)
    ends = jnp.cumsum(counts)
    starts = ends - counts
    pad = lambda v, last: jnp.concatenate([v, last])
    ends = pad(ends, jnp.full((1,), group_len, jnp.int32))
    starts = pad(starts, ends[-2:-1])
    return starts, ends


def attention_rule(slots):
    runs = slots * LEVELS + 1
    rule = np.zeros((LANES, LANES), np.float32)
    for a in range(runs):
        for b in range(runs):
            slot_a, level_a = (slots, 0) if a == runs - 1 else (a % slots, a // slots)
            slot_b, level_b = (slots, 0) if b == runs - 1 else (b % slots, b // slots)
            if slot_a != slot_b or level_b > level_a:
                rule[HALF_LANES + a, HALF_LANES + b] = -BIG
    return rule


def from_heads(blocks):
    heads, mid, _ = blocks.shape
    return blocks.reshape(heads, mid, 2, HALF_LANES).transpose(2, 1, 0, 3).reshape(2 * mid, -1)


def to_heads(rows):
    tokens = rows.shape[0]
    split = rows.reshape(2, tokens // 2, HEADS, HALF_LANES)
    return split.transpose(2, 1, 0, 3).reshape(HEADS, tokens // 2, LANES)


def fast_shards(
    feature_map,
    condition,
    item_lengths,
    cotangent,
    code_book,
    qkv_state,
    out_state,
    up_state,
    down_state,
    ada_state,
    embed_state,
    vector_state,
):
    tok_rows, model_width = cotangent.shape
    low, f32 = jnp.bfloat16, jnp.float32
    half = model_width // 2
    core, wide = lax.axis_index("dp"), lax.axis_index("wide")
    group_len = tok_rows * lax.axis_size("wide")
    tokens_all = lax.axis_size("dp") * group_len
    lengths = item_lengths[0]
    slot_count = lengths.shape[0]
    swap = [(0, 1), (1, 0)]

    states = (qkv_state, out_state, up_state, down_state, ada_state)
    flipped = tuple(stacked[1].astype(low).T for stacked in states[:4])
    w_ada = ada_state[1].astype(low)

    silu_own = jax.nn.silu(condition).astype(low)
    silu_all = lax.all_gather(silu_own, "dp", axis=0, tiled=True)
    silu_rows = lax.dynamic_slice_in_dim(silu_all, core * half, half, 1)
    ada_part = jnp.dot(silu_rows, w_ada, preferred_element_type=f32)
    ada_theirs = lax.dynamic_slice_in_dim(ada_part, (1 - core) * slot_count, slot_count, 0)
    ada_mine = lax.dynamic_slice_in_dim(ada_part, core * slot_count, slot_count, 0)
    ada_mine = ada_mine + lax.ppermute(ada_theirs, "dp", swap)
    ada_block = jnp.pad(ada_mine, ((0, 8 - slot_count), (0, 0)))

    g_qkv, ada_gathered = gather_weights([flipped[0]], ada_block, 0)
    g_out, g_up, g_down = gather_weights(list(flipped[1:]), None, 1)
    ada_product = ada_gathered[:, :slot_count].transpose(1, 0, 2).reshape(slot_count, -1)
    w_qkv, w_out, w_up, w_down = (g.reshape(2, -1, g.shape[-1]) for g in (g_qkv, g_out, g_up, g_down))

    starts, ends = run_bounds(lengths, group_len)
    positions = wide * tok_rows + jnp.arange(tok_rows, dtype=jnp.int32)
    after_start = positions[:, None] >= starts[None, :]
    before_end = positions[:, None] < ends[None, :]
    runs_of = (after_start & before_end).astype(f32)
    live_rows = 1.0 - runs_of[:, -1:]
    left_ok = 1.0 - jnp.sum(((positions[:, None] == starts[None, :]) & before_end).astype(f32), axis=1)
    right_ok = 1.0 - jnp.sum(((positions[:, None] == ends[None, :] - 1) & after_start).astype(f32), axis=1)
    one_hot = jnp.sum(runs_of[:, :-1].reshape(tok_rows, LEVELS, slot_count), axis=1)

    rimmed = padded(feature_map, (("wide", 1),), 1)
    smooth = smooth_map(feature_map, left_ok, right_ok, rimmed[:, :-2], rimmed[:, 2:])
    embed_w = embed_state[1]
    vectors = vector_state[1]
    gain = vectors[7:8]
    x_zero = (
        lax.dot_general(smooth, embed_w, (((0,), (0,)), ((), ())), precision=HIGHEST_PRECISION)
        + vectors[6]
    )
    ada_all = ada_product + vectors[:6].reshape(-1)
    token_ada = jnp.dot(one_hot, ada_all, precision=HIGHEST_PRECISION)
    gate_one, gate_two, scale_one, scale_two, shift_one, shift_two = jnp.split(token_ada, 6, axis=1)
    h_one_low = pre_norm(x_zero, scale_one, shift_one).astype(low)

    pack, kept_qk = project_heads(h_one_low, w_qkv, gain)
    got = lax.all_to_all(pack, "wide", 0, 0, tiled=True)
    groups = same_limits(key_limits(group_len, slot_count))
    lane_pad = lambda v: jnp.pad(v, (HALF_LANES, HALF_LANES - v.shape[0]))[None]
    rule = jnp.asarray(attention_rule(slot_count), low)
    att_pack, *kept = attend(got, lane_pad(starts), lane_pad(ends), rule, groups)
    attn_low = from_heads(lax.all_to_all(att_pack, "wide", 0, 0, tiled=True))

    attn_proj = against(attn_low[:, :half], w_out[0]) + against(attn_low[:, half:], w_out[1])
    x_one = x_zero + gate_one * attn_proj
    h_two_low = pre_norm(x_one, scale_two, shift_two).astype(low)
    hidden_pre = against(h_two_low[:, :half], w_up[0]) + against(h_two_low[:, half:], w_up[1])
    act_low = jax.nn.gelu(hidden_pre, approximate=True).astype(low)
    hidden_half = w_down.shape[2]
    mlp_out = against(act_low[:, :hidden_half], w_down[0]) + against(act_low[:, hidden_half:], w_down[1])
    x_two = x_one + gate_two * mlp_out
    block_out = (x_two * live_rows).astype(low)
    logits = against(block_out, code_book)
    code_mass = jnp.sum(jax.nn.softmax(logits, axis=-1) * live_rows, axis=0)

    g_two = cotangent.astype(f32) * live_rows
    d_mlp = (gate_two * g_two).astype(low)
    d_gate_two = g_two * mlp_out

    def summed_over_cores(grad_rows, inputs):
        width = inputs.shape[1] // 2
        other = lax.dynamic_slice_in_dim(inputs, (1 - core) * width, width, 1)
        own = lax.dynamic_slice_in_dim(inputs, core * width, width, 1)
        theirs = lax.ppermute(contract_rows(grad_rows, other).astype(low), "dp", swap)
        total = (contract_rows(grad_rows, own) + theirs.astype(f32)).astype(low)
        return total.reshape(4, 4, -1, width)

    def both_halves(values, weights):
        return jnp.concatenate(
            [jnp.dot(values, weights[h], preferred_element_type=f32) for h in range(2)], axis=1
        )

    p_down = summed_over_cores(d_mlp, act_low)
    d_act = both_halves(d_mlp, w_down)
    _, gelu_back = jax.vjp(lambda inputs: jax.nn.gelu(inputs, approximate=True), hidden_pre)
    d_hidden = gelu_back(d_act)[0].astype(low)
    p_up = summed_over_cores(d_hidden, h_two_low)
    d_h_two = both_halves(d_hidden, w_up)
    _, norm_back_two = jax.vjp(pre_norm, x_one, scale_two, shift_two)
    d_x_one, d_scale_two, d_shift_two = norm_back_two(d_h_two)
    d_x_one = d_x_one + g_two
    d_attn = (gate_one * d_x_one).astype(low)
    d_gate_one = d_x_one * attn_proj
    p_out = summed_over_cores(d_attn, attn_low)
    d_attended = both_halves(d_attn, w_out).astype(low)
    s_out, s_up, s_down = scatter_grads([p_out, p_up, p_down], 2)

    back = lax.all_to_all(to_heads(d_attended), "wide", 0, 0, tiled=True)
    d_pack = attend_back(back, kept, groups)
    d_got = lax.all_to_all(d_pack, "wide", 0, 0, tiled=True)
    d_projected_low, d_gain = heads_backward(d_got, kept_qk, gain)
    p_qkv = summed_over_cores(d_projected_low, h_one_low)
    (s_qkv,) = scatter_grads([p_qkv], 3)
    d_h_one = both_halves(d_projected_low, w_qkv)
    _, norm_back_one = jax.vjp(pre_norm, x_zero, scale_one, shift_one)
    d_x_zero, d_scale_one, d_shift_one = norm_back_one(d_h_one)
    d_x_zero = d_x_zero + d_x_one
    d_token_ada = jnp.concatenate(
        [d_gate_one, d_gate_two, d_scale_one, d_scale_two, d_shift_one, d_shift_two], axis=1
    )
    d_ada_part = contract_rows(one_hot, d_token_ada, HIGHEST_PRECISION)
    d_smooth = lax.dot_general(embed_w, d_x_zero, (((1,), (1,)), ((), ())), precision=HIGHEST_PRECISION)
    d_embed = lax.dot_general(smooth, d_x_zero, (((1,), (0,)), ((), ())), precision=HIGHEST_PRECISION)
    grad_share = d_smooth / (2.0 + left_ok + right_ok)
    rim_share = padded(grad_share, (("wide", 1),), 1)
    map_grad = 2.0 * grad_share + left_ok * rim_share[:, :-2] + right_ok * rim_share[:, 2:]

    wides = lax.axis_size("wide")
    ada_rows = d_ada_part.reshape(slot_count, wides, -1, LANES)
    per_slot = ada_rows.shape[2]
    ada_rows = ada_rows.transpose(1, 0, 2, 3).reshape(wides, -1, LANES)
    code_rows = code_mass.reshape(-1, model_width)
    common = jnp.concatenate([d_embed, jnp.sum(d_x_zero, axis=0)[None], d_gain, code_rows], axis=0)
    common_rows = common.shape[0]
    common = common.reshape(common_rows, wides, -1).transpose(1, 0, 2).reshape(wides, -1, LANES)
    plain_rows = common.shape[1]
    small_in = jnp.concatenate([ada_rows, common], axis=1)
    ada_count = ada_rows.shape[1]
    d_ada_both, sums = small_sums(small_in, ada_count, slot_count, 4)
    common_sum = sums[:, :plain_rows].reshape(wides, common_rows, -1).transpose(1, 0, 2)
    common_sum = common_sum.reshape(common_rows, model_width)
    embed_rows = embed_w.shape[0]
    d_embed_all = common_sum[:embed_rows]
    bias_sum = sums[:, plain_rows:].reshape(6, model_width)
    d_vectors_all = jnp.concatenate([bias_sum, common_sum[embed_rows : embed_rows + 2]], axis=0)
    histogram = common_sum[embed_rows + 2 :].reshape(-1) * (code_book.shape[0] / tokens_all)
    d_ada_own = d_ada_both.reshape(2 * slot_count, per_slot * LANES)
    grad_ada = contract_rows(silu_rows.astype(f32), d_ada_own, HIGHEST_PRECISION)

    owned_grads = (s_qkv.T, s_out.T, s_up.T, s_down.T, grad_ada)
    root_tokens = math.sqrt(tokens_all)
    spreads = (
        model_width ** (-0.5),
        (model_width // 16) ** (-0.5),
        model_width ** (-0.5),
        w_up.shape[1] ** (-0.5),
        model_width ** (-0.5),
    )
    new_states = tuple(
        nesterov(stacked, gradient, BASE_RATE * spread_w / (factor_g * root_tokens), WEIGHT_DECAY)
        for stacked, gradient, spread_w, factor_g in zip(states, owned_grads, spreads, GRAD_FACTORS)
    )
    embed_new = nesterov(
        embed_state, d_embed_all, BASE_RATE * embed_rows ** (-0.5) / (EMBED_FACTOR * root_tokens), 0.0
    )
    vector_new = nesterov(vector_state, d_vectors_all, VECTOR_RATE / root_tokens, 0.0)
    outputs = [block_out, map_grad, histogram]
    for state in new_states:
        outputs += [state, state[1].astype(low)]
    return tuple(outputs + [embed_new, vector_new, d_vectors_all[7]])


def solution(mesh):
    body = fast_shards if dict(mesh.shape) == {"dp": 2, "wide": 16} else shards
    in_specs = (
        P(None, ("dp", "wide")),
        P("dp", None),
        P("dp", None),
        P(("dp", "wide"), None),
        P(),
        P(None, "dp", "wide"),
        P(None, "dp", "wide"),
        P(None, "dp", "wide"),
        P(None, "dp", "wide"),
        P(None, "dp", "wide"),
        P(),
        P(),
    )
    out_specs = (
        P(("dp", "wide"), None),
        P(None, ("dp", "wide")),
        P(),
        P(None, "dp", "wide"),
        P("dp", "wide"),
        P(None, "dp", "wide"),
        P("dp", "wide"),
        P(None, "dp", "wide"),
        P("dp", "wide"),
        P(None, "dp", "wide"),
        P("dp", "wide"),
        P(None, "dp", "wide"),
        P("dp", "wide"),
        P(),
        P(),
        P(),
    )
    return jax.shard_map(body, mesh=mesh, in_specs=in_specs, out_specs=out_specs, check_vma=False)
```

```python
import functools
import math

import jax
import jax.numpy as jnp
import numpy as np
from jax import lax
from jax.experimental import pallas as pl
from jax.experimental.pallas import tpu as pltpu
from jax.sharding import PartitionSpec as P

HEADS = 16
LEVELS = 10
STEP = 7


SHORT_SIDES = (1, 2, 3, 4, 5, 6, 8, 10, 13, 16)
LONG_SIDES = (1, 2, 3, 4, 6, 9, 13, 18, 24, 32)
MASKED = -1e30
NORM_EPS = 1e-06
MOMENTUM = 0.9
WEIGHT_DECAY = 0.05
BASE_RATE = 0.37
VECTOR_RATE = 0.22
GRAD_FACTORS = (0.15, 0.1, 0.3, 0.35, 0.3)
EMBED_FACTOR = 0.6
HIGHEST_PRECISION = lax.Precision.HIGHEST


def padded(cells, sides, width):
    for axis, dim in sides:
        count = lax.axis_size(axis)
        ends = count - 1
        head = lax.slice_in_dim(cells, 0, width, axis=dim)
        tail = lax.slice_in_dim(cells, cells.shape[dim] - width, cells.shape[dim], axis=dim)
        cells = jnp.concatenate(
            [
                lax.ppermute(tail, axis, [(i, (i + 1) % count) for i in range(ends)]),
                cells,
                lax.ppermute(head, axis, [((i + 1) % count, i) for i in range(ends)]),
            ],
            axis=dim,
        )
    return cells


def layout(lengths, positions, group_len):
    short_sq = jnp.array([side * side for side in SHORT_SIDES[:LEVELS]], jnp.int32)
    long_sq = jnp.array([side * side for side in LONG_SIDES[:LEVELS]], jnp.int32)
    short_total = sum((side * side for side in SHORT_SIDES[:LEVELS]))
    long_total = sum((side * side for side in LONG_SIDES[:LEVELS]))
    slot_count = lengths.shape[0]
    counts = jnp.where(
        lengths[None, :] == long_total,
        long_sq[:, None],
        jnp.where(lengths[None, :] == short_total, short_sq[:, None], 0),
    )
    unused = group_len - jnp.sum(lengths)
    ordered = jnp.concatenate([counts.reshape(-1), unused[None]])
    boundary = jnp.cumsum(ordered)
    segment = jnp.sum((boundary[None, :] <= positions[:, None]).astype(jnp.int32), axis=1)
    segment = jnp.minimum(segment, ordered.shape[0] - 1)
    unused_id = slot_count * LEVELS
    tok_level = jnp.where(segment >= unused_id, 0, segment // slot_count)
    tok_slot = jnp.where(segment >= unused_id, slot_count, segment % slot_count)
    return (tok_slot, tok_level, segment)


def pre_norm(inputs, scaling, offset_add):
    row_mean = jnp.mean(inputs, axis=-1, keepdims=True)
    centred = inputs - row_mean
    spread = jnp.mean(centred * centred, axis=-1, keepdims=True)
    return centred * lax.rsqrt(spread + NORM_EPS) * (1.0 + scaling) + offset_add


def unit_heads(inputs):
    shaped = inputs.reshape(inputs.shape[0], HEADS, -1)
    shaped = shaped * lax.rsqrt(jnp.sum(shaped * shaped, axis=-1, keepdims=True) + NORM_EPS)
    return shaped.reshape(inputs.shape)


def split_heads(projected, q_gain):
    queries, key_part, value_part = jnp.split(projected, 3, axis=1)
    head_scale = math.sqrt(queries.shape[1] // HEADS)
    return (unit_heads(queries) * (head_scale * (1.0 + q_gain)), unit_heads(key_part), value_part)


def smooth_map(values, left_ok, right_ok, before, following):
    return (left_ok * before + 2.0 * values + right_ok * following) / (2.0 + left_ok + right_ok)


def nesterov(stacked, gradient, step_rate, decay_rate):
    moment, weight, average = (stacked[0], stacked[1], stacked[2])
    step_grad = gradient + decay_rate * weight
    new_moment = MOMENTUM * moment + step_rate * step_grad
    new_weight = weight - (step_rate * step_grad + MOMENTUM * new_moment)
    retain = min(0.999, (1.0 + STEP) / (10.0 + STEP))
    new_average = retain * average + (1.0 - retain) * new_weight
    return jnp.stack([new_moment, new_weight, new_average])


def contract_rows(left_side, right_side, precision=None):
    return lax.dot_general(
        left_side,
        right_side,
        (((0,), (0,)), ((), ())),
        precision=precision,
        preferred_element_type=jnp.float32,
    )


def against(left_side, right_side):
    return lax.dot_general(
        left_side, right_side, (((1,), (1,)), ((), ())), preferred_element_type=jnp.float32
    )


def shards(
    feature_map,
    condition,
    item_lengths,
    cotangent,
    code_book,
    qkv_state,
    out_state,
    up_state,
    down_state,
    ada_state,
    embed_state,
    vector_state,
):
    tok_rows = cotangent.shape[0]
    model_width = cotangent.shape[1]
    head_dim = model_width // HEADS
    wide_count = lax.axis_size("wide")
    group_len = tok_rows * wide_count
    tokens_all = lax.axis_size("dp") * group_len
    lengths = item_lengths[0]
    slot_count = lengths.shape[0]
    positions = lax.axis_index("wide") * tok_rows + jnp.arange(tok_rows, dtype=jnp.int32)
    tok_slot, tok_level, segment = layout(lengths, positions, group_len)
    live_rows = (tok_slot < slot_count).astype(jnp.float32)[:, None]
    left_ok = ((layout(lengths, positions - 1, group_len)[2] == segment) & (positions > 0)).astype(
        jnp.float32
    )
    right_ok = (
        (layout(lengths, positions + 1, group_len)[2] == segment) & (positions < group_len - 1)
    ).astype(jnp.float32)
    rimmed = padded(feature_map, (("wide", 1),), 1)
    smooth = smooth_map(feature_map, left_ok, right_ok, rimmed[:, :-2], rimmed[:, 2:])
    states = (qkv_state, out_state, up_state, down_state, ada_state)
    masters = tuple((stacked[1].astype(jnp.bfloat16) for stacked in states))
    columns = (
        lax.all_gather(masters[0], "wide", axis=1, tiled=True),
        lax.all_gather(masters[1], "wide", axis=1, tiled=True),
        lax.all_gather(masters[2], "wide", axis=1, tiled=True),
        lax.all_gather(masters[3], "wide", axis=1, tiled=True),
    )
    ada_piece = lax.all_gather(masters[4], "wide", axis=1, tiled=True)
    w_qkv, w_out, w_up, w_down, w_ada = (
        lax.all_gather(columns[0], "dp", axis=0, tiled=True),
        lax.all_gather(columns[1], "dp", axis=0, tiled=True),
        lax.all_gather(columns[2], "dp", axis=0, tiled=True),
        lax.all_gather(columns[3], "dp", axis=0, tiled=True),
        lax.all_gather(ada_piece, "dp", axis=0, tiled=True),
    )
    embed_w = embed_state[1]
    vectors = vector_state[1]
    x_zero = (
        lax.dot_general(smooth, embed_w, (((0,), (0,)), ((), ())), precision=HIGHEST_PRECISION)
        + vectors[6]
    )
    silu_cond = jax.nn.silu(condition).astype(jnp.bfloat16)
    ada_product = jnp.dot(silu_cond, w_ada, preferred_element_type=jnp.float32)
    ada_all = ada_product + vectors[:6].reshape(-1)
    one_hot = (tok_slot[:, None] == jnp.arange(slot_count, dtype=jnp.int32)[None, :]).astype(
        jnp.float32
    )
    token_ada = jnp.dot(one_hot, ada_all, precision=HIGHEST_PRECISION)
    gate_one, gate_two, scale_one, scale_two, shift_one, shift_two = jnp.split(token_ada, 6, axis=1)
    h_one_low = pre_norm(x_zero, scale_one, shift_one).astype(jnp.bfloat16)
    projected = jnp.dot(h_one_low, w_qkv, preferred_element_type=jnp.float32)
    (q_unit, k_unit, v_full), heads_back = jax.vjp(split_heads, projected, vectors[7])
    queries = q_unit.astype(jnp.bfloat16)
    keys_low = k_unit.astype(jnp.bfloat16)
    values_low = v_full.astype(jnp.bfloat16)
    query_heads = queries.reshape(tok_rows, HEADS, head_dim)

    def blockwise(advance, running, pieces, first_row):
        key_count = pieces[0].shape[0]
        block_size = math.gcd(key_count, 1024)

        def per_block(current, offset):
            key_part = tuple(
                (lax.dynamic_slice_in_dim(piece_arr, offset, block_size, 0) for piece_arr in pieces)
            )
            first_key = first_row + offset
            k_slot, k_level, _ = layout(
                lengths, first_key + jnp.arange(block_size, dtype=jnp.int32), group_len
            )
            allowed = (tok_slot[:, None] == k_slot[None, :]) & (
                k_level[None, :] <= tok_level[:, None]
            )
            current = advance(current, key_part, allowed, first_key)
            return (current, None)

        offsets = jnp.arange(key_count // block_size, dtype=jnp.int32) * block_size
        return lax.scan(per_block, running, offsets)[0]

    def scores_of(key_block, allowed):
        raw_scores = jnp.einsum(
            "qhd,khd->hqk",
            query_heads,
            key_block.reshape(-1, HEADS, head_dim),
            preferred_element_type=jnp.float32,
        )
        return jnp.where(allowed[None], raw_scores, MASKED)

    def stats_step(running, key_part, allowed, first_key):
        scores = scores_of(key_part[0], allowed)
        top_score, exp_total = running
        new_top = jnp.maximum(top_score, jnp.max(scores, axis=-1, keepdims=True))
        exp_total = exp_total * jnp.exp(top_score - new_top) + jnp.sum(
            jnp.exp(scores - new_top), axis=-1, keepdims=True
        )
        return (new_top, exp_total)

    kv_rows = (
        lax.all_gather(keys_low, "wide", axis=0, tiled=True),
        lax.all_gather(values_low, "wide", axis=0, tiled=True),
    )
    start_stats = (
        jnp.full((HEADS, tok_rows, 1), MASKED, jnp.float32),
        jnp.zeros((HEADS, tok_rows, 1), jnp.float32),
    )
    top_score, exp_total = blockwise(stats_step, start_stats, kv_rows, 0)
    log_total = top_score + jnp.log(exp_total)

    def value_step(running, key_part, allowed, first_key):
        attn_probs = jnp.exp(scores_of(key_part[0], allowed) - log_total).astype(jnp.bfloat16)
        return running + jnp.einsum(
            "hqk,khd->qhd",
            attn_probs,
            key_part[1].reshape(-1, HEADS, head_dim),
            preferred_element_type=jnp.float32,
        )

    attended = blockwise(
        value_step, jnp.zeros((tok_rows, HEADS, head_dim), jnp.float32), kv_rows, 0
    )
    attn_low = attended.reshape(tok_rows, model_width).astype(jnp.bfloat16)
    attn_proj = jnp.dot(attn_low, w_out, preferred_element_type=jnp.float32)
    x_one = x_zero + gate_one * attn_proj
    h_two_low = pre_norm(x_one, scale_two, shift_two).astype(jnp.bfloat16)
    hidden_pre = jnp.dot(h_two_low, w_up, preferred_element_type=jnp.float32)
    act_low = jax.nn.gelu(hidden_pre, approximate=True).astype(jnp.bfloat16)
    mlp_out = jnp.dot(act_low, w_down, preferred_element_type=jnp.float32)
    x_two = x_one + gate_two * mlp_out
    block_out = (x_two * live_rows).astype(jnp.bfloat16)
    logits = against(block_out, code_book)
    code_mass = jnp.sum(jax.nn.softmax(logits, axis=-1) * live_rows, axis=0)
    g_two = cotangent.astype(jnp.float32) * live_rows
    d_mlp = (gate_two * g_two).astype(jnp.bfloat16)
    d_gate_two = g_two * mlp_out
    dw_down = contract_rows(act_low, d_mlp)
    d_act = against(d_mlp, w_down)
    _, gelu_back = jax.vjp(lambda inputs: jax.nn.gelu(inputs, approximate=True), hidden_pre)
    d_hidden = gelu_back(d_act)[0].astype(jnp.bfloat16)
    dw_up = contract_rows(h_two_low, d_hidden)
    d_h_two = against(d_hidden, w_up)
    _, norm_back_two = jax.vjp(pre_norm, x_one, scale_two, shift_two)
    d_x_one, d_scale_two, d_shift_two = norm_back_two(d_h_two)
    d_x_one = d_x_one + g_two
    d_attn = (gate_one * d_x_one).astype(jnp.bfloat16)
    d_gate_one = d_x_one * attn_proj
    dw_out = contract_rows(attn_low, d_attn)
    grad_flat = against(d_attn, w_out).astype(jnp.bfloat16)
    grad_heads = grad_flat.reshape(tok_rows, HEADS, head_dim)

    def delta_step(running, key_part, allowed, first_key):
        attn_probs = jnp.exp(scores_of(key_part[0], allowed) - log_total)
        d_probs = jnp.einsum(
            "qhd,khd->hqk",
            grad_heads,
            key_part[1].reshape(-1, HEADS, head_dim),
            preferred_element_type=jnp.float32,
        )
        return running + jnp.sum(attn_probs * d_probs, axis=-1, keepdims=True)

    row_delta = blockwise(delta_step, jnp.zeros((HEADS, tok_rows, 1), jnp.float32), kv_rows, 0)

    def grad_step(running, key_part, allowed, first_key):
        d_query, d_keys, d_values = running
        key_heads = key_part[0].reshape(-1, HEADS, head_dim)
        value_heads = key_part[1].reshape(-1, HEADS, head_dim)
        block_rows = key_part[0].shape[0]
        attn_probs = jnp.exp(scores_of(key_part[0], allowed) - log_total)
        d_probs = jnp.einsum(
            "qhd,khd->hqk", grad_heads, value_heads, preferred_element_type=jnp.float32
        )
        d_scores = (attn_probs * (d_probs - row_delta)).astype(jnp.bfloat16)
        d_query = d_query + jnp.einsum(
            "hqk,khd->qhd", d_scores, key_heads, preferred_element_type=jnp.float32
        )
        key_grad = jnp.einsum(
            "hqk,qhd->khd", d_scores, query_heads, preferred_element_type=jnp.float32
        )
        value_grad = jnp.einsum(
            "hqk,qhd->khd",
            attn_probs.astype(jnp.bfloat16),
            grad_heads,
            preferred_element_type=jnp.float32,
        )
        key_sum = lax.dynamic_slice_in_dim(d_keys, first_key, block_rows, 0) + key_grad.reshape(
            block_rows, model_width
        )
        value_sum = lax.dynamic_slice_in_dim(
            d_values, first_key, block_rows, 0
        ) + value_grad.reshape(block_rows, model_width)
        d_keys = lax.dynamic_update_slice_in_dim(d_keys, key_sum, first_key, 0)
        d_values = lax.dynamic_update_slice_in_dim(d_values, value_sum, first_key, 0)
        return (d_query, d_keys, d_values)

    grad_init = (
        jnp.zeros((tok_rows, HEADS, head_dim), jnp.float32),
        jnp.zeros((group_len, model_width), jnp.float32),
        jnp.zeros((group_len, model_width), jnp.float32),
    )
    d_query, d_keys, d_values = blockwise(grad_step, grad_init, kv_rows, 0)
    d_keys_own, d_values_own = (
        lax.psum_scatter(
            d_keys.astype(jnp.bfloat16), "wide", scatter_dimension=0, tiled=True
        ).astype(jnp.float32),
        lax.psum_scatter(
            d_values.astype(jnp.bfloat16), "wide", scatter_dimension=0, tiled=True
        ).astype(jnp.float32),
    )
    d_projected, d_gain = heads_back(
        (d_query.reshape(tok_rows, model_width), d_keys_own, d_values_own)
    )
    d_projected_low = d_projected.astype(jnp.bfloat16)
    dw_qkv = contract_rows(h_one_low, d_projected_low)
    d_h_one = against(d_projected_low, w_qkv)
    _, norm_back_one = jax.vjp(pre_norm, x_zero, scale_one, shift_one)
    d_x_zero, d_scale_one, d_shift_one = norm_back_one(d_h_one)
    d_x_zero = d_x_zero + d_x_one
    d_token_ada = jnp.concatenate(
        [d_gate_one, d_gate_two, d_scale_one, d_scale_two, d_shift_one, d_shift_two], axis=1
    )
    d_ada_all = contract_rows(one_hot, d_token_ada, HIGHEST_PRECISION)
    d_smooth = lax.dot_general(
        embed_w, d_x_zero, (((1,), (1,)), ((), ())), precision=HIGHEST_PRECISION
    )
    d_embed = lax.dot_general(
        smooth, d_x_zero, (((1,), (0,)), ((), ())), precision=HIGHEST_PRECISION
    )
    d_vectors = jnp.concatenate(
        [
            jnp.sum(d_ada_all, axis=0).reshape(6, model_width),
            jnp.sum(d_x_zero, axis=0)[None],
            d_gain[None],
        ],
        axis=0,
    )
    grad_share = d_smooth / (2.0 + left_ok + right_ok)
    rim_share = padded(grad_share, (("wide", 1),), 1)
    map_grad = 2.0 * grad_share + left_ok * rim_share[:, :-2] + right_ok * rim_share[:, 2:]
    d_embed_all, d_vectors_all, mass_all = lax.psum((d_embed, d_vectors, code_mass), ("dp", "wide"))
    histogram = mass_all * (code_book.shape[0] / tokens_all)
    ada_term = contract_rows(silu_cond.astype(jnp.float32), d_ada_all, HIGHEST_PRECISION)
    split_cols = (
        lax.psum_scatter(
            dw_qkv.astype(jnp.bfloat16), "wide", scatter_dimension=1, tiled=True
        ).astype(jnp.float32),
        lax.psum_scatter(
            dw_out.astype(jnp.bfloat16), "wide", scatter_dimension=1, tiled=True
        ).astype(jnp.float32),
        lax.psum_scatter(
            dw_up.astype(jnp.bfloat16), "wide", scatter_dimension=1, tiled=True
        ).astype(jnp.float32),
        lax.psum_scatter(
            dw_down.astype(jnp.bfloat16), "wide", scatter_dimension=1, tiled=True
        ).astype(jnp.float32),
        lax.psum_scatter(
            ada_term.astype(jnp.bfloat16), "wide", scatter_dimension=1, tiled=True
        ).astype(jnp.float32),
    )
    ada_cols = split_cols[4]
    owned_grads = (
        lax.psum_scatter(
            split_cols[0].astype(jnp.bfloat16), "dp", scatter_dimension=0, tiled=True
        ).astype(jnp.float32),
        lax.psum_scatter(
            split_cols[1].astype(jnp.bfloat16), "dp", scatter_dimension=0, tiled=True
        ).astype(jnp.float32),
        lax.psum_scatter(
            split_cols[2].astype(jnp.bfloat16), "dp", scatter_dimension=0, tiled=True
        ).astype(jnp.float32),
        lax.psum_scatter(
            split_cols[3].astype(jnp.bfloat16), "dp", scatter_dimension=0, tiled=True
        ).astype(jnp.float32),
        lax.psum_scatter(
            ada_cols.astype(jnp.bfloat16), "dp", scatter_dimension=0, tiled=True
        ).astype(jnp.float32),
    )
    root_tokens = math.sqrt(tokens_all)
    spreads = (
        model_width ** (-0.5),
        (model_width // 16) ** (-0.5),
        model_width ** (-0.5),
        w_up.shape[1] ** (-0.5),
        model_width ** (-0.5),
    )
    new_states = tuple(
        (
            nesterov(
                stacked, gradient, BASE_RATE * spread_w / (factor_g * root_tokens), WEIGHT_DECAY
            )
            for stacked, gradient, spread_w, factor_g in zip(
                states, owned_grads, spreads, GRAD_FACTORS
            )
        )
    )
    embed_new = nesterov(
        embed_state,
        d_embed_all,
        BASE_RATE * embed_w.shape[0] ** (-0.5) / (EMBED_FACTOR * root_tokens),
        0.0,
    )
    vector_new = nesterov(vector_state, d_vectors_all, VECTOR_RATE / root_tokens, 0.0)
    return (
        block_out,
        map_grad,
        histogram,
        new_states[0],
        new_states[0][1].astype(jnp.bfloat16),
        new_states[1],
        new_states[1][1].astype(jnp.bfloat16),
        new_states[2],
        new_states[2][1].astype(jnp.bfloat16),
        new_states[3],
        new_states[3][1].astype(jnp.bfloat16),
        new_states[4],
        new_states[4][1].astype(jnp.bfloat16),
        embed_new,
        vector_new,
        d_vectors_all[7],
    )


MESH_ID = pl.DeviceIdType.MESH
ANY = pl.BlockSpec(memory_space=pl.ANY)
VM = pl.BlockSpec(memory_space=pltpu.VMEM)
VMEM_BYTES = 56 * 1024 * 1024
LANES = 128
HALF_LANES = 64
BIG = 1e30


def nt(left_side, right_side):
    return lax.dot_general(
        left_side, right_side, (((1,), (1,)), ((), ())), preferred_element_type=jnp.float32
    )


def nn(left_side, right_side):
    return lax.dot_general(
        left_side, right_side, (((1,), (0,)), ((), ())), preferred_element_type=jnp.float32
    )


def entry_barrier(peers):
    barrier = pltpu.get_barrier_semaphore()
    for peer in peers:
        pl.semaphore_signal(barrier, inc=1, device_id=peer, device_id_type=MESH_ID)
    pl.semaphore_wait(barrier, len(peers))


def place():
    core, wide = lax.axis_index("dp"), lax.axis_index("wide")
    return core, wide // 4, wide % 4


def at_dev(core, z, yx):
    return (core, z * 4 + yx)


def scatter_kernel(count, *refs):
    parts = refs[:count]
    outs = refs[count : 2 * count]
    bufs = refs[2 * count : 2 * count + 8 * count]
    sems = refs[2 * count + 8 * count :]
    send, recv = sems
    core, z, yx = place()
    x_dev, y_dev = at_dev(core, z, yx ^ 1), at_dev(core, z, yx ^ 2)
    z_devs = [None] + [at_dev(core, lax.rem(z + r, 4), yx) for r in (1, 2, 3)]
    entry_barrier([x_dev, y_dev] + z_devs[1:])
    pending = []

    def push(i, slot, src, dst, device):
        copy = pltpu.make_async_remote_copy(
            src_ref=src,
            dst_ref=dst,
            send_sem=send.at[i, slot],
            recv_sem=recv.at[i, slot],
            device_id=device,
            device_id_type=MESH_ID,
        )
        copy.start()
        pending.append(copy)
        return copy

    def part(i, dz, d):
        return parts[i].at[lax.rem(z + dz, 4), yx ^ d]

    def f32(ref):
        return ref[...].astype(jnp.float32)

    arrivals = []
    for i in range(count):
        a_x, a_y, r_x, r_y, t_x, t_y, s_z, r_z = bufs[8 * i : 8 * i + 8]
        here = {}
        for j, dz in enumerate((0, 1)):
            here["ax", dz] = push(i, j, part(i, dz, 3), a_x.at[j], x_dev)
        for j, dz in enumerate((2, 3)):
            here["ay", dz] = push(i, 2 + j, part(i, dz, 3), a_y.at[j], y_dev)
        for j, dz in enumerate((0, 1)):
            here["rx", dz] = push(i, 4 + dz, part(i, dz, 1), r_x.at[dz], x_dev)
        for j, dz in enumerate((2, 3)):
            here["ry", dz] = push(i, 8 + dz, part(i, dz, 2), r_y.at[dz], y_dev)
        arrivals.append(here)
    for i in range(count):
        a_x, a_y, r_x, r_y, t_x, t_y, s_z, r_z = bufs[8 * i : 8 * i + 8]
        here = arrivals[i]
        for j, (low, high) in enumerate(((1, 2), (0, 3))):
            here["ax", low].wait_recv()
            t_y[j] = (f32(part(i, low, 2)) + f32(a_x.at[low])).astype(jnp.bfloat16)
            here["ry", low] = push(i, 8 + low, t_y.at[j], r_y.at[low], y_dev)
            here["ay", high].wait_recv()
            t_x[j] = (f32(part(i, high, 1)) + f32(a_y.at[high - 2])).astype(jnp.bfloat16)
            here["rx", high] = push(i, 4 + high, t_x.at[j], r_x.at[high], x_dev)
    for i in range(count):
        a_x, a_y, r_x, r_y, t_x, t_y, s_z, r_z = bufs[8 * i : 8 * i + 8]
        here = arrivals[i]
        for dz in (1, 2, 3, 0):
            here["rx", dz].wait_recv()
            here["ry", dz].wait_recv()
            total = f32(part(i, dz, 0)) + f32(r_x.at[dz]) + f32(r_y.at[dz])
            if dz:
                s_z[dz - 1] = total.astype(jnp.bfloat16)
                here["rz", dz] = push(i, 12 + dz, s_z.at[dz - 1], r_z.at[dz - 1], z_devs[dz])
            else:
                outs[i][...] = total
    for i in range(count):
        r_z = bufs[8 * i + 7]
        for dz in (1, 2, 3):
            arrivals[i]["rz", dz].wait_recv()
        outs[i][...] += f32(r_z.at[0]) + f32(r_z.at[1]) + f32(r_z.at[2])
    for copy in pending:
        copy.wait_send()


def scatter_grads(parts, call_id):
    count = len(parts)
    scratch = []
    for part in parts:
        for depth in (2, 2, 4, 4, 2, 2, 3, 3):
            scratch.append(pltpu.VMEM((depth,) + part.shape[2:], jnp.bfloat16))
    dma = pltpu.SemaphoreType.DMA
    scratch += [dma((count, 16)), dma((count, 16))]
    return pl.pallas_call(
        functools.partial(scatter_kernel, count),
        out_shape=[jax.ShapeDtypeStruct(part.shape[2:], jnp.float32) for part in parts],
        in_specs=[VM] * count,
        out_specs=[VM] * count,
        scratch_shapes=scratch,
        compiler_params=pltpu.CompilerParams(
            collective_id=call_id, has_side_effects=True, vmem_limit_bytes=VMEM_BYTES
        ),
    )(*parts)


def small_kernel(ada_rows, slots, part_ref, ada_ref, all_ref, landed, summed, other, mine, *sems):
    send_a, recv_a, send_b, recv_b, send_s, recv_s = sems
    core, z, yx = place()
    wide = z * 4 + yx
    sib = (1 - core, wide)
    peers = [(core, wide ^ r) for r in range(1, 16)]
    entry_barrier(peers + [sib])
    first = []
    for r in range(1, 16):
        copy = pltpu.make_async_remote_copy(
            src_ref=part_ref.at[wide ^ r],
            dst_ref=landed.at[r],
            send_sem=send_a.at[r],
            recv_sem=recv_a.at[r],
            device_id=peers[r - 1],
            device_id_type=MESH_ID,
        )
        copy.start()
        first.append(copy)
    total = part_ref[wide]
    for r, copy in enumerate(first):
        copy.wait_recv()
        total = total + landed[r + 1]
    summed[...] = total
    swap = pltpu.make_async_remote_copy(
        src_ref=summed,
        dst_ref=other,
        send_sem=send_s,
        recv_sem=recv_s,
        device_id=sib,
        device_id_type=MESH_ID,
    )
    swap.start()
    swap.wait()
    ada_ref[core] = summed[0:ada_rows]
    ada_ref[1 - core] = other[0:ada_rows]
    both = summed[...] + other[...]
    rest = both.shape[0] - ada_rows
    width = ada_rows // slots
    bias = both[0:width]
    for j in range(1, slots):
        bias = bias + both[j * width : (j + 1) * width]
    mine[0:rest] = both[ada_rows:]
    mine[rest : rest + width] = bias
    all_ref[wide] = mine[...]
    second = []
    for r in range(1, 16):
        copy = pltpu.make_async_remote_copy(
            src_ref=mine,
            dst_ref=all_ref.at[wide],
            send_sem=send_b.at[r],
            recv_sem=recv_b.at[r],
            device_id=peers[r - 1],
            device_id_type=MESH_ID,
        )
        copy.start()
        second.append(copy)
    for copy in second:
        copy.wait_recv()
    for copy in first + second:
        copy.wait_send()


def small_sums(parts, ada_rows, slots, call_id):
    rows = parts.shape[1]
    out_rows = rows - ada_rows + ada_rows // slots
    dma = pltpu.SemaphoreType.DMA
    f32 = jnp.float32
    return pl.pallas_call(
        functools.partial(small_kernel, ada_rows, slots),
        out_shape=[
            jax.ShapeDtypeStruct((2, ada_rows, LANES), f32),
            jax.ShapeDtypeStruct((16, out_rows, LANES), f32),
        ],
        in_specs=[VM],
        out_specs=[VM, VM],
        scratch_shapes=[
            pltpu.VMEM((16, rows, LANES), f32),
            pltpu.VMEM((rows, LANES), f32),
            pltpu.VMEM((rows, LANES), f32),
            pltpu.VMEM((out_rows, LANES), f32),
            dma((16,)),
            dma((16,)),
            dma((16,)),
            dma((16,)),
            dma,
            dma,
        ],
        compiler_params=pltpu.CompilerParams(collective_id=call_id, has_side_effects=True),
    )(parts)


def lane_iota(shape):
    return lax.broadcasted_iota(jnp.int32, shape, len(shape) - 1)


def swap_halves(pair):
    return pltpu.roll(pair, HALF_LANES, 1)


def head_sums(values):
    width = values.shape[1]
    rows = lax.broadcasted_iota(jnp.int32, (width, width), 0) // HALF_LANES
    cols = lax.broadcasted_iota(jnp.int32, (width, width), 1) // HALF_LANES
    ones = (rows == cols).astype(jnp.float32)
    return lax.dot_general(
        values,
        ones,
        (((1,), (0,)), ((), ())),
        precision=HIGHEST_PRECISION,
        preferred_element_type=jnp.float32,
    )


def heads_back_kernel(got_ref, kept_ref, gain_ref, out_ref, gain_grad_ref):
    tokens = kept_ref.shape[0]
    width = kept_ref.shape[1] // 2
    mid = tokens // 2
    f32, low = jnp.float32, jnp.bfloat16
    lane = lane_iota((tokens, LANES))
    lane_mid = lane_iota((mid, LANES))

    def unnormalize(values, grad):
        inverse = lax.rsqrt(head_sums(values * values) + NORM_EPS)
        unit = values * inverse
        return inverse * (grad - unit * head_sums(unit * grad)), unit

    def step(pair, carry):
        cols = pl.ds(pl.multiple_of(pair * LANES, LANES), LANES)
        key_cols = pl.ds(pl.multiple_of(pair * LANES + width, LANES), LANES)
        val_cols = pl.ds(pl.multiple_of(pair * LANES + 2 * width, LANES), LANES)
        even = got_ref[2 * pair].astype(f32)
        odd = got_ref[2 * pair + 1].astype(f32)
        even_qk, odd_qk = even[:tokens], odd[:tokens]
        d_query = jnp.where(lane < HALF_LANES, even_qk, swap_halves(odd_qk))
        d_key = jnp.where(lane < HALF_LANES, swap_halves(even_qk), odd_qk)
        even_v, odd_v = even[tokens:], odd[tokens:]
        out_ref[0:mid, val_cols] = jnp.where(lane_mid < HALF_LANES, even_v, swap_halves(odd_v)).astype(low)
        out_ref[mid:, val_cols] = jnp.where(lane_mid < HALF_LANES, swap_halves(even_v), odd_v).astype(low)
        scaled = d_query * (8.0 * (1.0 + gain_ref[:, cols]))
        d_q, unit = unnormalize(kept_ref[:, cols], scaled)
        gain_grad_ref[:, cols] = jnp.sum(d_query * unit, axis=0, keepdims=True) * 8.0
        out_ref[:, cols] = d_q.astype(low)
        out_ref[:, key_cols] = unnormalize(kept_ref[:, key_cols], d_key)[0].astype(low)
        return carry

    lax.fori_loop(0, width // LANES, step, 0)


def heads_backward(got, kept, gain):
    tokens, width = kept.shape[0], kept.shape[1] // 2
    return pl.pallas_call(
        heads_back_kernel,
        out_shape=[
            jax.ShapeDtypeStruct((tokens, 3 * width), jnp.bfloat16),
            jax.ShapeDtypeStruct((1, width), jnp.float32),
        ],
        in_specs=[VM] * 3,
        out_specs=[VM] * 2,
        compiler_params=pltpu.CompilerParams(vmem_limit_bytes=VMEM_BYTES),
    )(got, kept, gain)


ROWS = 256
CHUNK = 512


def key_limits(group_len, slots):
    short_total = sum(side * side for side in SHORT_SIDES)
    long_total = sum(side * side for side in LONG_SIDES)
    limits = [0] * (group_len // ROWS)
    for longs in range(1, slots + 1):
        for shorts in range(slots - longs + 1):
            total = longs * long_total + shorts * short_total
            if not group_len - short_total < total <= group_len:
                continue
            ends, position = [], 0
            for long_side, short_side in zip(LONG_SIDES, SHORT_SIDES):
                position += longs * long_side**2 + shorts * short_side**2
                ends.append(position)
            ends.append(group_len)
            for block in range(len(limits)):
                last = block * ROWS + ROWS - 1
                seen = min(end for end in ends if end > last)
                limits[block] = max(limits[block], -(-seen // LANES) * LANES)
    return limits


def same_limits(limits):
    groups = []
    for block, limit in enumerate(limits):
        if groups and groups[-1][2] == limit:
            groups[-1][1] = block + 1
        else:
            groups.append([block, block + 1, limit])
    return groups


def fold_lanes(values, combine):
    total = values[:, :LANES]
    for j in range(1, values.shape[1] // LANES):
        total = combine(total, values[:, j * LANES : (j + 1) * LANES])
    return total


def split_three(values):
    high = values.astype(jnp.bfloat16).astype(jnp.float32)
    rest = values - high
    mid = rest.astype(jnp.bfloat16).astype(jnp.float32)
    return high, mid, rest - mid


def lanes_three(lane, first, values, otherwise):
    high, mid, rest = split_three(values)
    return jnp.where(
        lane == first, high, jnp.where(lane == first + 1, mid, jnp.where(lane == first + 2, rest, otherwise))
    )


def attend_back_kernel(
    groups, got_ref, out32_ref, q_ref, k_ref, kt_ref, vt_ref, pack_ref, g_ref, gt_ref, qt_ref, dq_ref, dkt_ref, dvt_ref
):
    owners = got_ref.shape[0]
    mid = got_ref.shape[1]
    tokens = 2 * mid
    two = 2 * tokens
    f32, low = jnp.float32, jnp.bfloat16
    lane = lane_iota((two, LANES))
    lane_mid = lane_iota((mid, LANES))

    def unpack(pair, carry):
        rows = pl.ds(pl.multiple_of(pair * two, two), two)
        pieces = []
        for e in range(2):
            g = got_ref[2 * pair + e].astype(f32)
            pieces += [g, swap_halves(g)]
        grad = jnp.where(lane < HALF_LANES, jnp.concatenate(pieces, axis=0), 0.0)
        delta = jnp.sum(grad * out32_ref[rows, :], axis=1, keepdims=True)
        grad = lanes_three(lane, HALF_LANES, -delta, grad)
        g_ref[rows, :] = grad.astype(low)
        gt_ref[:, rows] = grad.T[:HALF_LANES].astype(low)
        qt_ref[:, rows] = q_ref[rows, :].astype(f32).T[:HALF_LANES].astype(low)
        return carry

    lax.fori_loop(0, owners // 2, unpack, 0)
    dkt_ref[...] = jnp.zeros_like(dkt_ref)
    dvt_ref[...] = jnp.zeros_like(dvt_ref)

    def query_block(limit, b, carry):
        rows = pl.ds(pl.multiple_of(b * ROWS, ROWS), ROWS)
        q, g = q_ref[rows, :], g_ref[rows, :]
        qt, gt = qt_ref[:, rows], gt_ref[:, rows]

        def chunk(cols, acc):
            p = jnp.exp(nn(q, kt_ref[:, cols]))
            ds = (p * nn(g, vt_ref[:, cols])).astype(low)
            dvt_ref[:, cols] += nn(gt, p.astype(low))
            dkt_ref[:, cols] += nn(qt, ds)
            return acc + nn(ds, k_ref[cols, :])

        whole, left = limit // CHUNK, limit % CHUNK
        acc = lax.fori_loop(
            0,
            whole,
            lambda c, acc: chunk(pl.ds(pl.multiple_of(c * CHUNK, CHUNK), CHUNK), acc),
            jnp.zeros((ROWS, LANES), f32),
        )
        if left:
            acc = chunk(slice(whole * CHUNK, limit), acc)
        dq_ref[rows, :] = acc
        return carry

    for first, last, limit in groups:
        lax.fori_loop(first, last, functools.partial(query_block, limit), 0)

    def send_out(pair, carry):
        first = pl.multiple_of(pair * two, two)
        rows = pl.ds(first, two)
        dkv = jnp.concatenate([dkt_ref[:, rows], dvt_ref[:, rows]], axis=0).T
        dq = dq_ref[rows, :]
        qk = jnp.where(lane < HALF_LANES, dq, swap_halves(dkv)).astype(low)
        for e in range(2):
            pack_ref[2 * pair + e, 0:tokens, :] = qk[e * tokens : (e + 1) * tokens]
            a = dkv[e * tokens : e * tokens + mid]
            b = dkv[e * tokens + mid : (e + 1) * tokens]
            pack_ref[2 * pair + e, tokens:, :] = jnp.where(lane_mid < HALF_LANES, swap_halves(a), b).astype(low)
        return carry

    lax.fori_loop(0, owners // 2, send_out, 0)


def attend_back(got, kept, groups):
    owners, mid, _ = got.shape
    group_len = owners * mid * 2
    low = jnp.bfloat16
    return pl.pallas_call(
        functools.partial(attend_back_kernel, groups),
        out_shape=jax.ShapeDtypeStruct((owners, 3 * mid, LANES), low),
        in_specs=[VM] * 6,
        out_specs=VM,
        scratch_shapes=[
            pltpu.VMEM((group_len, LANES), low),
            pltpu.VMEM((HALF_LANES, group_len), low),
            pltpu.VMEM((HALF_LANES, group_len), low),
            pltpu.VMEM((group_len, LANES), jnp.float32),
            pltpu.VMEM((HALF_LANES, group_len), jnp.float32),
            pltpu.VMEM((HALF_LANES, group_len), jnp.float32),
        ],
        compiler_params=pltpu.CompilerParams(vmem_limit_bytes=VMEM_BYTES),
    )(got, *kept)


class Gather:
    KINDS = ("up", "down", "x", "y", "turn")

    def __init__(self, shards, fulls, sems, pieces):
        self.shards, self.fulls, self.pieces = shards, fulls, pieces
        self.send, self.recv, self.send_s, self.recv_s, self.local = sems
        self.core, self.z, self.yx = place()
        core, z, yx = self.core, self.z, self.yx
        self.up_dev, self.down_dev = at_dev(core, lax.min(z + 1, 3), yx), at_dev(core, lax.max(z - 1, 0), yx)
        self.x_dev, self.y_dev = at_dev(core, z, yx ^ 1), at_dev(core, z, yx ^ 2)
        self.sib = at_dev(1 - core, z, yx)
        self.ends = []

    @staticmethod
    def scratch(count):
        dma = pltpu.SemaphoreType.DMA
        return [dma((count, 5, 4)), dma((count, 4, 4)), dma((count, 4, 4)), dma((count, 4, 4)), dma((count,))]

    def spot(self, p, z_at, d, core=None):
        i, first, rows = self.pieces[p]
        core = self.core if core is None else core
        size = self.shards[i].shape[0]
        start = pl.multiple_of((z_at * 4 + (self.yx ^ d)) * size + first, 16)
        return self.fulls[i].at[core, pl.ds(start, rows)]

    def copy(self, p, kind, z_at, d, src=None):
        there = {0: 0, 1: 0, 2: 1, 3: 2, 4: 3}[kind]
        ref = self.spot(p, z_at, d)
        device = (self.up_dev, self.down_dev, self.x_dev, self.y_dev)[kind] if kind < 4 else (self.y_dev if d == 1 else self.x_dev)
        return pltpu.make_async_remote_copy(
            src_ref=ref if src is None else src,
            dst_ref=ref,
            send_sem=self.send.at[p, kind, z_at],
            recv_sem=self.recv.at[p, there, z_at],
            device_id=device,
            device_id_type=MESH_ID,
        )

    def go(self, condition, p, kind, z_at, d, src=None):
        def start():
            self.copy(p, kind, z_at, d, src).start()

        def end():
            self.copy(p, kind, z_at, d, src).wait_send()

        if condition is None:
            start()
            self.ends.append(end)
        else:
            pl.when(condition)(start)
            self.ends.append(lambda: pl.when(condition)(end))

    def across(self, p, d):
        for z_at in range(4):
            ref = self.spot(p, z_at, d)
            copy = pltpu.make_async_remote_copy(
                src_ref=ref,
                dst_ref=ref,
                send_sem=self.send_s.at[p, d, z_at],
                recv_sem=self.recv_s.at[p, d, z_at],
                device_id=self.sib,
                device_id_type=MESH_ID,
            )
            copy.start()
            self.ends.append(copy.wait_send)

    def arrive(self, p, kind, z_at, d):
        ref = self.spot(p, z_at, d)
        pltpu.make_async_copy(ref, ref, self.recv.at[p, kind, z_at]).wait()

    def own(self, p):
        i, first, rows = self.pieces[p]
        src = self.shards[i].at[pl.ds(first, rows)]
        z = self.z
        self.go(z < 3, p, 0, z, 0, src)
        self.go(z > 0, p, 1, z, 0, src)
        self.go(None, p, 2, z, 0, src)
        self.go(None, p, 3, z, 0, src)
        copy = pltpu.make_async_copy(src, self.spot(p, z, 0), self.local.at[p])
        copy.start()
        self.locals_ = getattr(self, "locals_", {})
        self.locals_[p] = copy

    def z_step(self, p, r):
        z = self.z
        for side in (-1, 1):
            there = (z - r >= 0) if side < 0 else (z + r <= 3)
            z_at = z + side * r

            def landed(z_at=z_at):
                self.arrive(p, 0, z_at, 0)

            pl.when(there)(landed)
            if side < 0:
                self.go(there & (z < 3), p, 0, z_at, 0)
            else:
                self.go(there & (z > 0), p, 1, z_at, 0)
            self.go(there, p, 2, z_at, 0)
            self.go(there, p, 3, z_at, 0)

    def plane_step(self, p, r):
        z = self.z
        for side in (-1, 1) if r else (0,):
            z_at = z + side * r
            there = None if not r else ((z - r >= 0) if side < 0 else (z + r <= 3))

            def landed(z_at=z_at):
                self.arrive(p, 1, z_at, 1)
                self.arrive(p, 2, z_at, 2)

            if there is None:
                landed()
            else:
                pl.when(there)(landed)
            low_z, high_z = z_at < 2, z_at >= 2
            self.go(low_z if there is None else there & low_z, p, 4, z_at, 1)
            self.go(high_z if there is None else there & high_z, p, 4, z_at, 2)

    def stage(self, p, s):
        if s == 0:
            self.own(p)
        elif s == 1:
            self.z_step(p, 1)
            self.plane_step(p, 0)
        elif s == 2:
            self.z_step(p, 2)
            self.plane_step(p, 1)
        elif s == 3:
            self.z_step(p, 3)
            self.locals_[p].wait()
            self.across(p, 0)
            self.plane_step(p, 2)
        elif s == 4:
            self.plane_step(p, 3)
            self.across(p, 1)
            self.across(p, 2)
        elif s == 5:
            for z_at in range(4):
                self.arrive(p, 3, z_at, 3)
            self.across(p, 3)

    STAGES = 6

    def steps(self):
        return len(self.pieces) + self.STAGES - 1

    def run(self, t):
        for s in range(self.STAGES):
            if 0 <= t - s < len(self.pieces):
                self.stage(t - s, s)

    def landed(self):
        for p in range(len(self.pieces)):
            for d in range(4):
                for z_at in range(4):
                    ref = self.spot(p, z_at, d, 1 - self.core)
                    pltpu.make_async_copy(ref, ref, self.recv_s.at[p, d, z_at]).wait()

    def finish(self):
        for end in self.ends:
            end()


def pieces_of(shards, splits):
    pieces = []
    for i, (shard, split) in enumerate(zip(shards, splits)):
        rows = shard.shape[0] // split
        pieces += [(i, j * rows, rows) for j in range(split)]
    return pieces


class Exchange:
    def __init__(self, out, landed, sems):
        self.out, self.landed = out, landed
        self.send, self.recv = sems
        self.core, z, yx = place()
        self.wide = z * 4 + yx

    def copy(self, w):
        return pltpu.make_async_remote_copy(
            src_ref=self.out.at[w],
            dst_ref=self.landed.at[self.wide],
            send_sem=self.send.at[w],
            recv_sem=self.recv.at[self.wide],
            device_id=(self.core, w),
            device_id_type=MESH_ID,
        )

    def push(self, w):
        pl.when(w != self.wide)(lambda: self.copy(w).start())

        def keep():
            self.landed[w] = self.out[w]

        pl.when(w == self.wide)(keep)

    def wait(self, w):
        def landed():
            ref = self.landed.at[w]
            pltpu.make_async_copy(ref, ref, self.recv.at[w]).wait()

        pl.when(w != self.wide)(landed)

    def finish(self):
        for w in range(16):
            pl.when(w != self.wide)(lambda w=w: self.copy(w).wait_send())


def front_kernel(groups, *refs):
    (s_qkv, s_out, s_up, s_down, ada_in, x_ref, one_hot_ref, vec_ref, starts_ref, ends_ref, rule_ref) = refs[:11]
    (f_qkv, f_out, f_up, f_down, ada_ref, h_ref, kept_ref, out32_ref, q_ref, k_ref, kt_ref, vt_ref, low_ref) = refs[11:24]
    (w_ref, send_ref, got_ref, back_send, back_got, v_ref, s_ref, load_sem) = refs[24:32]
    sems = refs[32:]
    first_flow = Gather([s_qkv], [f_qkv], sems[:5], pieces_of([s_qkv], (2,)))
    flow = Gather([s_out, s_up, s_down], [f_out, f_up, f_down], sems[5:10], pieces_of([s_out, s_up, s_down], (1, 2, 2)))
    ada_send, ada_recv = sems[10:12]
    there = Exchange(send_ref, got_ref, sems[12:14])
    home = Exchange(back_send, back_got, sems[14:16])
    core, z, yx = place()
    wide = z * 4 + yx
    tokens, width = x_ref.shape
    half = width // 2
    mid = tokens // 2
    two = 2 * tokens
    f32, low = jnp.float32, jnp.bfloat16
    entry_barrier([(core, wide ^ r) for r in range(1, 16)] + [(1 - core, wide)])

    first_flow.run(0)
    ada_copies = []
    for r in range(1, 16):
        copy = pltpu.make_async_remote_copy(
            src_ref=ada_in,
            dst_ref=ada_ref.at[wide],
            send_sem=ada_send.at[r],
            recv_sem=ada_recv.at[r],
            device_id=(core, wide ^ r),
            device_id_type=MESH_ID,
        )
        copy.start()
        ada_copies.append(copy)
    ada_ref[wide] = ada_in[...]
    first_flow.run(1)
    x = x_ref[...]
    centred = x - jnp.mean(x, axis=1, keepdims=True)
    unit = centred * lax.rsqrt(jnp.mean(centred * centred, axis=1, keepdims=True) + NORM_EPS)
    first_flow.run(2)
    for copy in ada_copies:
        copy.wait_recv()
    ada = jnp.concatenate([ada_ref[w] for w in range(16)], axis=1)

    def of_tokens(block):
        rows = ada[:, block * width : (block + 1) * width] + vec_ref[block : block + 1, :]
        return lax.dot_general(
            one_hot_ref[...],
            rows,
            (((1,), (0,)), ((), ())),
            precision=HIGHEST_PRECISION,
            preferred_element_type=f32,
        )

    h_ref[...] = (unit * (1.0 + of_tokens(2)) + of_tokens(4)).astype(low)
    for t in range(3, first_flow.steps()):
        first_flow.run(t)
    flow.run(0)
    first_flow.landed()

    group = 256
    loads = []

    def load(j):
        g = lax.rem(z + 1 + j, 4)
        out = []
        for c in range(2):
            for part in range(3):
                rows = pl.ds(pl.multiple_of(g * group + part * width, group), group)
                out.append(pltpu.make_async_copy(f_qkv.at[c, rows], w_ref.at[j, c, part], load_sem.at[j, c, part]))
        return out

    for j in range(4):
        loads.append(load(j))
        for copy in loads[-1]:
            copy.start()
    lane = lane_iota((tokens, LANES))
    lane_mid = lane_iota((mid, LANES))
    for j in range(4):
        g = lax.rem(z + 1 + j, 4)
        first = pl.multiple_of(g * group, group)
        for copy in loads[j]:
            copy.wait()

        def project(part):
            return nt(h_ref[:, :half], w_ref[j, 0, part]) + nt(h_ref[:, half:], w_ref[j, 1, part])

        q_all, k_all, v_all = (project(part) for part in range(3))
        kept_ref[:, pl.ds(first, group)] = q_all
        kept_ref[:, pl.ds(pl.multiple_of(first + width, group), group)] = k_all
        q_all = q_all * lax.rsqrt(head_sums(q_all * q_all) + NORM_EPS)
        q_all = q_all * (8.0 * (1.0 + vec_ref[7:8, pl.ds(first, group)]))
        k_all = k_all * lax.rsqrt(head_sums(k_all * k_all) + NORM_EPS)
        for pair in range(group // LANES):
            cols = slice(pair * LANES, (pair + 1) * LANES)
            q, k, v = q_all[:, cols], k_all[:, cols], v_all[:, cols]
            head = g * (group // HALF_LANES) + 2 * pair
            send_ref[head, 0:tokens, :] = jnp.where(lane < HALF_LANES, q, swap_halves(k)).astype(low)
            send_ref[head + 1, 0:tokens, :] = jnp.where(lane < HALF_LANES, swap_halves(q), k).astype(low)
            v_a, v_b = v[:mid], v[mid:]
            send_ref[head, tokens:, :] = jnp.where(lane_mid < HALF_LANES, v_a, swap_halves(v_b)).astype(low)
            send_ref[head + 1, tokens:, :] = jnp.where(lane_mid < HALF_LANES, swap_halves(v_a), v_b).astype(low)
        for e in range(4):
            there.push(g * 4 + e)
        if j == 1:
            flow.run(1)

    lane_two = lane_iota((two, LANES))

    def unpack(pair, carry):
        for e in range(2):
            there.wait(2 * pair + e)
        first = pl.multiple_of(pair * two, two)
        qk = jnp.concatenate([got_ref[2 * pair + e, 0:tokens, :].astype(f32) for e in range(2)], axis=0)
        spot = first + lax.broadcasted_iota(jnp.int32, (two, LANES), 0)
        runs = ((spot >= starts_ref[...]) & (spot < ends_ref[...])).astype(f32)
        barred = nn(runs.astype(low), rule_ref[...])
        rows = pl.ds(first, two)
        q_ref[rows, :] = jnp.where(lane_two < HALF_LANES, qk, barred).astype(low)
        tail = jnp.where(lane_two >= LANES - 3, 1.0, runs)
        keys = jnp.where(lane_two < HALF_LANES, swap_halves(qk), tail)
        k_ref[rows, :] = keys.astype(low)
        kt_ref[:, rows] = keys.T.astype(low)
        ones = ((lane_mid >= HALF_LANES) & (lane_mid < HALF_LANES + 3)).astype(f32)
        pieces = []
        for e in range(2):
            v = got_ref[2 * pair + e, tokens:, :].astype(f32)
            pieces.append(jnp.where(lane_mid < HALF_LANES, v, ones))
            pieces.append(jnp.where(lane_mid < HALF_LANES, swap_halves(v), ones))
        values = jnp.concatenate(pieces, axis=0)
        v_ref[rows, :] = values.astype(low)
        vt_ref[:, rows] = values.T.astype(low)
        return carry

    lane_q = lane_iota((ROWS, LANES))

    def query_block(limit, b, carry):
        rows = pl.ds(pl.multiple_of(b * ROWS, ROWS), ROWS)
        q = q_ref[rows, :]

        def score(c, top):
            cols = pl.ds(pl.multiple_of(c * CHUNK, CHUNK), CHUNK)
            s = nn(q, kt_ref[:, cols])
            s_ref[:, cols] = s
            return jnp.maximum(top, fold_lanes(s, jnp.maximum))

        whole, left = limit // CHUNK, limit % CHUNK
        top = lax.fori_loop(0, whole, score, jnp.full((ROWS, LANES), -3e38, f32))
        if left:
            tail = slice(whole * CHUNK, limit)
            s = nn(q, kt_ref[:, tail])
            s_ref[:, tail] = s
            top = jnp.maximum(top, fold_lanes(s, jnp.maximum))
        peak = jnp.max(top, axis=1, keepdims=True)

        def weigh(cols, carry):
            total, acc = carry
            p = jnp.exp(s_ref[:, cols] - peak)
            return total + fold_lanes(p, jnp.add), acc + nn(p.astype(low), v_ref[cols, :])

        zero = jnp.zeros((ROWS, LANES), f32)
        total, acc = lax.fori_loop(
            0,
            whole,
            lambda c, carry: weigh(pl.ds(pl.multiple_of(c * CHUNK, CHUNK), CHUNK), carry),
            (zero, zero),
        )
        if left:
            total, acc = weigh(slice(whole * CHUNK, limit), (total, acc))
        total = jnp.sum(total, axis=1, keepdims=True)
        out32_ref[rows, :] = acc / total
        log_total = peak + jnp.log(total)
        q_ref[rows, :] = lanes_three(lane_q, LANES - 3, -log_total, q.astype(f32)).astype(low)
        return carry

    def give_back(w, carry):
        rows = pl.multiple_of(w * tokens, tokens)
        a = out32_ref[pl.ds(rows, mid), :]
        b = out32_ref[pl.ds(pl.multiple_of(rows + mid, mid), mid), :]
        back_send[w] = jnp.where(lane_mid < HALF_LANES, a, swap_halves(b)).astype(low)
        home.push(w)
        return carry

    lax.fori_loop(0, 4, unpack, 0)
    flow.run(2)
    lax.fori_loop(4, 8, unpack, 0)
    flow.run(3)
    plane = 4 * tokens // ROWS
    t = 4
    for p in range(4):
        for first, last, limit in groups:
            begin, end = max(first, p * plane), min(last, (p + 1) * plane)
            if begin < end:
                lax.fori_loop(begin, end, functools.partial(query_block, limit), 0)
        lax.fori_loop(4 * p, 4 * p + 4, give_back, 0)
        if p and t < flow.steps():
            flow.run(t)
            t += 1
    for i in range(t, flow.steps()):
        flow.run(i)
    for pair in range(8):
        home.wait(2 * pair)
        home.wait(2 * pair + 1)
        cols = slice(pair * LANES, (pair + 1) * LANES)
        even, odd = back_got[2 * pair].astype(f32), back_got[2 * pair + 1].astype(f32)
        low_ref[0:mid, cols] = jnp.where(lane_mid < HALF_LANES, even, swap_halves(odd)).astype(low)
        low_ref[mid:, cols] = jnp.where(lane_mid < HALF_LANES, swap_halves(even), odd).astype(low)
    flow.landed()
    first_flow.finish()
    flow.finish()
    there.finish()
    home.finish()
    for copy in ada_copies:
        copy.wait_send()


def front(shards, ada_block, x_zero, one_hot, vectors, starts, ends, rule, groups):
    tokens, width = x_zero.shape
    group_len = 16 * tokens
    f32, low = jnp.float32, jnp.bfloat16
    dma = pltpu.SemaphoreType.DMA
    shape = jax.ShapeDtypeStruct
    fulls = [shape((2, 16 * s.shape[0], s.shape[1]), low) for s in shards]
    outs = fulls + [
        shape((16,) + ada_block.shape, f32),
        shape((tokens, width), low),
        shape((tokens, 2 * width), f32),
        shape((group_len, LANES), f32),
        shape((group_len, LANES), low),
        shape((group_len, LANES), low),
        shape((LANES, group_len), low),
        shape((LANES, group_len), low),
        shape((tokens, width), low),
    ]
    packed, mid = tokens * 3 // 2, tokens // 2
    scratch = [
        pltpu.VMEM((4, 2, 3, 256, width // 2), low),
        pltpu.VMEM((16, packed, LANES), low),
        pltpu.VMEM((16, packed, LANES), low),
        pltpu.VMEM((16, mid, LANES), low),
        pltpu.VMEM((16, mid, LANES), low),
        pltpu.VMEM((group_len, LANES), low),
        pltpu.VMEM((ROWS, group_len), f32),
        dma((4, 2, 3)),
    ]
    scratch += Gather.scratch(2) + Gather.scratch(5) + [dma((16,)) for _ in range(6)]
    return pl.pallas_call(
        functools.partial(front_kernel, groups),
        out_shape=outs,
        in_specs=[ANY] * 4 + [VM] * 7,
        out_specs=[ANY] * 4 + [VM] * 9,
        scratch_shapes=scratch,
        compiler_params=pltpu.CompilerParams(
            collective_id=0, has_side_effects=True, vmem_limit_bytes=VMEM_BYTES
        ),
    )(*shards, ada_block, x_zero, one_hot, vectors, starts, ends, rule)


def run_bounds(lengths, group_len):
    short_sq = jnp.array([side * side for side in SHORT_SIDES], jnp.int32)
    long_sq = jnp.array([side * side for side in LONG_SIDES], jnp.int32)
    counts = jnp.where(
        lengths[None, :] == sum(side * side for side in LONG_SIDES),
        long_sq[:, None],
        jnp.where(lengths[None, :] == sum(side * side for side in SHORT_SIDES), short_sq[:, None], 0),
    ).reshape(-1)
    ends = jnp.cumsum(counts)
    starts = ends - counts
    pad = lambda v, last: jnp.concatenate([v, last])
    ends = pad(ends, jnp.full((1,), group_len, jnp.int32))
    starts = pad(starts, ends[-2:-1])
    return starts, ends


def attention_rule(slots):
    runs = slots * LEVELS + 1
    rule = np.zeros((LANES, LANES), np.float32)
    for a in range(runs):
        for b in range(runs):
            slot_a, level_a = (slots, 0) if a == runs - 1 else (a % slots, a // slots)
            slot_b, level_b = (slots, 0) if b == runs - 1 else (b % slots, b // slots)
            if slot_a != slot_b or level_b > level_a:
                rule[HALF_LANES + a, HALF_LANES + b] = -BIG
    return rule


def to_heads(rows):
    tokens = rows.shape[0]
    split = rows.reshape(2, tokens // 2, HEADS, HALF_LANES)
    return split.transpose(2, 1, 0, 3).reshape(HEADS, tokens // 2, LANES)


def fast_shards(
    feature_map,
    condition,
    item_lengths,
    cotangent,
    code_book,
    qkv_state,
    out_state,
    up_state,
    down_state,
    ada_state,
    embed_state,
    vector_state,
):
    tok_rows, model_width = cotangent.shape
    low, f32 = jnp.bfloat16, jnp.float32
    half = model_width // 2
    core, wide = lax.axis_index("dp"), lax.axis_index("wide")
    group_len = tok_rows * lax.axis_size("wide")
    tokens_all = lax.axis_size("dp") * group_len
    lengths = item_lengths[0]
    slot_count = lengths.shape[0]
    swap = [(0, 1), (1, 0)]

    states = (qkv_state, out_state, up_state, down_state, ada_state)
    flipped = tuple(stacked[1].astype(low).T for stacked in states[:4])
    w_ada = ada_state[1].astype(low)

    silu_own = jax.nn.silu(condition).astype(low)
    silu_all = lax.all_gather(silu_own, "dp", axis=0, tiled=True)
    silu_rows = lax.dynamic_slice_in_dim(silu_all, core * half, half, 1)
    ada_part = jnp.dot(silu_rows, w_ada, preferred_element_type=f32)
    ada_theirs = lax.dynamic_slice_in_dim(ada_part, (1 - core) * slot_count, slot_count, 0)
    ada_mine = lax.dynamic_slice_in_dim(ada_part, core * slot_count, slot_count, 0)
    ada_mine = ada_mine + lax.ppermute(ada_theirs, "dp", swap)
    ada_block = jnp.pad(ada_mine, ((0, 8 - slot_count), (0, 0)))

    starts, ends = run_bounds(lengths, group_len)
    positions = wide * tok_rows + jnp.arange(tok_rows, dtype=jnp.int32)
    after_start = positions[:, None] >= starts[None, :]
    before_end = positions[:, None] < ends[None, :]
    runs_of = (after_start & before_end).astype(f32)
    live_rows = 1.0 - runs_of[:, -1:]
    left_ok = 1.0 - jnp.sum(((positions[:, None] == starts[None, :]) & before_end).astype(f32), axis=1)
    right_ok = 1.0 - jnp.sum(((positions[:, None] == ends[None, :] - 1) & after_start).astype(f32), axis=1)
    one_hot = jnp.sum(runs_of[:, :-1].reshape(tok_rows, LEVELS, slot_count), axis=1)

    rimmed = padded(feature_map, (("wide", 1),), 1)
    smooth = smooth_map(feature_map, left_ok, right_ok, rimmed[:, :-2], rimmed[:, 2:])
    embed_w = embed_state[1]
    vectors = vector_state[1]
    gain = vectors[7:8]
    x_zero = (
        lax.dot_general(smooth, embed_w, (((0,), (0,)), ((), ())), precision=HIGHEST_PRECISION)
        + vectors[6]
    )
    groups = same_limits(key_limits(group_len, slot_count))
    lane_pad = lambda v: jnp.pad(v, (HALF_LANES, HALF_LANES - v.shape[0]))[None]
    rule = jnp.asarray(attention_rule(slot_count), low)
    one_hot_wide = jnp.pad(one_hot, ((0, 0), (0, 8 - slot_count)))
    (w_qkv, w_out, w_up, w_down, ada_gathered, h_one_low, kept_qk, out32, *kept, attn_low) = front(
        flipped, ada_block, x_zero, one_hot_wide, vectors, lane_pad(starts), lane_pad(ends), rule, groups
    )
    kept = [out32] + kept
    ada_product = ada_gathered[:, :slot_count].transpose(1, 0, 2).reshape(slot_count, -1)
    ada_all = ada_product + vectors[:6].reshape(-1)
    token_ada = jnp.dot(one_hot, ada_all, precision=HIGHEST_PRECISION)
    gate_one, gate_two, scale_one, scale_two, shift_one, shift_two = jnp.split(token_ada, 6, axis=1)

    attn_proj = against(attn_low[:, :half], w_out[0]) + against(attn_low[:, half:], w_out[1])
    x_one = x_zero + gate_one * attn_proj
    h_two_low = pre_norm(x_one, scale_two, shift_two).astype(low)
    hidden_pre = against(h_two_low[:, :half], w_up[0]) + against(h_two_low[:, half:], w_up[1])
    act_low = jax.nn.gelu(hidden_pre, approximate=True).astype(low)
    hidden_half = w_down.shape[2]
    mlp_out = against(act_low[:, :hidden_half], w_down[0]) + against(act_low[:, hidden_half:], w_down[1])
    x_two = x_one + gate_two * mlp_out
    block_out = (x_two * live_rows).astype(low)
    logits = against(block_out, code_book)
    code_mass = jnp.sum(jax.nn.softmax(logits, axis=-1) * live_rows, axis=0)

    g_two = cotangent.astype(f32) * live_rows
    d_mlp = (gate_two * g_two).astype(low)
    d_gate_two = g_two * mlp_out

    def summed_over_cores(grad_rows, inputs):
        width = inputs.shape[1] // 2
        other = lax.dynamic_slice_in_dim(inputs, (1 - core) * width, width, 1)
        own = lax.dynamic_slice_in_dim(inputs, core * width, width, 1)
        theirs = lax.ppermute(contract_rows(grad_rows, other).astype(low), "dp", swap)
        total = (contract_rows(grad_rows, own) + theirs.astype(f32)).astype(low)
        return total.reshape(4, 4, -1, width)

    def both_halves(values, weights):
        return jnp.concatenate(
            [jnp.dot(values, weights[h], preferred_element_type=f32) for h in range(2)], axis=1
        )

    p_down = summed_over_cores(d_mlp, act_low)
    d_act = both_halves(d_mlp, w_down)
    _, gelu_back = jax.vjp(lambda inputs: jax.nn.gelu(inputs, approximate=True), hidden_pre)
    d_hidden = gelu_back(d_act)[0].astype(low)
    p_up = summed_over_cores(d_hidden, h_two_low)
    d_h_two = both_halves(d_hidden, w_up)
    _, norm_back_two = jax.vjp(pre_norm, x_one, scale_two, shift_two)
    d_x_one, d_scale_two, d_shift_two = norm_back_two(d_h_two)
    d_x_one = d_x_one + g_two
    d_attn = (gate_one * d_x_one).astype(low)
    d_gate_one = d_x_one * attn_proj
    p_out = summed_over_cores(d_attn, attn_low)
    d_attended = both_halves(d_attn, w_out).astype(low)
    s_out, s_up, s_down = scatter_grads([p_out, p_up, p_down], 2)

    back = lax.all_to_all(to_heads(d_attended), "wide", 0, 0, tiled=True)
    d_pack = attend_back(back, kept, groups)
    d_got = lax.all_to_all(d_pack, "wide", 0, 0, tiled=True)
    d_projected_low, d_gain = heads_backward(d_got, kept_qk, gain)
    p_qkv = summed_over_cores(d_projected_low, h_one_low)
    (s_qkv,) = scatter_grads([p_qkv], 3)
    d_h_one = both_halves(d_projected_low, w_qkv)
    _, norm_back_one = jax.vjp(pre_norm, x_zero, scale_one, shift_one)
    d_x_zero, d_scale_one, d_shift_one = norm_back_one(d_h_one)
    d_x_zero = d_x_zero + d_x_one
    d_token_ada = jnp.concatenate(
        [d_gate_one, d_gate_two, d_scale_one, d_scale_two, d_shift_one, d_shift_two], axis=1
    )
    d_ada_part = contract_rows(one_hot, d_token_ada, HIGHEST_PRECISION)
    d_smooth = lax.dot_general(embed_w, d_x_zero, (((1,), (1,)), ((), ())), precision=HIGHEST_PRECISION)
    d_embed = lax.dot_general(smooth, d_x_zero, (((1,), (0,)), ((), ())), precision=HIGHEST_PRECISION)
    grad_share = d_smooth / (2.0 + left_ok + right_ok)
    rim_share = padded(grad_share, (("wide", 1),), 1)
    map_grad = 2.0 * grad_share + left_ok * rim_share[:, :-2] + right_ok * rim_share[:, 2:]

    wides = lax.axis_size("wide")
    ada_rows = d_ada_part.reshape(slot_count, wides, -1, LANES)
    per_slot = ada_rows.shape[2]
    ada_rows = ada_rows.transpose(1, 0, 2, 3).reshape(wides, -1, LANES)
    code_rows = code_mass.reshape(-1, model_width)
    common = jnp.concatenate([d_embed, jnp.sum(d_x_zero, axis=0)[None], d_gain, code_rows], axis=0)
    common_rows = common.shape[0]
    common = common.reshape(common_rows, wides, -1).transpose(1, 0, 2).reshape(wides, -1, LANES)
    plain_rows = common.shape[1]
    small_in = jnp.concatenate([ada_rows, common], axis=1)
    ada_count = ada_rows.shape[1]
    d_ada_both, sums = small_sums(small_in, ada_count, slot_count, 4)
    common_sum = sums[:, :plain_rows].reshape(wides, common_rows, -1).transpose(1, 0, 2)
    common_sum = common_sum.reshape(common_rows, model_width)
    embed_rows = embed_w.shape[0]
    d_embed_all = common_sum[:embed_rows]
    bias_sum = sums[:, plain_rows:].reshape(6, model_width)
    d_vectors_all = jnp.concatenate([bias_sum, common_sum[embed_rows : embed_rows + 2]], axis=0)
    histogram = common_sum[embed_rows + 2 :].reshape(-1) * (code_book.shape[0] / tokens_all)
    d_ada_own = d_ada_both.reshape(2 * slot_count, per_slot * LANES)
    grad_ada = contract_rows(silu_rows.astype(f32), d_ada_own, HIGHEST_PRECISION)

    owned_grads = (s_qkv.T, s_out.T, s_up.T, s_down.T, grad_ada)
    root_tokens = math.sqrt(tokens_all)
    spreads = (
        model_width ** (-0.5),
        (model_width // 16) ** (-0.5),
        model_width ** (-0.5),
        w_up.shape[1] ** (-0.5),
        model_width ** (-0.5),
    )
    new_states = tuple(
        nesterov(stacked, gradient, BASE_RATE * spread_w / (factor_g * root_tokens), WEIGHT_DECAY)
        for stacked, gradient, spread_w, factor_g in zip(states, owned_grads, spreads, GRAD_FACTORS)
    )
    embed_new = nesterov(
        embed_state, d_embed_all, BASE_RATE * embed_rows ** (-0.5) / (EMBED_FACTOR * root_tokens), 0.0
    )
    vector_new = nesterov(vector_state, d_vectors_all, VECTOR_RATE / root_tokens, 0.0)
    outputs = [block_out, map_grad, histogram]
    for state in new_states:
        outputs += [state, state[1].astype(low)]
    return tuple(outputs + [embed_new, vector_new, d_vectors_all[7]])


def solution(mesh):
    body = fast_shards if dict(mesh.shape) == {"dp": 2, "wide": 16} else shards
    in_specs = (
        P(None, ("dp", "wide")),
        P("dp", None),
        P("dp", None),
        P(("dp", "wide"), None),
        P(),
        P(None, "dp", "wide"),
        P(None, "dp", "wide"),
        P(None, "dp", "wide"),
        P(None, "dp", "wide"),
        P(None, "dp", "wide"),
        P(),
        P(),
    )
    out_specs = (
        P(("dp", "wide"), None),
        P(None, ("dp", "wide")),
        P(),
        P(None, "dp", "wide"),
        P("dp", "wide"),
        P(None, "dp", "wide"),
        P("dp", "wide"),
        P(None, "dp", "wide"),
        P("dp", "wide"),
        P(None, "dp", "wide"),
        P("dp", "wide"),
        P(None, "dp", "wide"),
        P("dp", "wide"),
        P(),
        P(),
        P(),
    )
    return jax.shard_map(body, mesh=mesh, in_specs=in_specs, out_specs=out_specs, check_vma=False)
```

```python
import functools
import math

import jax
import jax.numpy as jnp
import numpy as np
from jax import lax
from jax.experimental import pallas as pl
from jax.experimental.pallas import tpu as pltpu
from jax.sharding import PartitionSpec as P

HEADS = 16
LEVELS = 10
STEP = 7


SHORT_SIDES = (1, 2, 3, 4, 5, 6, 8, 10, 13, 16)
LONG_SIDES = (1, 2, 3, 4, 6, 9, 13, 18, 24, 32)
MASKED = -1e30
NORM_EPS = 1e-06
MOMENTUM = 0.9
WEIGHT_DECAY = 0.05
BASE_RATE = 0.37
VECTOR_RATE = 0.22
GRAD_FACTORS = (0.15, 0.1, 0.3, 0.35, 0.3)
EMBED_FACTOR = 0.6
HIGHEST_PRECISION = lax.Precision.HIGHEST


def padded(cells, sides, width):
    for axis, dim in sides:
        count = lax.axis_size(axis)
        ends = count - 1
        head = lax.slice_in_dim(cells, 0, width, axis=dim)
        tail = lax.slice_in_dim(cells, cells.shape[dim] - width, cells.shape[dim], axis=dim)
        cells = jnp.concatenate(
            [
                lax.ppermute(tail, axis, [(i, (i + 1) % count) for i in range(ends)]),
                cells,
                lax.ppermute(head, axis, [((i + 1) % count, i) for i in range(ends)]),
            ],
            axis=dim,
        )
    return cells


def layout(lengths, positions, group_len):
    short_sq = jnp.array([side * side for side in SHORT_SIDES[:LEVELS]], jnp.int32)
    long_sq = jnp.array([side * side for side in LONG_SIDES[:LEVELS]], jnp.int32)
    short_total = sum((side * side for side in SHORT_SIDES[:LEVELS]))
    long_total = sum((side * side for side in LONG_SIDES[:LEVELS]))
    slot_count = lengths.shape[0]
    counts = jnp.where(
        lengths[None, :] == long_total,
        long_sq[:, None],
        jnp.where(lengths[None, :] == short_total, short_sq[:, None], 0),
    )
    unused = group_len - jnp.sum(lengths)
    ordered = jnp.concatenate([counts.reshape(-1), unused[None]])
    boundary = jnp.cumsum(ordered)
    segment = jnp.sum((boundary[None, :] <= positions[:, None]).astype(jnp.int32), axis=1)
    segment = jnp.minimum(segment, ordered.shape[0] - 1)
    unused_id = slot_count * LEVELS
    tok_level = jnp.where(segment >= unused_id, 0, segment // slot_count)
    tok_slot = jnp.where(segment >= unused_id, slot_count, segment % slot_count)
    return (tok_slot, tok_level, segment)


def pre_norm(inputs, scaling, offset_add):
    row_mean = jnp.mean(inputs, axis=-1, keepdims=True)
    centred = inputs - row_mean
    spread = jnp.mean(centred * centred, axis=-1, keepdims=True)
    return centred * lax.rsqrt(spread + NORM_EPS) * (1.0 + scaling) + offset_add


def unit_heads(inputs):
    shaped = inputs.reshape(inputs.shape[0], HEADS, -1)
    shaped = shaped * lax.rsqrt(jnp.sum(shaped * shaped, axis=-1, keepdims=True) + NORM_EPS)
    return shaped.reshape(inputs.shape)


def split_heads(projected, q_gain):
    queries, key_part, value_part = jnp.split(projected, 3, axis=1)
    head_scale = math.sqrt(queries.shape[1] // HEADS)
    return (unit_heads(queries) * (head_scale * (1.0 + q_gain)), unit_heads(key_part), value_part)


def smooth_map(values, left_ok, right_ok, before, following):
    return (left_ok * before + 2.0 * values + right_ok * following) / (2.0 + left_ok + right_ok)


def nesterov(stacked, gradient, step_rate, decay_rate):
    moment, weight, average = (stacked[0], stacked[1], stacked[2])
    step_grad = gradient + decay_rate * weight
    new_moment = MOMENTUM * moment + step_rate * step_grad
    new_weight = weight - (step_rate * step_grad + MOMENTUM * new_moment)
    retain = min(0.999, (1.0 + STEP) / (10.0 + STEP))
    new_average = retain * average + (1.0 - retain) * new_weight
    return jnp.stack([new_moment, new_weight, new_average])


def contract_rows(left_side, right_side, precision=None):
    return lax.dot_general(
        left_side,
        right_side,
        (((0,), (0,)), ((), ())),
        precision=precision,
        preferred_element_type=jnp.float32,
    )


def against(left_side, right_side):
    return lax.dot_general(
        left_side, right_side, (((1,), (1,)), ((), ())), preferred_element_type=jnp.float32
    )


def shards(
    feature_map,
    condition,
    item_lengths,
    cotangent,
    code_book,
    qkv_state,
    out_state,
    up_state,
    down_state,
    ada_state,
    embed_state,
    vector_state,
):
    tok_rows = cotangent.shape[0]
    model_width = cotangent.shape[1]
    head_dim = model_width // HEADS
    wide_count = lax.axis_size("wide")
    group_len = tok_rows * wide_count
    tokens_all = lax.axis_size("dp") * group_len
    lengths = item_lengths[0]
    slot_count = lengths.shape[0]
    positions = lax.axis_index("wide") * tok_rows + jnp.arange(tok_rows, dtype=jnp.int32)
    tok_slot, tok_level, segment = layout(lengths, positions, group_len)
    live_rows = (tok_slot < slot_count).astype(jnp.float32)[:, None]
    left_ok = ((layout(lengths, positions - 1, group_len)[2] == segment) & (positions > 0)).astype(
        jnp.float32
    )
    right_ok = (
        (layout(lengths, positions + 1, group_len)[2] == segment) & (positions < group_len - 1)
    ).astype(jnp.float32)
    rimmed = padded(feature_map, (("wide", 1),), 1)
    smooth = smooth_map(feature_map, left_ok, right_ok, rimmed[:, :-2], rimmed[:, 2:])
    states = (qkv_state, out_state, up_state, down_state, ada_state)
    masters = tuple((stacked[1].astype(jnp.bfloat16) for stacked in states))
    columns = (
        lax.all_gather(masters[0], "wide", axis=1, tiled=True),
        lax.all_gather(masters[1], "wide", axis=1, tiled=True),
        lax.all_gather(masters[2], "wide", axis=1, tiled=True),
        lax.all_gather(masters[3], "wide", axis=1, tiled=True),
    )
    ada_piece = lax.all_gather(masters[4], "wide", axis=1, tiled=True)
    w_qkv, w_out, w_up, w_down, w_ada = (
        lax.all_gather(columns[0], "dp", axis=0, tiled=True),
        lax.all_gather(columns[1], "dp", axis=0, tiled=True),
        lax.all_gather(columns[2], "dp", axis=0, tiled=True),
        lax.all_gather(columns[3], "dp", axis=0, tiled=True),
        lax.all_gather(ada_piece, "dp", axis=0, tiled=True),
    )
    embed_w = embed_state[1]
    vectors = vector_state[1]
    x_zero = (
        lax.dot_general(smooth, embed_w, (((0,), (0,)), ((), ())), precision=HIGHEST_PRECISION)
        + vectors[6]
    )
    silu_cond = jax.nn.silu(condition).astype(jnp.bfloat16)
    ada_product = jnp.dot(silu_cond, w_ada, preferred_element_type=jnp.float32)
    ada_all = ada_product + vectors[:6].reshape(-1)
    one_hot = (tok_slot[:, None] == jnp.arange(slot_count, dtype=jnp.int32)[None, :]).astype(
        jnp.float32
    )
    token_ada = jnp.dot(one_hot, ada_all, precision=HIGHEST_PRECISION)
    gate_one, gate_two, scale_one, scale_two, shift_one, shift_two = jnp.split(token_ada, 6, axis=1)
    h_one_low = pre_norm(x_zero, scale_one, shift_one).astype(jnp.bfloat16)
    projected = jnp.dot(h_one_low, w_qkv, preferred_element_type=jnp.float32)
    (q_unit, k_unit, v_full), heads_back = jax.vjp(split_heads, projected, vectors[7])
    queries = q_unit.astype(jnp.bfloat16)
    keys_low = k_unit.astype(jnp.bfloat16)
    values_low = v_full.astype(jnp.bfloat16)
    query_heads = queries.reshape(tok_rows, HEADS, head_dim)

    def blockwise(advance, running, pieces, first_row):
        key_count = pieces[0].shape[0]
        block_size = math.gcd(key_count, 1024)

        def per_block(current, offset):
            key_part = tuple(
                (lax.dynamic_slice_in_dim(piece_arr, offset, block_size, 0) for piece_arr in pieces)
            )
            first_key = first_row + offset
            k_slot, k_level, _ = layout(
                lengths, first_key + jnp.arange(block_size, dtype=jnp.int32), group_len
            )
            allowed = (tok_slot[:, None] == k_slot[None, :]) & (
                k_level[None, :] <= tok_level[:, None]
            )
            current = advance(current, key_part, allowed, first_key)
            return (current, None)

        offsets = jnp.arange(key_count // block_size, dtype=jnp.int32) * block_size
        return lax.scan(per_block, running, offsets)[0]

    def scores_of(key_block, allowed):
        raw_scores = jnp.einsum(
            "qhd,khd->hqk",
            query_heads,
            key_block.reshape(-1, HEADS, head_dim),
            preferred_element_type=jnp.float32,
        )
        return jnp.where(allowed[None], raw_scores, MASKED)

    def stats_step(running, key_part, allowed, first_key):
        scores = scores_of(key_part[0], allowed)
        top_score, exp_total = running
        new_top = jnp.maximum(top_score, jnp.max(scores, axis=-1, keepdims=True))
        exp_total = exp_total * jnp.exp(top_score - new_top) + jnp.sum(
            jnp.exp(scores - new_top), axis=-1, keepdims=True
        )
        return (new_top, exp_total)

    kv_rows = (
        lax.all_gather(keys_low, "wide", axis=0, tiled=True),
        lax.all_gather(values_low, "wide", axis=0, tiled=True),
    )
    start_stats = (
        jnp.full((HEADS, tok_rows, 1), MASKED, jnp.float32),
        jnp.zeros((HEADS, tok_rows, 1), jnp.float32),
    )
    top_score, exp_total = blockwise(stats_step, start_stats, kv_rows, 0)
    log_total = top_score + jnp.log(exp_total)

    def value_step(running, key_part, allowed, first_key):
        attn_probs = jnp.exp(scores_of(key_part[0], allowed) - log_total).astype(jnp.bfloat16)
        return running + jnp.einsum(
            "hqk,khd->qhd",
            attn_probs,
            key_part[1].reshape(-1, HEADS, head_dim),
            preferred_element_type=jnp.float32,
        )

    attended = blockwise(
        value_step, jnp.zeros((tok_rows, HEADS, head_dim), jnp.float32), kv_rows, 0
    )
    attn_low = attended.reshape(tok_rows, model_width).astype(jnp.bfloat16)
    attn_proj = jnp.dot(attn_low, w_out, preferred_element_type=jnp.float32)
    x_one = x_zero + gate_one * attn_proj
    h_two_low = pre_norm(x_one, scale_two, shift_two).astype(jnp.bfloat16)
    hidden_pre = jnp.dot(h_two_low, w_up, preferred_element_type=jnp.float32)
    act_low = jax.nn.gelu(hidden_pre, approximate=True).astype(jnp.bfloat16)
    mlp_out = jnp.dot(act_low, w_down, preferred_element_type=jnp.float32)
    x_two = x_one + gate_two * mlp_out
    block_out = (x_two * live_rows).astype(jnp.bfloat16)
    logits = against(block_out, code_book)
    code_mass = jnp.sum(jax.nn.softmax(logits, axis=-1) * live_rows, axis=0)
    g_two = cotangent.astype(jnp.float32) * live_rows
    d_mlp = (gate_two * g_two).astype(jnp.bfloat16)
    d_gate_two = g_two * mlp_out
    dw_down = contract_rows(act_low, d_mlp)
    d_act = against(d_mlp, w_down)
    _, gelu_back = jax.vjp(lambda inputs: jax.nn.gelu(inputs, approximate=True), hidden_pre)
    d_hidden = gelu_back(d_act)[0].astype(jnp.bfloat16)
    dw_up = contract_rows(h_two_low, d_hidden)
    d_h_two = against(d_hidden, w_up)
    _, norm_back_two = jax.vjp(pre_norm, x_one, scale_two, shift_two)
    d_x_one, d_scale_two, d_shift_two = norm_back_two(d_h_two)
    d_x_one = d_x_one + g_two
    d_attn = (gate_one * d_x_one).astype(jnp.bfloat16)
    d_gate_one = d_x_one * attn_proj
    dw_out = contract_rows(attn_low, d_attn)
    grad_flat = against(d_attn, w_out).astype(jnp.bfloat16)
    grad_heads = grad_flat.reshape(tok_rows, HEADS, head_dim)

    def delta_step(running, key_part, allowed, first_key):
        attn_probs = jnp.exp(scores_of(key_part[0], allowed) - log_total)
        d_probs = jnp.einsum(
            "qhd,khd->hqk",
            grad_heads,
            key_part[1].reshape(-1, HEADS, head_dim),
            preferred_element_type=jnp.float32,
        )
        return running + jnp.sum(attn_probs * d_probs, axis=-1, keepdims=True)

    row_delta = blockwise(delta_step, jnp.zeros((HEADS, tok_rows, 1), jnp.float32), kv_rows, 0)

    def grad_step(running, key_part, allowed, first_key):
        d_query, d_keys, d_values = running
        key_heads = key_part[0].reshape(-1, HEADS, head_dim)
        value_heads = key_part[1].reshape(-1, HEADS, head_dim)
        block_rows = key_part[0].shape[0]
        attn_probs = jnp.exp(scores_of(key_part[0], allowed) - log_total)
        d_probs = jnp.einsum(
            "qhd,khd->hqk", grad_heads, value_heads, preferred_element_type=jnp.float32
        )
        d_scores = (attn_probs * (d_probs - row_delta)).astype(jnp.bfloat16)
        d_query = d_query + jnp.einsum(
            "hqk,khd->qhd", d_scores, key_heads, preferred_element_type=jnp.float32
        )
        key_grad = jnp.einsum(
            "hqk,qhd->khd", d_scores, query_heads, preferred_element_type=jnp.float32
        )
        value_grad = jnp.einsum(
            "hqk,qhd->khd",
            attn_probs.astype(jnp.bfloat16),
            grad_heads,
            preferred_element_type=jnp.float32,
        )
        key_sum = lax.dynamic_slice_in_dim(d_keys, first_key, block_rows, 0) + key_grad.reshape(
            block_rows, model_width
        )
        value_sum = lax.dynamic_slice_in_dim(
            d_values, first_key, block_rows, 0
        ) + value_grad.reshape(block_rows, model_width)
        d_keys = lax.dynamic_update_slice_in_dim(d_keys, key_sum, first_key, 0)
        d_values = lax.dynamic_update_slice_in_dim(d_values, value_sum, first_key, 0)
        return (d_query, d_keys, d_values)

    grad_init = (
        jnp.zeros((tok_rows, HEADS, head_dim), jnp.float32),
        jnp.zeros((group_len, model_width), jnp.float32),
        jnp.zeros((group_len, model_width), jnp.float32),
    )
    d_query, d_keys, d_values = blockwise(grad_step, grad_init, kv_rows, 0)
    d_keys_own, d_values_own = (
        lax.psum_scatter(
            d_keys.astype(jnp.bfloat16), "wide", scatter_dimension=0, tiled=True
        ).astype(jnp.float32),
        lax.psum_scatter(
            d_values.astype(jnp.bfloat16), "wide", scatter_dimension=0, tiled=True
        ).astype(jnp.float32),
    )
    d_projected, d_gain = heads_back(
        (d_query.reshape(tok_rows, model_width), d_keys_own, d_values_own)
    )
    d_projected_low = d_projected.astype(jnp.bfloat16)
    dw_qkv = contract_rows(h_one_low, d_projected_low)
    d_h_one = against(d_projected_low, w_qkv)
    _, norm_back_one = jax.vjp(pre_norm, x_zero, scale_one, shift_one)
    d_x_zero, d_scale_one, d_shift_one = norm_back_one(d_h_one)
    d_x_zero = d_x_zero + d_x_one
    d_token_ada = jnp.concatenate(
        [d_gate_one, d_gate_two, d_scale_one, d_scale_two, d_shift_one, d_shift_two], axis=1
    )
    d_ada_all = contract_rows(one_hot, d_token_ada, HIGHEST_PRECISION)
    d_smooth = lax.dot_general(
        embed_w, d_x_zero, (((1,), (1,)), ((), ())), precision=HIGHEST_PRECISION
    )
    d_embed = lax.dot_general(
        smooth, d_x_zero, (((1,), (0,)), ((), ())), precision=HIGHEST_PRECISION
    )
    d_vectors = jnp.concatenate(
        [
            jnp.sum(d_ada_all, axis=0).reshape(6, model_width),
            jnp.sum(d_x_zero, axis=0)[None],
            d_gain[None],
        ],
        axis=0,
    )
    grad_share = d_smooth / (2.0 + left_ok + right_ok)
    rim_share = padded(grad_share, (("wide", 1),), 1)
    map_grad = 2.0 * grad_share + left_ok * rim_share[:, :-2] + right_ok * rim_share[:, 2:]
    d_embed_all, d_vectors_all, mass_all = lax.psum((d_embed, d_vectors, code_mass), ("dp", "wide"))
    histogram = mass_all * (code_book.shape[0] / tokens_all)
    ada_term = contract_rows(silu_cond.astype(jnp.float32), d_ada_all, HIGHEST_PRECISION)
    split_cols = (
        lax.psum_scatter(
            dw_qkv.astype(jnp.bfloat16), "wide", scatter_dimension=1, tiled=True
        ).astype(jnp.float32),
        lax.psum_scatter(
            dw_out.astype(jnp.bfloat16), "wide", scatter_dimension=1, tiled=True
        ).astype(jnp.float32),
        lax.psum_scatter(
            dw_up.astype(jnp.bfloat16), "wide", scatter_dimension=1, tiled=True
        ).astype(jnp.float32),
        lax.psum_scatter(
            dw_down.astype(jnp.bfloat16), "wide", scatter_dimension=1, tiled=True
        ).astype(jnp.float32),
        lax.psum_scatter(
            ada_term.astype(jnp.bfloat16), "wide", scatter_dimension=1, tiled=True
        ).astype(jnp.float32),
    )
    ada_cols = split_cols[4]
    owned_grads = (
        lax.psum_scatter(
            split_cols[0].astype(jnp.bfloat16), "dp", scatter_dimension=0, tiled=True
        ).astype(jnp.float32),
        lax.psum_scatter(
            split_cols[1].astype(jnp.bfloat16), "dp", scatter_dimension=0, tiled=True
        ).astype(jnp.float32),
        lax.psum_scatter(
            split_cols[2].astype(jnp.bfloat16), "dp", scatter_dimension=0, tiled=True
        ).astype(jnp.float32),
        lax.psum_scatter(
            split_cols[3].astype(jnp.bfloat16), "dp", scatter_dimension=0, tiled=True
        ).astype(jnp.float32),
        lax.psum_scatter(
            ada_cols.astype(jnp.bfloat16), "dp", scatter_dimension=0, tiled=True
        ).astype(jnp.float32),
    )
    root_tokens = math.sqrt(tokens_all)
    spreads = (
        model_width ** (-0.5),
        (model_width // 16) ** (-0.5),
        model_width ** (-0.5),
        w_up.shape[1] ** (-0.5),
        model_width ** (-0.5),
    )
    new_states = tuple(
        (
            nesterov(
                stacked, gradient, BASE_RATE * spread_w / (factor_g * root_tokens), WEIGHT_DECAY
            )
            for stacked, gradient, spread_w, factor_g in zip(
                states, owned_grads, spreads, GRAD_FACTORS
            )
        )
    )
    embed_new = nesterov(
        embed_state,
        d_embed_all,
        BASE_RATE * embed_w.shape[0] ** (-0.5) / (EMBED_FACTOR * root_tokens),
        0.0,
    )
    vector_new = nesterov(vector_state, d_vectors_all, VECTOR_RATE / root_tokens, 0.0)
    return (
        block_out,
        map_grad,
        histogram,
        new_states[0],
        new_states[0][1].astype(jnp.bfloat16),
        new_states[1],
        new_states[1][1].astype(jnp.bfloat16),
        new_states[2],
        new_states[2][1].astype(jnp.bfloat16),
        new_states[3],
        new_states[3][1].astype(jnp.bfloat16),
        new_states[4],
        new_states[4][1].astype(jnp.bfloat16),
        embed_new,
        vector_new,
        d_vectors_all[7],
    )


MESH_ID = pl.DeviceIdType.MESH
ANY = pl.BlockSpec(memory_space=pl.ANY)
VM = pl.BlockSpec(memory_space=pltpu.VMEM)
VMEM_BYTES = 56 * 1024 * 1024
LANES = 128
HALF_LANES = 64
BIG = 1e30


def nt(left_side, right_side):
    return lax.dot_general(
        left_side, right_side, (((1,), (1,)), ((), ())), preferred_element_type=jnp.float32
    )


def nn(left_side, right_side):
    return lax.dot_general(
        left_side, right_side, (((1,), (0,)), ((), ())), preferred_element_type=jnp.float32
    )


def entry_barrier(peers):
    barrier = pltpu.get_barrier_semaphore()
    for peer in peers:
        pl.semaphore_signal(barrier, inc=1, device_id=peer, device_id_type=MESH_ID)
    pl.semaphore_wait(barrier, len(peers))


def place():
    core, wide = lax.axis_index("dp"), lax.axis_index("wide")
    return core, wide // 4, wide % 4


def at_dev(core, z, yx):
    return (core, z * 4 + yx)


def lane_iota(shape):
    return lax.broadcasted_iota(jnp.int32, shape, len(shape) - 1)


def swap_halves(pair):
    return pltpu.roll(pair, HALF_LANES, 1)


def head_sums(values):
    width = values.shape[1]
    rows = lax.broadcasted_iota(jnp.int32, (width, width), 0) // HALF_LANES
    cols = lax.broadcasted_iota(jnp.int32, (width, width), 1) // HALF_LANES
    ones = (rows == cols).astype(jnp.float32)
    return lax.dot_general(
        values,
        ones,
        (((1,), (0,)), ((), ())),
        precision=HIGHEST_PRECISION,
        preferred_element_type=jnp.float32,
    )


ROWS = 256
CHUNK = 512


def key_limits(group_len, slots):
    short_total = sum(side * side for side in SHORT_SIDES)
    long_total = sum(side * side for side in LONG_SIDES)
    limits = [0] * (group_len // ROWS)
    for longs in range(1, slots + 1):
        for shorts in range(slots - longs + 1):
            total = longs * long_total + shorts * short_total
            if not group_len - short_total < total <= group_len:
                continue
            ends, position = [], 0
            for long_side, short_side in zip(LONG_SIDES, SHORT_SIDES):
                position += longs * long_side**2 + shorts * short_side**2
                ends.append(position)
            ends.append(group_len)
            for block in range(len(limits)):
                last = block * ROWS + ROWS - 1
                seen = min(end for end in ends if end > last)
                limits[block] = max(limits[block], -(-seen // LANES) * LANES)
    return limits


def same_limits(limits):
    groups = []
    for block, limit in enumerate(limits):
        if groups and groups[-1][2] == limit:
            groups[-1][1] = block + 1
        else:
            groups.append([block, block + 1, limit])
    return groups


def fold_lanes(values, combine):
    total = values[:, :LANES]
    for j in range(1, values.shape[1] // LANES):
        total = combine(total, values[:, j * LANES : (j + 1) * LANES])
    return total


def split_three(values):
    high = values.astype(jnp.bfloat16).astype(jnp.float32)
    rest = values - high
    mid = rest.astype(jnp.bfloat16).astype(jnp.float32)
    return high, mid, rest - mid


def lanes_three(lane, first, values, otherwise):
    high, mid, rest = split_three(values)
    return jnp.where(
        lane == first, high, jnp.where(lane == first + 1, mid, jnp.where(lane == first + 2, rest, otherwise))
    )


class Gather:
    KINDS = ("up", "down", "x", "y", "turn")

    def __init__(self, shards, fulls, sems, pieces):
        self.shards, self.fulls, self.pieces = shards, fulls, pieces
        self.send, self.recv, self.send_s, self.recv_s, self.local = sems
        self.core, self.z, self.yx = place()
        core, z, yx = self.core, self.z, self.yx
        self.up_dev, self.down_dev = at_dev(core, lax.min(z + 1, 3), yx), at_dev(core, lax.max(z - 1, 0), yx)
        self.x_dev, self.y_dev = at_dev(core, z, yx ^ 1), at_dev(core, z, yx ^ 2)
        self.sib = at_dev(1 - core, z, yx)
        self.ends = []

    @staticmethod
    def scratch(count):
        dma = pltpu.SemaphoreType.DMA
        return [dma((count, 5, 4)), dma((count, 4, 4)), dma((count, 4, 4)), dma((count, 4, 4)), dma((count,))]

    def spot(self, p, z_at, d, core=None):
        i, first, rows = self.pieces[p]
        core = self.core if core is None else core
        size = self.shards[i].shape[0]
        start = pl.multiple_of((z_at * 4 + (self.yx ^ d)) * size + first, 16)
        return self.fulls[i].at[core, pl.ds(start, rows)]

    def copy(self, p, kind, z_at, d, src=None):
        there = {0: 0, 1: 0, 2: 1, 3: 2, 4: 3}[kind]
        ref = self.spot(p, z_at, d)
        device = (self.up_dev, self.down_dev, self.x_dev, self.y_dev)[kind] if kind < 4 else (self.y_dev if d == 1 else self.x_dev)
        return pltpu.make_async_remote_copy(
            src_ref=ref if src is None else src,
            dst_ref=ref,
            send_sem=self.send.at[p, kind, z_at],
            recv_sem=self.recv.at[p, there, z_at],
            device_id=device,
            device_id_type=MESH_ID,
        )

    def go(self, condition, p, kind, z_at, d, src=None):
        def start():
            self.copy(p, kind, z_at, d, src).start()

        def end():
            self.copy(p, kind, z_at, d, src).wait_send()

        if condition is None:
            start()
            self.ends.append(end)
        else:
            pl.when(condition)(start)
            self.ends.append(lambda: pl.when(condition)(end))

    def across(self, p, d):
        for z_at in range(4):
            ref = self.spot(p, z_at, d)
            copy = pltpu.make_async_remote_copy(
                src_ref=ref,
                dst_ref=ref,
                send_sem=self.send_s.at[p, d, z_at],
                recv_sem=self.recv_s.at[p, d, z_at],
                device_id=self.sib,
                device_id_type=MESH_ID,
            )
            copy.start()
            self.ends.append(copy.wait_send)

    def arrive(self, p, kind, z_at, d):
        ref = self.spot(p, z_at, d)
        pltpu.make_async_copy(ref, ref, self.recv.at[p, kind, z_at]).wait()

    def own(self, p):
        i, first, rows = self.pieces[p]
        src = self.shards[i].at[pl.ds(first, rows)]
        z = self.z
        self.go(z < 3, p, 0, z, 0, src)
        self.go(z > 0, p, 1, z, 0, src)
        self.go(None, p, 2, z, 0, src)
        self.go(None, p, 3, z, 0, src)
        copy = pltpu.make_async_copy(src, self.spot(p, z, 0), self.local.at[p])
        copy.start()
        self.locals_ = getattr(self, "locals_", {})
        self.locals_[p] = copy

    def z_step(self, p, r):
        z = self.z
        for side in (-1, 1):
            there = (z - r >= 0) if side < 0 else (z + r <= 3)
            z_at = z + side * r

            def landed(z_at=z_at):
                self.arrive(p, 0, z_at, 0)

            pl.when(there)(landed)
            if side < 0:
                self.go(there & (z < 3), p, 0, z_at, 0)
            else:
                self.go(there & (z > 0), p, 1, z_at, 0)
            self.go(there, p, 2, z_at, 0)
            self.go(there, p, 3, z_at, 0)

    def plane_step(self, p, r):
        z = self.z
        for side in (-1, 1) if r else (0,):
            z_at = z + side * r
            there = None if not r else ((z - r >= 0) if side < 0 else (z + r <= 3))

            def landed(z_at=z_at):
                self.arrive(p, 1, z_at, 1)
                self.arrive(p, 2, z_at, 2)

            if there is None:
                landed()
            else:
                pl.when(there)(landed)
            low_z, high_z = z_at < 2, z_at >= 2
            self.go(low_z if there is None else there & low_z, p, 4, z_at, 1)
            self.go(high_z if there is None else there & high_z, p, 4, z_at, 2)

    def stage(self, p, s):
        if s == 0:
            self.own(p)
        elif s == 1:
            self.z_step(p, 1)
            self.plane_step(p, 0)
        elif s == 2:
            self.z_step(p, 2)
            self.plane_step(p, 1)
        elif s == 3:
            self.z_step(p, 3)
            self.locals_[p].wait()
            self.across(p, 0)
            self.plane_step(p, 2)
        elif s == 4:
            self.plane_step(p, 3)
            self.across(p, 1)
            self.across(p, 2)
        elif s == 5:
            for z_at in range(4):
                self.arrive(p, 3, z_at, 3)
            self.across(p, 3)

    STAGES = 6

    def steps(self):
        return len(self.pieces) + self.STAGES - 1

    def run(self, t):
        for s in range(self.STAGES):
            if 0 <= t - s < len(self.pieces):
                self.stage(t - s, s)

    def landed(self):
        for p in range(len(self.pieces)):
            for d in range(4):
                for z_at in range(4):
                    ref = self.spot(p, z_at, d, 1 - self.core)
                    pltpu.make_async_copy(ref, ref, self.recv_s.at[p, d, z_at]).wait()

    def finish(self):
        for end in self.ends:
            end()


def pieces_of(shards, splits):
    pieces = []
    for i, (shard, split) in enumerate(zip(shards, splits)):
        rows = shard.shape[0] // split
        pieces += [(i, j * rows, rows) for j in range(split)]
    return pieces


class Exchange:
    def __init__(self, out, landed, sems):
        self.out, self.landed = out, landed
        self.send, self.recv = sems
        self.core, z, yx = place()
        self.wide = z * 4 + yx

    def copy(self, w):
        return pltpu.make_async_remote_copy(
            src_ref=self.out.at[w],
            dst_ref=self.landed.at[self.wide],
            send_sem=self.send.at[w],
            recv_sem=self.recv.at[self.wide],
            device_id=(self.core, w),
            device_id_type=MESH_ID,
        )

    def push(self, w):
        pl.when(w != self.wide)(lambda: self.copy(w).start())

        def keep():
            self.landed[w] = self.out[w]

        pl.when(w == self.wide)(keep)

    def wait(self, w):
        def landed():
            ref = self.landed.at[w]
            pltpu.make_async_copy(ref, ref, self.recv.at[w]).wait()

        pl.when(w != self.wide)(landed)

    def finish(self):
        for w in range(16):
            pl.when(w != self.wide)(lambda w=w: self.copy(w).wait_send())


def front_kernel(groups, *refs):
    (s_qkv, s_out, s_up, s_down, ada_in, x_ref, one_hot_ref, vec_ref, starts_ref, ends_ref, rule_ref) = refs[:11]
    (f_qkv, f_out, f_up, f_down, ada_ref, h_ref, kept_ref, out32_ref, q_ref, k_ref, kt_ref, vt_ref, low_ref) = refs[11:24]
    (w_ref, send_ref, got_ref, back_send, back_got, v_ref, s_ref, load_sem) = refs[24:32]
    sems = refs[32:]
    first_flow = Gather([s_qkv], [f_qkv], sems[:5], pieces_of([s_qkv], (2,)))
    flow = Gather([s_out, s_up, s_down], [f_out, f_up, f_down], sems[5:10], pieces_of([s_out, s_up, s_down], (1, 2, 2)))
    ada_send, ada_recv = sems[10:12]
    there = Exchange(send_ref, got_ref, sems[12:14])
    home = Exchange(back_send, back_got, sems[14:16])
    core, z, yx = place()
    wide = z * 4 + yx
    tokens, width = x_ref.shape
    half = width // 2
    mid = tokens // 2
    two = 2 * tokens
    f32, low = jnp.float32, jnp.bfloat16
    entry_barrier([(core, wide ^ r) for r in range(1, 16)] + [(1 - core, wide)])

    first_flow.run(0)
    ada_copies = []
    for r in range(1, 16):
        copy = pltpu.make_async_remote_copy(
            src_ref=ada_in,
            dst_ref=ada_ref.at[wide],
            send_sem=ada_send.at[r],
            recv_sem=ada_recv.at[r],
            device_id=(core, wide ^ r),
            device_id_type=MESH_ID,
        )
        copy.start()
        ada_copies.append(copy)
    ada_ref[wide] = ada_in[...]
    first_flow.run(1)
    x = x_ref[...]
    centred = x - jnp.mean(x, axis=1, keepdims=True)
    unit = centred * lax.rsqrt(jnp.mean(centred * centred, axis=1, keepdims=True) + NORM_EPS)
    first_flow.run(2)
    for copy in ada_copies:
        copy.wait_recv()
    ada = jnp.concatenate([ada_ref[w] for w in range(16)], axis=1)

    def of_tokens(block):
        rows = ada[:, block * width : (block + 1) * width] + vec_ref[block : block + 1, :]
        return lax.dot_general(
            one_hot_ref[...],
            rows,
            (((1,), (0,)), ((), ())),
            precision=HIGHEST_PRECISION,
            preferred_element_type=f32,
        )

    h_ref[...] = (unit * (1.0 + of_tokens(2)) + of_tokens(4)).astype(low)
    for t in range(3, first_flow.steps()):
        first_flow.run(t)
    flow.run(0)
    first_flow.landed()

    group = 256
    loads = []

    def load(j):
        g = lax.rem(z + 1 + j, 4)
        out = []
        for c in range(2):
            for part in range(3):
                rows = pl.ds(pl.multiple_of(g * group + part * width, group), group)
                out.append(pltpu.make_async_copy(f_qkv.at[c, rows], w_ref.at[j, c, part], load_sem.at[j, c, part]))
        return out

    for j in range(4):
        loads.append(load(j))
        for copy in loads[-1]:
            copy.start()
    lane = lane_iota((tokens, LANES))
    lane_mid = lane_iota((mid, LANES))
    for j in range(4):
        g = lax.rem(z + 1 + j, 4)
        first = pl.multiple_of(g * group, group)
        for copy in loads[j]:
            copy.wait()

        def project(part):
            return nt(h_ref[:, :half], w_ref[j, 0, part]) + nt(h_ref[:, half:], w_ref[j, 1, part])

        q_all, k_all, v_all = (project(part) for part in range(3))
        kept_ref[:, pl.ds(first, group)] = q_all
        kept_ref[:, pl.ds(pl.multiple_of(first + width, group), group)] = k_all
        q_all = q_all * lax.rsqrt(head_sums(q_all * q_all) + NORM_EPS)
        q_all = q_all * (8.0 * (1.0 + vec_ref[7:8, pl.ds(first, group)]))
        k_all = k_all * lax.rsqrt(head_sums(k_all * k_all) + NORM_EPS)
        for pair in range(group // LANES):
            cols = slice(pair * LANES, (pair + 1) * LANES)
            q, k, v = q_all[:, cols], k_all[:, cols], v_all[:, cols]
            head = g * (group // HALF_LANES) + 2 * pair
            send_ref[head, 0:tokens, :] = jnp.where(lane < HALF_LANES, q, swap_halves(k)).astype(low)
            send_ref[head + 1, 0:tokens, :] = jnp.where(lane < HALF_LANES, swap_halves(q), k).astype(low)
            v_a, v_b = v[:mid], v[mid:]
            send_ref[head, tokens:, :] = jnp.where(lane_mid < HALF_LANES, v_a, swap_halves(v_b)).astype(low)
            send_ref[head + 1, tokens:, :] = jnp.where(lane_mid < HALF_LANES, swap_halves(v_a), v_b).astype(low)
        for e in range(4):
            there.push(g * 4 + e)
        if j == 1:
            flow.run(1)

    lane_two = lane_iota((two, LANES))

    def unpack(pair, carry):
        for e in range(2):
            there.wait(2 * pair + e)
        first = pl.multiple_of(pair * two, two)
        qk = jnp.concatenate([got_ref[2 * pair + e, 0:tokens, :].astype(f32) for e in range(2)], axis=0)
        spot = first + lax.broadcasted_iota(jnp.int32, (two, LANES), 0)
        runs = ((spot >= starts_ref[...]) & (spot < ends_ref[...])).astype(f32)
        barred = nn(runs.astype(low), rule_ref[...])
        rows = pl.ds(first, two)
        q_ref[rows, :] = jnp.where(lane_two < HALF_LANES, qk, barred).astype(low)
        tail = jnp.where(lane_two >= LANES - 3, 1.0, runs)
        keys = jnp.where(lane_two < HALF_LANES, swap_halves(qk), tail)
        k_ref[rows, :] = keys.astype(low)
        kt_ref[:, rows] = keys.T.astype(low)
        ones = ((lane_mid >= HALF_LANES) & (lane_mid < HALF_LANES + 3)).astype(f32)
        pieces = []
        for e in range(2):
            v = got_ref[2 * pair + e, tokens:, :].astype(f32)
            pieces.append(jnp.where(lane_mid < HALF_LANES, v, ones))
            pieces.append(jnp.where(lane_mid < HALF_LANES, swap_halves(v), ones))
        values = jnp.concatenate(pieces, axis=0)
        v_ref[rows, :] = values.astype(low)
        vt_ref[:, rows] = values.T.astype(low)
        return carry

    lane_q = lane_iota((ROWS, LANES))

    def query_block(limit, b, carry):
        rows = pl.ds(pl.multiple_of(b * ROWS, ROWS), ROWS)
        q = q_ref[rows, :]

        def score(c, top):
            cols = pl.ds(pl.multiple_of(c * CHUNK, CHUNK), CHUNK)
            s = nn(q, kt_ref[:, cols])
            s_ref[:, cols] = s
            return jnp.maximum(top, fold_lanes(s, jnp.maximum))

        whole, left = limit // CHUNK, limit % CHUNK
        top = lax.fori_loop(0, whole, score, jnp.full((ROWS, LANES), -3e38, f32))
        if left:
            tail = slice(whole * CHUNK, limit)
            s = nn(q, kt_ref[:, tail])
            s_ref[:, tail] = s
            top = jnp.maximum(top, fold_lanes(s, jnp.maximum))
        peak = jnp.max(top, axis=1, keepdims=True)

        def weigh(cols, carry):
            total, acc = carry
            p = jnp.exp(s_ref[:, cols] - peak)
            return total + fold_lanes(p, jnp.add), acc + nn(p.astype(low), v_ref[cols, :])

        zero = jnp.zeros((ROWS, LANES), f32)
        total, acc = lax.fori_loop(
            0,
            whole,
            lambda c, carry: weigh(pl.ds(pl.multiple_of(c * CHUNK, CHUNK), CHUNK), carry),
            (zero, zero),
        )
        if left:
            total, acc = weigh(slice(whole * CHUNK, limit), (total, acc))
        total = jnp.sum(total, axis=1, keepdims=True)
        out32_ref[rows, :] = acc / total
        log_total = peak + jnp.log(total)
        q_ref[rows, :] = lanes_three(lane_q, LANES - 3, -log_total, q.astype(f32)).astype(low)
        return carry

    def give_back(w, carry):
        rows = pl.multiple_of(w * tokens, tokens)
        a = out32_ref[pl.ds(rows, mid), :]
        b = out32_ref[pl.ds(pl.multiple_of(rows + mid, mid), mid), :]
        back_send[w] = jnp.where(lane_mid < HALF_LANES, a, swap_halves(b)).astype(low)
        home.push(w)
        return carry

    lax.fori_loop(0, 4, unpack, 0)
    flow.run(2)
    lax.fori_loop(4, 8, unpack, 0)
    flow.run(3)
    plane = 4 * tokens // ROWS
    t = 4
    for p in range(4):
        for first, last, limit in groups:
            begin, end = max(first, p * plane), min(last, (p + 1) * plane)
            if begin < end:
                lax.fori_loop(begin, end, functools.partial(query_block, limit), 0)
        lax.fori_loop(4 * p, 4 * p + 4, give_back, 0)
        if p and t < flow.steps():
            flow.run(t)
            t += 1
    for i in range(t, flow.steps()):
        flow.run(i)
    for pair in range(8):
        home.wait(2 * pair)
        home.wait(2 * pair + 1)
        cols = slice(pair * LANES, (pair + 1) * LANES)
        even, odd = back_got[2 * pair].astype(f32), back_got[2 * pair + 1].astype(f32)
        low_ref[0:mid, cols] = jnp.where(lane_mid < HALF_LANES, even, swap_halves(odd)).astype(low)
        low_ref[mid:, cols] = jnp.where(lane_mid < HALF_LANES, swap_halves(even), odd).astype(low)
    flow.landed()
    first_flow.finish()
    flow.finish()
    there.finish()
    home.finish()
    for copy in ada_copies:
        copy.wait_send()


def front(shards, ada_block, x_zero, one_hot, vectors, starts, ends, rule, groups):
    tokens, width = x_zero.shape
    group_len = 16 * tokens
    f32, low = jnp.float32, jnp.bfloat16
    dma = pltpu.SemaphoreType.DMA
    shape = jax.ShapeDtypeStruct
    fulls = [shape((2, 16 * s.shape[0], s.shape[1]), low) for s in shards]
    outs = fulls + [
        shape((16,) + ada_block.shape, f32),
        shape((tokens, width), low),
        shape((tokens, 2 * width), f32),
        shape((group_len, LANES), f32),
        shape((group_len, LANES), low),
        shape((group_len, LANES), low),
        shape((LANES, group_len), low),
        shape((LANES, group_len), low),
        shape((tokens, width), low),
    ]
    packed, mid = tokens * 3 // 2, tokens // 2
    scratch = [
        pltpu.VMEM((4, 2, 3, 256, width // 2), low),
        pltpu.VMEM((16, packed, LANES), low),
        pltpu.VMEM((16, packed, LANES), low),
        pltpu.VMEM((16, mid, LANES), low),
        pltpu.VMEM((16, mid, LANES), low),
        pltpu.VMEM((group_len, LANES), low),
        pltpu.VMEM((ROWS, group_len), f32),
        dma((4, 2, 3)),
    ]
    scratch += Gather.scratch(2) + Gather.scratch(5) + [dma((16,)) for _ in range(6)]
    return pl.pallas_call(
        functools.partial(front_kernel, groups),
        out_shape=outs,
        in_specs=[ANY] * 4 + [VM] * 7,
        out_specs=[ANY] * 4 + [VM] * 9,
        scratch_shapes=scratch,
        compiler_params=pltpu.CompilerParams(
            collective_id=0, has_side_effects=True, vmem_limit_bytes=VMEM_BYTES
        ),
    )(*shards, ada_block, x_zero, one_hot, vectors, starts, ends, rule)


class Scatter:
    STAGES = 6

    def __init__(self, parts, outs, bufs, sems, pieces):
        self.parts, self.outs, self.bufs, self.pieces = parts, outs, bufs, pieces
        self.send, self.recv = sems
        core, z, yx = place()
        self.z, self.yx = z, yx
        self.x_dev, self.y_dev = at_dev(core, z, yx ^ 1), at_dev(core, z, yx ^ 2)
        self.up_dev, self.down_dev = at_dev(core, lax.min(z + 1, 3), yx), at_dev(core, lax.max(z - 1, 0), yx)
        self.ends = []

    @staticmethod
    def scratch(shapes, count):
        low = jnp.bfloat16
        out = []
        for rows, cols in shapes:
            out += [pltpu.VMEM((depth, rows, cols), low) for depth in (2, 2, 4, 4, 3, 3)]
        dma = pltpu.SemaphoreType.DMA
        return out + [dma((count, 8)), dma((count, 8))]

    def push(self, p, slot, src, dst, device):
        copy = pltpu.make_async_remote_copy(
            src_ref=src,
            dst_ref=dst,
            send_sem=self.send.at[p, slot],
            recv_sem=self.recv.at[p, slot],
            device_id=device,
            device_id_type=MESH_ID,
        )
        copy.start()
        return copy

    def arrive(self, p, slot, ref):
        pltpu.make_async_copy(ref, ref, self.recv.at[p, slot]).wait()

    def stage(self, p, s):
        i, first, rows = self.pieces[p]
        rows = pl.ds(first, rows)
        part = self.parts[i]
        names = ("turn_x", "turn_y", "rx", "ry", "up", "down")
        buf = dict(zip(names, self.bufs[6 * i : 6 * i + 6]))
        z, yx = self.z, self.yx
        f32, low = jnp.float32, jnp.bfloat16
        lo2, hi2 = pl.ds(0, 2), pl.ds(2, 2)

        def view(name, which):
            return buf[name].at[which, rows]

        def wide(ref):
            return ref[...].astype(f32)

        def hop(condition, slot, name, which, device):
            ref = view(name, which)

            def start():
                self.push(p, slot, ref, ref, device)

            def end():
                pltpu.make_async_copy(ref, ref, self.send.at[p, slot]).wait()

            pl.when(condition)(start)
            self.ends.append(lambda: pl.when(condition)(end))

        if s == 0:
            copies = [
                self.push(p, 0, part.at[lo2, yx ^ 3, rows], view("turn_x", lo2), self.x_dev),
                self.push(p, 1, part.at[hi2, yx ^ 3, rows], view("turn_y", lo2), self.y_dev),
                self.push(p, 2, part.at[lo2, yx ^ 1, rows], view("rx", lo2), self.x_dev),
                self.push(p, 3, part.at[hi2, yx ^ 2, rows], view("ry", hi2), self.y_dev),
            ]
            self.ends += [copy.wait_send for copy in copies]
        elif s == 1:
            turn = view("turn_x", lo2)
            self.arrive(p, 0, turn)
            turn[...] = (wide(part.at[lo2, yx ^ 2, rows]) + wide(turn)).astype(low)
            self.ends.append(self.push(p, 4, turn, view("ry", lo2), self.y_dev).wait_send)
            turn = view("turn_y", lo2)
            self.arrive(p, 1, turn)
            turn[...] = (wide(part.at[hi2, yx ^ 1, rows]) + wide(turn)).astype(low)
            self.ends.append(self.push(p, 5, turn, view("rx", hi2), self.x_dev).wait_send)
        elif s == 2:
            self.arrive(p, 2, view("rx", lo2))
            self.arrive(p, 3, view("ry", hi2))
            self.arrive(p, 4, view("ry", lo2))
            self.arrive(p, 5, view("rx", hi2))
            self.outs[i][rows] = wide(part.at[z, yx, rows]) + wide(view("rx", z)) + wide(view("ry", z))
            for z_at in range(4):
                total = wide(part.at[z_at, yx, rows]) + wide(view("rx", z_at)) + wide(view("ry", z_at))
                view("rx", z_at)[...] = total.astype(low)

            def first_up():
                view("up", pl.ds(0, 3))[...] = view("rx", pl.ds(1, 3))[...]

            def first_down():
                view("down", pl.ds(0, 3))[...] = view("rx", pl.ds(0, 3))[...]

            pl.when(z == 0)(first_up)
            hop(z == 0, 6, "up", pl.ds(0, 3), self.up_dev)
            pl.when(z == 3)(first_down)
            hop(z == 3, 7, "down", pl.ds(0, 3), self.down_dev)
        elif s in (3, 4):
            at = s - 2
            count = 3 - at

            def add_up():
                self.arrive(p, 6, view("up", pl.ds(at - 1, count + 1)))
                ref = view("up", pl.ds(at, count))
                ref[...] = (wide(ref) + wide(view("rx", pl.ds(at + 1, count)))).astype(low)

            def add_down():
                self.arrive(p, 7, view("down", pl.ds(0, count + 1)))
                ref = view("down", pl.ds(0, count))
                ref[...] = (wide(ref) + wide(view("rx", pl.ds(0, count)))).astype(low)

            pl.when(z == at)(add_up)
            hop(z == at, 6, "up", pl.ds(at, count), self.up_dev)
            pl.when(z == 3 - at)(add_down)
            hop(z == 3 - at, 7, "down", pl.ds(0, count), self.down_dev)
        else:
            out = self.outs[i].at[rows]

            def end_low():
                self.arrive(p, 7, view("down", pl.ds(0, 1)))
                out[...] += wide(view("down", 0))

            def end_high():
                self.arrive(p, 6, view("up", pl.ds(2, 1)))
                out[...] += wide(view("up", 2))

            def end_inner(at):
                out[...] += wide(view("up", at - 1)) + wide(view("down", at))

            pl.when(z == 0)(end_low)
            pl.when(z == 1)(lambda: end_inner(1))
            pl.when(z == 2)(lambda: end_inner(2))
            pl.when(z == 3)(end_high)

    def steps(self):
        return len(self.pieces) + self.STAGES - 1

    def run(self, t):
        for s in reversed(range(self.STAGES)):
            if 0 <= t - s < len(self.pieces):
                self.stage(t - s, s)

    def finish(self):
        for end in self.ends:
            end()


COMMON_ROWS = 48


def back_kernel(groups, splits, *refs):
    (
        d_att, out32_ref, q_ref, k_ref, kt_ref, vt_ref, kept_ref, vec_ref, h_ref, w_any,
        p_down, p_up, p_out, x_ref, scale_ref, dx_one, hot_ref, g_one, g_two, g_scale, g_shift,
        smooth_ref, embed_ref, mass_ref, ok_ref,
    ) = refs[:25]
    (o_down, o_up, o_out, o_qkv, ada_both, common_all, bias_all, map_ref) = refs[25:33]
    (
        send_ref, got_ref, back_send, back_got, g_ref, gt_ref, qt_ref, dq_ref, dkt_ref, dvt_ref,
        w_ref, dproj, h_both, p_qkv, dh_ref, ada_ref, com_ref, ada_land, com_land, ada_sum, com_sum, ada_sib, com_sib,
        bias_own, com_own, edge, edge_left, edge_right,
    ) = refs[33:61]
    rest = refs[61:]
    flow_bufs, rest = rest[:18], rest[18:]
    flow_sems, rest = rest[:2], rest[2:]
    last_bufs, rest = rest[:6], rest[6:]
    last_sems, rest = rest[:2], rest[2:]
    (ex_s, ex_r, home_s, home_r, w_sem, sib_s, sib_r, small_s, small_r, spread_s, spread_r, edge_s, edge_r) = rest
    core, z, yx = place()
    wide = z * 4 + yx
    sib = (1 - core, wide)
    f32, low = jnp.float32, jnp.bfloat16
    tokens, width = h_ref.shape
    half = width // 2
    mid = tokens // 2
    two = 2 * tokens
    flow = Scatter([p_down, p_up, p_out], [o_down, o_up, o_out], flow_bufs, flow_sems, splits[0])
    last = Scatter([p_qkv], [o_qkv], last_bufs, last_sems, splits[1])
    there = Exchange(back_send, back_got, (ex_s, ex_r))
    home = Exchange(send_ref, got_ref, (home_s, home_r))
    entry_barrier([(core, wide ^ r) for r in range(1, 16)] + [sib])

    def to_sib(slot, src, dst):
        copy = pltpu.make_async_remote_copy(
            src_ref=src, dst_ref=dst, send_sem=sib_s.at[slot], recv_sem=sib_r.at[slot], device_id=sib, device_id_type=MESH_ID
        )
        copy.start()
        return copy

    lane = lane_iota((two, LANES))
    lane_tok = lane_iota((tokens, LANES))
    lane_mid = lane_iota((mid, LANES))

    def pack(pair, carry):
        cols = pl.ds(pl.multiple_of(pair * LANES, LANES), LANES)
        a, b = d_att[0:mid, cols].astype(f32), d_att[mid:, cols].astype(f32)
        back_send[2 * pair] = jnp.where(lane_mid < HALF_LANES, a, swap_halves(b)).astype(low)
        back_send[2 * pair + 1] = jnp.where(lane_mid < HALF_LANES, swap_halves(a), b).astype(low)
        there.push(2 * pair)
        there.push(2 * pair + 1)
        return carry

    lax.fori_loop(0, 8, pack, 0)
    slab = 3 * width // 4

    def w_load(j):
        rows = pl.ds(j * slab, slab)
        return pltpu.make_async_copy(w_any.at[:, rows], w_ref.at[j % 2], w_sem.at[j % 2])

    w_load(0).start()
    w_load(1).start()
    theirs = pl.ds(pl.multiple_of((1 - core) * half, half), half)
    mine = pl.ds(pl.multiple_of(core * half, half), half)
    h_copy = to_sib(0, h_ref.at[:, theirs], h_both.at[core])
    h_both[core] = h_ref[:, mine]
    flow.run(0)
    dkt_ref[...] = jnp.zeros_like(dkt_ref)
    dvt_ref[...] = jnp.zeros_like(dvt_ref)

    def unpack(pair, carry):
        there.wait(2 * pair)
        there.wait(2 * pair + 1)
        rows = pl.ds(pl.multiple_of(pair * two, two), two)
        pieces = []
        for e in range(2):
            g = back_got[2 * pair + e].astype(f32)
            pieces += [g, swap_halves(g)]
        grad = jnp.where(lane < HALF_LANES, jnp.concatenate(pieces, axis=0), 0.0)
        delta = jnp.sum(grad * out32_ref[rows, :], axis=1, keepdims=True)
        grad = lanes_three(lane, HALF_LANES, -delta, grad)
        g_ref[rows, :] = grad.astype(low)
        gt_ref[:, rows] = grad.T[:HALF_LANES].astype(low)
        qt_ref[:, rows] = q_ref[rows, :].astype(f32).T[:HALF_LANES].astype(low)
        return carry

    lax.fori_loop(0, 8, unpack, 0)
    flow.run(1)

    def query_block(limit, b, carry):
        rows = pl.ds(pl.multiple_of(b * ROWS, ROWS), ROWS)
        q, g = q_ref[rows, :], g_ref[rows, :]
        qt, gt = qt_ref[:, rows], gt_ref[:, rows]

        def chunk(cols, acc):
            p = jnp.exp(nn(q, kt_ref[:, cols]))
            ds = (p * nn(g, vt_ref[:, cols])).astype(low)
            dvt_ref[:, cols] += nn(gt, p.astype(low))
            dkt_ref[:, cols] += nn(qt, ds)
            return acc + nn(ds, k_ref[cols, :])

        whole, left = limit // CHUNK, limit % CHUNK
        acc = lax.fori_loop(
            0,
            whole,
            lambda c, acc: chunk(pl.ds(pl.multiple_of(c * CHUNK, CHUNK), CHUNK), acc),
            jnp.zeros((ROWS, LANES), f32),
        )
        if left:
            acc = chunk(slice(whole * CHUNK, limit), acc)
        dq_ref[rows, :] = acc
        return carry

    t = 2
    for first, stop, limit in groups:
        for begin in range(first, stop, 2):
            end = min(begin + 2, stop)
            lax.fori_loop(begin, end, functools.partial(query_block, limit), 0)
            if begin >= 3 and t < flow.steps():
                flow.run(t)
                t += 1

    def send_out(pair, carry):
        rows = pl.ds(pl.multiple_of(pair * two, two), two)
        dkv = jnp.concatenate([dkt_ref[:, rows], dvt_ref[:, rows]], axis=0).T
        qk = jnp.where(lane < HALF_LANES, dq_ref[rows, :], swap_halves(dkv)).astype(low)
        for e in range(2):
            send_ref[2 * pair + e, 0:tokens, :] = qk[e * tokens : (e + 1) * tokens]
            a = dkv[e * tokens : e * tokens + mid]
            b = dkv[e * tokens + mid : (e + 1) * tokens]
            send_ref[2 * pair + e, tokens:, :] = jnp.where(lane_mid < HALF_LANES, swap_halves(a), b).astype(low)
            home.push(2 * pair + e)
        return carry

    lax.fori_loop(0, 8, send_out, 0)

    def per_slot(values):
        return lax.dot_general(
            hot_ref[...],
            values,
            (((1,), (0,)), ((), ())),
            precision=HIGHEST_PRECISION,
            preferred_element_type=f32,
        )

    for block, ref in ((0, g_one), (1, g_two), (3, g_scale), (5, g_shift)):
        ada_ref[:, block * width : (block + 1) * width] = per_slot(ref[...])
    while t < flow.steps() - 2:
        flow.run(t)
        t += 1

    def unnormalize(values, grad):
        inverse = lax.rsqrt(head_sums(values * values) + NORM_EPS)
        unit = values * inverse
        return inverse * (grad - unit * head_sums(unit * grad)), unit

    com_ref[...] = jnp.zeros_like(com_ref)

    def heads_back(pair, carry):
        home.wait(2 * pair)
        home.wait(2 * pair + 1)
        cols = pl.ds(pl.multiple_of(pair * LANES, LANES), LANES)
        key_cols = pl.ds(pl.multiple_of(pair * LANES + width, LANES), LANES)
        val_cols = pl.ds(pl.multiple_of(pair * LANES + 2 * width, LANES), LANES)
        even = got_ref[2 * pair].astype(f32)
        odd = got_ref[2 * pair + 1].astype(f32)
        even_qk, odd_qk = even[:tokens], odd[:tokens]
        d_query = jnp.where(lane_tok < HALF_LANES, even_qk, swap_halves(odd_qk))
        d_key = jnp.where(lane_tok < HALF_LANES, swap_halves(even_qk), odd_qk)
        even_v, odd_v = even[tokens:], odd[tokens:]
        dproj[core, 0:mid, val_cols] = jnp.where(lane_mid < HALF_LANES, even_v, swap_halves(odd_v)).astype(low)
        dproj[core, mid:, val_cols] = jnp.where(lane_mid < HALF_LANES, swap_halves(even_v), odd_v).astype(low)
        scaled = d_query * (8.0 * (1.0 + vec_ref[7:8, cols]))
        d_q, unit = unnormalize(kept_ref[:, cols], scaled)
        com_ref[33:34, cols] = jnp.sum(d_query * unit, axis=0, keepdims=True) * 8.0
        dproj[core, :, cols] = d_q.astype(low)
        dproj[core, :, key_cols] = unnormalize(kept_ref[:, key_cols], d_key)[0].astype(low)
        return carry

    lax.fori_loop(0, 8, heads_back, 0)
    d_copy = to_sib(1, dproj.at[core], dproj.at[core])

    for j in range(4):
        w_load(j).wait()
        for c in range(2):
            part = nn(dproj[core, :, j * slab : (j + 1) * slab], w_ref[j % 2, c])
            cols = slice(c * half, (c + 1) * half)
            dh_ref[:, cols] = part if j == 0 else dh_ref[:, cols] + part
        if j < 2:
            w_load(j + 2).start()
    h_copy.wait_recv()
    d_copy.wait_recv()

    def weight_grad(c, carry):
        cols = pl.ds(pl.multiple_of(c * two, two), two)
        total = nn(dproj[0, :, cols].astype(f32).T.astype(low), h_both[0])
        total = total + nn(dproj[1, :, cols].astype(f32).T.astype(low), h_both[1])
        p_qkv[c // 2, pl.ds(2 * (c % 2), 2)] = total.astype(low).reshape(2, tokens, half)
        return carry

    lax.fori_loop(0, 8, weight_grad, 0)
    last.run(0)
    while t < flow.steps():
        flow.run(t)
        t += 1

    x = x_ref[...]
    centred = x - jnp.mean(x, axis=1, keepdims=True)
    rstd = lax.rsqrt(jnp.mean(centred * centred, axis=1, keepdims=True) + NORM_EPS)
    unit = centred * rstd
    d_h = dh_ref[...]
    ada_ref[:, 2 * width : 3 * width] = per_slot(d_h * unit)
    ada_ref[:, 4 * width : 5 * width] = per_slot(d_h)
    d_unit = d_h * (1.0 + scale_ref[...])
    d_x = rstd * (
        d_unit
        - jnp.mean(d_unit, axis=1, keepdims=True)
        - unit * jnp.mean(d_unit * unit, axis=1, keepdims=True)
    )
    d_x = d_x + dx_one[...]
    last.run(1)
    com_ref[0:32, :] = lax.dot_general(
        smooth_ref[...], d_x, (((1,), (0,)), ((), ())), precision=HIGHEST_PRECISION, preferred_element_type=f32
    )
    com_ref[32:33, :] = jnp.sum(d_x, axis=0, keepdims=True)
    com_ref[34:38, :] = mass_ref[...]
    small = []
    quarter = COMMON_ROWS // 2

    def common_part(ref, w):
        rows = pl.ds(pl.multiple_of((w // 8) * quarter, 8), quarter)
        return ref.at[rows, pl.ds(pl.multiple_of((w % 8) * LANES, LANES), LANES)]

    ada_width = 6 * width // 16

    def ada_part(ref, w):
        return ref.at[:, pl.ds(pl.multiple_of(w * ada_width, LANES), ada_width)]

    def spread(sem_s, sem_r, r, slot, src, dst):
        copy = pltpu.make_async_remote_copy(
            src_ref=src,
            dst_ref=dst,
            send_sem=sem_s.at[slot, r],
            recv_sem=sem_r.at[slot, r],
            device_id=(core, wide ^ r),
            device_id_type=MESH_ID,
        )
        copy.start()
        return copy

    for r in range(1, 16):
        small.append(spread(small_s, small_r, r, 0, ada_part(ada_ref, wide ^ r), ada_land.at[r]))
        small.append(spread(small_s, small_r, r, 1, common_part(com_ref, wide ^ r), com_land.at[r]))
    d_smooth = lax.dot_general(
        embed_ref[...], d_x, (((1,), (1,)), ((), ())), precision=HIGHEST_PRECISION, preferred_element_type=f32
    )
    left, right = ok_ref[0:1, :], ok_ref[1:2, :]
    share = d_smooth / (2.0 + left + right)
    spot = lane_iota((32, LANES))
    edge[...] = jnp.where(spot == 0, share[:, 0:1], jnp.where(spot == 1, share[:, tokens - 1 : tokens], 0.0))

    def edge_copy(slot, dst, shift):
        return pltpu.make_async_remote_copy(
            src_ref=edge,
            dst_ref=dst,
            send_sem=edge_s.at[slot],
            recv_sem=edge_r.at[slot],
            device_id=(core, lax.rem(wide + shift, 16)),
            device_id_type=MESH_ID,
        )

    to_right, to_left = edge_copy(0, edge_left, 1), edge_copy(1, edge_right, 15)
    last.run(2)
    ada_total, com_total = ada_part(ada_ref, wide)[...], common_part(com_ref, wide)[...]
    for copy in small:
        copy.wait_recv()
    for r in range(1, 16):
        ada_total = ada_total + ada_land[r]
        com_total = com_total + com_land[r]
    ada_sum[...] = ada_total
    com_sum[...] = com_total
    swaps = [to_sib(2, ada_sum, ada_sib), to_sib(3, com_sum, com_sib)]
    last.run(3)
    for copy in swaps:
        copy.wait_recv()
    ada_both[core] = ada_sum[...]
    ada_both[1 - core] = ada_sib[...]
    bias = jnp.sum(ada_sum[...] + ada_sib[...], axis=0, keepdims=True)
    bias_own[...] = jnp.broadcast_to(bias, bias_own.shape)
    com_own[...] = com_sum[...] + com_sib[...]
    ada_part(bias_all, wide)[...] = bias_own[...]
    common_part(common_all, wide)[...] = com_own[...]
    back = []
    for r in range(1, 16):
        back.append(spread(spread_s, spread_r, r, 0, bias_own, ada_part(bias_all, wide)))
        back.append(spread(spread_s, spread_r, r, 1, com_own, common_part(common_all, wide)))
    for i in range(4, last.steps()):
        last.run(i)
    to_right.start()
    to_left.start()
    to_right.wait_recv()
    to_left.wait_recv()
    column = lane_iota((32, tokens))
    before = jnp.where(column == 0, edge_left[:, 1:2], jnp.roll(share, 1, axis=1))
    after = jnp.where(column == tokens - 1, edge_right[:, 0:1], jnp.roll(share, -1, axis=1))
    map_ref[...] = 2.0 * share + left * before + right * after
    for copy in back:
        copy.wait_recv()
    for copy in small + swaps + back + [h_copy, d_copy, to_right, to_left]:
        copy.wait_send()
    flow.finish()
    last.finish()
    there.finish()
    home.finish()


def back(args, groups, splits, call_id):
    d_att, out32 = args[0], args[1]
    tokens, width = d_att.shape
    group_len = 16 * tokens
    half, mid, packed = width // 2, tokens // 2, tokens * 3 // 2
    f32, low = jnp.float32, jnp.bfloat16
    dma = pltpu.SemaphoreType.DMA
    shape = jax.ShapeDtypeStruct
    parts = args[10:13]
    sizes = [p.shape[2:] for p in parts] + [(3 * width // 16, half)]
    counts = [p.shape[2] for p in parts]
    first = pieces_of([shape(s, f32) for s in sizes[:3]], splits[0])
    second = pieces_of([shape(sizes[3], f32)], splits[1])
    ada_width, quarter = 6 * width // 16, COMMON_ROWS // 2
    outs = [shape(s, f32) for s in sizes] + [
        shape((2, 8, ada_width), f32),
        shape((COMMON_ROWS, width), f32),
        shape((8, 6 * width), f32),
        shape((32, tokens), f32),
    ]
    vm = pltpu.VMEM
    scratch = [
        vm((16, packed, LANES), low),
        vm((16, packed, LANES), low),
        vm((16, mid, LANES), low),
        vm((16, mid, LANES), low),
        vm((group_len, LANES), low),
        vm((HALF_LANES, group_len), low),
        vm((HALF_LANES, group_len), low),
        vm((group_len, LANES), f32),
        vm((HALF_LANES, group_len), f32),
        vm((HALF_LANES, group_len), f32),
        vm((2, 2, 3 * width // 4, half), low),
        vm((2, tokens, 3 * width), low),
        vm((2, tokens, half), low),
        vm((4, 4) + sizes[3], low),
        vm((tokens, width), f32),
        vm((8, 6 * width), f32),
        vm((COMMON_ROWS, width), f32),
        vm((16, 8, ada_width), f32),
        vm((16, quarter, LANES), f32),
        vm((8, ada_width), f32),
        vm((quarter, LANES), f32),
        vm((8, ada_width), f32),
        vm((quarter, LANES), f32),
        vm((8, ada_width), f32),
        vm((quarter, LANES), f32),
        vm((32, LANES), f32),
        vm((32, LANES), f32),
        vm((32, LANES), f32),
    ]
    scratch += Scatter.scratch(sizes[:3], len(first)) + Scatter.scratch(sizes[3:], len(second))
    scratch += [dma((16,)) for _ in range(4)] + [dma((2,)), dma((4,)), dma((4,))]
    scratch += [dma((2, 16)) for _ in range(4)] + [dma((2,)), dma((2,))]
    return pl.pallas_call(
        functools.partial(back_kernel, groups, (first, second)),
        out_shape=outs,
        in_specs=[VM] * 9 + [ANY] + [VM] * 15,
        out_specs=[VM] * 8,
        scratch_shapes=scratch,
        compiler_params=pltpu.CompilerParams(
            collective_id=call_id, has_side_effects=True, vmem_limit_bytes=60 * 1024 * 1024
        ),
    )(*args)


def run_bounds(lengths, group_len):
    short_sq = jnp.array([side * side for side in SHORT_SIDES], jnp.int32)
    long_sq = jnp.array([side * side for side in LONG_SIDES], jnp.int32)
    counts = jnp.where(
        lengths[None, :] == sum(side * side for side in LONG_SIDES),
        long_sq[:, None],
        jnp.where(lengths[None, :] == sum(side * side for side in SHORT_SIDES), short_sq[:, None], 0),
    ).reshape(-1)
    ends = jnp.cumsum(counts)
    starts = ends - counts
    pad = lambda v, last: jnp.concatenate([v, last])
    ends = pad(ends, jnp.full((1,), group_len, jnp.int32))
    starts = pad(starts, ends[-2:-1])
    return starts, ends


def attention_rule(slots):
    runs = slots * LEVELS + 1
    rule = np.zeros((LANES, LANES), np.float32)
    for a in range(runs):
        for b in range(runs):
            slot_a, level_a = (slots, 0) if a == runs - 1 else (a % slots, a // slots)
            slot_b, level_b = (slots, 0) if b == runs - 1 else (b % slots, b // slots)
            if slot_a != slot_b or level_b > level_a:
                rule[HALF_LANES + a, HALF_LANES + b] = -BIG
    return rule


def fast_shards(
    feature_map,
    condition,
    item_lengths,
    cotangent,
    code_book,
    qkv_state,
    out_state,
    up_state,
    down_state,
    ada_state,
    embed_state,
    vector_state,
):
    tok_rows, model_width = cotangent.shape
    low, f32 = jnp.bfloat16, jnp.float32
    half = model_width // 2
    core, wide = lax.axis_index("dp"), lax.axis_index("wide")
    group_len = tok_rows * lax.axis_size("wide")
    tokens_all = lax.axis_size("dp") * group_len
    lengths = item_lengths[0]
    slot_count = lengths.shape[0]
    swap = [(0, 1), (1, 0)]

    states = (qkv_state, out_state, up_state, down_state, ada_state)
    flipped = tuple(stacked[1].astype(low).T for stacked in states[:4])
    w_ada = ada_state[1].astype(low)

    silu_own = jax.nn.silu(condition).astype(low)
    silu_all = lax.all_gather(silu_own, "dp", axis=0, tiled=True)
    silu_rows = lax.dynamic_slice_in_dim(silu_all, core * half, half, 1)
    ada_part = jnp.dot(silu_rows, w_ada, preferred_element_type=f32)
    ada_theirs = lax.dynamic_slice_in_dim(ada_part, (1 - core) * slot_count, slot_count, 0)
    ada_mine = lax.dynamic_slice_in_dim(ada_part, core * slot_count, slot_count, 0)
    ada_mine = ada_mine + lax.ppermute(ada_theirs, "dp", swap)
    ada_block = jnp.pad(ada_mine, ((0, 8 - slot_count), (0, 0)))

    starts, ends = run_bounds(lengths, group_len)
    positions = wide * tok_rows + jnp.arange(tok_rows, dtype=jnp.int32)
    after_start = positions[:, None] >= starts[None, :]
    before_end = positions[:, None] < ends[None, :]
    runs_of = (after_start & before_end).astype(f32)
    live_rows = 1.0 - runs_of[:, -1:]
    left_ok = 1.0 - jnp.sum(((positions[:, None] == starts[None, :]) & before_end).astype(f32), axis=1)
    right_ok = 1.0 - jnp.sum(((positions[:, None] == ends[None, :] - 1) & after_start).astype(f32), axis=1)
    one_hot = jnp.sum(runs_of[:, :-1].reshape(tok_rows, LEVELS, slot_count), axis=1)

    rimmed = padded(feature_map, (("wide", 1),), 1)
    smooth = smooth_map(feature_map, left_ok, right_ok, rimmed[:, :-2], rimmed[:, 2:])
    embed_w = embed_state[1]
    vectors = vector_state[1]
    gain = vectors[7:8]
    x_zero = (
        lax.dot_general(smooth, embed_w, (((0,), (0,)), ((), ())), precision=HIGHEST_PRECISION)
        + vectors[6]
    )
    groups = same_limits(key_limits(group_len, slot_count))
    lane_pad = lambda v: jnp.pad(v, (HALF_LANES, HALF_LANES - v.shape[0]))[None]
    rule = jnp.asarray(attention_rule(slot_count), low)
    one_hot_wide = jnp.pad(one_hot, ((0, 0), (0, 8 - slot_count)))
    (w_qkv, w_out, w_up, w_down, ada_gathered, h_one_low, kept_qk, out32, *kept, attn_low) = front(
        flipped, ada_block, x_zero, one_hot_wide, vectors, lane_pad(starts), lane_pad(ends), rule, groups
    )
    kept = [out32] + kept
    ada_product = ada_gathered[:, :slot_count].transpose(1, 0, 2).reshape(slot_count, -1)
    ada_all = ada_product + vectors[:6].reshape(-1)
    token_ada = jnp.dot(one_hot, ada_all, precision=HIGHEST_PRECISION)
    gate_one, gate_two, scale_one, scale_two, shift_one, shift_two = jnp.split(token_ada, 6, axis=1)

    attn_proj = against(attn_low[:, :half], w_out[0]) + against(attn_low[:, half:], w_out[1])
    x_one = x_zero + gate_one * attn_proj
    h_two_low = pre_norm(x_one, scale_two, shift_two).astype(low)
    hidden_pre = against(h_two_low[:, :half], w_up[0]) + against(h_two_low[:, half:], w_up[1])
    act_low = jax.nn.gelu(hidden_pre, approximate=True).astype(low)
    hidden_half = w_down.shape[2]
    mlp_out = against(act_low[:, :hidden_half], w_down[0]) + against(act_low[:, hidden_half:], w_down[1])
    x_two = x_one + gate_two * mlp_out
    block_out = (x_two * live_rows).astype(low)
    logits = against(block_out, code_book)
    code_mass = jnp.sum(jax.nn.softmax(logits, axis=-1) * live_rows, axis=0)

    g_two = cotangent.astype(f32) * live_rows
    d_mlp = (gate_two * g_two).astype(low)
    d_gate_two = g_two * mlp_out

    def summed_over_cores(grad_rows, inputs):
        width = inputs.shape[1] // 2
        other = lax.dynamic_slice_in_dim(inputs, (1 - core) * width, width, 1)
        own = lax.dynamic_slice_in_dim(inputs, core * width, width, 1)
        their_rows, theirs = lax.ppermute((grad_rows, other), "dp", swap)
        total = contract_rows(grad_rows, own) + contract_rows(their_rows, theirs)
        return total.astype(low).reshape(4, 4, -1, width)

    def both_halves(values, weights):
        return jnp.concatenate(
            [jnp.dot(values, weights[h], preferred_element_type=f32) for h in range(2)], axis=1
        )

    p_down = summed_over_cores(d_mlp, act_low)
    d_act = both_halves(d_mlp, w_down)
    _, gelu_back = jax.vjp(lambda inputs: jax.nn.gelu(inputs, approximate=True), hidden_pre)
    d_hidden = gelu_back(d_act)[0].astype(low)
    p_up = summed_over_cores(d_hidden, h_two_low)
    d_h_two = both_halves(d_hidden, w_up)
    _, norm_back_two = jax.vjp(pre_norm, x_one, scale_two, shift_two)
    d_x_one, d_scale_two, d_shift_two = norm_back_two(d_h_two)
    d_x_one = d_x_one + g_two
    d_attn = (gate_one * d_x_one).astype(low)
    d_gate_one = d_x_one * attn_proj
    p_out = summed_over_cores(d_attn, attn_low)
    d_attended = both_halves(d_attn, w_out).astype(low)
    flags = jnp.pad(jnp.stack([left_ok, right_ok]), ((0, 6), (0, 0)))
    hot_rows = one_hot_wide.T
    mass_rows = code_mass.reshape(-1, model_width)
    s_down, s_up, s_out, s_qkv, d_ada_both, common_sum, bias_sum, map_grad = back(
        [d_attended, *kept, kept_qk, vectors, h_one_low, w_qkv, p_down, p_up, p_out, x_zero, scale_one, d_x_one]
        + [hot_rows, d_gate_one, d_gate_two, d_scale_two, d_shift_two, smooth, embed_w, mass_rows, flags],
        groups,
        ((2, 2, 1), (2,)),
        1,
    )
    embed_rows = embed_w.shape[0]
    d_embed_all = common_sum[:embed_rows]
    bias_rows = bias_sum[0].reshape(6, model_width)
    d_vectors_all = jnp.concatenate([bias_rows, common_sum[embed_rows : embed_rows + 2]], axis=0)
    mass_all = common_sum[embed_rows + 2 : embed_rows + 2 + mass_rows.shape[0]]
    histogram = mass_all.reshape(-1) * (code_book.shape[0] / tokens_all)
    d_ada_own = d_ada_both[:, :slot_count].reshape(2 * slot_count, -1)
    grad_ada = contract_rows(silu_rows.astype(f32), d_ada_own, HIGHEST_PRECISION)

    owned_grads = (s_qkv.T, s_out.T, s_up.T, s_down.T, grad_ada)
    root_tokens = math.sqrt(tokens_all)
    spreads = (
        model_width ** (-0.5),
        (model_width // 16) ** (-0.5),
        model_width ** (-0.5),
        w_up.shape[1] ** (-0.5),
        model_width ** (-0.5),
    )
    new_states = tuple(
        nesterov(stacked, gradient, BASE_RATE * spread_w / (factor_g * root_tokens), WEIGHT_DECAY)
        for stacked, gradient, spread_w, factor_g in zip(states, owned_grads, spreads, GRAD_FACTORS)
    )
    embed_new = nesterov(
        embed_state, d_embed_all, BASE_RATE * embed_rows ** (-0.5) / (EMBED_FACTOR * root_tokens), 0.0
    )
    vector_new = nesterov(vector_state, d_vectors_all, VECTOR_RATE / root_tokens, 0.0)
    outputs = [block_out, map_grad, histogram]
    for state in new_states:
        outputs += [state, state[1].astype(low)]
    return tuple(outputs + [embed_new, vector_new, d_vectors_all[7]])


def solution(mesh):
    body = fast_shards if dict(mesh.shape) == {"dp": 2, "wide": 16} else shards
    in_specs = (
        P(None, ("dp", "wide")),
        P("dp", None),
        P("dp", None),
        P(("dp", "wide"), None),
        P(),
        P(None, "dp", "wide"),
        P(None, "dp", "wide"),
        P(None, "dp", "wide"),
        P(None, "dp", "wide"),
        P(None, "dp", "wide"),
        P(),
        P(),
    )
    out_specs = (
        P(("dp", "wide"), None),
        P(None, ("dp", "wide")),
        P(),
        P(None, "dp", "wide"),
        P("dp", "wide"),
        P(None, "dp", "wide"),
        P("dp", "wide"),
        P(None, "dp", "wide"),
        P("dp", "wide"),
        P(None, "dp", "wide"),
        P("dp", "wide"),
        P(None, "dp", "wide"),
        P("dp", "wide"),
        P(),
        P(),
        P(),
    )
    return jax.shard_map(body, mesh=mesh, in_specs=in_specs, out_specs=out_specs, check_vma=False)
```

```python
import functools
import math

import jax
import jax.numpy as jnp
import numpy as np
from jax import lax
from jax.experimental import pallas as pl
from jax.experimental.pallas import tpu as pltpu
from jax.sharding import PartitionSpec as P

HEADS = 16
LEVELS = 10
STEP = 7


SHORT_SIDES = (1, 2, 3, 4, 5, 6, 8, 10, 13, 16)
LONG_SIDES = (1, 2, 3, 4, 6, 9, 13, 18, 24, 32)
MASKED = -1e30
NORM_EPS = 1e-06
MOMENTUM = 0.9
WEIGHT_DECAY = 0.05
BASE_RATE = 0.37
VECTOR_RATE = 0.22
GRAD_FACTORS = (0.15, 0.1, 0.3, 0.35, 0.3)
EMBED_FACTOR = 0.6
HIGHEST_PRECISION = lax.Precision.HIGHEST


def padded(cells, sides, width):
    for axis, dim in sides:
        count = lax.axis_size(axis)
        ends = count - 1
        head = lax.slice_in_dim(cells, 0, width, axis=dim)
        tail = lax.slice_in_dim(cells, cells.shape[dim] - width, cells.shape[dim], axis=dim)
        cells = jnp.concatenate(
            [
                lax.ppermute(tail, axis, [(i, (i + 1) % count) for i in range(ends)]),
                cells,
                lax.ppermute(head, axis, [((i + 1) % count, i) for i in range(ends)]),
            ],
            axis=dim,
        )
    return cells


def layout(lengths, positions, group_len):
    short_sq = jnp.array([side * side for side in SHORT_SIDES[:LEVELS]], jnp.int32)
    long_sq = jnp.array([side * side for side in LONG_SIDES[:LEVELS]], jnp.int32)
    short_total = sum((side * side for side in SHORT_SIDES[:LEVELS]))
    long_total = sum((side * side for side in LONG_SIDES[:LEVELS]))
    slot_count = lengths.shape[0]
    counts = jnp.where(
        lengths[None, :] == long_total,
        long_sq[:, None],
        jnp.where(lengths[None, :] == short_total, short_sq[:, None], 0),
    )
    unused = group_len - jnp.sum(lengths)
    ordered = jnp.concatenate([counts.reshape(-1), unused[None]])
    boundary = jnp.cumsum(ordered)
    segment = jnp.sum((boundary[None, :] <= positions[:, None]).astype(jnp.int32), axis=1)
    segment = jnp.minimum(segment, ordered.shape[0] - 1)
    unused_id = slot_count * LEVELS
    tok_level = jnp.where(segment >= unused_id, 0, segment // slot_count)
    tok_slot = jnp.where(segment >= unused_id, slot_count, segment % slot_count)
    return (tok_slot, tok_level, segment)


def pre_norm(inputs, scaling, offset_add):
    row_mean = jnp.mean(inputs, axis=-1, keepdims=True)
    centred = inputs - row_mean
    spread = jnp.mean(centred * centred, axis=-1, keepdims=True)
    return centred * lax.rsqrt(spread + NORM_EPS) * (1.0 + scaling) + offset_add


def unit_heads(inputs):
    shaped = inputs.reshape(inputs.shape[0], HEADS, -1)
    shaped = shaped * lax.rsqrt(jnp.sum(shaped * shaped, axis=-1, keepdims=True) + NORM_EPS)
    return shaped.reshape(inputs.shape)


def split_heads(projected, q_gain):
    queries, key_part, value_part = jnp.split(projected, 3, axis=1)
    head_scale = math.sqrt(queries.shape[1] // HEADS)
    return (unit_heads(queries) * (head_scale * (1.0 + q_gain)), unit_heads(key_part), value_part)


def smooth_map(values, left_ok, right_ok, before, following):
    return (left_ok * before + 2.0 * values + right_ok * following) / (2.0 + left_ok + right_ok)


def nesterov(stacked, gradient, step_rate, decay_rate):
    moment, weight, average = (stacked[0], stacked[1], stacked[2])
    step_grad = gradient + decay_rate * weight
    new_moment = MOMENTUM * moment + step_rate * step_grad
    new_weight = weight - (step_rate * step_grad + MOMENTUM * new_moment)
    retain = min(0.999, (1.0 + STEP) / (10.0 + STEP))
    new_average = retain * average + (1.0 - retain) * new_weight
    return jnp.stack([new_moment, new_weight, new_average])


def contract_rows(left_side, right_side, precision=None):
    return lax.dot_general(
        left_side,
        right_side,
        (((0,), (0,)), ((), ())),
        precision=precision,
        preferred_element_type=jnp.float32,
    )


def against(left_side, right_side):
    return lax.dot_general(
        left_side, right_side, (((1,), (1,)), ((), ())), preferred_element_type=jnp.float32
    )


def shards(
    feature_map,
    condition,
    item_lengths,
    cotangent,
    code_book,
    qkv_state,
    out_state,
    up_state,
    down_state,
    ada_state,
    embed_state,
    vector_state,
):
    tok_rows = cotangent.shape[0]
    model_width = cotangent.shape[1]
    head_dim = model_width // HEADS
    wide_count = lax.axis_size("wide")
    group_len = tok_rows * wide_count
    tokens_all = lax.axis_size("dp") * group_len
    lengths = item_lengths[0]
    slot_count = lengths.shape[0]
    positions = lax.axis_index("wide") * tok_rows + jnp.arange(tok_rows, dtype=jnp.int32)
    tok_slot, tok_level, segment = layout(lengths, positions, group_len)
    live_rows = (tok_slot < slot_count).astype(jnp.float32)[:, None]
    left_ok = ((layout(lengths, positions - 1, group_len)[2] == segment) & (positions > 0)).astype(
        jnp.float32
    )
    right_ok = (
        (layout(lengths, positions + 1, group_len)[2] == segment) & (positions < group_len - 1)
    ).astype(jnp.float32)
    rimmed = padded(feature_map, (("wide", 1),), 1)
    smooth = smooth_map(feature_map, left_ok, right_ok, rimmed[:, :-2], rimmed[:, 2:])
    states = (qkv_state, out_state, up_state, down_state, ada_state)
    masters = tuple((stacked[1].astype(jnp.bfloat16) for stacked in states))
    columns = (
        lax.all_gather(masters[0], "wide", axis=1, tiled=True),
        lax.all_gather(masters[1], "wide", axis=1, tiled=True),
        lax.all_gather(masters[2], "wide", axis=1, tiled=True),
        lax.all_gather(masters[3], "wide", axis=1, tiled=True),
    )
    ada_piece = lax.all_gather(masters[4], "wide", axis=1, tiled=True)
    w_qkv, w_out, w_up, w_down, w_ada = (
        lax.all_gather(columns[0], "dp", axis=0, tiled=True),
        lax.all_gather(columns[1], "dp", axis=0, tiled=True),
        lax.all_gather(columns[2], "dp", axis=0, tiled=True),
        lax.all_gather(columns[3], "dp", axis=0, tiled=True),
        lax.all_gather(ada_piece, "dp", axis=0, tiled=True),
    )
    embed_w = embed_state[1]
    vectors = vector_state[1]
    x_zero = (
        lax.dot_general(smooth, embed_w, (((0,), (0,)), ((), ())), precision=HIGHEST_PRECISION)
        + vectors[6]
    )
    silu_cond = jax.nn.silu(condition).astype(jnp.bfloat16)
    ada_product = jnp.dot(silu_cond, w_ada, preferred_element_type=jnp.float32)
    ada_all = ada_product + vectors[:6].reshape(-1)
    one_hot = (tok_slot[:, None] == jnp.arange(slot_count, dtype=jnp.int32)[None, :]).astype(
        jnp.float32
    )
    token_ada = jnp.dot(one_hot, ada_all, precision=HIGHEST_PRECISION)
    gate_one, gate_two, scale_one, scale_two, shift_one, shift_two = jnp.split(token_ada, 6, axis=1)
    h_one_low = pre_norm(x_zero, scale_one, shift_one).astype(jnp.bfloat16)
    projected = jnp.dot(h_one_low, w_qkv, preferred_element_type=jnp.float32)
    (q_unit, k_unit, v_full), heads_back = jax.vjp(split_heads, projected, vectors[7])
    queries = q_unit.astype(jnp.bfloat16)
    keys_low = k_unit.astype(jnp.bfloat16)
    values_low = v_full.astype(jnp.bfloat16)
    query_heads = queries.reshape(tok_rows, HEADS, head_dim)

    def blockwise(advance, running, pieces, first_row):
        key_count = pieces[0].shape[0]
        block_size = math.gcd(key_count, 1024)

        def per_block(current, offset):
            key_part = tuple(
                (lax.dynamic_slice_in_dim(piece_arr, offset, block_size, 0) for piece_arr in pieces)
            )
            first_key = first_row + offset
            k_slot, k_level, _ = layout(
                lengths, first_key + jnp.arange(block_size, dtype=jnp.int32), group_len
            )
            allowed = (tok_slot[:, None] == k_slot[None, :]) & (
                k_level[None, :] <= tok_level[:, None]
            )
            current = advance(current, key_part, allowed, first_key)
            return (current, None)

        offsets = jnp.arange(key_count // block_size, dtype=jnp.int32) * block_size
        return lax.scan(per_block, running, offsets)[0]

    def scores_of(key_block, allowed):
        raw_scores = jnp.einsum(
            "qhd,khd->hqk",
            query_heads,
            key_block.reshape(-1, HEADS, head_dim),
            preferred_element_type=jnp.float32,
        )
        return jnp.where(allowed[None], raw_scores, MASKED)

    def stats_step(running, key_part, allowed, first_key):
        scores = scores_of(key_part[0], allowed)
        top_score, exp_total = running
        new_top = jnp.maximum(top_score, jnp.max(scores, axis=-1, keepdims=True))
        exp_total = exp_total * jnp.exp(top_score - new_top) + jnp.sum(
            jnp.exp(scores - new_top), axis=-1, keepdims=True
        )
        return (new_top, exp_total)

    kv_rows = (
        lax.all_gather(keys_low, "wide", axis=0, tiled=True),
        lax.all_gather(values_low, "wide", axis=0, tiled=True),
    )
    start_stats = (
        jnp.full((HEADS, tok_rows, 1), MASKED, jnp.float32),
        jnp.zeros((HEADS, tok_rows, 1), jnp.float32),
    )
    top_score, exp_total = blockwise(stats_step, start_stats, kv_rows, 0)
    log_total = top_score + jnp.log(exp_total)

    def value_step(running, key_part, allowed, first_key):
        attn_probs = jnp.exp(scores_of(key_part[0], allowed) - log_total).astype(jnp.bfloat16)
        return running + jnp.einsum(
            "hqk,khd->qhd",
            attn_probs,
            key_part[1].reshape(-1, HEADS, head_dim),
            preferred_element_type=jnp.float32,
        )

    attended = blockwise(
        value_step, jnp.zeros((tok_rows, HEADS, head_dim), jnp.float32), kv_rows, 0
    )
    attn_low = attended.reshape(tok_rows, model_width).astype(jnp.bfloat16)
    attn_proj = jnp.dot(attn_low, w_out, preferred_element_type=jnp.float32)
    x_one = x_zero + gate_one * attn_proj
    h_two_low = pre_norm(x_one, scale_two, shift_two).astype(jnp.bfloat16)
    hidden_pre = jnp.dot(h_two_low, w_up, preferred_element_type=jnp.float32)
    act_low = jax.nn.gelu(hidden_pre, approximate=True).astype(jnp.bfloat16)
    mlp_out = jnp.dot(act_low, w_down, preferred_element_type=jnp.float32)
    x_two = x_one + gate_two * mlp_out
    block_out = (x_two * live_rows).astype(jnp.bfloat16)
    logits = against(block_out, code_book)
    code_mass = jnp.sum(jax.nn.softmax(logits, axis=-1) * live_rows, axis=0)
    g_two = cotangent.astype(jnp.float32) * live_rows
    d_mlp = (gate_two * g_two).astype(jnp.bfloat16)
    d_gate_two = g_two * mlp_out
    dw_down = contract_rows(act_low, d_mlp)
    d_act = against(d_mlp, w_down)
    _, gelu_back = jax.vjp(lambda inputs: jax.nn.gelu(inputs, approximate=True), hidden_pre)
    d_hidden = gelu_back(d_act)[0].astype(jnp.bfloat16)
    dw_up = contract_rows(h_two_low, d_hidden)
    d_h_two = against(d_hidden, w_up)
    _, norm_back_two = jax.vjp(pre_norm, x_one, scale_two, shift_two)
    d_x_one, d_scale_two, d_shift_two = norm_back_two(d_h_two)
    d_x_one = d_x_one + g_two
    d_attn = (gate_one * d_x_one).astype(jnp.bfloat16)
    d_gate_one = d_x_one * attn_proj
    dw_out = contract_rows(attn_low, d_attn)
    grad_flat = against(d_attn, w_out).astype(jnp.bfloat16)
    grad_heads = grad_flat.reshape(tok_rows, HEADS, head_dim)

    def delta_step(running, key_part, allowed, first_key):
        attn_probs = jnp.exp(scores_of(key_part[0], allowed) - log_total)
        d_probs = jnp.einsum(
            "qhd,khd->hqk",
            grad_heads,
            key_part[1].reshape(-1, HEADS, head_dim),
            preferred_element_type=jnp.float32,
        )
        return running + jnp.sum(attn_probs * d_probs, axis=-1, keepdims=True)

    row_delta = blockwise(delta_step, jnp.zeros((HEADS, tok_rows, 1), jnp.float32), kv_rows, 0)

    def grad_step(running, key_part, allowed, first_key):
        d_query, d_keys, d_values = running
        key_heads = key_part[0].reshape(-1, HEADS, head_dim)
        value_heads = key_part[1].reshape(-1, HEADS, head_dim)
        block_rows = key_part[0].shape[0]
        attn_probs = jnp.exp(scores_of(key_part[0], allowed) - log_total)
        d_probs = jnp.einsum(
            "qhd,khd->hqk", grad_heads, value_heads, preferred_element_type=jnp.float32
        )
        d_scores = (attn_probs * (d_probs - row_delta)).astype(jnp.bfloat16)
        d_query = d_query + jnp.einsum(
            "hqk,khd->qhd", d_scores, key_heads, preferred_element_type=jnp.float32
        )
        key_grad = jnp.einsum(
            "hqk,qhd->khd", d_scores, query_heads, preferred_element_type=jnp.float32
        )
        value_grad = jnp.einsum(
            "hqk,qhd->khd",
            attn_probs.astype(jnp.bfloat16),
            grad_heads,
            preferred_element_type=jnp.float32,
        )
        key_sum = lax.dynamic_slice_in_dim(d_keys, first_key, block_rows, 0) + key_grad.reshape(
            block_rows, model_width
        )
        value_sum = lax.dynamic_slice_in_dim(
            d_values, first_key, block_rows, 0
        ) + value_grad.reshape(block_rows, model_width)
        d_keys = lax.dynamic_update_slice_in_dim(d_keys, key_sum, first_key, 0)
        d_values = lax.dynamic_update_slice_in_dim(d_values, value_sum, first_key, 0)
        return (d_query, d_keys, d_values)

    grad_init = (
        jnp.zeros((tok_rows, HEADS, head_dim), jnp.float32),
        jnp.zeros((group_len, model_width), jnp.float32),
        jnp.zeros((group_len, model_width), jnp.float32),
    )
    d_query, d_keys, d_values = blockwise(grad_step, grad_init, kv_rows, 0)
    d_keys_own, d_values_own = (
        lax.psum_scatter(
            d_keys.astype(jnp.bfloat16), "wide", scatter_dimension=0, tiled=True
        ).astype(jnp.float32),
        lax.psum_scatter(
            d_values.astype(jnp.bfloat16), "wide", scatter_dimension=0, tiled=True
        ).astype(jnp.float32),
    )
    d_projected, d_gain = heads_back(
        (d_query.reshape(tok_rows, model_width), d_keys_own, d_values_own)
    )
    d_projected_low = d_projected.astype(jnp.bfloat16)
    dw_qkv = contract_rows(h_one_low, d_projected_low)
    d_h_one = against(d_projected_low, w_qkv)
    _, norm_back_one = jax.vjp(pre_norm, x_zero, scale_one, shift_one)
    d_x_zero, d_scale_one, d_shift_one = norm_back_one(d_h_one)
    d_x_zero = d_x_zero + d_x_one
    d_token_ada = jnp.concatenate(
        [d_gate_one, d_gate_two, d_scale_one, d_scale_two, d_shift_one, d_shift_two], axis=1
    )
    d_ada_all = contract_rows(one_hot, d_token_ada, HIGHEST_PRECISION)
    d_smooth = lax.dot_general(
        embed_w, d_x_zero, (((1,), (1,)), ((), ())), precision=HIGHEST_PRECISION
    )
    d_embed = lax.dot_general(
        smooth, d_x_zero, (((1,), (0,)), ((), ())), precision=HIGHEST_PRECISION
    )
    d_vectors = jnp.concatenate(
        [
            jnp.sum(d_ada_all, axis=0).reshape(6, model_width),
            jnp.sum(d_x_zero, axis=0)[None],
            d_gain[None],
        ],
        axis=0,
    )
    grad_share = d_smooth / (2.0 + left_ok + right_ok)
    rim_share = padded(grad_share, (("wide", 1),), 1)
    map_grad = 2.0 * grad_share + left_ok * rim_share[:, :-2] + right_ok * rim_share[:, 2:]
    d_embed_all, d_vectors_all, mass_all = lax.psum((d_embed, d_vectors, code_mass), ("dp", "wide"))
    histogram = mass_all * (code_book.shape[0] / tokens_all)
    ada_term = contract_rows(silu_cond.astype(jnp.float32), d_ada_all, HIGHEST_PRECISION)
    split_cols = (
        lax.psum_scatter(
            dw_qkv.astype(jnp.bfloat16), "wide", scatter_dimension=1, tiled=True
        ).astype(jnp.float32),
        lax.psum_scatter(
            dw_out.astype(jnp.bfloat16), "wide", scatter_dimension=1, tiled=True
        ).astype(jnp.float32),
        lax.psum_scatter(
            dw_up.astype(jnp.bfloat16), "wide", scatter_dimension=1, tiled=True
        ).astype(jnp.float32),
        lax.psum_scatter(
            dw_down.astype(jnp.bfloat16), "wide", scatter_dimension=1, tiled=True
        ).astype(jnp.float32),
        lax.psum_scatter(
            ada_term.astype(jnp.bfloat16), "wide", scatter_dimension=1, tiled=True
        ).astype(jnp.float32),
    )
    ada_cols = split_cols[4]
    owned_grads = (
        lax.psum_scatter(
            split_cols[0].astype(jnp.bfloat16), "dp", scatter_dimension=0, tiled=True
        ).astype(jnp.float32),
        lax.psum_scatter(
            split_cols[1].astype(jnp.bfloat16), "dp", scatter_dimension=0, tiled=True
        ).astype(jnp.float32),
        lax.psum_scatter(
            split_cols[2].astype(jnp.bfloat16), "dp", scatter_dimension=0, tiled=True
        ).astype(jnp.float32),
        lax.psum_scatter(
            split_cols[3].astype(jnp.bfloat16), "dp", scatter_dimension=0, tiled=True
        ).astype(jnp.float32),
        lax.psum_scatter(
            ada_cols.astype(jnp.bfloat16), "dp", scatter_dimension=0, tiled=True
        ).astype(jnp.float32),
    )
    root_tokens = math.sqrt(tokens_all)
    spreads = (
        model_width ** (-0.5),
        (model_width // 16) ** (-0.5),
        model_width ** (-0.5),
        w_up.shape[1] ** (-0.5),
        model_width ** (-0.5),
    )
    new_states = tuple(
        (
            nesterov(
                stacked, gradient, BASE_RATE * spread_w / (factor_g * root_tokens), WEIGHT_DECAY
            )
            for stacked, gradient, spread_w, factor_g in zip(
                states, owned_grads, spreads, GRAD_FACTORS
            )
        )
    )
    embed_new = nesterov(
        embed_state,
        d_embed_all,
        BASE_RATE * embed_w.shape[0] ** (-0.5) / (EMBED_FACTOR * root_tokens),
        0.0,
    )
    vector_new = nesterov(vector_state, d_vectors_all, VECTOR_RATE / root_tokens, 0.0)
    return (
        block_out,
        map_grad,
        histogram,
        new_states[0],
        new_states[0][1].astype(jnp.bfloat16),
        new_states[1],
        new_states[1][1].astype(jnp.bfloat16),
        new_states[2],
        new_states[2][1].astype(jnp.bfloat16),
        new_states[3],
        new_states[3][1].astype(jnp.bfloat16),
        new_states[4],
        new_states[4][1].astype(jnp.bfloat16),
        embed_new,
        vector_new,
        d_vectors_all[7],
    )


MESH_ID = pl.DeviceIdType.MESH
ANY = pl.BlockSpec(memory_space=pl.ANY)
VM = pl.BlockSpec(memory_space=pltpu.VMEM)
VMEM_BYTES = 56 * 1024 * 1024
SHORT_TOTAL = sum(side * side for side in SHORT_SIDES)
LONG_TOTAL = sum(side * side for side in LONG_SIDES)
GELU_SCALE = math.sqrt(2.0 / math.pi)
GELU_CUBE = 0.044715
LANES = 128
HALF_LANES = 64
BIG = 1e30


def nt(left_side, right_side):
    return lax.dot_general(
        left_side, right_side, (((1,), (1,)), ((), ())), preferred_element_type=jnp.float32
    )


def nn(left_side, right_side):
    return lax.dot_general(
        left_side, right_side, (((1,), (0,)), ((), ())), preferred_element_type=jnp.float32
    )


def entry_barrier(peers):
    barrier = pltpu.get_barrier_semaphore()
    for peer in peers:
        pl.semaphore_signal(barrier, inc=1, device_id=peer, device_id_type=MESH_ID)
    pl.semaphore_wait(barrier, len(peers))


def place():
    core, wide = lax.axis_index("dp"), lax.axis_index("wide")
    return core, wide // 4, wide % 4


def at_dev(core, z, yx):
    return (core, z * 4 + yx)


def lane_iota(shape):
    return lax.broadcasted_iota(jnp.int32, shape, len(shape) - 1)


def swap_halves(pair):
    return pltpu.roll(pair, HALF_LANES, 1)


def head_sums(values):
    width = values.shape[1]
    rows = lax.broadcasted_iota(jnp.int32, (width, width), 0) // HALF_LANES
    cols = lax.broadcasted_iota(jnp.int32, (width, width), 1) // HALF_LANES
    ones = (rows == cols).astype(jnp.float32)
    return lax.dot_general(
        values,
        ones,
        (((1,), (0,)), ((), ())),
        precision=HIGHEST_PRECISION,
        preferred_element_type=jnp.float32,
    )


ROWS = 256
CHUNK = 512


def key_limits(group_len, slots):
    short_total = sum(side * side for side in SHORT_SIDES)
    long_total = sum(side * side for side in LONG_SIDES)
    limits = [0] * (group_len // ROWS)
    for longs in range(1, slots + 1):
        for shorts in range(slots - longs + 1):
            total = longs * long_total + shorts * short_total
            if not group_len - short_total < total <= group_len:
                continue
            ends, position = [], 0
            for long_side, short_side in zip(LONG_SIDES, SHORT_SIDES):
                position += longs * long_side**2 + shorts * short_side**2
                ends.append(position)
            ends.append(group_len)
            for block in range(len(limits)):
                last = block * ROWS + ROWS - 1
                seen = min(end for end in ends if end > last)
                limits[block] = max(limits[block], -(-seen // LANES) * LANES)
    return limits


def same_limits(limits):
    groups = []
    for block, limit in enumerate(limits):
        if groups and groups[-1][2] == limit:
            groups[-1][1] = block + 1
        else:
            groups.append([block, block + 1, limit])
    return groups


def fold_lanes(values, combine):
    total = values[:, :LANES]
    for j in range(1, values.shape[1] // LANES):
        total = combine(total, values[:, j * LANES : (j + 1) * LANES])
    return total


def split_three(values):
    high = values.astype(jnp.bfloat16).astype(jnp.float32)
    rest = values - high
    mid = rest.astype(jnp.bfloat16).astype(jnp.float32)
    return high, mid, rest - mid


def lanes_three(lane, first, values, otherwise):
    high, mid, rest = split_three(values)
    return jnp.where(
        lane == first, high, jnp.where(lane == first + 1, mid, jnp.where(lane == first + 2, rest, otherwise))
    )


class Gather:
    KINDS = ("up", "down", "x", "y", "turn")

    def __init__(self, shards, fulls, sems, pieces):
        self.shards, self.fulls, self.pieces = shards, fulls, pieces
        self.send, self.recv, self.send_s, self.recv_s, self.local = sems
        self.core, self.z, self.yx = place()
        core, z, yx = self.core, self.z, self.yx
        self.up_dev, self.down_dev = at_dev(core, lax.min(z + 1, 3), yx), at_dev(core, lax.max(z - 1, 0), yx)
        self.x_dev, self.y_dev = at_dev(core, z, yx ^ 1), at_dev(core, z, yx ^ 2)
        self.sib = at_dev(1 - core, z, yx)
        self.ends = []

    @staticmethod
    def scratch(count):
        dma = pltpu.SemaphoreType.DMA
        return [dma((count, 5, 4)), dma((count, 4, 4)), dma((count, 4, 4)), dma((count, 4, 4)), dma((count,))]

    def spot(self, p, z_at, d, core=None):
        i, first, rows = self.pieces[p]
        core = self.core if core is None else core
        size = self.shards[i].shape[0]
        start = pl.multiple_of((z_at * 4 + (self.yx ^ d)) * size + first, 16)
        return self.fulls[i].at[core, pl.ds(start, rows)]

    def copy(self, p, kind, z_at, d, src=None):
        there = {0: 0, 1: 0, 2: 1, 3: 2, 4: 3}[kind]
        ref = self.spot(p, z_at, d)
        device = (self.up_dev, self.down_dev, self.x_dev, self.y_dev)[kind] if kind < 4 else (self.y_dev if d == 1 else self.x_dev)
        return pltpu.make_async_remote_copy(
            src_ref=ref if src is None else src,
            dst_ref=ref,
            send_sem=self.send.at[p, kind, z_at],
            recv_sem=self.recv.at[p, there, z_at],
            device_id=device,
            device_id_type=MESH_ID,
        )

    def go(self, condition, p, kind, z_at, d, src=None):
        def start():
            self.copy(p, kind, z_at, d, src).start()

        def end():
            self.copy(p, kind, z_at, d, src).wait_send()

        if condition is None:
            start()
            self.ends.append(end)
        else:
            pl.when(condition)(start)
            self.ends.append(lambda: pl.when(condition)(end))

    def across(self, p, d):
        for z_at in range(4):
            ref = self.spot(p, z_at, d)
            copy = pltpu.make_async_remote_copy(
                src_ref=ref,
                dst_ref=ref,
                send_sem=self.send_s.at[p, d, z_at],
                recv_sem=self.recv_s.at[p, d, z_at],
                device_id=self.sib,
                device_id_type=MESH_ID,
            )
            copy.start()
            self.ends.append(copy.wait_send)

    def arrive(self, p, kind, z_at, d):
        ref = self.spot(p, z_at, d)
        pltpu.make_async_copy(ref, ref, self.recv.at[p, kind, z_at]).wait()

    def own(self, p):
        i, first, rows = self.pieces[p]
        src = self.shards[i].at[pl.ds(first, rows)]
        z = self.z
        self.go(z < 3, p, 0, z, 0, src)
        self.go(z > 0, p, 1, z, 0, src)
        self.go(None, p, 2, z, 0, src)
        self.go(None, p, 3, z, 0, src)
        copy = pltpu.make_async_copy(src, self.spot(p, z, 0), self.local.at[p])
        copy.start()
        self.locals_ = getattr(self, "locals_", {})
        self.locals_[p] = copy

    def z_step(self, p, r):
        z = self.z
        for side in (-1, 1):
            there = (z - r >= 0) if side < 0 else (z + r <= 3)
            z_at = z + side * r

            def landed(z_at=z_at):
                self.arrive(p, 0, z_at, 0)

            pl.when(there)(landed)
            if side < 0:
                self.go(there & (z < 3), p, 0, z_at, 0)
            else:
                self.go(there & (z > 0), p, 1, z_at, 0)
            self.go(there, p, 2, z_at, 0)
            self.go(there, p, 3, z_at, 0)

    def plane_step(self, p, r):
        z = self.z
        for side in (-1, 1) if r else (0,):
            z_at = z + side * r
            there = None if not r else ((z - r >= 0) if side < 0 else (z + r <= 3))

            def landed(z_at=z_at):
                self.arrive(p, 1, z_at, 1)
                self.arrive(p, 2, z_at, 2)

            if there is None:
                landed()
            else:
                pl.when(there)(landed)
            low_z, high_z = z_at < 2, z_at >= 2
            self.go(low_z if there is None else there & low_z, p, 4, z_at, 1)
            self.go(high_z if there is None else there & high_z, p, 4, z_at, 2)

    def stage(self, p, s):
        if s == 0:
            self.own(p)
        elif s == 1:
            self.z_step(p, 1)
            self.plane_step(p, 0)
        elif s == 2:
            self.z_step(p, 2)
            self.plane_step(p, 1)
        elif s == 3:
            self.z_step(p, 3)
            self.locals_[p].wait()
            self.across(p, 0)
            self.plane_step(p, 2)
        elif s == 4:
            self.plane_step(p, 3)
            self.across(p, 1)
            self.across(p, 2)
        elif s == 5:
            for z_at in range(4):
                self.arrive(p, 3, z_at, 3)
            self.across(p, 3)

    STAGES = 6

    def steps(self):
        return len(self.pieces) + self.STAGES - 1

    def run(self, t):
        for s in range(self.STAGES):
            if 0 <= t - s < len(self.pieces):
                self.stage(t - s, s)

    def landed(self, which=None):
        for p in range(len(self.pieces)) if which is None else which:
            for d in range(4):
                for z_at in range(4):
                    ref = self.spot(p, z_at, d, 1 - self.core)
                    pltpu.make_async_copy(ref, ref, self.recv_s.at[p, d, z_at]).wait()

    def finish(self):
        for end in self.ends:
            end()


def pieces_of(shards, splits):
    pieces = []
    for i, (shard, split) in enumerate(zip(shards, splits)):
        rows = shard.shape[0] // split
        pieces += [(i, j * rows, rows) for j in range(split)]
    return pieces


class Exchange:
    def __init__(self, out, landed, sems):
        self.out, self.landed = out, landed
        self.send, self.recv = sems
        self.core, z, yx = place()
        self.wide = z * 4 + yx

    def copy(self, w):
        return pltpu.make_async_remote_copy(
            src_ref=self.out.at[w],
            dst_ref=self.landed.at[self.wide],
            send_sem=self.send.at[w],
            recv_sem=self.recv.at[self.wide],
            device_id=(self.core, w),
            device_id_type=MESH_ID,
        )

    def push(self, w):
        pl.when(w != self.wide)(lambda: self.copy(w).start())

        def keep():
            self.landed[w] = self.out[w]

        pl.when(w == self.wide)(keep)

    def wait(self, w):
        def landed():
            ref = self.landed.at[w]
            pltpu.make_async_copy(ref, ref, self.recv.at[w]).wait()

        pl.when(w != self.wide)(landed)

    def finish(self):
        for w in range(16):
            pl.when(w != self.wide)(lambda w=w: self.copy(w).wait_send())


def column_of(row):
    return jnp.broadcast_to(row, (LANES, row.shape[1])).T[:, 0:1]


def exact(left_side, right_side, contract=(1, 0)):
    return lax.dot_general(
        left_side,
        right_side,
        (((contract[0],), (contract[1],)), ((), ())),
        precision=HIGHEST_PRECISION,
        preferred_element_type=jnp.float32,
    )


def gelu(values):
    return 0.5 * values * (1.0 + jnp.tanh(GELU_SCALE * (values + GELU_CUBE * values * values * values)))


def front_kernel(groups, slots, *refs):
    (s_qkv, s_out, s_up, s_down, cond_ref, ada_any, map_ref, embed_ref, vec3_ref, len_ref, squares_ref, tri_ref, pick_ref, rule_ref) = refs[:14]
    (f_qkv, f_out, f_up, f_down, ada_ref, h_ref, kept_ref, out32_ref, q_ref, k_ref, kt_ref, vt_ref, low_ref) = refs[14:27]
    (x_ref, smooth_ref, flags_ref, hot_ref, silu_ref, proj_ref, one_ref, two_ref, pre_ref, act_ref) = refs[27:37]
    (w_ref, send_ref, got_ref, back_send, back_got, v_ref, s_ref, load_sem) = refs[37:45]
    (w_ada, silu_own, theirs, ours, ada_in, edge, edge_left, edge_right, wo_ref, wu_ref) = refs[45:55]
    sems = refs[55:]
    first_flow = Gather([s_qkv], [f_qkv], sems[:5], pieces_of([s_qkv], (2,)))
    flow = Gather([s_out, s_up, s_down], [f_out, f_up, f_down], sems[5:10], pieces_of([s_out, s_up, s_down], (1, 2, 2)))
    ada_send, ada_recv = sems[10:12]
    there = Exchange(send_ref, got_ref, sems[12:14])
    home = Exchange(back_send, back_got, sems[14:16])
    ada_sem, sib_s, sib_r, edge_s, edge_r, wo_sem, wu_sem = sems[16:23]
    core, z, yx = place()
    wide = z * 4 + yx
    sib = (1 - core, wide)
    tokens, width = x_ref.shape
    half = width // 2
    mid = tokens // 2
    two = 2 * tokens
    group_len = q_ref.shape[0]
    f32, low = jnp.float32, jnp.bfloat16
    vec_ref = vec3_ref.at[1]
    entry_barrier([(core, wide ^ r) for r in range(1, 16)] + [sib])

    def to_sib(slot, src, dst):
        copy = pltpu.make_async_remote_copy(
            src_ref=src, dst_ref=dst, send_sem=sib_s.at[slot], recv_sem=sib_r.at[slot], device_id=sib, device_id_type=MESH_ID
        )
        copy.start()
        return copy

    first_flow.run(0)
    ada_copy = pltpu.make_async_copy(ada_any.at[1], w_ada, ada_sem)
    ada_copy.start()
    cond = cond_ref[...]
    silu = (cond / (1.0 + jnp.exp(-cond))).astype(low).astype(f32)
    silu_own[...] = jnp.zeros_like(silu_own)
    silu_own[0:slots, :] = silu
    their_half = pl.ds(pl.multiple_of((1 - core) * half, half), half)
    my_half = pl.ds(pl.multiple_of(core * half, half), half)
    silu_copy = to_sib(0, silu_own.at[:, their_half], silu_ref.at[core])
    silu_ref[core] = silu_own[:, my_half]
    spot = lane_iota((32, LANES))
    cells = map_ref[...]
    edge[...] = jnp.where(spot == 0, cells[:, 0:1], jnp.where(spot == 1, cells[:, tokens - 1 : tokens], 0.0))

    def edge_copy(slot, dst, shift):
        return pltpu.make_async_remote_copy(
            src_ref=edge,
            dst_ref=dst,
            send_sem=edge_s.at[slot],
            recv_sem=edge_r.at[slot],
            device_id=(core, lax.rem(wide + shift, 16)),
            device_id_type=MESH_ID,
        )

    edges = [edge_copy(0, edge_left, 1), edge_copy(1, edge_right, 15)]
    for copy in edges:
        copy.start()
    first_flow.run(1)

    run_lane = lane_iota((1, LANES))
    run_slot = lax.rem(run_lane - HALF_LANES + slots * LANES, slots)
    lens = jnp.zeros((1, LANES), jnp.int32)
    for j in range(slots):
        lens = jnp.where(run_slot == j, len_ref[0:1, j : j + 1], lens)
    counts = jnp.where(lens == LONG_TOTAL, squares_ref[0:1, :], jnp.where(lens == SHORT_TOTAL, squares_ref[1:2, :], 0.0))
    unused = group_len - jnp.sum(counts, axis=1, keepdims=True)
    counts = jnp.where(run_lane == HALF_LANES + slots * LEVELS, unused, counts)
    ends = exact(jnp.broadcast_to(counts, (8, LANES)), tri_ref[...])[0:1, :]
    starts = ends - counts
    start_col, end_col = column_of(starts), column_of(ends)
    here = (wide * tokens + lane_iota((1, tokens))).astype(f32)
    left = 1.0 - jnp.sum(((here == start_col) & (here < end_col)).astype(f32), axis=0, keepdims=True)
    right = 1.0 - jnp.sum(((here == end_col - 1.0) & (here >= start_col)).astype(f32), axis=0, keepdims=True)
    flags_ref[...] = jnp.zeros_like(flags_ref)
    flags_ref[0:1, :] = left
    flags_ref[1:2, :] = right
    row_at = (wide * tokens + lax.broadcasted_iota(jnp.int32, (tokens, LANES), 0)).astype(f32)
    my_runs = ((row_at >= starts) & (row_at < ends)).astype(low)
    hot = nn(my_runs, pick_ref[...])[:, 0:8]
    hot_ref[...] = hot

    ada_copy.wait()
    w_low = w_ada[...].astype(low)
    silu_copy.wait_recv()
    theirs[...] = nn(silu_ref[1 - core].astype(low), w_low)
    part_copy = to_sib(1, theirs, ours)
    mine = nn(silu_ref[core].astype(low), w_low)
    first_flow.run(2)

    for copy in edges:
        copy.wait_recv()
    column = lane_iota((32, tokens))
    before = jnp.where(column == 0, edge_left[:, 1:2], jnp.roll(cells, 1, axis=1))
    after = jnp.where(column == tokens - 1, edge_right[:, 0:1], jnp.roll(cells, -1, axis=1))
    smooth = smooth_map(cells, left, right, before, after)
    smooth_ref[...] = smooth
    x = exact(smooth, embed_ref[1], (0, 0)) + vec_ref[6:7, :]
    x_ref[...] = x
    part_copy.wait_recv()
    ada_in[...] = mine + ours[...]
    ada_copies = []
    for r in range(1, 16):
        copy = pltpu.make_async_remote_copy(
            src_ref=ada_in,
            dst_ref=ada_ref.at[wide],
            send_sem=ada_send.at[r],
            recv_sem=ada_recv.at[r],
            device_id=(core, wide ^ r),
            device_id_type=MESH_ID,
        )
        copy.start()
        ada_copies.append(copy)
    ada_ref[wide] = ada_in[...]

    def standard(values):
        centred = values - jnp.mean(values, axis=1, keepdims=True)
        return centred * lax.rsqrt(jnp.mean(centred * centred, axis=1, keepdims=True) + NORM_EPS)

    unit = standard(x)
    first_flow.run(3)
    for copy in ada_copies:
        copy.wait_recv()
    ada = jnp.concatenate([ada_ref[w] for w in range(16)], axis=1)

    def of_tokens(block):
        return exact(hot, ada[:, block * width : (block + 1) * width] + vec_ref[block : block + 1, :])

    h_ref[...] = (unit * (1.0 + of_tokens(2)) + of_tokens(4)).astype(low)
    for t in range(4, first_flow.steps()):
        first_flow.run(t)
    next_tick = [0]

    def tick(n):
        for _ in range(n):
            if next_tick[0] < flow.steps():
                flow.run(next_tick[0])
                next_tick[0] += 1

    tick(1)
    first_flow.landed()

    group = 256
    loads = []

    def load(j):
        g = lax.rem(z + 1 + j, 4)
        out = []
        for c in range(2):
            for part in range(3):
                rows = pl.ds(pl.multiple_of(g * group + part * width, group), group)
                out.append(pltpu.make_async_copy(f_qkv.at[c, rows], w_ref.at[j, c, part], load_sem.at[j, c, part]))
        return out

    for j in range(4):
        loads.append(load(j))
        for copy in loads[-1]:
            copy.start()
    lane = lane_iota((tokens, LANES))
    lane_mid = lane_iota((mid, LANES))
    for j in range(4):
        g = lax.rem(z + 1 + j, 4)
        first = pl.multiple_of(g * group, group)
        for copy in loads[j]:
            copy.wait()

        def project(part):
            return nt(h_ref[:, :half], w_ref[j, 0, part]) + nt(h_ref[:, half:], w_ref[j, 1, part])

        q_all, k_all, v_all = (project(part) for part in range(3))
        for pair in range(group // LANES):
            cols = slice(pair * LANES, (pair + 1) * LANES)
            at = g * (group // LANES) + pair
            kept_ref[at] = q_all[:, cols]
            kept_ref[at + width // LANES] = k_all[:, cols]
        q_all = q_all * lax.rsqrt(head_sums(q_all * q_all) + NORM_EPS)
        q_all = q_all * (8.0 * (1.0 + vec_ref[7:8, pl.ds(first, group)]))
        k_all = k_all * lax.rsqrt(head_sums(k_all * k_all) + NORM_EPS)
        for pair in range(group // LANES):
            cols = slice(pair * LANES, (pair + 1) * LANES)
            q, k, v = q_all[:, cols], k_all[:, cols], v_all[:, cols]
            head = g * (group // HALF_LANES) + 2 * pair
            send_ref[head, 0:tokens, :] = jnp.where(lane < HALF_LANES, q, swap_halves(k)).astype(low)
            send_ref[head + 1, 0:tokens, :] = jnp.where(lane < HALF_LANES, swap_halves(q), k).astype(low)
            v_a, v_b = v[:mid], v[mid:]
            send_ref[head, tokens:, :] = jnp.where(lane_mid < HALF_LANES, v_a, swap_halves(v_b)).astype(low)
            send_ref[head + 1, tokens:, :] = jnp.where(lane_mid < HALF_LANES, swap_halves(v_a), v_b).astype(low)
        for e in range(4):
            there.push(g * 4 + e)
        tick((0, 1, 0, 0)[j])

    lane_two = lane_iota((two, LANES))

    def unpack(pair, carry):
        for e in range(2):
            there.wait(2 * pair + e)
        first = pl.multiple_of(pair * two, two)
        qk = jnp.concatenate([got_ref[2 * pair + e, 0:tokens, :].astype(f32) for e in range(2)], axis=0)
        spot = (first + lax.broadcasted_iota(jnp.int32, (two, LANES), 0)).astype(f32)
        runs = ((spot >= starts) & (spot < ends)).astype(f32)
        barred = nn(runs.astype(low), rule_ref[...])
        rows = pl.ds(first, two)
        q_ref[rows, :] = jnp.where(lane_two < HALF_LANES, qk, barred).astype(low)
        tail = jnp.where(lane_two >= LANES - 3, 1.0, runs)
        keys = jnp.where(lane_two < HALF_LANES, swap_halves(qk), tail)
        k_ref[rows, :] = keys.astype(low)
        kt_ref[:, rows] = keys.T.astype(low)
        ones = ((lane_mid >= HALF_LANES) & (lane_mid < HALF_LANES + 3)).astype(f32)
        pieces = []
        for e in range(2):
            v = got_ref[2 * pair + e, tokens:, :].astype(f32)
            pieces.append(jnp.where(lane_mid < HALF_LANES, v, ones))
            pieces.append(jnp.where(lane_mid < HALF_LANES, swap_halves(v), ones))
        values = jnp.concatenate(pieces, axis=0)
        v_ref[rows, :] = values.astype(low)
        vt_ref[:, rows] = values.T.astype(low)
        return carry

    lane_q = lane_iota((ROWS, LANES))

    def query_block(limit, b, carry):
        rows = pl.ds(pl.multiple_of(b * ROWS, ROWS), ROWS)
        q = q_ref[rows, :]

        def score(c, top):
            cols = pl.ds(pl.multiple_of(c * CHUNK, CHUNK), CHUNK)
            s = nn(q, kt_ref[:, cols])
            s_ref[:, cols] = s
            return jnp.maximum(top, fold_lanes(s, jnp.maximum))

        whole, left = limit // CHUNK, limit % CHUNK
        top = lax.fori_loop(0, whole, score, jnp.full((ROWS, LANES), -3e38, f32))
        if left:
            tail = slice(whole * CHUNK, limit)
            s = nn(q, kt_ref[:, tail])
            s_ref[:, tail] = s
            top = jnp.maximum(top, fold_lanes(s, jnp.maximum))
        peak = jnp.max(top, axis=1, keepdims=True)

        def weigh(cols, carry):
            total, acc = carry
            p = jnp.exp(s_ref[:, cols] - peak)
            return total + fold_lanes(p, jnp.add), acc + nn(p.astype(low), v_ref[cols, :])

        zero = jnp.zeros((ROWS, LANES), f32)
        total, acc = lax.fori_loop(
            0,
            whole,
            lambda c, carry: weigh(pl.ds(pl.multiple_of(c * CHUNK, CHUNK), CHUNK), carry),
            (zero, zero),
        )
        if left:
            total, acc = weigh(slice(whole * CHUNK, limit), (total, acc))
        total = jnp.sum(total, axis=1, keepdims=True)
        out32_ref[rows, :] = acc / total
        log_total = peak + jnp.log(total)
        q_ref[rows, :] = lanes_three(lane_q, LANES - 3, -log_total, q.astype(f32)).astype(low)
        return carry

    def give_back(w, carry):
        rows = pl.multiple_of(w * tokens, tokens)
        a = out32_ref[pl.ds(rows, mid), :]
        b = out32_ref[pl.ds(pl.multiple_of(rows + mid, mid), mid), :]
        back_send[w] = jnp.where(lane_mid < HALF_LANES, a, swap_halves(b)).astype(low)
        home.push(w)
        return carry

    for i in range(4):
        lax.fori_loop(2 * i, 2 * i + 2, unpack, 0)
        tick((0, 1, 0, 1)[i])
    plane = 4 * tokens // ROWS
    done = 0
    for p in range(4):
        for first, last, limit in groups:
            begin, end = max(first, p * plane), min(last, (p + 1) * plane)
            if begin < end:
                lax.fori_loop(begin, end, functools.partial(query_block, limit), 0)
                tick((0, 1, 0, 1, 0, 1, 0, 1)[done])
                done += 1
        lax.fori_loop(4 * p, 4 * p + 4, give_back, 0)
    tick(1)
    while next_tick[0] < 8:
        tick(1)
    flow.landed((0,))
    wo_copy = pltpu.make_async_copy(f_out, wo_ref, wo_sem)
    wo_copy.start()
    for pair in range(8):
        home.wait(2 * pair)
        home.wait(2 * pair + 1)
        cols = slice(pair * LANES, (pair + 1) * LANES)
        even, odd = back_got[2 * pair].astype(f32), back_got[2 * pair + 1].astype(f32)
        low_ref[0:mid, cols] = jnp.where(lane_mid < HALF_LANES, even, swap_halves(odd)).astype(low)
        low_ref[mid:, cols] = jnp.where(lane_mid < HALF_LANES, swap_halves(even), odd).astype(low)

    wo_copy.wait()
    proj = nt(low_ref[:, :half], wo_ref[0]) + nt(low_ref[:, half:], wo_ref[1])
    proj_ref[...] = proj
    x_one = x_ref[...] + of_tokens(0) * proj
    one_ref[...] = x_one
    two_ref[...] = (standard(x_one) * (1.0 + of_tokens(3)) + of_tokens(5)).astype(low)
    flow.landed((1, 2))
    step = 512
    hidden = pre_ref.shape[1]

    def load_up(c):
        rows = pl.ds(pl.multiple_of(c * step, step), step)
        slot = lax.rem(c, 2)
        return pltpu.make_async_copy(f_up.at[:, rows], wu_ref.at[slot], wu_sem.at[slot])

    load_up(0).start()

    def up_step(c, carry):
        pl.when(c + 1 < hidden // step)(lambda: load_up(c + 1).start())
        load_up(c).wait()
        w = wu_ref.at[lax.rem(c, 2)]
        pre = nt(two_ref[:, :half], w[0]) + nt(two_ref[:, half:], w[1])
        cols = pl.ds(pl.multiple_of(c * step, step), step)
        pre_ref[:, cols] = pre
        act_ref[:, cols] = gelu(pre).astype(low)
        return carry

    for i in range(2):
        lax.fori_loop(4 * i, 4 * i + 4, up_step, 0)
        tick(1)
    tick(flow.steps())
    flow.landed(range(3, 5))
    first_flow.finish()
    flow.finish()
    there.finish()
    home.finish()
    for copy in ada_copies + edges + [silu_copy, part_copy]:
        copy.wait_send()


def front(shards, condition, ada_state, cells, embed_state, vector_state, lengths, tables, groups):
    width = condition.shape[1]
    tokens = cells.shape[1]
    slots = lengths.shape[1]
    group_len = 16 * tokens
    hidden = 16 * shards[2].shape[0]
    f32, low = jnp.float32, jnp.bfloat16
    dma = pltpu.SemaphoreType.DMA
    shape = jax.ShapeDtypeStruct
    ada_width = ada_state.shape[2]
    fulls = [shape((2, 16 * s.shape[0], s.shape[1]), low) for s in shards]
    outs = fulls + [
        shape((16, 8, ada_width), f32),
        shape((tokens, width), low),
        shape((2 * width // LANES, tokens, LANES), f32),
        shape((group_len, LANES), f32),
        shape((group_len, LANES), low),
        shape((group_len, LANES), low),
        shape((LANES, group_len), low),
        shape((LANES, group_len), low),
        shape((tokens, width), low),
        shape((tokens, width), f32),
        shape(cells.shape, f32),
        shape((8, tokens), f32),
        shape((tokens, 8), f32),
        shape((2, 8, width // 2), f32),
        shape((tokens, width), f32),
        shape((tokens, width), f32),
        shape((tokens, width), low),
        shape((tokens, hidden), f32),
        shape((tokens, hidden), low),
    ]
    packed, mid = tokens * 3 // 2, tokens // 2
    scratch = [
        pltpu.VMEM((4, 2, 3, 256, width // 2), low),
        pltpu.VMEM((16, packed, LANES), low),
        pltpu.VMEM((16, packed, LANES), low),
        pltpu.VMEM((16, mid, LANES), low),
        pltpu.VMEM((16, mid, LANES), low),
        pltpu.VMEM((group_len, LANES), low),
        pltpu.VMEM((ROWS, group_len), f32),
        dma((4, 2, 3)),
        pltpu.VMEM(ada_state.shape[1:], f32),
        pltpu.VMEM((8, width), f32),
        pltpu.VMEM((8, ada_width), f32),
        pltpu.VMEM((8, ada_width), f32),
        pltpu.VMEM((8, ada_width), f32),
        pltpu.VMEM((32, LANES), f32),
        pltpu.VMEM((32, LANES), f32),
        pltpu.VMEM((32, LANES), f32),
        pltpu.VMEM((2, width, width // 2), low),
        pltpu.VMEM((2, 2, 512, width // 2), low),
    ]
    scratch += Gather.scratch(2) + Gather.scratch(5) + [dma((16,)) for _ in range(6)]
    scratch += [dma, dma((2,)), dma((2,)), dma((2,)), dma((2,)), dma, dma((2,))]
    return pl.pallas_call(
        functools.partial(front_kernel, groups, slots),
        out_shape=outs,
        in_specs=[ANY] * 4 + [VM, ANY] + [VM] * 8,
        out_specs=[ANY] * 4 + [VM] * 19,
        scratch_shapes=scratch,
        compiler_params=pltpu.CompilerParams(
            collective_id=0, has_side_effects=True, vmem_limit_bytes=VMEM_BYTES
        ),
    )(*shards, condition, ada_state, cells, embed_state, vector_state, lengths, *tables)


class Scatter:
    STAGES = 6

    def __init__(self, parts, outs, bufs, sems, pieces):
        self.parts, self.outs, self.bufs, self.pieces = parts, outs, bufs, pieces
        self.send, self.recv = sems
        self.parts_left = {}
        core, z, yx = place()
        self.z, self.yx = z, yx
        self.x_dev, self.y_dev = at_dev(core, z, yx ^ 1), at_dev(core, z, yx ^ 2)
        self.up_dev, self.down_dev = at_dev(core, lax.min(z + 1, 3), yx), at_dev(core, lax.max(z - 1, 0), yx)
        self.ends = []

    @staticmethod
    def scratch(shapes, count):
        low = jnp.bfloat16
        out = []
        for rows, cols in shapes:
            out += [pltpu.VMEM((depth, rows, cols), low) for depth in (2, 2, 4, 4, 3, 3)]
        dma = pltpu.SemaphoreType.DMA
        return out + [dma((count, 8)), dma((count, 8))]

    def push(self, p, slot, src, dst, device):
        copy = pltpu.make_async_remote_copy(
            src_ref=src,
            dst_ref=dst,
            send_sem=self.send.at[p, slot],
            recv_sem=self.recv.at[p, slot],
            device_id=device,
            device_id_type=MESH_ID,
        )
        copy.start()
        return copy

    def arrive(self, p, slot, ref):
        pltpu.make_async_copy(ref, ref, self.recv.at[p, slot]).wait()

    def stage(self, p, s):
        i, first, rows = self.pieces[p]
        rows = pl.ds(first, rows)
        part = self.parts[i]
        names = ("turn_x", "turn_y", "rx", "ry", "up", "down")
        buf = dict(zip(names, self.bufs[6 * i : 6 * i + 6]))
        z, yx = self.z, self.yx
        f32, low = jnp.float32, jnp.bfloat16
        lo2, hi2 = pl.ds(0, 2), pl.ds(2, 2)

        def view(name, which):
            return buf[name].at[which, rows]

        def wide(ref):
            return ref[...].astype(f32)

        def hop(condition, slot, name, which, device):
            ref = view(name, which)

            def start():
                self.push(p, slot, ref, ref, device)

            def end():
                pltpu.make_async_copy(ref, ref, self.send.at[p, slot]).wait()

            pl.when(condition)(start)
            self.ends.append(lambda: pl.when(condition)(end))

        if s == 0:
            copies = [
                self.push(p, 0, part.at[lo2, yx ^ 3, rows], view("turn_x", lo2), self.x_dev),
                self.push(p, 1, part.at[hi2, yx ^ 3, rows], view("turn_y", lo2), self.y_dev),
                self.push(p, 2, part.at[lo2, yx ^ 1, rows], view("rx", lo2), self.x_dev),
                self.push(p, 3, part.at[hi2, yx ^ 2, rows], view("ry", hi2), self.y_dev),
            ]
            self.parts_left[p] = [copy.wait_send for copy in copies]
        elif s == 1:
            turn = view("turn_x", lo2)
            self.arrive(p, 0, turn)
            turn[...] = (wide(part.at[lo2, yx ^ 2, rows]) + wide(turn)).astype(low)
            self.ends.append(self.push(p, 4, turn, view("ry", lo2), self.y_dev).wait_send)
            turn = view("turn_y", lo2)
            self.arrive(p, 1, turn)
            turn[...] = (wide(part.at[hi2, yx ^ 1, rows]) + wide(turn)).astype(low)
            self.ends.append(self.push(p, 5, turn, view("rx", hi2), self.x_dev).wait_send)
        elif s == 2:
            self.arrive(p, 2, view("rx", lo2))
            self.arrive(p, 3, view("ry", hi2))
            self.arrive(p, 4, view("ry", lo2))
            self.arrive(p, 5, view("rx", hi2))
            self.outs[i][rows] = wide(part.at[z, yx, rows]) + wide(view("rx", z)) + wide(view("ry", z))
            for z_at in range(4):
                total = wide(part.at[z_at, yx, rows]) + wide(view("rx", z_at)) + wide(view("ry", z_at))
                view("rx", z_at)[...] = total.astype(low)

            def first_up():
                view("up", pl.ds(0, 3))[...] = view("rx", pl.ds(1, 3))[...]

            def first_down():
                view("down", pl.ds(0, 3))[...] = view("rx", pl.ds(0, 3))[...]

            pl.when(z == 0)(first_up)
            hop(z == 0, 6, "up", pl.ds(0, 3), self.up_dev)
            pl.when(z == 3)(first_down)
            hop(z == 3, 7, "down", pl.ds(0, 3), self.down_dev)
        elif s in (3, 4):
            at = s - 2
            count = 3 - at

            def add_up():
                self.arrive(p, 6, view("up", pl.ds(at - 1, count + 1)))
                ref = view("up", pl.ds(at, count))
                ref[...] = (wide(ref) + wide(view("rx", pl.ds(at + 1, count)))).astype(low)

            def add_down():
                self.arrive(p, 7, view("down", pl.ds(0, count + 1)))
                ref = view("down", pl.ds(0, count))
                ref[...] = (wide(ref) + wide(view("rx", pl.ds(0, count)))).astype(low)

            pl.when(z == at)(add_up)
            hop(z == at, 6, "up", pl.ds(at, count), self.up_dev)
            pl.when(z == 3 - at)(add_down)
            hop(z == 3 - at, 7, "down", pl.ds(0, count), self.down_dev)
        else:
            out = self.outs[i].at[rows]

            def end_low():
                self.arrive(p, 7, view("down", pl.ds(0, 1)))
                out[...] += wide(view("down", 0))

            def end_high():
                self.arrive(p, 6, view("up", pl.ds(2, 1)))
                out[...] += wide(view("up", 2))

            def end_inner(at):
                out[...] += wide(view("up", at - 1)) + wide(view("down", at))

            pl.when(z == 0)(end_low)
            pl.when(z == 1)(lambda: end_inner(1))
            pl.when(z == 2)(lambda: end_inner(2))
            pl.when(z == 3)(end_high)

    def steps(self):
        return len(self.pieces) + self.STAGES - 1

    def run(self, t):
        for s in reversed(range(self.STAGES)):
            if 0 <= t - s < len(self.pieces):
                self.stage(t - s, s)

    def sent(self, p):
        for end in self.parts_left.pop(p, ()):
            end()

    def finish(self):
        for p in list(self.parts_left):
            self.sent(p)
        for end in self.ends:
            end()


COMMON_ROWS = 48


def standard_of(values):
    centred = values - jnp.mean(values, axis=1, keepdims=True)
    rstd = lax.rsqrt(jnp.mean(centred * centred, axis=1, keepdims=True) + NORM_EPS)
    return centred * rstd, rstd


def standard_back(unit, rstd, d_unit):
    along = jnp.mean(d_unit * unit, axis=1, keepdims=True)
    return rstd * (d_unit - jnp.mean(d_unit, axis=1, keepdims=True) - unit * along)


def gelu_slope(values):
    square = values * values
    inner = jnp.tanh(GELU_SCALE * (values + GELU_CUBE * values * square))
    slope = GELU_SCALE * (1.0 + 3.0 * GELU_CUBE * square)
    return 0.5 * (1.0 + inner) + 0.5 * values * (1.0 - inner * inner) * slope


def back_kernel(groups, splits, *refs):
    (
        cot_ref, hot_ref, ada_in, vec3_ref, x_ref, one_ref, proj_ref, h_any, two_any, low_any, act_any, pre_any,
        w_any, wo_any, wu_any, wd_any, book_any, out32_any, q_ref, k_ref, kt_ref, vt_ref, kept_any,
        smooth_ref, embed_ref, ok_ref,
    ) = refs[:26]
    (o_down, o_up, o_out, o_qkv, ada_both, common_all, bias_all, map_ref, block_ref) = refs[26:35]
    (
        send_ref, got_ref, back_send, back_got, g_ref, gt_ref, qt_ref, dq_ref, dkt_ref, dvt_ref,
        w_buf, dhid, h_both, dh_ref, ada_ref, com_ref, ada_land, com_land, ada_sum, com_sum, ada_sib, com_sib,
        bias_own, com_own, edge, edge_left, edge_right,
        act_half, dmlp, two_half, low_half, dattn, mlp_ref, dx_one, act_buf, pre_buf, d_att, p_down, p_up, p_out,
    ) = refs[35:75]
    rest = refs[75:]
    flow_bufs, rest = rest[:18], rest[18:]
    flow_sems, rest = rest[:2], rest[2:]
    last_bufs, rest = rest[:6], rest[6:]
    last_sems, rest = rest[:2], rest[2:]
    (
        ex_s, ex_r, home_s, home_r, w_sem, sib_s, sib_r, small_s, small_r, spread_s, spread_r, edge_s, edge_r,
        hid_s, hid_r, half_sem, kept_sem, free_sem,
    ) = rest
    core, z, yx = place()
    wide = z * 4 + yx
    sib = (1 - core, wide)
    f32, low = jnp.float32, jnp.bfloat16
    tokens, width = x_ref.shape
    half = width // 2
    hidden = dhid.shape[2]
    mid = tokens // 2
    two = 2 * tokens
    step = 512
    vec_ref = vec3_ref.at[1]
    dproj = dhid.at[:, :, pl.ds(0, 3 * width)]
    p_qkv = p_up.at[:, :, pl.ds(0, tokens)]
    flow = Scatter([p_down, p_up, p_out], [o_down, o_up, o_out], flow_bufs, flow_sems, splits[0])
    last = Scatter([p_qkv], [o_qkv], last_bufs, last_sems, splits[1])
    there = Exchange(back_send, back_got, (ex_s, ex_r))
    home = Exchange(send_ref, got_ref, (home_s, home_r))
    entry_barrier([(core, wide ^ r) for r in range(1, 16)] + [sib])

    def to_sib(slot, src, dst):
        copy = pltpu.make_async_remote_copy(
            src_ref=src, dst_ref=dst, send_sem=sib_s.at[slot], recv_sem=sib_r.at[slot], device_id=sib, device_id_type=MESH_ID
        )
        copy.start()
        return copy

    next_tick = [0]

    def tick(n):
        for _ in range(n):
            if next_tick[0] < flow.steps():
                flow.run(next_tick[0])
                next_tick[0] += 1

    lane = lane_iota((two, LANES))
    lane_tok = lane_iota((tokens, LANES))
    lane_mid = lane_iota((mid, LANES))

    def load_chunk(c):
        slot = lax.rem(c, 2)
        cols = pl.ds(pl.multiple_of(c * step, step), step)
        down_cols = pl.ds(pl.multiple_of(lax.rem(c, hidden // 2 // step) * step, step), step)
        down = wd_any.at[c // (hidden // 2 // step)]
        pairs = [
            (down.at[pl.ds(0, half), down_cols], w_buf.at[slot, 0]),
            (down.at[pl.ds(half, half), down_cols], w_buf.at[slot, 1]),
            (wu_any.at[0, cols], w_buf.at[slot, 2]),
            (wu_any.at[1, cols], w_buf.at[slot, 3]),
            (act_any.at[:, cols], act_buf.at[slot]),
            (pre_any.at[:, cols], pre_buf.at[slot]),
        ]
        return [pltpu.make_async_copy(src, dst, w_sem.at[slot, i]) for i, (src, dst) in enumerate(pairs)]

    def start_chunk(c):
        for copy in load_chunk(c):
            copy.start()

    start_chunk(0)
    out32_copy = pltpu.make_async_copy(out32_any, dq_ref, kept_sem)
    out32_copy.start()
    theirs = pl.ds(pl.multiple_of((1 - core) * half, half), half)
    mine = pl.ds(pl.multiple_of(core * half, half), half)
    hid_half = hidden // 2
    hid_theirs = pl.ds(pl.multiple_of((1 - core) * hid_half, hid_half), hid_half)
    hid_mine = pl.ds(pl.multiple_of(core * hid_half, hid_half), hid_half)
    ada = jnp.concatenate([ada_in[w] for w in range(16)], axis=1)
    hot = hot_ref[...]

    def of_tokens(block):
        return exact(hot, ada[:, block * width : (block + 1) * width] + vec_ref[block : block + 1, :])

    live = jnp.sum(hot, axis=1, keepdims=True)
    gate_two = of_tokens(1)
    dmlp[core] = (gate_two * (cot_ref[...].astype(f32) * live)).astype(low)
    sib_copies = [
        to_sib(0, dmlp.at[core], dmlp.at[core]),
        to_sib(1, act_any.at[:, hid_theirs], act_half.at[core]),
        to_sib(2, two_any.at[:, theirs], two_half.at[core]),
        to_sib(3, low_any.at[:, theirs], low_half.at[core]),
        to_sib(4, h_any.at[:, theirs], h_both.at[core]),
    ]
    half_copies = [
        pltpu.make_async_copy(src, dst.at[core], half_sem.at[i])
        for i, (src, dst) in enumerate(
            [
                (act_any.at[:, hid_mine], act_half),
                (two_any.at[:, mine], two_half),
                (low_any.at[:, mine], low_half),
                (h_any.at[:, mine], h_both),
            ]
        )
    ]
    for copy in half_copies:
        copy.start()
    mlp_ref[...] = jnp.zeros_like(mlp_ref)
    dh_ref[...] = jnp.zeros_like(dh_ref)

    def hid_copy(c):
        cols = pl.ds(pl.multiple_of(c * step, step), step)
        return pltpu.make_async_remote_copy(
            src_ref=dhid.at[core, :, cols],
            dst_ref=dhid.at[core, :, cols],
            send_sem=hid_s.at[c],
            recv_sem=hid_r.at[c],
            device_id=sib,
            device_id_type=MESH_ID,
        )

    def hidden_step(c, carry):
        pl.when(c + 1 < hidden // step)(lambda: start_chunk(c + 1))
        for copy in load_chunk(c):
            copy.wait()
        slot = lax.rem(c, 2)
        w = w_buf.at[slot]
        d_out = dmlp.at[core]
        d_act = nn(d_out[:, :half], w[0]) + nn(d_out[:, half:], w[1])
        d_hid = (d_act * gelu_slope(pre_buf[slot])).astype(low)
        dhid[core, :, pl.ds(pl.multiple_of(c * step, step), step)] = d_hid
        hid_copy(c).start()
        act = act_buf[slot]
        mlp_ref[:, :half] += nt(act, w[0])
        mlp_ref[:, half:] += nt(act, w[1])
        dh_ref[:, :half] += nn(d_hid, w[2])
        dh_ref[:, half:] += nn(d_hid, w[3])
        return carry

    chunks = hidden // step
    lax.fori_loop(0, 3, hidden_step, 0)
    sib_copies[0].wait_recv()
    sib_copies[1].wait_recv()
    half_copies[0].wait()

    def gradient(grads, inputs, out, rows, shard, lanes):
        def body(c, carry):
            cols = pl.ds(pl.multiple_of(c * rows, LANES), rows)
            total = nn(grads[0, :, cols].astype(f32).T.astype(low), inputs[0])
            total = total + nn(grads[1, :, cols].astype(f32).T.astype(low), inputs[1])
            count = rows // shard
            out[c * count // 4, pl.ds(lax.rem(c * count, 4), count)] = total.astype(low).reshape(count, shard, lanes)
            return carry

        return body

    lax.fori_loop(0, width // LANES, gradient(dmlp, act_half, p_down, LANES, width // 16, hid_half), 0)
    tick(1)
    lax.fori_loop(3, chunks, hidden_step, 0)
    tick(1)

    wo_copies = [
        pltpu.make_async_copy(wo_any.at[c, pl.ds(r * half, half)], w_buf.at[0, 2 * c + r], w_sem.at[0, 2 * c + r])
        for c in range(2)
        for r in range(2)
    ]
    for copy in wo_copies:
        copy.start()
    unit, rstd = standard_of(one_ref[...])
    g_two = cot_ref[...].astype(f32) * live
    d_one = standard_back(unit, rstd, dh_ref[...] * (1.0 + of_tokens(3))) + g_two
    dx_one[...] = d_one
    dattn[core] = (of_tokens(0) * d_one).astype(low)
    sib_copies.append(to_sib(5, dattn.at[core], dattn.at[core]))
    for copy in wo_copies:
        copy.wait()
    for c in range(2):
        part = nn(dattn[core, :, :half], w_buf[0, 2 * c]) + nn(dattn[core, :, half:], w_buf[0, 2 * c + 1])
        d_att[:, c * half : (c + 1) * half] = part.astype(low)

    def pack(pair, carry):
        cols = pl.ds(pl.multiple_of(pair * LANES, LANES), LANES)
        a, b = d_att[0:mid, cols].astype(f32), d_att[mid:, cols].astype(f32)
        back_send[2 * pair] = jnp.where(lane_mid < HALF_LANES, a, swap_halves(b)).astype(low)
        back_send[2 * pair + 1] = jnp.where(lane_mid < HALF_LANES, swap_halves(a), b).astype(low)
        there.push(2 * pair)
        there.push(2 * pair + 1)
        return carry

    lax.fori_loop(0, 8, pack, 0)

    def per_slot(values):
        return exact(hot, values, (0, 0))

    ada_ref[:, 3 * width : 4 * width] = per_slot(dh_ref[...] * unit)
    ada_ref[:, 5 * width : 6 * width] = per_slot(dh_ref[...])
    ada_ref[:, 0:width] = per_slot(d_one * proj_ref[...])
    ada_ref[:, width : 2 * width] = per_slot(g_two * mlp_ref[...])
    block_ref[...] = (live * (one_ref[...] + gate_two * mlp_ref[...])).astype(low)
    for c in range(chunks):
        hid_copy(c).wait_recv()
    half_copies[1].wait()
    sib_copies[2].wait_recv()
    lax.fori_loop(0, hidden // 256, gradient(dhid, two_half, p_up, 256, hidden // 16, half), 0)
    for c in range(chunks):
        hid_copy(c).wait_send()
    pl.semaphore_signal(free_sem, inc=1, device_id=sib, device_id_type=MESH_ID)
    tick(1)
    half_copies[2].wait()
    sib_copies[3].wait_recv()
    sib_copies[5].wait_recv()
    lax.fori_loop(0, width // LANES, gradient(dattn, low_half, p_out, LANES, width // 16, half), 0)
    tick(1)
    dkt_ref[...] = jnp.zeros_like(dkt_ref)
    dvt_ref[...] = jnp.zeros_like(dvt_ref)

    def unpack(pair, carry):
        there.wait(2 * pair)
        there.wait(2 * pair + 1)
        rows = pl.ds(pl.multiple_of(pair * two, two), two)
        pieces = []
        for e in range(2):
            g = back_got[2 * pair + e].astype(f32)
            pieces += [g, swap_halves(g)]
        grad = jnp.where(lane < HALF_LANES, jnp.concatenate(pieces, axis=0), 0.0)
        delta = jnp.sum(grad * dq_ref[rows, :], axis=1, keepdims=True)
        grad = lanes_three(lane, HALF_LANES, -delta, grad)
        g_ref[rows, :] = grad.astype(low)
        gt_ref[:, rows] = grad.T[:HALF_LANES].astype(low)
        qt_ref[:, rows] = q_ref[rows, :].astype(f32).T[:HALF_LANES].astype(low)
        return carry

    out32_copy.wait()
    for i in range(4):
        lax.fori_loop(2 * i, 2 * i + 2, unpack, 0)
        tick((0, 1, 0, 0)[i])

    def query_block(limit, b, carry):
        rows = pl.ds(pl.multiple_of(b * ROWS, ROWS), ROWS)
        q, g = q_ref[rows, :], g_ref[rows, :]
        qt, gt = qt_ref[:, rows], gt_ref[:, rows]

        def chunk(cols, acc):
            p = jnp.exp(nn(q, kt_ref[:, cols]))
            ds = (p * nn(g, vt_ref[:, cols])).astype(low)
            dvt_ref[:, cols] += nn(gt, p.astype(low))
            dkt_ref[:, cols] += nn(qt, ds)
            return acc + nn(ds, k_ref[cols, :])

        whole, left = limit // CHUNK, limit % CHUNK
        acc = lax.fori_loop(
            0,
            whole,
            lambda c, acc: chunk(pl.ds(pl.multiple_of(c * CHUNK, CHUNK), CHUNK), acc),
            jnp.zeros((ROWS, LANES), f32),
        )
        if left:
            acc = chunk(slice(whole * CHUNK, limit), acc)
        dq_ref[rows, :] = acc
        return carry

    for first, stop, limit in groups:
        for b in range(first, stop):
            lax.fori_loop(b, b + 1, functools.partial(query_block, limit), 0)
            tick((0, 0, 0, 1, 0, 1, 0, 1, 0, 1, 0, 0)[b])

    def send_out(pair, carry):
        rows = pl.ds(pl.multiple_of(pair * two, two), two)
        dkv = jnp.concatenate([dkt_ref[:, rows], dvt_ref[:, rows]], axis=0).T
        qk = jnp.where(lane < HALF_LANES, dq_ref[rows, :], swap_halves(dkv)).astype(low)
        for e in range(2):
            send_ref[2 * pair + e, 0:tokens, :] = qk[e * tokens : (e + 1) * tokens]
            a = dkv[e * tokens : e * tokens + mid]
            b = dkv[e * tokens + mid : (e + 1) * tokens]
            send_ref[2 * pair + e, tokens:, :] = jnp.where(lane_mid < HALF_LANES, swap_halves(a), b).astype(low)
            home.push(2 * pair + e)
        return carry

    lax.fori_loop(0, 8, send_out, 0)

    kept_copy = pltpu.make_async_copy(kept_any, dq_ref, kept_sem)
    kept_copy.start()
    tick(1)
    com_ref[...] = jnp.zeros_like(com_ref)

    def load_codes(c):
        slot = lax.rem(c, 2)
        rows = pl.ds(pl.multiple_of(lax.rem(c, chunks) * step, step), step)
        return [
            pltpu.make_async_copy(book_any.at[rows, pl.ds(r * half, half)], w_buf.at[slot, r], w_sem.at[slot, r])
            for r in range(2)
        ]

    def start_codes(c):
        for copy in load_codes(c):
            copy.start()

    start_codes(0)

    def logits_of(c):
        pl.when(c + 1 < 2 * chunks)(lambda: start_codes(c + 1))
        for copy in load_codes(c):
            copy.wait()
        w = w_buf.at[lax.rem(c, 2)]
        return nt(block_ref[:, :half], w[0]) + nt(block_ref[:, half:], w[1])

    def sum_codes(c, carry):
        top, total = carry
        logits = logits_of(c)
        new_top = jnp.maximum(top, jnp.max(logits, axis=1, keepdims=True))
        return new_top, total * jnp.exp(top - new_top) + jnp.sum(jnp.exp(logits - new_top), axis=1, keepdims=True)

    start = (jnp.full((tokens, 1), -3e38, f32), jnp.zeros((tokens, 1), f32))
    top, total = lax.fori_loop(0, chunks, sum_codes, start)
    share_of = live / total
    for c in range(chunks):
        mass = jnp.sum(jnp.exp(logits_of(chunks + c) - top) * share_of, axis=0, keepdims=True)
        com_ref[34 + c // 2 : 35 + c // 2, (c % 2) * step : (c % 2 + 1) * step] = mass
    slabs = 3 * width // step

    def load_w(j):
        rows = pl.ds(j * step, step)
        return [pltpu.make_async_copy(w_any.at[c, rows], w_buf.at[j % 2, c], w_sem.at[j % 2, c]) for c in range(2)]

    for j in range(2):
        for copy in load_w(j):
            copy.start()
    kept_copy.wait()

    def unnormalize(values, grad):
        inverse = lax.rsqrt(head_sums(values * values) + NORM_EPS)
        unit = values * inverse
        return inverse * (grad - unit * head_sums(unit * grad)), unit

    def heads_back(pair, carry):
        home.wait(2 * pair)
        home.wait(2 * pair + 1)
        cols = pl.ds(pl.multiple_of(pair * LANES, LANES), LANES)
        key_cols = pl.ds(pl.multiple_of(pair * LANES + width, LANES), LANES)
        val_cols = pl.ds(pl.multiple_of(pair * LANES + 2 * width, LANES), LANES)
        even = got_ref[2 * pair].astype(f32)
        odd = got_ref[2 * pair + 1].astype(f32)
        even_qk, odd_qk = even[:tokens], odd[:tokens]
        d_query = jnp.where(lane_tok < HALF_LANES, even_qk, swap_halves(odd_qk))
        d_key = jnp.where(lane_tok < HALF_LANES, swap_halves(even_qk), odd_qk)
        even_v, odd_v = even[tokens:], odd[tokens:]
        dproj[core, 0:mid, val_cols] = jnp.where(lane_mid < HALF_LANES, even_v, swap_halves(odd_v)).astype(low)
        dproj[core, mid:, val_cols] = jnp.where(lane_mid < HALF_LANES, swap_halves(even_v), odd_v).astype(low)
        scaled = d_query * (8.0 * (1.0 + vec_ref[7:8, cols]))
        d_q, unit = unnormalize(dq_ref[pl.ds(pl.multiple_of(pair * tokens, tokens), tokens), :], scaled)
        com_ref[33:34, cols] = jnp.sum(d_query * unit, axis=0, keepdims=True) * 8.0
        dproj[core, :, cols] = d_q.astype(low)
        dproj[core, :, key_cols] = unnormalize(dq_ref[pl.ds(pl.multiple_of((pair + 8) * tokens, tokens), tokens), :], d_key)[0].astype(low)
        return carry

    lax.fori_loop(0, 8, heads_back, 0)
    pl.semaphore_wait(free_sem, 1)
    d_copy = to_sib(6, dproj.at[core], dproj.at[core])

    for j in range(slabs):
        for copy in load_w(j):
            copy.wait()
        for c in range(2):
            part = nn(dproj[core, :, j * step : (j + 1) * step], w_buf[j % 2, c])
            cols = slice(c * half, (c + 1) * half)
            dh_ref[:, cols] = part if j == 0 else dh_ref[:, cols] + part
        if j + 2 < slabs:
            for copy in load_w(j + 2):
                copy.start()
    half_copies[3].wait()
    sib_copies[4].wait_recv()
    d_copy.wait_recv()

    def weight_grad(c, carry):
        cols = pl.ds(pl.multiple_of(c * two, two), two)
        total = nn(dproj[0, :, cols].astype(f32).T.astype(low), h_both[0])
        total = total + nn(dproj[1, :, cols].astype(f32).T.astype(low), h_both[1])
        p_qkv[c // 2, pl.ds(2 * (c % 2), 2)] = total.astype(low).reshape(2, tokens, half)
        return carry

    assert next_tick[0] >= 6
    for p in range(len(splits[0])):
        flow.sent(p)
    lax.fori_loop(0, 8, weight_grad, 0)
    last.run(0)
    tick(flow.steps())

    unit, rstd = standard_of(x_ref[...])
    d_h = dh_ref[...]
    ada_ref[:, 2 * width : 3 * width] = per_slot(d_h * unit)
    ada_ref[:, 4 * width : 5 * width] = per_slot(d_h)
    d_x = standard_back(unit, rstd, d_h * (1.0 + of_tokens(2))) + dx_one[...]
    last.run(1)
    com_ref[0:32, :] = lax.dot_general(
        smooth_ref[...], d_x, (((1,), (0,)), ((), ())), precision=HIGHEST_PRECISION, preferred_element_type=f32
    )
    com_ref[32:33, :] = jnp.sum(d_x, axis=0, keepdims=True)
    small = []
    quarter = COMMON_ROWS // 2

    def common_part(ref, w):
        rows = pl.ds(pl.multiple_of((w // 8) * quarter, 8), quarter)
        return ref.at[rows, pl.ds(pl.multiple_of((w % 8) * LANES, LANES), LANES)]

    ada_width = 6 * width // 16

    def ada_part(ref, w):
        return ref.at[:, pl.ds(pl.multiple_of(w * ada_width, LANES), ada_width)]

    def spread(sem_s, sem_r, r, slot, src, dst):
        copy = pltpu.make_async_remote_copy(
            src_ref=src,
            dst_ref=dst,
            send_sem=sem_s.at[slot, r],
            recv_sem=sem_r.at[slot, r],
            device_id=(core, wide ^ r),
            device_id_type=MESH_ID,
        )
        copy.start()
        return copy

    for r in range(1, 16):
        small.append(spread(small_s, small_r, r, 0, ada_part(ada_ref, wide ^ r), ada_land.at[r]))
        small.append(spread(small_s, small_r, r, 1, common_part(com_ref, wide ^ r), com_land.at[r]))
    d_smooth = lax.dot_general(
        embed_ref[1], d_x, (((1,), (1,)), ((), ())), precision=HIGHEST_PRECISION, preferred_element_type=f32
    )
    left, right = ok_ref[0:1, :], ok_ref[1:2, :]
    share = d_smooth / (2.0 + left + right)
    spot = lane_iota((32, LANES))
    edge[...] = jnp.where(spot == 0, share[:, 0:1], jnp.where(spot == 1, share[:, tokens - 1 : tokens], 0.0))

    def edge_copy(slot, dst, shift):
        return pltpu.make_async_remote_copy(
            src_ref=edge,
            dst_ref=dst,
            send_sem=edge_s.at[slot],
            recv_sem=edge_r.at[slot],
            device_id=(core, lax.rem(wide + shift, 16)),
            device_id_type=MESH_ID,
        )

    to_right, to_left = edge_copy(0, edge_left, 1), edge_copy(1, edge_right, 15)
    last.run(2)
    ada_total, com_total = ada_part(ada_ref, wide)[...], common_part(com_ref, wide)[...]
    for copy in small:
        copy.wait_recv()
    for r in range(1, 16):
        ada_total = ada_total + ada_land[r]
        com_total = com_total + com_land[r]
    ada_sum[...] = ada_total
    com_sum[...] = com_total
    swaps = [to_sib(7, ada_sum, ada_sib), to_sib(8, com_sum, com_sib)]
    last.run(3)
    for copy in swaps:
        copy.wait_recv()
    ada_both[core] = ada_sum[...]
    ada_both[1 - core] = ada_sib[...]
    bias = jnp.sum(ada_sum[...] + ada_sib[...], axis=0, keepdims=True)
    bias_own[...] = jnp.broadcast_to(bias, bias_own.shape)
    com_own[...] = com_sum[...] + com_sib[...]
    ada_part(bias_all, wide)[...] = bias_own[...]
    common_part(common_all, wide)[...] = com_own[...]
    back = []
    for r in range(1, 16):
        back.append(spread(spread_s, spread_r, r, 0, bias_own, ada_part(bias_all, wide)))
        back.append(spread(spread_s, spread_r, r, 1, com_own, common_part(common_all, wide)))
    for i in range(4, last.steps()):
        last.run(i)
    to_right.start()
    to_left.start()
    to_right.wait_recv()
    to_left.wait_recv()
    column = lane_iota((32, tokens))
    before = jnp.where(column == 0, edge_left[:, 1:2], jnp.roll(share, 1, axis=1))
    after = jnp.where(column == tokens - 1, edge_right[:, 0:1], jnp.roll(share, -1, axis=1))
    map_ref[...] = 2.0 * share + left * before + right * after
    for copy in back:
        copy.wait_recv()
    for copy in small + swaps + back + sib_copies + [d_copy, to_right, to_left]:
        copy.wait_send()
    flow.finish()
    last.finish()
    there.finish()
    home.finish()


def back(args, groups, splits, call_id):
    x_zero, act = args[4], args[10]
    tokens, width = x_zero.shape
    hidden = act.shape[1]
    group_len = 16 * tokens
    half, mid, packed = width // 2, tokens // 2, tokens * 3 // 2
    f32, low = jnp.float32, jnp.bfloat16
    dma = pltpu.SemaphoreType.DMA
    shape = jax.ShapeDtypeStruct
    sizes = [(width // 16, hidden // 2), (hidden // 16, half), (width // 16, half), (3 * width // 16, half)]
    first = pieces_of([shape(s, f32) for s in sizes[:3]], splits[0])
    second = pieces_of([shape(sizes[3], f32)], splits[1])
    ada_width, quarter = 6 * width // 16, COMMON_ROWS // 2
    outs = [shape(s, f32) for s in sizes] + [
        shape((2, 8, ada_width), f32),
        shape((COMMON_ROWS, width), f32),
        shape((8, 6 * width), f32),
        shape((32, tokens), f32),
        shape((tokens, width), low),
    ]
    vm = pltpu.VMEM
    scratch = [
        vm((16, packed, LANES), low),
        vm((16, packed, LANES), low),
        vm((16, mid, LANES), low),
        vm((16, mid, LANES), low),
        vm((group_len, LANES), low),
        vm((HALF_LANES, group_len), low),
        vm((HALF_LANES, group_len), low),
        vm((group_len, LANES), f32),
        vm((HALF_LANES, group_len), f32),
        vm((HALF_LANES, group_len), f32),
        vm((2, 4, 512, half), low),
        vm((2, tokens, hidden), low),
        vm((2, tokens, half), low),
        vm((tokens, width), f32),
        vm((8, 6 * width), f32),
        vm((COMMON_ROWS, width), f32),
        vm((16, 8, ada_width), f32),
        vm((16, quarter, LANES), f32),
        vm((8, ada_width), f32),
        vm((quarter, LANES), f32),
        vm((8, ada_width), f32),
        vm((quarter, LANES), f32),
        vm((8, ada_width), f32),
        vm((quarter, LANES), f32),
        vm((32, LANES), f32),
        vm((32, LANES), f32),
        vm((32, LANES), f32),
        vm((2, tokens, hidden // 2), low),
        vm((2, tokens, width), low),
        vm((2, tokens, half), low),
        vm((2, tokens, half), low),
        vm((2, tokens, width), low),
        vm((tokens, width), f32),
        vm((tokens, width), f32),
        vm((2, tokens, 512), low),
        vm((2, tokens, 512), f32),
        vm((tokens, width), low),
    ] + [vm((4, 4) + s, low) for s in sizes[:3]]
    scratch += Scatter.scratch(sizes[:3], len(first)) + Scatter.scratch(sizes[3:], len(second))
    scratch += [dma((16,)) for _ in range(4)] + [dma((2, 6)), dma((16,)), dma((16,))]
    scratch += [dma((2, 16)) for _ in range(4)] + [dma((2,)), dma((2,))]
    scratch += [dma((8,)), dma((8,)), dma((4,)), dma, pltpu.SemaphoreType.REGULAR]
    return pl.pallas_call(
        functools.partial(back_kernel, groups, (first, second)),
        out_shape=outs,
        in_specs=[VM] * 7 + [ANY] * 11 + [VM] * 4 + [ANY] + [VM] * 3,
        out_specs=[VM] * 9,
        scratch_shapes=scratch,
        compiler_params=pltpu.CompilerParams(
            collective_id=call_id, has_side_effects=True, vmem_limit_bytes=63 * 1024 * 1024
        ),
    )(*args)


def run_tables(slots):
    squares = np.zeros((8, LANES), np.float32)
    pick = np.zeros((LANES, LANES), np.float32)
    for run in range(slots * LEVELS):
        squares[0, HALF_LANES + run] = LONG_SIDES[run // slots] ** 2
        squares[1, HALF_LANES + run] = SHORT_SIDES[run // slots] ** 2
        pick[HALF_LANES + run, run % slots] = 1.0
    tri = np.triu(np.ones((LANES, LANES), np.float32))
    low = jnp.bfloat16
    return [jnp.asarray(squares), jnp.asarray(tri), jnp.asarray(pick, low), jnp.asarray(attention_rule(slots), low)]


def attention_rule(slots):
    runs = slots * LEVELS + 1
    rule = np.zeros((LANES, LANES), np.float32)
    for a in range(runs):
        for b in range(runs):
            slot_a, level_a = (slots, 0) if a == runs - 1 else (a % slots, a // slots)
            slot_b, level_b = (slots, 0) if b == runs - 1 else (b % slots, b // slots)
            if slot_a != slot_b or level_b > level_a:
                rule[HALF_LANES + a, HALF_LANES + b] = -BIG
    return rule


def fast_shards(
    feature_map,
    condition,
    item_lengths,
    cotangent,
    code_book,
    qkv_state,
    out_state,
    up_state,
    down_state,
    ada_state,
    embed_state,
    vector_state,
):
    tok_rows, model_width = cotangent.shape
    low, f32 = jnp.bfloat16, jnp.float32
    group_len = tok_rows * lax.axis_size("wide")
    tokens_all = lax.axis_size("dp") * group_len
    lengths = item_lengths[0]
    slot_count = lengths.shape[0]

    states = (qkv_state, out_state, up_state, down_state, ada_state)
    flipped = tuple(stacked[1].astype(low).T for stacked in states[:4])
    groups = same_limits(key_limits(group_len, slot_count))
    (
        w_qkv, w_out, w_up, w_down, ada_gathered, h_one_low, kept_qk, out32, q_own, k_own, kt_own, vt_own, attn_low,
        x_zero, smooth, flags, one_hot_wide, silu_rows, attn_proj, x_one, h_two_low, hidden_pre, act_low,
    ) = front(
        flipped,
        condition,
        ada_state,
        feature_map,
        embed_state,
        vector_state,
        item_lengths,
        run_tables(slot_count),
        groups,
    )
    embed_w = embed_state[1]
    s_down, s_up, s_out, s_qkv, d_ada_both, common_sum, bias_sum, map_grad, block_out = back(
        [cotangent, one_hot_wide, ada_gathered, vector_state, x_zero, x_one, attn_proj, h_one_low, h_two_low, attn_low]
        + [act_low, hidden_pre, w_qkv, w_out, w_up, w_down, code_book, out32, q_own, k_own, kt_own, vt_own]
        + [kept_qk.reshape(-1, LANES), smooth, embed_state, flags],
        groups,
        ((2, 2, 1), (2,)),
        1,
    )
    embed_rows = embed_w.shape[0]
    d_embed_all = common_sum[:embed_rows]
    bias_rows = bias_sum[0].reshape(6, model_width)
    d_vectors_all = jnp.concatenate([bias_rows, common_sum[embed_rows : embed_rows + 2]], axis=0)
    mass_all = common_sum[embed_rows + 2 : embed_rows + 2 + code_book.shape[0] // model_width]
    histogram = mass_all.reshape(-1) * (code_book.shape[0] / tokens_all)
    d_ada_own = d_ada_both.reshape(16, -1)
    grad_ada = contract_rows(silu_rows.reshape(16, -1), d_ada_own, HIGHEST_PRECISION)

    owned_grads = (s_qkv.T, s_out.T, s_up.T, s_down.T, grad_ada)
    root_tokens = math.sqrt(tokens_all)
    spreads = (
        model_width ** (-0.5),
        (model_width // 16) ** (-0.5),
        model_width ** (-0.5),
        w_up.shape[1] ** (-0.5),
        model_width ** (-0.5),
    )
    new_states = tuple(
        nesterov(stacked, gradient, BASE_RATE * spread_w / (factor_g * root_tokens), WEIGHT_DECAY)
        for stacked, gradient, spread_w, factor_g in zip(states, owned_grads, spreads, GRAD_FACTORS)
    )
    embed_new = nesterov(
        embed_state, d_embed_all, BASE_RATE * embed_rows ** (-0.5) / (EMBED_FACTOR * root_tokens), 0.0
    )
    vector_new = nesterov(vector_state, d_vectors_all, VECTOR_RATE / root_tokens, 0.0)
    outputs = [block_out, map_grad, histogram]
    for state in new_states:
        outputs += [state, state[1].astype(low)]
    return tuple(outputs + [embed_new, vector_new, d_vectors_all[7]])


def solution(mesh):
    body = fast_shards if dict(mesh.shape) == {"dp": 2, "wide": 16} else shards
    in_specs = (
        P(None, ("dp", "wide")),
        P("dp", None),
        P("dp", None),
        P(("dp", "wide"), None),
        P(),
        P(None, "dp", "wide"),
        P(None, "dp", "wide"),
        P(None, "dp", "wide"),
        P(None, "dp", "wide"),
        P(None, "dp", "wide"),
        P(),
        P(),
    )
    out_specs = (
        P(("dp", "wide"), None),
        P(None, ("dp", "wide")),
        P(),
        P(None, "dp", "wide"),
        P("dp", "wide"),
        P(None, "dp", "wide"),
        P("dp", "wide"),
        P(None, "dp", "wide"),
        P("dp", "wide"),
        P(None, "dp", "wide"),
        P("dp", "wide"),
        P(None, "dp", "wide"),
        P("dp", "wide"),
        P(),
        P(),
        P(),
    )
    return jax.shard_map(body, mesh=mesh, in_specs=in_specs, out_specs=out_specs, check_vma=False)
```

```python
import functools
import math

import jax
import jax.numpy as jnp
import numpy as np
from jax import lax
from jax.experimental import pallas as pl
from jax.experimental.pallas import tpu as pltpu
from jax.sharding import PartitionSpec as P

HEADS = 16
LEVELS = 10
STEP = 7


SHORT_SIDES = (1, 2, 3, 4, 5, 6, 8, 10, 13, 16)
LONG_SIDES = (1, 2, 3, 4, 6, 9, 13, 18, 24, 32)
MASKED = -1e30
NORM_EPS = 1e-06
MOMENTUM = 0.9
WEIGHT_DECAY = 0.05
BASE_RATE = 0.37
VECTOR_RATE = 0.22
GRAD_FACTORS = (0.15, 0.1, 0.3, 0.35, 0.3)
EMBED_FACTOR = 0.6
HIGHEST_PRECISION = lax.Precision.HIGHEST


def padded(cells, sides, width):
    for axis, dim in sides:
        count = lax.axis_size(axis)
        ends = count - 1
        head = lax.slice_in_dim(cells, 0, width, axis=dim)
        tail = lax.slice_in_dim(cells, cells.shape[dim] - width, cells.shape[dim], axis=dim)
        cells = jnp.concatenate(
            [
                lax.ppermute(tail, axis, [(i, (i + 1) % count) for i in range(ends)]),
                cells,
                lax.ppermute(head, axis, [((i + 1) % count, i) for i in range(ends)]),
            ],
            axis=dim,
        )
    return cells


def layout(lengths, positions, group_len):
    short_sq = jnp.array([side * side for side in SHORT_SIDES[:LEVELS]], jnp.int32)
    long_sq = jnp.array([side * side for side in LONG_SIDES[:LEVELS]], jnp.int32)
    short_total = sum((side * side for side in SHORT_SIDES[:LEVELS]))
    long_total = sum((side * side for side in LONG_SIDES[:LEVELS]))
    slot_count = lengths.shape[0]
    counts = jnp.where(
        lengths[None, :] == long_total,
        long_sq[:, None],
        jnp.where(lengths[None, :] == short_total, short_sq[:, None], 0),
    )
    unused = group_len - jnp.sum(lengths)
    ordered = jnp.concatenate([counts.reshape(-1), unused[None]])
    boundary = jnp.cumsum(ordered)
    segment = jnp.sum((boundary[None, :] <= positions[:, None]).astype(jnp.int32), axis=1)
    segment = jnp.minimum(segment, ordered.shape[0] - 1)
    unused_id = slot_count * LEVELS
    tok_level = jnp.where(segment >= unused_id, 0, segment // slot_count)
    tok_slot = jnp.where(segment >= unused_id, slot_count, segment % slot_count)
    return (tok_slot, tok_level, segment)


def pre_norm(inputs, scaling, offset_add):
    row_mean = jnp.mean(inputs, axis=-1, keepdims=True)
    centred = inputs - row_mean
    spread = jnp.mean(centred * centred, axis=-1, keepdims=True)
    return centred * lax.rsqrt(spread + NORM_EPS) * (1.0 + scaling) + offset_add


def unit_heads(inputs):
    shaped = inputs.reshape(inputs.shape[0], HEADS, -1)
    shaped = shaped * lax.rsqrt(jnp.sum(shaped * shaped, axis=-1, keepdims=True) + NORM_EPS)
    return shaped.reshape(inputs.shape)


def split_heads(projected, q_gain):
    queries, key_part, value_part = jnp.split(projected, 3, axis=1)
    head_scale = math.sqrt(queries.shape[1] // HEADS)
    return (unit_heads(queries) * (head_scale * (1.0 + q_gain)), unit_heads(key_part), value_part)


def smooth_map(values, left_ok, right_ok, before, following):
    return (left_ok * before + 2.0 * values + right_ok * following) / (2.0 + left_ok + right_ok)


def nesterov(stacked, gradient, step_rate, decay_rate):
    moment, weight, average = (stacked[0], stacked[1], stacked[2])
    step_grad = gradient + decay_rate * weight
    new_moment = MOMENTUM * moment + step_rate * step_grad
    new_weight = weight - (step_rate * step_grad + MOMENTUM * new_moment)
    retain = min(0.999, (1.0 + STEP) / (10.0 + STEP))
    new_average = retain * average + (1.0 - retain) * new_weight
    return jnp.stack([new_moment, new_weight, new_average])


def contract_rows(left_side, right_side, precision=None):
    return lax.dot_general(
        left_side,
        right_side,
        (((0,), (0,)), ((), ())),
        precision=precision,
        preferred_element_type=jnp.float32,
    )


def against(left_side, right_side):
    return lax.dot_general(
        left_side, right_side, (((1,), (1,)), ((), ())), preferred_element_type=jnp.float32
    )


def shards(
    feature_map,
    condition,
    item_lengths,
    cotangent,
    code_book,
    qkv_state,
    out_state,
    up_state,
    down_state,
    ada_state,
    embed_state,
    vector_state,
):
    tok_rows = cotangent.shape[0]
    model_width = cotangent.shape[1]
    head_dim = model_width // HEADS
    wide_count = lax.axis_size("wide")
    group_len = tok_rows * wide_count
    tokens_all = lax.axis_size("dp") * group_len
    lengths = item_lengths[0]
    slot_count = lengths.shape[0]
    positions = lax.axis_index("wide") * tok_rows + jnp.arange(tok_rows, dtype=jnp.int32)
    tok_slot, tok_level, segment = layout(lengths, positions, group_len)
    live_rows = (tok_slot < slot_count).astype(jnp.float32)[:, None]
    left_ok = ((layout(lengths, positions - 1, group_len)[2] == segment) & (positions > 0)).astype(
        jnp.float32
    )
    right_ok = (
        (layout(lengths, positions + 1, group_len)[2] == segment) & (positions < group_len - 1)
    ).astype(jnp.float32)
    rimmed = padded(feature_map, (("wide", 1),), 1)
    smooth = smooth_map(feature_map, left_ok, right_ok, rimmed[:, :-2], rimmed[:, 2:])
    states = (qkv_state, out_state, up_state, down_state, ada_state)
    masters = tuple((stacked[1].astype(jnp.bfloat16) for stacked in states))
    columns = (
        lax.all_gather(masters[0], "wide", axis=1, tiled=True),
        lax.all_gather(masters[1], "wide", axis=1, tiled=True),
        lax.all_gather(masters[2], "wide", axis=1, tiled=True),
        lax.all_gather(masters[3], "wide", axis=1, tiled=True),
    )
    ada_piece = lax.all_gather(masters[4], "wide", axis=1, tiled=True)
    w_qkv, w_out, w_up, w_down, w_ada = (
        lax.all_gather(columns[0], "dp", axis=0, tiled=True),
        lax.all_gather(columns[1], "dp", axis=0, tiled=True),
        lax.all_gather(columns[2], "dp", axis=0, tiled=True),
        lax.all_gather(columns[3], "dp", axis=0, tiled=True),
        lax.all_gather(ada_piece, "dp", axis=0, tiled=True),
    )
    embed_w = embed_state[1]
    vectors = vector_state[1]
    x_zero = (
        lax.dot_general(smooth, embed_w, (((0,), (0,)), ((), ())), precision=HIGHEST_PRECISION)
        + vectors[6]
    )
    silu_cond = jax.nn.silu(condition).astype(jnp.bfloat16)
    ada_product = jnp.dot(silu_cond, w_ada, preferred_element_type=jnp.float32)
    ada_all = ada_product + vectors[:6].reshape(-1)
    one_hot = (tok_slot[:, None] == jnp.arange(slot_count, dtype=jnp.int32)[None, :]).astype(
        jnp.float32
    )
    token_ada = jnp.dot(one_hot, ada_all, precision=HIGHEST_PRECISION)
    gate_one, gate_two, scale_one, scale_two, shift_one, shift_two = jnp.split(token_ada, 6, axis=1)
    h_one_low = pre_norm(x_zero, scale_one, shift_one).astype(jnp.bfloat16)
    projected = jnp.dot(h_one_low, w_qkv, preferred_element_type=jnp.float32)
    (q_unit, k_unit, v_full), heads_back = jax.vjp(split_heads, projected, vectors[7])
    queries = q_unit.astype(jnp.bfloat16)
    keys_low = k_unit.astype(jnp.bfloat16)
    values_low = v_full.astype(jnp.bfloat16)
    query_heads = queries.reshape(tok_rows, HEADS, head_dim)

    def blockwise(advance, running, pieces, first_row):
        key_count = pieces[0].shape[0]
        block_size = math.gcd(key_count, 1024)

        def per_block(current, offset):
            key_part = tuple(
                (lax.dynamic_slice_in_dim(piece_arr, offset, block_size, 0) for piece_arr in pieces)
            )
            first_key = first_row + offset
            k_slot, k_level, _ = layout(
                lengths, first_key + jnp.arange(block_size, dtype=jnp.int32), group_len
            )
            allowed = (tok_slot[:, None] == k_slot[None, :]) & (
                k_level[None, :] <= tok_level[:, None]
            )
            current = advance(current, key_part, allowed, first_key)
            return (current, None)

        offsets = jnp.arange(key_count // block_size, dtype=jnp.int32) * block_size
        return lax.scan(per_block, running, offsets)[0]

    def scores_of(key_block, allowed):
        raw_scores = jnp.einsum(
            "qhd,khd->hqk",
            query_heads,
            key_block.reshape(-1, HEADS, head_dim),
            preferred_element_type=jnp.float32,
        )
        return jnp.where(allowed[None], raw_scores, MASKED)

    def stats_step(running, key_part, allowed, first_key):
        scores = scores_of(key_part[0], allowed)
        top_score, exp_total = running
        new_top = jnp.maximum(top_score, jnp.max(scores, axis=-1, keepdims=True))
        exp_total = exp_total * jnp.exp(top_score - new_top) + jnp.sum(
            jnp.exp(scores - new_top), axis=-1, keepdims=True
        )
        return (new_top, exp_total)

    kv_rows = (
        lax.all_gather(keys_low, "wide", axis=0, tiled=True),
        lax.all_gather(values_low, "wide", axis=0, tiled=True),
    )
    start_stats = (
        jnp.full((HEADS, tok_rows, 1), MASKED, jnp.float32),
        jnp.zeros((HEADS, tok_rows, 1), jnp.float32),
    )
    top_score, exp_total = blockwise(stats_step, start_stats, kv_rows, 0)
    log_total = top_score + jnp.log(exp_total)

    def value_step(running, key_part, allowed, first_key):
        attn_probs = jnp.exp(scores_of(key_part[0], allowed) - log_total).astype(jnp.bfloat16)
        return running + jnp.einsum(
            "hqk,khd->qhd",
            attn_probs,
            key_part[1].reshape(-1, HEADS, head_dim),
            preferred_element_type=jnp.float32,
        )

    attended = blockwise(
        value_step, jnp.zeros((tok_rows, HEADS, head_dim), jnp.float32), kv_rows, 0
    )
    attn_low = attended.reshape(tok_rows, model_width).astype(jnp.bfloat16)
    attn_proj = jnp.dot(attn_low, w_out, preferred_element_type=jnp.float32)
    x_one = x_zero + gate_one * attn_proj
    h_two_low = pre_norm(x_one, scale_two, shift_two).astype(jnp.bfloat16)
    hidden_pre = jnp.dot(h_two_low, w_up, preferred_element_type=jnp.float32)
    act_low = jax.nn.gelu(hidden_pre, approximate=True).astype(jnp.bfloat16)
    mlp_out = jnp.dot(act_low, w_down, preferred_element_type=jnp.float32)
    x_two = x_one + gate_two * mlp_out
    block_out = (x_two * live_rows).astype(jnp.bfloat16)
    logits = against(block_out, code_book)
    code_mass = jnp.sum(jax.nn.softmax(logits, axis=-1) * live_rows, axis=0)
    g_two = cotangent.astype(jnp.float32) * live_rows
    d_mlp = (gate_two * g_two).astype(jnp.bfloat16)
    d_gate_two = g_two * mlp_out
    dw_down = contract_rows(act_low, d_mlp)
    d_act = against(d_mlp, w_down)
    _, gelu_back = jax.vjp(lambda inputs: jax.nn.gelu(inputs, approximate=True), hidden_pre)
    d_hidden = gelu_back(d_act)[0].astype(jnp.bfloat16)
    dw_up = contract_rows(h_two_low, d_hidden)
    d_h_two = against(d_hidden, w_up)
    _, norm_back_two = jax.vjp(pre_norm, x_one, scale_two, shift_two)
    d_x_one, d_scale_two, d_shift_two = norm_back_two(d_h_two)
    d_x_one = d_x_one + g_two
    d_attn = (gate_one * d_x_one).astype(jnp.bfloat16)
    d_gate_one = d_x_one * attn_proj
    dw_out = contract_rows(attn_low, d_attn)
    grad_flat = against(d_attn, w_out).astype(jnp.bfloat16)
    grad_heads = grad_flat.reshape(tok_rows, HEADS, head_dim)

    def delta_step(running, key_part, allowed, first_key):
        attn_probs = jnp.exp(scores_of(key_part[0], allowed) - log_total)
        d_probs = jnp.einsum(
            "qhd,khd->hqk",
            grad_heads,
            key_part[1].reshape(-1, HEADS, head_dim),
            preferred_element_type=jnp.float32,
        )
        return running + jnp.sum(attn_probs * d_probs, axis=-1, keepdims=True)

    row_delta = blockwise(delta_step, jnp.zeros((HEADS, tok_rows, 1), jnp.float32), kv_rows, 0)

    def grad_step(running, key_part, allowed, first_key):
        d_query, d_keys, d_values = running
        key_heads = key_part[0].reshape(-1, HEADS, head_dim)
        value_heads = key_part[1].reshape(-1, HEADS, head_dim)
        block_rows = key_part[0].shape[0]
        attn_probs = jnp.exp(scores_of(key_part[0], allowed) - log_total)
        d_probs = jnp.einsum(
            "qhd,khd->hqk", grad_heads, value_heads, preferred_element_type=jnp.float32
        )
        d_scores = (attn_probs * (d_probs - row_delta)).astype(jnp.bfloat16)
        d_query = d_query + jnp.einsum(
            "hqk,khd->qhd", d_scores, key_heads, preferred_element_type=jnp.float32
        )
        key_grad = jnp.einsum(
            "hqk,qhd->khd", d_scores, query_heads, preferred_element_type=jnp.float32
        )
        value_grad = jnp.einsum(
            "hqk,qhd->khd",
            attn_probs.astype(jnp.bfloat16),
            grad_heads,
            preferred_element_type=jnp.float32,
        )
        key_sum = lax.dynamic_slice_in_dim(d_keys, first_key, block_rows, 0) + key_grad.reshape(
            block_rows, model_width
        )
        value_sum = lax.dynamic_slice_in_dim(
            d_values, first_key, block_rows, 0
        ) + value_grad.reshape(block_rows, model_width)
        d_keys = lax.dynamic_update_slice_in_dim(d_keys, key_sum, first_key, 0)
        d_values = lax.dynamic_update_slice_in_dim(d_values, value_sum, first_key, 0)
        return (d_query, d_keys, d_values)

    grad_init = (
        jnp.zeros((tok_rows, HEADS, head_dim), jnp.float32),
        jnp.zeros((group_len, model_width), jnp.float32),
        jnp.zeros((group_len, model_width), jnp.float32),
    )
    d_query, d_keys, d_values = blockwise(grad_step, grad_init, kv_rows, 0)
    d_keys_own, d_values_own = (
        lax.psum_scatter(
            d_keys.astype(jnp.bfloat16), "wide", scatter_dimension=0, tiled=True
        ).astype(jnp.float32),
        lax.psum_scatter(
            d_values.astype(jnp.bfloat16), "wide", scatter_dimension=0, tiled=True
        ).astype(jnp.float32),
    )
    d_projected, d_gain = heads_back(
        (d_query.reshape(tok_rows, model_width), d_keys_own, d_values_own)
    )
    d_projected_low = d_projected.astype(jnp.bfloat16)
    dw_qkv = contract_rows(h_one_low, d_projected_low)
    d_h_one = against(d_projected_low, w_qkv)
    _, norm_back_one = jax.vjp(pre_norm, x_zero, scale_one, shift_one)
    d_x_zero, d_scale_one, d_shift_one = norm_back_one(d_h_one)
    d_x_zero = d_x_zero + d_x_one
    d_token_ada = jnp.concatenate(
        [d_gate_one, d_gate_two, d_scale_one, d_scale_two, d_shift_one, d_shift_two], axis=1
    )
    d_ada_all = contract_rows(one_hot, d_token_ada, HIGHEST_PRECISION)
    d_smooth = lax.dot_general(
        embed_w, d_x_zero, (((1,), (1,)), ((), ())), precision=HIGHEST_PRECISION
    )
    d_embed = lax.dot_general(
        smooth, d_x_zero, (((1,), (0,)), ((), ())), precision=HIGHEST_PRECISION
    )
    d_vectors = jnp.concatenate(
        [
            jnp.sum(d_ada_all, axis=0).reshape(6, model_width),
            jnp.sum(d_x_zero, axis=0)[None],
            d_gain[None],
        ],
        axis=0,
    )
    grad_share = d_smooth / (2.0 + left_ok + right_ok)
    rim_share = padded(grad_share, (("wide", 1),), 1)
    map_grad = 2.0 * grad_share + left_ok * rim_share[:, :-2] + right_ok * rim_share[:, 2:]
    d_embed_all, d_vectors_all, mass_all = lax.psum((d_embed, d_vectors, code_mass), ("dp", "wide"))
    histogram = mass_all * (code_book.shape[0] / tokens_all)
    ada_term = contract_rows(silu_cond.astype(jnp.float32), d_ada_all, HIGHEST_PRECISION)
    split_cols = (
        lax.psum_scatter(
            dw_qkv.astype(jnp.bfloat16), "wide", scatter_dimension=1, tiled=True
        ).astype(jnp.float32),
        lax.psum_scatter(
            dw_out.astype(jnp.bfloat16), "wide", scatter_dimension=1, tiled=True
        ).astype(jnp.float32),
        lax.psum_scatter(
            dw_up.astype(jnp.bfloat16), "wide", scatter_dimension=1, tiled=True
        ).astype(jnp.float32),
        lax.psum_scatter(
            dw_down.astype(jnp.bfloat16), "wide", scatter_dimension=1, tiled=True
        ).astype(jnp.float32),
        lax.psum_scatter(
            ada_term.astype(jnp.bfloat16), "wide", scatter_dimension=1, tiled=True
        ).astype(jnp.float32),
    )
    ada_cols = split_cols[4]
    owned_grads = (
        lax.psum_scatter(
            split_cols[0].astype(jnp.bfloat16), "dp", scatter_dimension=0, tiled=True
        ).astype(jnp.float32),
        lax.psum_scatter(
            split_cols[1].astype(jnp.bfloat16), "dp", scatter_dimension=0, tiled=True
        ).astype(jnp.float32),
        lax.psum_scatter(
            split_cols[2].astype(jnp.bfloat16), "dp", scatter_dimension=0, tiled=True
        ).astype(jnp.float32),
        lax.psum_scatter(
            split_cols[3].astype(jnp.bfloat16), "dp", scatter_dimension=0, tiled=True
        ).astype(jnp.float32),
        lax.psum_scatter(
            ada_cols.astype(jnp.bfloat16), "dp", scatter_dimension=0, tiled=True
        ).astype(jnp.float32),
    )
    root_tokens = math.sqrt(tokens_all)
    spreads = (
        model_width ** (-0.5),
        (model_width // 16) ** (-0.5),
        model_width ** (-0.5),
        w_up.shape[1] ** (-0.5),
        model_width ** (-0.5),
    )
    new_states = tuple(
        (
            nesterov(
                stacked, gradient, BASE_RATE * spread_w / (factor_g * root_tokens), WEIGHT_DECAY
            )
            for stacked, gradient, spread_w, factor_g in zip(
                states, owned_grads, spreads, GRAD_FACTORS
            )
        )
    )
    embed_new = nesterov(
        embed_state,
        d_embed_all,
        BASE_RATE * embed_w.shape[0] ** (-0.5) / (EMBED_FACTOR * root_tokens),
        0.0,
    )
    vector_new = nesterov(vector_state, d_vectors_all, VECTOR_RATE / root_tokens, 0.0)
    return (
        block_out,
        map_grad,
        histogram,
        new_states[0],
        new_states[0][1].astype(jnp.bfloat16),
        new_states[1],
        new_states[1][1].astype(jnp.bfloat16),
        new_states[2],
        new_states[2][1].astype(jnp.bfloat16),
        new_states[3],
        new_states[3][1].astype(jnp.bfloat16),
        new_states[4],
        new_states[4][1].astype(jnp.bfloat16),
        embed_new,
        vector_new,
        d_vectors_all[7],
    )


MESH_ID = pl.DeviceIdType.MESH
ANY = pl.BlockSpec(memory_space=pl.ANY)
VM = pl.BlockSpec(memory_space=pltpu.VMEM)
VMEM_BYTES = 56 * 1024 * 1024
SHORT_TOTAL = sum(side * side for side in SHORT_SIDES)
LONG_TOTAL = sum(side * side for side in LONG_SIDES)
GELU_SCALE = math.sqrt(2.0 / math.pi)
GELU_CUBE = 0.044715
LANES = 128
HALF_LANES = 64
BIG = 1e30


def nt(left_side, right_side):
    return lax.dot_general(
        left_side, right_side, (((1,), (1,)), ((), ())), preferred_element_type=jnp.float32
    )


def nn(left_side, right_side):
    return lax.dot_general(
        left_side, right_side, (((1,), (0,)), ((), ())), preferred_element_type=jnp.float32
    )


def entry_barrier(peers):
    barrier = pltpu.get_barrier_semaphore()
    for peer in peers:
        pl.semaphore_signal(barrier, inc=1, device_id=peer, device_id_type=MESH_ID)
    pl.semaphore_wait(barrier, len(peers))


def place():
    core, wide = lax.axis_index("dp"), lax.axis_index("wide")
    return core, wide // 4, wide % 4


def at_dev(core, z, yx):
    return (core, z * 4 + yx)


def lane_iota(shape):
    return lax.broadcasted_iota(jnp.int32, shape, len(shape) - 1)


def swap_halves(pair):
    return pltpu.roll(pair, HALF_LANES, 1)


def head_sums(values):
    width = values.shape[1]
    rows = lax.broadcasted_iota(jnp.int32, (width, width), 0) // HALF_LANES
    cols = lax.broadcasted_iota(jnp.int32, (width, width), 1) // HALF_LANES
    ones = (rows == cols).astype(jnp.float32)
    return lax.dot_general(
        values,
        ones,
        (((1,), (0,)), ((), ())),
        precision=HIGHEST_PRECISION,
        preferred_element_type=jnp.float32,
    )


ROWS = 256
CHUNK = 512


def key_limits(group_len, slots):
    short_total = sum(side * side for side in SHORT_SIDES)
    long_total = sum(side * side for side in LONG_SIDES)
    limits = [0] * (group_len // ROWS)
    for longs in range(1, slots + 1):
        for shorts in range(slots - longs + 1):
            total = longs * long_total + shorts * short_total
            if not group_len - short_total < total <= group_len:
                continue
            ends, position = [], 0
            for long_side, short_side in zip(LONG_SIDES, SHORT_SIDES):
                position += longs * long_side**2 + shorts * short_side**2
                ends.append(position)
            ends.append(group_len)
            for block in range(len(limits)):
                last = block * ROWS + ROWS - 1
                seen = min(end for end in ends if end > last)
                limits[block] = max(limits[block], -(-seen // LANES) * LANES)
    return limits


def same_limits(limits):
    groups = []
    for block, limit in enumerate(limits):
        if groups and groups[-1][2] == limit:
            groups[-1][1] = block + 1
        else:
            groups.append([block, block + 1, limit])
    return groups


def fold_lanes(values, combine):
    total = values[:, :LANES]
    for j in range(1, values.shape[1] // LANES):
        total = combine(total, values[:, j * LANES : (j + 1) * LANES])
    return total


def split_three(values):
    high = values.astype(jnp.bfloat16).astype(jnp.float32)
    rest = values - high
    mid = rest.astype(jnp.bfloat16).astype(jnp.float32)
    return high, mid, rest - mid


def lanes_three(lane, first, values, otherwise):
    high, mid, rest = split_three(values)
    return jnp.where(
        lane == first, high, jnp.where(lane == first + 1, mid, jnp.where(lane == first + 2, rest, otherwise))
    )


class Gather:
    KINDS = ("up", "down", "x", "y", "turn")

    def __init__(self, shards, fulls, sems, pieces):
        self.shards, self.fulls, self.pieces = shards, fulls, pieces
        self.send, self.recv, self.send_s, self.recv_s, self.local = sems
        self.core, self.z, self.yx = place()
        core, z, yx = self.core, self.z, self.yx
        self.up_dev, self.down_dev = at_dev(core, lax.min(z + 1, 3), yx), at_dev(core, lax.max(z - 1, 0), yx)
        self.x_dev, self.y_dev = at_dev(core, z, yx ^ 1), at_dev(core, z, yx ^ 2)
        self.sib = at_dev(1 - core, z, yx)
        self.ends = []

    @staticmethod
    def scratch(count):
        dma = pltpu.SemaphoreType.DMA
        return [dma((count, 5, 4)), dma((count, 4, 4)), dma((count, 4, 4)), dma((count, 4, 4)), dma((count,))]

    def spot(self, p, z_at, d, core=None):
        i, first, rows = self.pieces[p]
        core = self.core if core is None else core
        size = self.shards[i].shape[0]
        start = pl.multiple_of((z_at * 4 + (self.yx ^ d)) * size + first, 16)
        return self.fulls[i].at[core, pl.ds(start, rows)]

    def copy(self, p, kind, z_at, d, src=None):
        there = {0: 0, 1: 0, 2: 1, 3: 2, 4: 3}[kind]
        ref = self.spot(p, z_at, d)
        device = (self.up_dev, self.down_dev, self.x_dev, self.y_dev)[kind] if kind < 4 else (self.y_dev if d == 1 else self.x_dev)
        return pltpu.make_async_remote_copy(
            src_ref=ref if src is None else src,
            dst_ref=ref,
            send_sem=self.send.at[p, kind, z_at],
            recv_sem=self.recv.at[p, there, z_at],
            device_id=device,
            device_id_type=MESH_ID,
        )

    def go(self, condition, p, kind, z_at, d, src=None):
        def start():
            self.copy(p, kind, z_at, d, src).start()

        def end():
            self.copy(p, kind, z_at, d, src).wait_send()

        if condition is None:
            start()
            self.ends.append(end)
        else:
            pl.when(condition)(start)
            self.ends.append(lambda: pl.when(condition)(end))

    def across(self, p, d):
        for z_at in range(4):
            ref = self.spot(p, z_at, d)
            copy = pltpu.make_async_remote_copy(
                src_ref=ref,
                dst_ref=ref,
                send_sem=self.send_s.at[p, d, z_at],
                recv_sem=self.recv_s.at[p, d, z_at],
                device_id=self.sib,
                device_id_type=MESH_ID,
            )
            copy.start()
            self.ends.append(copy.wait_send)

    def arrive(self, p, kind, z_at, d):
        ref = self.spot(p, z_at, d)
        pltpu.make_async_copy(ref, ref, self.recv.at[p, kind, z_at]).wait()

    def own(self, p):
        i, first, rows = self.pieces[p]
        src = self.shards[i].at[pl.ds(first, rows)]
        z = self.z
        self.go(z < 3, p, 0, z, 0, src)
        self.go(z > 0, p, 1, z, 0, src)
        self.go(None, p, 2, z, 0, src)
        self.go(None, p, 3, z, 0, src)
        copy = pltpu.make_async_copy(src, self.spot(p, z, 0), self.local.at[p])
        copy.start()
        self.locals_ = getattr(self, "locals_", {})
        self.locals_[p] = copy

    def z_step(self, p, r):
        z = self.z
        for side in (-1, 1):
            there = (z - r >= 0) if side < 0 else (z + r <= 3)
            z_at = z + side * r

            def landed(z_at=z_at):
                self.arrive(p, 0, z_at, 0)

            pl.when(there)(landed)
            if side < 0:
                self.go(there & (z < 3), p, 0, z_at, 0)
            else:
                self.go(there & (z > 0), p, 1, z_at, 0)
            self.go(there, p, 2, z_at, 0)
            self.go(there, p, 3, z_at, 0)

    def plane_step(self, p, r):
        z = self.z
        for side in (-1, 1) if r else (0,):
            z_at = z + side * r
            there = None if not r else ((z - r >= 0) if side < 0 else (z + r <= 3))

            def landed(z_at=z_at):
                self.arrive(p, 1, z_at, 1)
                self.arrive(p, 2, z_at, 2)

            if there is None:
                landed()
            else:
                pl.when(there)(landed)
            low_z, high_z = z_at < 2, z_at >= 2
            self.go(low_z if there is None else there & low_z, p, 4, z_at, 1)
            self.go(high_z if there is None else there & high_z, p, 4, z_at, 2)

    def stage(self, p, s):
        if s == 0:
            self.own(p)
        elif s == 1:
            self.z_step(p, 1)
            self.plane_step(p, 0)
        elif s == 2:
            self.z_step(p, 2)
            self.plane_step(p, 1)
        elif s == 3:
            self.z_step(p, 3)
            self.locals_[p].wait()
            self.across(p, 0)
            self.plane_step(p, 2)
        elif s == 4:
            self.plane_step(p, 3)
            self.across(p, 1)
            self.across(p, 2)
        elif s == 5:
            for z_at in range(4):
                self.arrive(p, 3, z_at, 3)
            self.across(p, 3)

    STAGES = 6

    def steps(self):
        return len(self.pieces) + self.STAGES - 1

    def run(self, t):
        for s in range(self.STAGES):
            if 0 <= t - s < len(self.pieces):
                self.stage(t - s, s)

    def landed(self, which=None):
        for p in range(len(self.pieces)) if which is None else which:
            for d in range(4):
                for z_at in range(4):
                    ref = self.spot(p, z_at, d, 1 - self.core)
                    pltpu.make_async_copy(ref, ref, self.recv_s.at[p, d, z_at]).wait()

    def finish(self):
        for end in self.ends:
            end()


def pieces_of(shards, splits):
    pieces = []
    for i, (shard, split) in enumerate(zip(shards, splits)):
        rows = shard.shape[0] // split
        pieces += [(i, j * rows, rows) for j in range(split)]
    return pieces


class Exchange:
    def __init__(self, out, landed, sems):
        self.out, self.landed = out, landed
        self.send, self.recv = sems
        self.core, z, yx = place()
        self.wide = z * 4 + yx

    def copy(self, w):
        return pltpu.make_async_remote_copy(
            src_ref=self.out.at[w],
            dst_ref=self.landed.at[self.wide],
            send_sem=self.send.at[w],
            recv_sem=self.recv.at[self.wide],
            device_id=(self.core, w),
            device_id_type=MESH_ID,
        )

    def push(self, w):
        pl.when(w != self.wide)(lambda: self.copy(w).start())

        def keep():
            self.landed[w] = self.out[w]

        pl.when(w == self.wide)(keep)

    def wait(self, w):
        def landed():
            ref = self.landed.at[w]
            pltpu.make_async_copy(ref, ref, self.recv.at[w]).wait()

        pl.when(w != self.wide)(landed)

    def finish(self):
        for w in range(16):
            pl.when(w != self.wide)(lambda w=w: self.copy(w).wait_send())


def column_of(row):
    return jnp.broadcast_to(row, (LANES, row.shape[1])).T[:, 0:1]


def exact(left_side, right_side, contract=(1, 0)):
    return lax.dot_general(
        left_side,
        right_side,
        (((contract[0],), (contract[1],)), ((), ())),
        precision=HIGHEST_PRECISION,
        preferred_element_type=jnp.float32,
    )


def gelu(values):
    return 0.5 * values * (1.0 + jnp.tanh(GELU_SCALE * (values + GELU_CUBE * values * values * values)))


def gradient(grads, inputs, out, rows, shard):
    count = rows // shard

    def body(c, carry):
        cols = pl.ds(pl.multiple_of(c * rows, LANES), rows)
        total = nn(grads[0, :, cols].astype(jnp.float32).T.astype(jnp.bfloat16), inputs[0])
        total = total + nn(grads[1, :, cols].astype(jnp.float32).T.astype(jnp.bfloat16), inputs[1])
        first = lax.rem(c * count, 4)
        out[c * count // 4, pl.ds(first, count)] = total.astype(jnp.bfloat16).reshape(count, shard, -1)
        return carry

    return body


def front_kernel(groups, slots, *refs):
    (s_qkv, s_out, s_up, s_down, cond_ref, ada_any, map_ref, embed_ref, vec3_ref, len_ref, squares_ref, tri_ref, pick_ref, rule_ref, cot_ref) = refs[:15]
    (f_qkv, f_out, f_up, f_down, ada_ref, h_ref, kept_ref, out32_ref, q_ref, k_ref, kt_ref, vt_ref, low_ref) = refs[15:28]
    (x_ref, smooth_ref, flags_ref, hot_ref, silu_ref, proj_ref, one_ref, two_ref, pre_ref, act_ref, p_down) = refs[28:39]
    (w_ref, send_ref, got_ref, back_send, back_got, v_ref, s_ref, load_sem) = refs[39:47]
    (w_ada, silu_own, theirs, ours, ada_in, edge, edge_left, edge_right, wo_ref, wu_ref, dmlp, act_half) = refs[47:59]
    sems = refs[59:]
    first_flow = Gather([s_qkv], [f_qkv], sems[:5], pieces_of([s_qkv], (2,)))
    flow = Gather([s_out, s_up, s_down], [f_out, f_up, f_down], sems[5:10], pieces_of([s_out, s_up, s_down], (1, 2, 2)))
    ada_send, ada_recv = sems[10:12]
    there = Exchange(send_ref, got_ref, sems[12:14])
    home = Exchange(back_send, back_got, sems[14:16])
    ada_sem, sib_s, sib_r, edge_s, edge_r, wo_sem, wu_sem = sems[16:23]
    core, z, yx = place()
    wide = z * 4 + yx
    sib = (1 - core, wide)
    tokens, width = x_ref.shape
    half = width // 2
    mid = tokens // 2
    two = 2 * tokens
    group_len = q_ref.shape[0]
    f32, low = jnp.float32, jnp.bfloat16
    vec_ref = vec3_ref.at[1]
    entry_barrier([(core, wide ^ r) for r in range(1, 16)] + [sib])

    def to_sib(slot, src, dst):
        copy = pltpu.make_async_remote_copy(
            src_ref=src, dst_ref=dst, send_sem=sib_s.at[slot], recv_sem=sib_r.at[slot], device_id=sib, device_id_type=MESH_ID
        )
        copy.start()
        return copy

    first_flow.run(0)
    ada_copy = pltpu.make_async_copy(ada_any.at[1], w_ada, ada_sem)
    ada_copy.start()
    cond = cond_ref[...]
    silu = (cond / (1.0 + jnp.exp(-cond))).astype(low).astype(f32)
    silu_own[...] = jnp.zeros_like(silu_own)
    silu_own[0:slots, :] = silu
    their_half = pl.ds(pl.multiple_of((1 - core) * half, half), half)
    my_half = pl.ds(pl.multiple_of(core * half, half), half)
    silu_copy = to_sib(0, silu_own.at[:, their_half], silu_ref.at[core])
    silu_ref[core] = silu_own[:, my_half]
    spot = lane_iota((32, LANES))
    cells = map_ref[...]
    edge[...] = jnp.where(spot == 0, cells[:, 0:1], jnp.where(spot == 1, cells[:, tokens - 1 : tokens], 0.0))

    def edge_copy(slot, dst, shift):
        return pltpu.make_async_remote_copy(
            src_ref=edge,
            dst_ref=dst,
            send_sem=edge_s.at[slot],
            recv_sem=edge_r.at[slot],
            device_id=(core, lax.rem(wide + shift, 16)),
            device_id_type=MESH_ID,
        )

    edges = [edge_copy(0, edge_left, 1), edge_copy(1, edge_right, 15)]
    for copy in edges:
        copy.start()
    first_flow.run(1)

    run_lane = lane_iota((1, LANES))
    run_slot = lax.rem(run_lane - HALF_LANES + slots * LANES, slots)
    lens = jnp.zeros((1, LANES), jnp.int32)
    for j in range(slots):
        lens = jnp.where(run_slot == j, len_ref[0:1, j : j + 1], lens)
    counts = jnp.where(lens == LONG_TOTAL, squares_ref[0:1, :], jnp.where(lens == SHORT_TOTAL, squares_ref[1:2, :], 0.0))
    unused = group_len - jnp.sum(counts, axis=1, keepdims=True)
    counts = jnp.where(run_lane == HALF_LANES + slots * LEVELS, unused, counts)
    ends = exact(jnp.broadcast_to(counts, (8, LANES)), tri_ref[...])[0:1, :]
    starts = ends - counts
    start_col, end_col = column_of(starts), column_of(ends)
    here = (wide * tokens + lane_iota((1, tokens))).astype(f32)
    left = 1.0 - jnp.sum(((here == start_col) & (here < end_col)).astype(f32), axis=0, keepdims=True)
    right = 1.0 - jnp.sum(((here == end_col - 1.0) & (here >= start_col)).astype(f32), axis=0, keepdims=True)
    flags_ref[...] = jnp.zeros_like(flags_ref)
    flags_ref[0:1, :] = left
    flags_ref[1:2, :] = right
    row_at = (wide * tokens + lax.broadcasted_iota(jnp.int32, (tokens, LANES), 0)).astype(f32)
    my_runs = ((row_at >= starts) & (row_at < ends)).astype(low)
    hot = nn(my_runs, pick_ref[...])[:, 0:8]
    hot_ref[...] = hot

    ada_copy.wait()
    w_low = w_ada[...].astype(low)
    silu_copy.wait_recv()
    theirs[...] = nn(silu_ref[1 - core].astype(low), w_low)
    part_copy = to_sib(1, theirs, ours)
    mine = nn(silu_ref[core].astype(low), w_low)
    first_flow.run(2)

    for copy in edges:
        copy.wait_recv()
    column = lane_iota((32, tokens))
    before = jnp.where(column == 0, edge_left[:, 1:2], jnp.roll(cells, 1, axis=1))
    after = jnp.where(column == tokens - 1, edge_right[:, 0:1], jnp.roll(cells, -1, axis=1))
    smooth = smooth_map(cells, left, right, before, after)
    smooth_ref[...] = smooth
    x = exact(smooth, embed_ref[1], (0, 0)) + vec_ref[6:7, :]
    x_ref[...] = x
    part_copy.wait_recv()
    ada_in[...] = mine + ours[...]
    ada_copies = []
    for r in range(1, 16):
        copy = pltpu.make_async_remote_copy(
            src_ref=ada_in,
            dst_ref=ada_ref.at[wide],
            send_sem=ada_send.at[r],
            recv_sem=ada_recv.at[r],
            device_id=(core, wide ^ r),
            device_id_type=MESH_ID,
        )
        copy.start()
        ada_copies.append(copy)
    ada_ref[wide] = ada_in[...]

    def standard(values):
        centred = values - jnp.mean(values, axis=1, keepdims=True)
        return centred * lax.rsqrt(jnp.mean(centred * centred, axis=1, keepdims=True) + NORM_EPS)

    unit = standard(x)
    first_flow.run(3)
    for copy in ada_copies:
        copy.wait_recv()
    ada = jnp.concatenate([ada_ref[w] for w in range(16)], axis=1)

    def of_tokens(block):
        return exact(hot, ada[:, block * width : (block + 1) * width] + vec_ref[block : block + 1, :])

    h_ref[...] = (unit * (1.0 + of_tokens(2)) + of_tokens(4)).astype(low)
    for t in range(4, first_flow.steps()):
        first_flow.run(t)
    next_tick = [0]

    def tick(n):
        for _ in range(n):
            if next_tick[0] < flow.steps():
                flow.run(next_tick[0])
                next_tick[0] += 1

    tick(1)
    first_flow.landed()

    group = 256
    loads = []

    def load(j):
        g = lax.rem(z + 1 + j, 4)
        out = []
        for c in range(2):
            for part in range(3):
                rows = pl.ds(pl.multiple_of(g * group + part * width, group), group)
                out.append(pltpu.make_async_copy(f_qkv.at[c, rows], w_ref.at[j, c, part], load_sem.at[j, c, part]))
        return out

    for j in range(4):
        loads.append(load(j))
        for copy in loads[-1]:
            copy.start()
    lane = lane_iota((tokens, LANES))
    lane_mid = lane_iota((mid, LANES))
    for j in range(4):
        g = lax.rem(z + 1 + j, 4)
        first = pl.multiple_of(g * group, group)
        for copy in loads[j]:
            copy.wait()

        def project(part):
            return nt(h_ref[:, :half], w_ref[j, 0, part]) + nt(h_ref[:, half:], w_ref[j, 1, part])

        q_all, k_all, v_all = (project(part) for part in range(3))
        for pair in range(group // LANES):
            cols = slice(pair * LANES, (pair + 1) * LANES)
            at = g * (group // LANES) + pair
            kept_ref[at] = q_all[:, cols]
            kept_ref[at + width // LANES] = k_all[:, cols]
        q_all = q_all * lax.rsqrt(head_sums(q_all * q_all) + NORM_EPS)
        q_all = q_all * (8.0 * (1.0 + vec_ref[7:8, pl.ds(first, group)]))
        k_all = k_all * lax.rsqrt(head_sums(k_all * k_all) + NORM_EPS)
        for pair in range(group // LANES):
            cols = slice(pair * LANES, (pair + 1) * LANES)
            q, k, v = q_all[:, cols], k_all[:, cols], v_all[:, cols]
            head = g * (group // HALF_LANES) + 2 * pair
            send_ref[head, 0:tokens, :] = jnp.where(lane < HALF_LANES, q, swap_halves(k)).astype(low)
            send_ref[head + 1, 0:tokens, :] = jnp.where(lane < HALF_LANES, swap_halves(q), k).astype(low)
            v_a, v_b = v[:mid], v[mid:]
            send_ref[head, tokens:, :] = jnp.where(lane_mid < HALF_LANES, v_a, swap_halves(v_b)).astype(low)
            send_ref[head + 1, tokens:, :] = jnp.where(lane_mid < HALF_LANES, swap_halves(v_a), v_b).astype(low)
        for e in range(4):
            there.push(g * 4 + e)
        tick((0, 1, 0, 0)[j])

    lane_two = lane_iota((two, LANES))

    def unpack(pair, carry):
        for e in range(2):
            there.wait(2 * pair + e)
        first = pl.multiple_of(pair * two, two)
        qk = jnp.concatenate([got_ref[2 * pair + e, 0:tokens, :].astype(f32) for e in range(2)], axis=0)
        spot = (first + lax.broadcasted_iota(jnp.int32, (two, LANES), 0)).astype(f32)
        runs = ((spot >= starts) & (spot < ends)).astype(f32)
        barred = nn(runs.astype(low), rule_ref[...])
        rows = pl.ds(first, two)
        q_ref[rows, :] = jnp.where(lane_two < HALF_LANES, qk, barred).astype(low)
        tail = jnp.where(lane_two >= LANES - 3, 1.0, runs)
        keys = jnp.where(lane_two < HALF_LANES, swap_halves(qk), tail)
        k_ref[rows, :] = keys.astype(low)
        kt_ref[:, rows] = keys.T.astype(low)
        ones = ((lane_mid >= HALF_LANES) & (lane_mid < HALF_LANES + 3)).astype(f32)
        pieces = []
        for e in range(2):
            v = got_ref[2 * pair + e, tokens:, :].astype(f32)
            pieces.append(jnp.where(lane_mid < HALF_LANES, v, ones))
            pieces.append(jnp.where(lane_mid < HALF_LANES, swap_halves(v), ones))
        values = jnp.concatenate(pieces, axis=0)
        v_ref[rows, :] = values.astype(low)
        vt_ref[:, rows] = values.T.astype(low)
        return carry

    lane_q = lane_iota((ROWS, LANES))

    def query_block(limit, b, carry):
        rows = pl.ds(pl.multiple_of(b * ROWS, ROWS), ROWS)
        q = q_ref[rows, :]

        def score(c, top):
            cols = pl.ds(pl.multiple_of(c * CHUNK, CHUNK), CHUNK)
            s = nn(q, kt_ref[:, cols])
            s_ref[:, cols] = s
            return jnp.maximum(top, fold_lanes(s, jnp.maximum))

        whole, left = limit // CHUNK, limit % CHUNK
        top = lax.fori_loop(0, whole, score, jnp.full((ROWS, LANES), -3e38, f32))
        if left:
            tail = slice(whole * CHUNK, limit)
            s = nn(q, kt_ref[:, tail])
            s_ref[:, tail] = s
            top = jnp.maximum(top, fold_lanes(s, jnp.maximum))
        peak = jnp.max(top, axis=1, keepdims=True)

        def weigh(cols, carry):
            total, acc = carry
            p = jnp.exp(s_ref[:, cols] - peak)
            return total + fold_lanes(p, jnp.add), acc + nn(p.astype(low), v_ref[cols, :])

        zero = jnp.zeros((ROWS, LANES), f32)
        total, acc = lax.fori_loop(
            0,
            whole,
            lambda c, carry: weigh(pl.ds(pl.multiple_of(c * CHUNK, CHUNK), CHUNK), carry),
            (zero, zero),
        )
        if left:
            total, acc = weigh(slice(whole * CHUNK, limit), (total, acc))
        total = jnp.sum(total, axis=1, keepdims=True)
        out32_ref[rows, :] = acc / total
        log_total = peak + jnp.log(total)
        q_ref[rows, :] = lanes_three(lane_q, LANES - 3, -log_total, q.astype(f32)).astype(low)
        return carry

    def give_back(w, carry):
        rows = pl.multiple_of(w * tokens, tokens)
        a = out32_ref[pl.ds(rows, mid), :]
        b = out32_ref[pl.ds(pl.multiple_of(rows + mid, mid), mid), :]
        back_send[w] = jnp.where(lane_mid < HALF_LANES, a, swap_halves(b)).astype(low)
        home.push(w)
        return carry

    for i in range(4):
        lax.fori_loop(2 * i, 2 * i + 2, unpack, 0)
        tick((0, 1, 0, 1)[i])
    plane = 4 * tokens // ROWS
    done = 0
    for p in range(4):
        for first, last, limit in groups:
            begin, end = max(first, p * plane), min(last, (p + 1) * plane)
            if begin < end:
                lax.fori_loop(begin, end, functools.partial(query_block, limit), 0)
                tick((0, 1, 0, 1, 0, 1, 0, 1)[done])
                done += 1
        lax.fori_loop(4 * p, 4 * p + 4, give_back, 0)
    tick(1)
    while next_tick[0] < 8:
        tick(1)
    flow.landed((0,))
    wo_copy = pltpu.make_async_copy(f_out, wo_ref, wo_sem)
    wo_copy.start()
    for pair in range(8):
        home.wait(2 * pair)
        home.wait(2 * pair + 1)
        cols = slice(pair * LANES, (pair + 1) * LANES)
        even, odd = back_got[2 * pair].astype(f32), back_got[2 * pair + 1].astype(f32)
        low_ref[0:mid, cols] = jnp.where(lane_mid < HALF_LANES, even, swap_halves(odd)).astype(low)
        low_ref[mid:, cols] = jnp.where(lane_mid < HALF_LANES, swap_halves(even), odd).astype(low)

    wo_copy.wait()
    proj = nt(low_ref[:, :half], wo_ref[0]) + nt(low_ref[:, half:], wo_ref[1])
    proj_ref[...] = proj
    x_one = x_ref[...] + of_tokens(0) * proj
    one_ref[...] = x_one
    two_ref[...] = (standard(x_one) * (1.0 + of_tokens(3)) + of_tokens(5)).astype(low)
    flow.landed((1, 2))
    step = 512
    hidden = pre_ref.shape[1]

    def load_up(c):
        rows = pl.ds(pl.multiple_of(c * step, step), step)
        slot = lax.rem(c, 2)
        return pltpu.make_async_copy(f_up.at[:, rows], wu_ref.at[slot], wu_sem.at[slot])

    load_up(0).start()

    def up_step(c, carry):
        pl.when(c + 1 < hidden // step)(lambda: load_up(c + 1).start())
        load_up(c).wait()
        w = wu_ref.at[lax.rem(c, 2)]
        pre = nt(two_ref[:, :half], w[0]) + nt(two_ref[:, half:], w[1])
        cols = pl.ds(pl.multiple_of(c * step, step), step)
        pre_ref[:, cols] = pre
        act_ref[:, cols] = gelu(pre).astype(low)
        return carry

    live = jnp.sum(hot, axis=1, keepdims=True)
    dmlp[core] = (of_tokens(1) * (cot_ref[...].astype(f32) * live)).astype(low)
    pair_copies = [to_sib(2, dmlp.at[core], dmlp.at[core])]
    hid_half = hidden // 2
    hid_theirs = pl.ds(pl.multiple_of((1 - core) * hid_half, hid_half), hid_half)
    hid_mine = pl.ds(pl.multiple_of(core * hid_half, hid_half), hid_half)
    for i in range(2):
        lax.fori_loop(4 * i, 4 * i + 4, up_step, 0)
        tick(1)
    pair_copies.append(to_sib(3, act_ref.at[:, hid_theirs], act_half.at[core]))
    act_half[core] = act_ref[:, hid_mine]
    tick(1)
    for copy in pair_copies:
        copy.wait_recv()
    lax.fori_loop(0, width // LANES, gradient(dmlp, act_half, p_down, LANES, width // 16), 0)
    tick(flow.steps())
    flow.landed(range(3, 5))
    first_flow.finish()
    flow.finish()
    there.finish()
    home.finish()
    for copy in ada_copies + edges + pair_copies + [silu_copy, part_copy]:
        copy.wait_send()


def front(shards, condition, ada_state, cells, embed_state, vector_state, lengths, tables, cotangent, groups):
    width = condition.shape[1]
    tokens = cells.shape[1]
    slots = lengths.shape[1]
    group_len = 16 * tokens
    hidden = 16 * shards[2].shape[0]
    f32, low = jnp.float32, jnp.bfloat16
    dma = pltpu.SemaphoreType.DMA
    shape = jax.ShapeDtypeStruct
    ada_width = ada_state.shape[2]
    fulls = [shape((2, 16 * s.shape[0], s.shape[1]), low) for s in shards]
    outs = fulls + [
        shape((16, 8, ada_width), f32),
        shape((tokens, width), low),
        shape((2 * width // LANES, tokens, LANES), f32),
        shape((group_len, LANES), f32),
        shape((group_len, LANES), low),
        shape((group_len, LANES), low),
        shape((LANES, group_len), low),
        shape((LANES, group_len), low),
        shape((tokens, width), low),
        shape((tokens, width), f32),
        shape(cells.shape, f32),
        shape((8, tokens), f32),
        shape((tokens, 8), f32),
        shape((2, 8, width // 2), f32),
        shape((tokens, width), f32),
        shape((tokens, width), f32),
        shape((tokens, width), low),
        shape((tokens, hidden), f32),
        shape((tokens, hidden), low),
        shape((4, 4, width // 16, hidden // 2), low),
    ]
    packed, mid = tokens * 3 // 2, tokens // 2
    scratch = [
        pltpu.VMEM((4, 2, 3, 256, width // 2), low),
        pltpu.VMEM((16, packed, LANES), low),
        pltpu.VMEM((16, packed, LANES), low),
        pltpu.VMEM((16, mid, LANES), low),
        pltpu.VMEM((16, mid, LANES), low),
        pltpu.VMEM((group_len, LANES), low),
        pltpu.VMEM((ROWS, group_len), f32),
        dma((4, 2, 3)),
        pltpu.VMEM(ada_state.shape[1:], f32),
        pltpu.VMEM((8, width), f32),
        pltpu.VMEM((8, ada_width), f32),
        pltpu.VMEM((8, ada_width), f32),
        pltpu.VMEM((8, ada_width), f32),
        pltpu.VMEM((32, LANES), f32),
        pltpu.VMEM((32, LANES), f32),
        pltpu.VMEM((32, LANES), f32),
        pltpu.VMEM((2, width, width // 2), low),
        pltpu.VMEM((2, 2, 512, width // 2), low),
        pltpu.VMEM((2, tokens, width), low),
        pltpu.VMEM((2, tokens, hidden // 2), low),
    ]
    scratch += Gather.scratch(2) + Gather.scratch(5) + [dma((16,)) for _ in range(6)]
    scratch += [dma, dma((4,)), dma((4,)), dma((2,)), dma((2,)), dma, dma((2,))]
    return pl.pallas_call(
        functools.partial(front_kernel, groups, slots),
        out_shape=outs,
        in_specs=[ANY] * 4 + [VM, ANY] + [VM] * 9,
        out_specs=[ANY] * 4 + [VM] * 20,
        scratch_shapes=scratch,
        compiler_params=pltpu.CompilerParams(
            collective_id=0, has_side_effects=True, vmem_limit_bytes=VMEM_BYTES
        ),
    )(*shards, condition, ada_state, cells, embed_state, vector_state, lengths, *tables, cotangent)


class Scatter:
    STAGES = 6

    def __init__(self, parts, outs, bufs, sems, pieces):
        self.parts, self.outs, self.bufs, self.pieces = parts, outs, bufs, pieces
        self.send, self.recv = sems
        self.parts_left = {}
        core, z, yx = place()
        self.z, self.yx = z, yx
        self.x_dev, self.y_dev = at_dev(core, z, yx ^ 1), at_dev(core, z, yx ^ 2)
        self.up_dev, self.down_dev = at_dev(core, lax.min(z + 1, 3), yx), at_dev(core, lax.max(z - 1, 0), yx)
        self.ends = []

    @staticmethod
    def scratch(shapes, count):
        low = jnp.bfloat16
        out = []
        for rows, cols in shapes:
            out += [pltpu.VMEM((depth, rows, cols), low) for depth in (2, 2, 4, 4, 3, 3)]
        dma = pltpu.SemaphoreType.DMA
        return out + [dma((count, 8)), dma((count, 8))]

    def push(self, p, slot, src, dst, device):
        copy = pltpu.make_async_remote_copy(
            src_ref=src,
            dst_ref=dst,
            send_sem=self.send.at[p, slot],
            recv_sem=self.recv.at[p, slot],
            device_id=device,
            device_id_type=MESH_ID,
        )
        copy.start()
        return copy

    def arrive(self, p, slot, ref):
        pltpu.make_async_copy(ref, ref, self.recv.at[p, slot]).wait()

    def stage(self, p, s):
        i, first, rows = self.pieces[p]
        rows = pl.ds(first, rows)
        part = self.parts[i]
        names = ("turn_x", "turn_y", "rx", "ry", "up", "down")
        buf = dict(zip(names, self.bufs[6 * i : 6 * i + 6]))
        z, yx = self.z, self.yx
        f32, low = jnp.float32, jnp.bfloat16
        lo2, hi2 = pl.ds(0, 2), pl.ds(2, 2)

        def view(name, which):
            return buf[name].at[which, rows]

        def wide(ref):
            return ref[...].astype(f32)

        def hop(condition, slot, name, which, device):
            ref = view(name, which)

            def start():
                self.push(p, slot, ref, ref, device)

            def end():
                pltpu.make_async_copy(ref, ref, self.send.at[p, slot]).wait()

            pl.when(condition)(start)
            self.ends.append(lambda: pl.when(condition)(end))

        if s == 0:
            copies = [
                self.push(p, 0, part.at[lo2, yx ^ 3, rows], view("turn_x", lo2), self.x_dev),
                self.push(p, 1, part.at[hi2, yx ^ 3, rows], view("turn_y", lo2), self.y_dev),
                self.push(p, 2, part.at[lo2, yx ^ 1, rows], view("rx", lo2), self.x_dev),
                self.push(p, 3, part.at[hi2, yx ^ 2, rows], view("ry", hi2), self.y_dev),
            ]
            self.parts_left[p] = [copy.wait_send for copy in copies]
        elif s == 1:
            turn = view("turn_x", lo2)
            self.arrive(p, 0, turn)
            turn[...] = (wide(part.at[lo2, yx ^ 2, rows]) + wide(turn)).astype(low)
            self.ends.append(self.push(p, 4, turn, view("ry", lo2), self.y_dev).wait_send)
            turn = view("turn_y", lo2)
            self.arrive(p, 1, turn)
            turn[...] = (wide(part.at[hi2, yx ^ 1, rows]) + wide(turn)).astype(low)
            self.ends.append(self.push(p, 5, turn, view("rx", hi2), self.x_dev).wait_send)
        elif s == 2:
            self.arrive(p, 2, view("rx", lo2))
            self.arrive(p, 3, view("ry", hi2))
            self.arrive(p, 4, view("ry", lo2))
            self.arrive(p, 5, view("rx", hi2))
            self.outs[i][rows] = wide(part.at[z, yx, rows]) + wide(view("rx", z)) + wide(view("ry", z))
            for z_at in range(4):
                total = wide(part.at[z_at, yx, rows]) + wide(view("rx", z_at)) + wide(view("ry", z_at))
                view("rx", z_at)[...] = total.astype(low)

            def first_up():
                view("up", pl.ds(0, 3))[...] = view("rx", pl.ds(1, 3))[...]

            def first_down():
                view("down", pl.ds(0, 3))[...] = view("rx", pl.ds(0, 3))[...]

            pl.when(z == 0)(first_up)
            hop(z == 0, 6, "up", pl.ds(0, 3), self.up_dev)
            pl.when(z == 3)(first_down)
            hop(z == 3, 7, "down", pl.ds(0, 3), self.down_dev)
        elif s in (3, 4):
            at = s - 2
            count = 3 - at

            def add_up():
                self.arrive(p, 6, view("up", pl.ds(at - 1, count + 1)))
                ref = view("up", pl.ds(at, count))
                ref[...] = (wide(ref) + wide(view("rx", pl.ds(at + 1, count)))).astype(low)

            def add_down():
                self.arrive(p, 7, view("down", pl.ds(0, count + 1)))
                ref = view("down", pl.ds(0, count))
                ref[...] = (wide(ref) + wide(view("rx", pl.ds(0, count)))).astype(low)

            pl.when(z == at)(add_up)
            hop(z == at, 6, "up", pl.ds(at, count), self.up_dev)
            pl.when(z == 3 - at)(add_down)
            hop(z == 3 - at, 7, "down", pl.ds(0, count), self.down_dev)
        else:
            out = self.outs[i].at[rows]

            def end_low():
                self.arrive(p, 7, view("down", pl.ds(0, 1)))
                out[...] += wide(view("down", 0))

            def end_high():
                self.arrive(p, 6, view("up", pl.ds(2, 1)))
                out[...] += wide(view("up", 2))

            def end_inner(at):
                out[...] += wide(view("up", at - 1)) + wide(view("down", at))

            pl.when(z == 0)(end_low)
            pl.when(z == 1)(lambda: end_inner(1))
            pl.when(z == 2)(lambda: end_inner(2))
            pl.when(z == 3)(end_high)

    def steps(self):
        return len(self.pieces) + self.STAGES - 1

    def run(self, t):
        for s in reversed(range(self.STAGES)):
            if 0 <= t - s < len(self.pieces):
                self.stage(t - s, s)

    def sent(self, p):
        for end in self.parts_left.pop(p, ()):
            end()

    def finish(self):
        for p in list(self.parts_left):
            self.sent(p)
        for end in self.ends:
            end()


COMMON_ROWS = 48
BACK_SPLITS = ((4, 4, 1), (3,))
BACK_TICKS = ((1, 1, 1, 1), (1, 0), (0, 0, 1, 0), (0, 0, 0, 0, 0, 1, 0, 0, 1, 0, 0, 1), (1, 1, 1), (1, 1))


def standard_of(values):
    centred = values - jnp.mean(values, axis=1, keepdims=True)
    rstd = lax.rsqrt(jnp.mean(centred * centred, axis=1, keepdims=True) + NORM_EPS)
    return centred * rstd, rstd


def standard_back(unit, rstd, d_unit):
    along = jnp.mean(d_unit * unit, axis=1, keepdims=True)
    return rstd * (d_unit - jnp.mean(d_unit, axis=1, keepdims=True) - unit * along)


def gelu_slope(values):
    square = values * values
    inner = jnp.tanh(GELU_SCALE * (values + GELU_CUBE * values * square))
    slope = GELU_SCALE * (1.0 + 3.0 * GELU_CUBE * square)
    return 0.5 * (1.0 + inner) + 0.5 * values * (1.0 - inner * inner) * slope


def back_kernel(groups, splits, *refs):
    (
        cot_ref, hot_ref, ada_in, vec3_ref, x_ref, one_ref, proj_ref, h_any, two_any, low_any, act_any, pre_any,
        w_any, wo_any, wu_any, wd_any, book_any, out32_any, q_ref, k_ref, kt_ref, vt_ref, kept_any,
        smooth_ref, embed_ref, ok_ref, p_down,
    ) = refs[:27]
    (o_down, o_up, o_out, o_qkv, ada_both, common_all, bias_all, map_ref, block_ref) = refs[27:36]
    (
        send_ref, got_ref, back_send, back_got, g_ref, gt_ref, qt_ref, dq_ref, dkt_ref, dvt_ref,
        w_buf, dhid, h_both, dh_ref, ada_ref, com_ref, ada_land, com_land, ada_sum, com_sum, ada_sib, com_sib,
        bias_own, com_own, edge, edge_left, edge_right,
        dmlp, two_half, low_half, dattn, mlp_ref, dx_one, act_buf, pre_buf, d_att, p_up, p_out,
    ) = refs[36:74]
    rest = refs[74:]
    flow_bufs, rest = rest[:18], rest[18:]
    flow_sems, rest = rest[:2], rest[2:]
    last_bufs, rest = rest[:6], rest[6:]
    last_sems, rest = rest[:2], rest[2:]
    (
        ex_s, ex_r, home_s, home_r, w_sem, sib_s, sib_r, small_s, small_r, spread_s, spread_r, edge_s, edge_r,
        hid_s, hid_r, half_sem, kept_sem, free_sem,
    ) = rest
    core, z, yx = place()
    wide = z * 4 + yx
    sib = (1 - core, wide)
    f32, low = jnp.float32, jnp.bfloat16
    tokens, width = x_ref.shape
    half = width // 2
    hidden = dhid.shape[2]
    mid = tokens // 2
    two = 2 * tokens
    step = 512
    vec_ref = vec3_ref.at[1]
    dproj = dhid.at[:, :, pl.ds(0, 3 * width)]
    p_qkv = p_up.at[:, :, pl.ds(0, tokens)]
    flow = Scatter([p_down, p_up, p_out], [o_down, o_up, o_out], flow_bufs, flow_sems, splits[0])
    last = Scatter([p_qkv], [o_qkv], last_bufs, last_sems, splits[1])
    there = Exchange(back_send, back_got, (ex_s, ex_r))
    home = Exchange(send_ref, got_ref, (home_s, home_r))
    entry_barrier([(core, wide ^ r) for r in range(1, 16)] + [sib])

    def to_sib(slot, src, dst):
        copy = pltpu.make_async_remote_copy(
            src_ref=src, dst_ref=dst, send_sem=sib_s.at[slot], recv_sem=sib_r.at[slot], device_id=sib, device_id_type=MESH_ID
        )
        copy.start()
        return copy

    next_tick = [0]

    def tick(n):
        for _ in range(n):
            if next_tick[0] < flow.steps():
                flow.run(next_tick[0])
                next_tick[0] += 1

    lane = lane_iota((two, LANES))
    lane_tok = lane_iota((tokens, LANES))
    lane_mid = lane_iota((mid, LANES))

    def load_chunk(c):
        slot = lax.rem(c, 2)
        cols = pl.ds(pl.multiple_of(c * step, step), step)
        down_cols = pl.ds(pl.multiple_of(lax.rem(c, hidden // 2 // step) * step, step), step)
        down = wd_any.at[c // (hidden // 2 // step)]
        pairs = [
            (down.at[pl.ds(0, half), down_cols], w_buf.at[slot, 0]),
            (down.at[pl.ds(half, half), down_cols], w_buf.at[slot, 1]),
            (wu_any.at[0, cols], w_buf.at[slot, 2]),
            (wu_any.at[1, cols], w_buf.at[slot, 3]),
            (act_any.at[:, cols], act_buf.at[slot]),
            (pre_any.at[:, cols], pre_buf.at[slot]),
        ]
        return [pltpu.make_async_copy(src, dst, w_sem.at[slot, i]) for i, (src, dst) in enumerate(pairs)]

    def start_chunk(c):
        for copy in load_chunk(c):
            copy.start()

    start_chunk(0)
    out32_copy = pltpu.make_async_copy(out32_any, dq_ref, kept_sem)
    out32_copy.start()
    theirs = pl.ds(pl.multiple_of((1 - core) * half, half), half)
    mine = pl.ds(pl.multiple_of(core * half, half), half)
    ada = jnp.concatenate([ada_in[w] for w in range(16)], axis=1)
    hot = hot_ref[...]

    def of_tokens(block):
        return exact(hot, ada[:, block * width : (block + 1) * width] + vec_ref[block : block + 1, :])

    live = jnp.sum(hot, axis=1, keepdims=True)
    gate_two = of_tokens(1)
    dmlp[...] = (gate_two * (cot_ref[...].astype(f32) * live)).astype(low)
    sib_copies = [
        to_sib(2, two_any.at[:, theirs], two_half.at[core]),
        to_sib(3, low_any.at[:, theirs], low_half.at[core]),
        to_sib(4, h_any.at[:, theirs], h_both.at[core]),
    ]
    half_copies = [
        pltpu.make_async_copy(src, dst.at[core], half_sem.at[i])
        for i, (src, dst) in enumerate(
            [
                (two_any.at[:, mine], two_half),
                (low_any.at[:, mine], low_half),
                (h_any.at[:, mine], h_both),
            ]
        )
    ]
    for copy in half_copies:
        copy.start()
    mlp_ref[...] = jnp.zeros_like(mlp_ref)
    dh_ref[...] = jnp.zeros_like(dh_ref)

    def hid_copy(c):
        cols = pl.ds(pl.multiple_of(c * step, step), step)
        return pltpu.make_async_remote_copy(
            src_ref=dhid.at[core, :, cols],
            dst_ref=dhid.at[core, :, cols],
            send_sem=hid_s.at[c],
            recv_sem=hid_r.at[c],
            device_id=sib,
            device_id_type=MESH_ID,
        )

    def hidden_step(c, carry):
        pl.when(c + 1 < hidden // step)(lambda: start_chunk(c + 1))
        for copy in load_chunk(c):
            copy.wait()
        slot = lax.rem(c, 2)
        w = w_buf.at[slot]
        d_act = nn(dmlp[:, :half], w[0]) + nn(dmlp[:, half:], w[1])
        d_hid = (d_act * gelu_slope(pre_buf[slot])).astype(low)
        dhid[core, :, pl.ds(pl.multiple_of(c * step, step), step)] = d_hid
        hid_copy(c).start()
        act = act_buf[slot]
        mlp_ref[:, :half] += nt(act, w[0])
        mlp_ref[:, half:] += nt(act, w[1])
        dh_ref[:, :half] += nn(d_hid, w[2])
        dh_ref[:, half:] += nn(d_hid, w[3])
        return carry

    chunks = hidden // step
    for i in range(4):
        tick(BACK_TICKS[0][i])
        lax.fori_loop(2 * i, 2 * i + 2, hidden_step, 0)

    wo_copies = [
        pltpu.make_async_copy(wo_any.at[c, pl.ds(r * half, half)], w_buf.at[0, 2 * c + r], w_sem.at[0, 2 * c + r])
        for c in range(2)
        for r in range(2)
    ]
    for copy in wo_copies:
        copy.start()
    unit, rstd = standard_of(one_ref[...])
    g_two = cot_ref[...].astype(f32) * live
    d_one = standard_back(unit, rstd, dh_ref[...] * (1.0 + of_tokens(3))) + g_two
    dx_one[...] = d_one
    dattn[core] = (of_tokens(0) * d_one).astype(low)
    sib_copies.append(to_sib(5, dattn.at[core], dattn.at[core]))
    for copy in wo_copies:
        copy.wait()
    for c in range(2):
        part = nn(dattn[core, :, :half], w_buf[0, 2 * c]) + nn(dattn[core, :, half:], w_buf[0, 2 * c + 1])
        d_att[:, c * half : (c + 1) * half] = part.astype(low)

    def pack(pair, carry):
        cols = pl.ds(pl.multiple_of(pair * LANES, LANES), LANES)
        a, b = d_att[0:mid, cols].astype(f32), d_att[mid:, cols].astype(f32)
        back_send[2 * pair] = jnp.where(lane_mid < HALF_LANES, a, swap_halves(b)).astype(low)
        back_send[2 * pair + 1] = jnp.where(lane_mid < HALF_LANES, swap_halves(a), b).astype(low)
        there.push(2 * pair)
        there.push(2 * pair + 1)
        return carry

    lax.fori_loop(0, 8, pack, 0)

    def per_slot(values):
        return exact(hot, values, (0, 0))

    ada_ref[:, 3 * width : 4 * width] = per_slot(dh_ref[...] * unit)
    ada_ref[:, 5 * width : 6 * width] = per_slot(dh_ref[...])
    ada_ref[:, 0:width] = per_slot(d_one * proj_ref[...])
    ada_ref[:, width : 2 * width] = per_slot(g_two * mlp_ref[...])
    block_ref[...] = (live * (one_ref[...] + gate_two * mlp_ref[...])).astype(low)
    for c in range(chunks):
        hid_copy(c).wait_recv()
    half_copies[0].wait()
    sib_copies[0].wait_recv()
    lax.fori_loop(0, hidden // 256, gradient(dhid, two_half, p_up, 256, hidden // 16), 0)
    for c in range(chunks):
        hid_copy(c).wait_send()
    pl.semaphore_signal(free_sem, inc=1, device_id=sib, device_id_type=MESH_ID)
    tick(BACK_TICKS[1][0])
    half_copies[1].wait()
    sib_copies[1].wait_recv()
    sib_copies[3].wait_recv()
    lax.fori_loop(0, width // LANES, gradient(dattn, low_half, p_out, LANES, width // 16), 0)
    tick(BACK_TICKS[1][1])
    dkt_ref[...] = jnp.zeros_like(dkt_ref)
    dvt_ref[...] = jnp.zeros_like(dvt_ref)

    def unpack(pair, carry):
        there.wait(2 * pair)
        there.wait(2 * pair + 1)
        rows = pl.ds(pl.multiple_of(pair * two, two), two)
        pieces = []
        for e in range(2):
            g = back_got[2 * pair + e].astype(f32)
            pieces += [g, swap_halves(g)]
        grad = jnp.where(lane < HALF_LANES, jnp.concatenate(pieces, axis=0), 0.0)
        delta = jnp.sum(grad * dq_ref[rows, :], axis=1, keepdims=True)
        grad = lanes_three(lane, HALF_LANES, -delta, grad)
        g_ref[rows, :] = grad.astype(low)
        gt_ref[:, rows] = grad.T[:HALF_LANES].astype(low)
        qt_ref[:, rows] = q_ref[rows, :].astype(f32).T[:HALF_LANES].astype(low)
        return carry

    out32_copy.wait()
    for i in range(4):
        lax.fori_loop(2 * i, 2 * i + 2, unpack, 0)
        tick(BACK_TICKS[2][i])

    def query_block(limit, b, carry):
        rows = pl.ds(pl.multiple_of(b * ROWS, ROWS), ROWS)
        q, g = q_ref[rows, :], g_ref[rows, :]
        qt, gt = qt_ref[:, rows], gt_ref[:, rows]

        def chunk(cols, acc):
            p = jnp.exp(nn(q, kt_ref[:, cols]))
            ds = (p * nn(g, vt_ref[:, cols])).astype(low)
            dvt_ref[:, cols] += nn(gt, p.astype(low))
            dkt_ref[:, cols] += nn(qt, ds)
            return acc + nn(ds, k_ref[cols, :])

        whole, left = limit // CHUNK, limit % CHUNK
        acc = lax.fori_loop(
            0,
            whole,
            lambda c, acc: chunk(pl.ds(pl.multiple_of(c * CHUNK, CHUNK), CHUNK), acc),
            jnp.zeros((ROWS, LANES), f32),
        )
        if left:
            acc = chunk(slice(whole * CHUNK, limit), acc)
        dq_ref[rows, :] = acc
        return carry

    for first, stop, limit in groups:
        for b in range(first, stop):
            lax.fori_loop(b, b + 1, functools.partial(query_block, limit), 0)
            tick(BACK_TICKS[3][b])

    def send_out(pair, carry):
        rows = pl.ds(pl.multiple_of(pair * two, two), two)
        dkv = jnp.concatenate([dkt_ref[:, rows], dvt_ref[:, rows]], axis=0).T
        qk = jnp.where(lane < HALF_LANES, dq_ref[rows, :], swap_halves(dkv)).astype(low)
        for e in range(2):
            send_ref[2 * pair + e, 0:tokens, :] = qk[e * tokens : (e + 1) * tokens]
            a = dkv[e * tokens : e * tokens + mid]
            b = dkv[e * tokens + mid : (e + 1) * tokens]
            send_ref[2 * pair + e, tokens:, :] = jnp.where(lane_mid < HALF_LANES, swap_halves(a), b).astype(low)
            home.push(2 * pair + e)
        return carry

    lax.fori_loop(0, 8, send_out, 0)

    kept_copy = pltpu.make_async_copy(kept_any, dq_ref, kept_sem)
    kept_copy.start()
    tick(BACK_TICKS[4][0])
    com_ref[...] = jnp.zeros_like(com_ref)

    def load_codes(c):
        slot = lax.rem(c, 2)
        rows = pl.ds(pl.multiple_of(lax.rem(c, chunks) * step, step), step)
        return [
            pltpu.make_async_copy(book_any.at[rows, pl.ds(r * half, half)], w_buf.at[slot, r], w_sem.at[slot, r])
            for r in range(2)
        ]

    def start_codes(c):
        for copy in load_codes(c):
            copy.start()

    start_codes(0)

    def logits_of(c):
        pl.when(c + 1 < 2 * chunks)(lambda: start_codes(c + 1))
        for copy in load_codes(c):
            copy.wait()
        w = w_buf.at[lax.rem(c, 2)]
        return nt(block_ref[:, :half], w[0]) + nt(block_ref[:, half:], w[1])

    def sum_codes(c, carry):
        top, total = carry
        logits = logits_of(c)
        new_top = jnp.maximum(top, jnp.max(logits, axis=1, keepdims=True))
        return new_top, total * jnp.exp(top - new_top) + jnp.sum(jnp.exp(logits - new_top), axis=1, keepdims=True)

    start = (jnp.full((tokens, 1), -3e38, f32), jnp.zeros((tokens, 1), f32))
    top, total = lax.fori_loop(0, chunks, sum_codes, start)
    share_of = live / total
    tick(BACK_TICKS[4][1])
    for c in range(chunks):
        mass = jnp.sum(jnp.exp(logits_of(chunks + c) - top) * share_of, axis=0, keepdims=True)
        com_ref[34 + c // 2 : 35 + c // 2, (c % 2) * step : (c % 2 + 1) * step] = mass
    slabs = 3 * width // step

    def load_w(j):
        rows = pl.ds(j * step, step)
        return [pltpu.make_async_copy(w_any.at[c, rows], w_buf.at[j % 2, c], w_sem.at[j % 2, c]) for c in range(2)]

    for j in range(2):
        for copy in load_w(j):
            copy.start()
    kept_copy.wait()
    tick(BACK_TICKS[4][2])

    def unnormalize(values, grad):
        inverse = lax.rsqrt(head_sums(values * values) + NORM_EPS)
        unit = values * inverse
        return inverse * (grad - unit * head_sums(unit * grad)), unit

    def heads_back(pair, carry):
        home.wait(2 * pair)
        home.wait(2 * pair + 1)
        cols = pl.ds(pl.multiple_of(pair * LANES, LANES), LANES)
        key_cols = pl.ds(pl.multiple_of(pair * LANES + width, LANES), LANES)
        val_cols = pl.ds(pl.multiple_of(pair * LANES + 2 * width, LANES), LANES)
        even = got_ref[2 * pair].astype(f32)
        odd = got_ref[2 * pair + 1].astype(f32)
        even_qk, odd_qk = even[:tokens], odd[:tokens]
        d_query = jnp.where(lane_tok < HALF_LANES, even_qk, swap_halves(odd_qk))
        d_key = jnp.where(lane_tok < HALF_LANES, swap_halves(even_qk), odd_qk)
        even_v, odd_v = even[tokens:], odd[tokens:]
        dproj[core, 0:mid, val_cols] = jnp.where(lane_mid < HALF_LANES, even_v, swap_halves(odd_v)).astype(low)
        dproj[core, mid:, val_cols] = jnp.where(lane_mid < HALF_LANES, swap_halves(even_v), odd_v).astype(low)
        scaled = d_query * (8.0 * (1.0 + vec_ref[7:8, cols]))
        d_q, unit = unnormalize(dq_ref[pl.ds(pl.multiple_of(pair * tokens, tokens), tokens), :], scaled)
        com_ref[33:34, cols] = jnp.sum(d_query * unit, axis=0, keepdims=True) * 8.0
        dproj[core, :, cols] = d_q.astype(low)
        dproj[core, :, key_cols] = unnormalize(dq_ref[pl.ds(pl.multiple_of((pair + 8) * tokens, tokens), tokens), :], d_key)[0].astype(low)
        return carry

    for i in range(2):
        lax.fori_loop(4 * i, 4 * i + 4, heads_back, 0)
        tick(BACK_TICKS[5][i])
    pl.semaphore_wait(free_sem, 1)
    d_copy = to_sib(6, dproj.at[core], dproj.at[core])

    for j in range(slabs):
        for copy in load_w(j):
            copy.wait()
        for c in range(2):
            part = nn(dproj[core, :, j * step : (j + 1) * step], w_buf[j % 2, c])
            cols = slice(c * half, (c + 1) * half)
            dh_ref[:, cols] = part if j == 0 else dh_ref[:, cols] + part
        if j + 2 < slabs:
            for copy in load_w(j + 2):
                copy.start()
    half_copies[2].wait()
    sib_copies[2].wait_recv()
    d_copy.wait_recv()

    def weight_grad(c, carry):
        cols = pl.ds(pl.multiple_of(c * two, two), two)
        total = nn(dproj[0, :, cols].astype(f32).T.astype(low), h_both[0])
        total = total + nn(dproj[1, :, cols].astype(f32).T.astype(low), h_both[1])
        p_qkv[c // 2, pl.ds(2 * (c % 2), 2)] = total.astype(low).reshape(2, tokens, half)
        return carry

    assert next_tick[0] >= len(splits[0]) + 2
    for p in range(len(splits[0])):
        flow.sent(p)
    lax.fori_loop(0, 8, weight_grad, 0)
    last.run(0)
    tick(flow.steps())

    unit, rstd = standard_of(x_ref[...])
    d_h = dh_ref[...]
    ada_ref[:, 2 * width : 3 * width] = per_slot(d_h * unit)
    ada_ref[:, 4 * width : 5 * width] = per_slot(d_h)
    d_x = standard_back(unit, rstd, d_h * (1.0 + of_tokens(2))) + dx_one[...]
    last.run(1)
    com_ref[0:32, :] = lax.dot_general(
        smooth_ref[...], d_x, (((1,), (0,)), ((), ())), precision=HIGHEST_PRECISION, preferred_element_type=f32
    )
    com_ref[32:33, :] = jnp.sum(d_x, axis=0, keepdims=True)
    small = []
    quarter = COMMON_ROWS // 2

    def common_part(ref, w):
        rows = pl.ds(pl.multiple_of((w // 8) * quarter, 8), quarter)
        return ref.at[rows, pl.ds(pl.multiple_of((w % 8) * LANES, LANES), LANES)]

    ada_width = 6 * width // 16

    def ada_part(ref, w):
        return ref.at[:, pl.ds(pl.multiple_of(w * ada_width, LANES), ada_width)]

    def spread(sem_s, sem_r, r, slot, src, dst):
        copy = pltpu.make_async_remote_copy(
            src_ref=src,
            dst_ref=dst,
            send_sem=sem_s.at[slot, r],
            recv_sem=sem_r.at[slot, r],
            device_id=(core, wide ^ r),
            device_id_type=MESH_ID,
        )
        copy.start()
        return copy

    for r in range(1, 16):
        small.append(spread(small_s, small_r, r, 0, ada_part(ada_ref, wide ^ r), ada_land.at[r]))
        small.append(spread(small_s, small_r, r, 1, common_part(com_ref, wide ^ r), com_land.at[r]))
    d_smooth = lax.dot_general(
        embed_ref[1], d_x, (((1,), (1,)), ((), ())), precision=HIGHEST_PRECISION, preferred_element_type=f32
    )
    left, right = ok_ref[0:1, :], ok_ref[1:2, :]
    share = d_smooth / (2.0 + left + right)
    spot = lane_iota((32, LANES))
    edge[...] = jnp.where(spot == 0, share[:, 0:1], jnp.where(spot == 1, share[:, tokens - 1 : tokens], 0.0))

    def edge_copy(slot, dst, shift):
        return pltpu.make_async_remote_copy(
            src_ref=edge,
            dst_ref=dst,
            send_sem=edge_s.at[slot],
            recv_sem=edge_r.at[slot],
            device_id=(core, lax.rem(wide + shift, 16)),
            device_id_type=MESH_ID,
        )

    to_right, to_left = edge_copy(0, edge_left, 1), edge_copy(1, edge_right, 15)
    last.run(2)
    ada_total, com_total = ada_part(ada_ref, wide)[...], common_part(com_ref, wide)[...]
    for copy in small:
        copy.wait_recv()
    for r in range(1, 16):
        ada_total = ada_total + ada_land[r]
        com_total = com_total + com_land[r]
    ada_sum[...] = ada_total
    com_sum[...] = com_total
    swaps = [to_sib(7, ada_sum, ada_sib), to_sib(8, com_sum, com_sib)]
    last.run(3)
    for copy in swaps:
        copy.wait_recv()
    ada_both[core] = ada_sum[...]
    ada_both[1 - core] = ada_sib[...]
    bias = jnp.sum(ada_sum[...] + ada_sib[...], axis=0, keepdims=True)
    bias_own[...] = jnp.broadcast_to(bias, bias_own.shape)
    com_own[...] = com_sum[...] + com_sib[...]
    ada_part(bias_all, wide)[...] = bias_own[...]
    common_part(common_all, wide)[...] = com_own[...]
    back = []
    for r in range(1, 16):
        back.append(spread(spread_s, spread_r, r, 0, bias_own, ada_part(bias_all, wide)))
        back.append(spread(spread_s, spread_r, r, 1, com_own, common_part(common_all, wide)))
    for i in range(4, last.steps()):
        last.run(i)
    to_right.start()
    to_left.start()
    to_right.wait_recv()
    to_left.wait_recv()
    column = lane_iota((32, tokens))
    before = jnp.where(column == 0, edge_left[:, 1:2], jnp.roll(share, 1, axis=1))
    after = jnp.where(column == tokens - 1, edge_right[:, 0:1], jnp.roll(share, -1, axis=1))
    map_ref[...] = 2.0 * share + left * before + right * after
    for copy in back:
        copy.wait_recv()
    for copy in small + swaps + back + sib_copies + [d_copy, to_right, to_left]:
        copy.wait_send()
    flow.finish()
    last.finish()
    there.finish()
    home.finish()


def back(args, groups, splits, call_id):
    x_zero, act = args[4], args[10]
    tokens, width = x_zero.shape
    hidden = act.shape[1]
    group_len = 16 * tokens
    half, mid, packed = width // 2, tokens // 2, tokens * 3 // 2
    f32, low = jnp.float32, jnp.bfloat16
    dma = pltpu.SemaphoreType.DMA
    shape = jax.ShapeDtypeStruct
    sizes = [(width // 16, hidden // 2), (hidden // 16, half), (width // 16, half), (3 * width // 16, half)]
    first = pieces_of([shape(s, f32) for s in sizes[:3]], splits[0])
    second = pieces_of([shape(sizes[3], f32)], splits[1])
    ada_width, quarter = 6 * width // 16, COMMON_ROWS // 2
    outs = [shape(s, f32) for s in sizes] + [
        shape((2, 8, ada_width), f32),
        shape((COMMON_ROWS, width), f32),
        shape((8, 6 * width), f32),
        shape((32, tokens), f32),
        shape((tokens, width), low),
    ]
    vm = pltpu.VMEM
    scratch = [
        vm((16, packed, LANES), low),
        vm((16, packed, LANES), low),
        vm((16, mid, LANES), low),
        vm((16, mid, LANES), low),
        vm((group_len, LANES), low),
        vm((HALF_LANES, group_len), low),
        vm((HALF_LANES, group_len), low),
        vm((group_len, LANES), f32),
        vm((HALF_LANES, group_len), f32),
        vm((HALF_LANES, group_len), f32),
        vm((2, 4, 512, half), low),
        vm((2, tokens, hidden), low),
        vm((2, tokens, half), low),
        vm((tokens, width), f32),
        vm((8, 6 * width), f32),
        vm((COMMON_ROWS, width), f32),
        vm((16, 8, ada_width), f32),
        vm((16, quarter, LANES), f32),
        vm((8, ada_width), f32),
        vm((quarter, LANES), f32),
        vm((8, ada_width), f32),
        vm((quarter, LANES), f32),
        vm((8, ada_width), f32),
        vm((quarter, LANES), f32),
        vm((32, LANES), f32),
        vm((32, LANES), f32),
        vm((32, LANES), f32),
        vm((tokens, width), low),
        vm((2, tokens, half), low),
        vm((2, tokens, half), low),
        vm((2, tokens, width), low),
        vm((tokens, width), f32),
        vm((tokens, width), f32),
        vm((2, tokens, 512), low),
        vm((2, tokens, 512), f32),
        vm((tokens, width), low),
    ] + [vm((4, 4) + s, low) for s in sizes[1:3]]
    scratch += Scatter.scratch(sizes[:3], len(first)) + Scatter.scratch(sizes[3:], len(second))
    scratch += [dma((16,)) for _ in range(4)] + [dma((2, 6)), dma((16,)), dma((16,))]
    scratch += [dma((2, 16)) for _ in range(4)] + [dma((2,)), dma((2,))]
    scratch += [dma((8,)), dma((8,)), dma((4,)), dma, pltpu.SemaphoreType.REGULAR]
    return pl.pallas_call(
        functools.partial(back_kernel, groups, (first, second)),
        out_shape=outs,
        in_specs=[VM] * 7 + [ANY] * 11 + [VM] * 4 + [ANY] + [VM] * 4,
        out_specs=[VM] * 9,
        scratch_shapes=scratch,
        compiler_params=pltpu.CompilerParams(
            collective_id=call_id, has_side_effects=True, vmem_limit_bytes=63 * 1024 * 1024
        ),
    )(*args)


def nesterov_rows(moment, weight, average, gradient, step_rate, decay_rate):
    step_grad = gradient + decay_rate * weight
    new_moment = MOMENTUM * moment + step_rate * step_grad
    new_weight = weight - (step_rate * step_grad + MOMENTUM * new_moment)
    retain = min(0.999, (1.0 + STEP) / (10.0 + STEP))
    return new_moment, new_weight, retain * average + (1.0 - retain) * new_weight


def update_kernel(rates, mass_scale, *refs):
    states = refs[:5]
    (embed_ref, vector_ref, s_down, s_up, s_out, s_qkv, d_ada, silu_ref, common_ref, bias_ref) = refs[5:15]
    news, copies = refs[15:20], refs[20:25]
    (embed_new, vector_new, mass_out, gain_out) = refs[25:29]
    held, lows = refs[29:34], refs[34:39]
    load_sem, store_sem, low_sem = refs[39:]
    width = vector_ref.shape[2]

    def grad_of(i):
        if i == 4:
            return exact(silu_ref[...], d_ada[...], (0, 0))
        return (s_qkv, s_out, None, s_down)[i][...] if i != 2 else s_up[...].T

    order = (3, 2, 4, 0, 1)
    loads = {i: pltpu.make_async_copy(states[i], held[i], load_sem.at[i]) for i in order}
    for i in order:
        loads[i].start()
    rows = embed_ref.shape[1]
    parts = nesterov_rows(embed_ref[0], embed_ref[1], embed_ref[2], common_ref[0:rows, :], rates[5], 0.0)
    for j in range(3):
        embed_new[j] = parts[j]
    for block in range(8):
        if block < 6:
            grad = bias_ref[0:1, block * width : (block + 1) * width]
        else:
            grad = common_ref[rows + block - 6 : rows + block - 5, :]
        here = slice(block, block + 1)
        parts = nesterov_rows(vector_ref[0, here], vector_ref[1, here], vector_ref[2, here], grad, rates[6], 0.0)
        for j in range(3):
            vector_new[j, here] = parts[j]
    per_row = width // LANES
    for r in range(per_row):
        cols = slice(r * LANES, (r + 1) * LANES)
        gain_out[r : r + 1, :] = common_ref[rows + 1 : rows + 2, cols]
        for a in range(mass_out.shape[0] // per_row):
            at = a * per_row + r
            mass_out[at : at + 1, :] = common_ref[rows + 2 + a : rows + 3 + a, cols] * mass_scale
    stores = []
    for i in order:
        loads[i].wait()
        parts = nesterov_rows(held[i][0], held[i][1], held[i][2], grad_of(i), rates[i], WEIGHT_DECAY)
        for j in range(3):
            held[i][j] = parts[j]
        lows[i][...] = parts[1].astype(jnp.bfloat16)
        stores.append(pltpu.make_async_copy(held[i], news[i], store_sem.at[i]))
        stores.append(pltpu.make_async_copy(lows[i], copies[i], low_sem.at[i]))
        for copy in stores[-2:]:
            copy.start()
    for copy in stores:
        copy.wait()


def update(states, embed_state, vector_state, grads, rates, codes, mass_scale):
    f32, low = jnp.float32, jnp.bfloat16
    shape = jax.ShapeDtypeStruct
    dma = pltpu.SemaphoreType.DMA
    width = vector_state.shape[2]
    outs = [shape(s.shape, f32) for s in states] + [shape(s.shape[1:], low) for s in states]
    outs += [shape(embed_state.shape, f32), shape(vector_state.shape, f32)]
    outs += [shape((codes // LANES, LANES), f32), shape((width // LANES, LANES), f32)]
    return pl.pallas_call(
        functools.partial(update_kernel, rates, mass_scale),
        out_shape=outs,
        in_specs=[ANY] * 5 + [VM] * 10,
        out_specs=[ANY] * 10 + [VM] * 4,
        scratch_shapes=[pltpu.VMEM(s.shape, f32) for s in states]
        + [pltpu.VMEM(s.shape[1:], low) for s in states]
        + [dma((5,)), dma((5,)), dma((5,))],
        compiler_params=pltpu.CompilerParams(vmem_limit_bytes=VMEM_BYTES),
    )(*states, embed_state, vector_state, *grads)


def run_tables(slots):
    squares = np.zeros((8, LANES), np.float32)
    pick = np.zeros((LANES, LANES), np.float32)
    for run in range(slots * LEVELS):
        squares[0, HALF_LANES + run] = LONG_SIDES[run // slots] ** 2
        squares[1, HALF_LANES + run] = SHORT_SIDES[run // slots] ** 2
        pick[HALF_LANES + run, run % slots] = 1.0
    tri = np.triu(np.ones((LANES, LANES), np.float32))
    low = jnp.bfloat16
    return [jnp.asarray(squares), jnp.asarray(tri), jnp.asarray(pick, low), jnp.asarray(attention_rule(slots), low)]


def attention_rule(slots):
    runs = slots * LEVELS + 1
    rule = np.zeros((LANES, LANES), np.float32)
    for a in range(runs):
        for b in range(runs):
            slot_a, level_a = (slots, 0) if a == runs - 1 else (a % slots, a // slots)
            slot_b, level_b = (slots, 0) if b == runs - 1 else (b % slots, b // slots)
            if slot_a != slot_b or level_b > level_a:
                rule[HALF_LANES + a, HALF_LANES + b] = -BIG
    return rule


def fast_shards(
    feature_map,
    condition,
    item_lengths,
    cotangent,
    code_book,
    qkv_state,
    out_state,
    up_state,
    down_state,
    ada_state,
    embed_state,
    vector_state,
):
    tok_rows, model_width = cotangent.shape
    low = jnp.bfloat16
    group_len = tok_rows * lax.axis_size("wide")
    tokens_all = lax.axis_size("dp") * group_len
    lengths = item_lengths[0]
    slot_count = lengths.shape[0]

    states = (qkv_state, out_state, up_state, down_state, ada_state)
    flipped = tuple(stacked[1].astype(low).T for stacked in states[:4])
    groups = same_limits(key_limits(group_len, slot_count))
    (
        w_qkv, w_out, w_up, w_down, ada_gathered, h_one_low, kept_qk, out32, q_own, k_own, kt_own, vt_own, attn_low,
        x_zero, smooth, flags, one_hot_wide, silu_rows, attn_proj, x_one, h_two_low, hidden_pre, act_low, p_down,
    ) = front(
        flipped,
        condition,
        ada_state,
        feature_map,
        embed_state,
        vector_state,
        item_lengths,
        run_tables(slot_count),
        cotangent,
        groups,
    )
    s_down, s_up, s_out, s_qkv, d_ada_both, common_sum, bias_sum, map_grad, block_out = back(
        [cotangent, one_hot_wide, ada_gathered, vector_state, x_zero, x_one, attn_proj, h_one_low, h_two_low, attn_low]
        + [act_low, hidden_pre, w_qkv, w_out, w_up, w_down, code_book, out32, q_own, k_own, kt_own, vt_own]
        + [kept_qk.reshape(-1, LANES), smooth, embed_state, flags, p_down],
        groups,
        BACK_SPLITS,
        1,
    )
    flip = lambda values: jnp.swapaxes(values, -1, -2)
    root_tokens = math.sqrt(tokens_all)
    spreads = (
        model_width ** (-0.5),
        (model_width // 16) ** (-0.5),
        model_width ** (-0.5),
        w_up.shape[1] ** (-0.5),
        model_width ** (-0.5),
    )
    rates = [BASE_RATE * spread_w / (factor_g * root_tokens) for spread_w, factor_g in zip(spreads, GRAD_FACTORS)]
    rates.append(BASE_RATE * embed_state.shape[1] ** (-0.5) / (EMBED_FACTOR * root_tokens))
    rates.append(VECTOR_RATE / root_tokens)
    codes = code_book.shape[0]
    results = update(
        [flip(qkv_state), flip(out_state), up_state, flip(down_state), ada_state],
        embed_state,
        vector_state,
        [s_down, s_up, s_out, s_qkv, d_ada_both.reshape(16, -1), silu_rows.reshape(16, -1), common_sum, bias_sum],
        tuple(rates),
        codes,
        codes / tokens_all,
    )
    outputs = [block_out, map_grad, results[12].reshape(-1)]
    for i in range(5):
        new, copied = results[i], results[5 + i]
        outputs += [flip(new), flip(copied)] if i in (0, 1, 3) else [new, copied]
    return tuple(outputs + [results[10], results[11], results[13].reshape(-1)])


def solution(mesh):
    body = fast_shards if dict(mesh.shape) == {"dp": 2, "wide": 16} else shards
    in_specs = (
        P(None, ("dp", "wide")),
        P("dp", None),
        P("dp", None),
        P(("dp", "wide"), None),
        P(),
        P(None, "dp", "wide"),
        P(None, "dp", "wide"),
        P(None, "dp", "wide"),
        P(None, "dp", "wide"),
        P(None, "dp", "wide"),
        P(),
        P(),
    )
    out_specs = (
        P(("dp", "wide"), None),
        P(None, ("dp", "wide")),
        P(),
        P(None, "dp", "wide"),
        P("dp", "wide"),
        P(None, "dp", "wide"),
        P("dp", "wide"),
        P(None, "dp", "wide"),
        P("dp", "wide"),
        P(None, "dp", "wide"),
        P("dp", "wide"),
        P(None, "dp", "wide"),
        P("dp", "wide"),
        P(),
        P(),
        P(),
    )
    return jax.shard_map(body, mesh=mesh, in_specs=in_specs, out_specs=out_specs, check_vma=False)
```

```python
import functools
import math

import jax
import jax.numpy as jnp
import numpy as np
from jax import lax
from jax.experimental import pallas as pl
from jax.experimental.pallas import tpu as pltpu
from jax.sharding import PartitionSpec as P

HEADS = 16
LEVELS = 10
STEP = 7


SHORT_SIDES = (1, 2, 3, 4, 5, 6, 8, 10, 13, 16)
LONG_SIDES = (1, 2, 3, 4, 6, 9, 13, 18, 24, 32)
MASKED = -1e30
NORM_EPS = 1e-06
MOMENTUM = 0.9
WEIGHT_DECAY = 0.05
BASE_RATE = 0.37
VECTOR_RATE = 0.22
GRAD_FACTORS = (0.15, 0.1, 0.3, 0.35, 0.3)
EMBED_FACTOR = 0.6
HIGHEST_PRECISION = lax.Precision.HIGHEST


def padded(cells, sides, width):
    for axis, dim in sides:
        count = lax.axis_size(axis)
        ends = count - 1
        head = lax.slice_in_dim(cells, 0, width, axis=dim)
        tail = lax.slice_in_dim(cells, cells.shape[dim] - width, cells.shape[dim], axis=dim)
        cells = jnp.concatenate(
            [
                lax.ppermute(tail, axis, [(i, (i + 1) % count) for i in range(ends)]),
                cells,
                lax.ppermute(head, axis, [((i + 1) % count, i) for i in range(ends)]),
            ],
            axis=dim,
        )
    return cells


def layout(lengths, positions, group_len):
    short_sq = jnp.array([side * side for side in SHORT_SIDES[:LEVELS]], jnp.int32)
    long_sq = jnp.array([side * side for side in LONG_SIDES[:LEVELS]], jnp.int32)
    short_total = sum((side * side for side in SHORT_SIDES[:LEVELS]))
    long_total = sum((side * side for side in LONG_SIDES[:LEVELS]))
    slot_count = lengths.shape[0]
    counts = jnp.where(
        lengths[None, :] == long_total,
        long_sq[:, None],
        jnp.where(lengths[None, :] == short_total, short_sq[:, None], 0),
    )
    unused = group_len - jnp.sum(lengths)
    ordered = jnp.concatenate([counts.reshape(-1), unused[None]])
    boundary = jnp.cumsum(ordered)
    segment = jnp.sum((boundary[None, :] <= positions[:, None]).astype(jnp.int32), axis=1)
    segment = jnp.minimum(segment, ordered.shape[0] - 1)
    unused_id = slot_count * LEVELS
    tok_level = jnp.where(segment >= unused_id, 0, segment // slot_count)
    tok_slot = jnp.where(segment >= unused_id, slot_count, segment % slot_count)
    return (tok_slot, tok_level, segment)


def pre_norm(inputs, scaling, offset_add):
    row_mean = jnp.mean(inputs, axis=-1, keepdims=True)
    centred = inputs - row_mean
    spread = jnp.mean(centred * centred, axis=-1, keepdims=True)
    return centred * lax.rsqrt(spread + NORM_EPS) * (1.0 + scaling) + offset_add


def unit_heads(inputs):
    shaped = inputs.reshape(inputs.shape[0], HEADS, -1)
    shaped = shaped * lax.rsqrt(jnp.sum(shaped * shaped, axis=-1, keepdims=True) + NORM_EPS)
    return shaped.reshape(inputs.shape)


def split_heads(projected, q_gain):
    queries, key_part, value_part = jnp.split(projected, 3, axis=1)
    head_scale = math.sqrt(queries.shape[1] // HEADS)
    return (unit_heads(queries) * (head_scale * (1.0 + q_gain)), unit_heads(key_part), value_part)


def smooth_map(values, left_ok, right_ok, before, following):
    return (left_ok * before + 2.0 * values + right_ok * following) / (2.0 + left_ok + right_ok)


def nesterov(stacked, gradient, step_rate, decay_rate):
    moment, weight, average = (stacked[0], stacked[1], stacked[2])
    step_grad = gradient + decay_rate * weight
    new_moment = MOMENTUM * moment + step_rate * step_grad
    new_weight = weight - (step_rate * step_grad + MOMENTUM * new_moment)
    retain = min(0.999, (1.0 + STEP) / (10.0 + STEP))
    new_average = retain * average + (1.0 - retain) * new_weight
    return jnp.stack([new_moment, new_weight, new_average])


def contract_rows(left_side, right_side, precision=None):
    return lax.dot_general(
        left_side,
        right_side,
        (((0,), (0,)), ((), ())),
        precision=precision,
        preferred_element_type=jnp.float32,
    )


def against(left_side, right_side):
    return lax.dot_general(
        left_side, right_side, (((1,), (1,)), ((), ())), preferred_element_type=jnp.float32
    )


def shards(
    feature_map,
    condition,
    item_lengths,
    cotangent,
    code_book,
    qkv_state,
    out_state,
    up_state,
    down_state,
    ada_state,
    embed_state,
    vector_state,
):
    tok_rows = cotangent.shape[0]
    model_width = cotangent.shape[1]
    head_dim = model_width // HEADS
    wide_count = lax.axis_size("wide")
    group_len = tok_rows * wide_count
    tokens_all = lax.axis_size("dp") * group_len
    lengths = item_lengths[0]
    slot_count = lengths.shape[0]
    positions = lax.axis_index("wide") * tok_rows + jnp.arange(tok_rows, dtype=jnp.int32)
    tok_slot, tok_level, segment = layout(lengths, positions, group_len)
    live_rows = (tok_slot < slot_count).astype(jnp.float32)[:, None]
    left_ok = ((layout(lengths, positions - 1, group_len)[2] == segment) & (positions > 0)).astype(
        jnp.float32
    )
    right_ok = (
        (layout(lengths, positions + 1, group_len)[2] == segment) & (positions < group_len - 1)
    ).astype(jnp.float32)
    rimmed = padded(feature_map, (("wide", 1),), 1)
    smooth = smooth_map(feature_map, left_ok, right_ok, rimmed[:, :-2], rimmed[:, 2:])
    states = (qkv_state, out_state, up_state, down_state, ada_state)
    masters = tuple((stacked[1].astype(jnp.bfloat16) for stacked in states))
    columns = (
        lax.all_gather(masters[0], "wide", axis=1, tiled=True),
        lax.all_gather(masters[1], "wide", axis=1, tiled=True),
        lax.all_gather(masters[2], "wide", axis=1, tiled=True),
        lax.all_gather(masters[3], "wide", axis=1, tiled=True),
    )
    ada_piece = lax.all_gather(masters[4], "wide", axis=1, tiled=True)
    w_qkv, w_out, w_up, w_down, w_ada = (
        lax.all_gather(columns[0], "dp", axis=0, tiled=True),
        lax.all_gather(columns[1], "dp", axis=0, tiled=True),
        lax.all_gather(columns[2], "dp", axis=0, tiled=True),
        lax.all_gather(columns[3], "dp", axis=0, tiled=True),
        lax.all_gather(ada_piece, "dp", axis=0, tiled=True),
    )
    embed_w = embed_state[1]
    vectors = vector_state[1]
    x_zero = (
        lax.dot_general(smooth, embed_w, (((0,), (0,)), ((), ())), precision=HIGHEST_PRECISION)
        + vectors[6]
    )
    silu_cond = jax.nn.silu(condition).astype(jnp.bfloat16)
    ada_product = jnp.dot(silu_cond, w_ada, preferred_element_type=jnp.float32)
    ada_all = ada_product + vectors[:6].reshape(-1)
    one_hot = (tok_slot[:, None] == jnp.arange(slot_count, dtype=jnp.int32)[None, :]).astype(
        jnp.float32
    )
    token_ada = jnp.dot(one_hot, ada_all, precision=HIGHEST_PRECISION)
    gate_one, gate_two, scale_one, scale_two, shift_one, shift_two = jnp.split(token_ada, 6, axis=1)
    h_one_low = pre_norm(x_zero, scale_one, shift_one).astype(jnp.bfloat16)
    projected = jnp.dot(h_one_low, w_qkv, preferred_element_type=jnp.float32)
    (q_unit, k_unit, v_full), heads_back = jax.vjp(split_heads, projected, vectors[7])
    queries = q_unit.astype(jnp.bfloat16)
    keys_low = k_unit.astype(jnp.bfloat16)
    values_low = v_full.astype(jnp.bfloat16)
    query_heads = queries.reshape(tok_rows, HEADS, head_dim)

    def blockwise(advance, running, pieces, first_row):
        key_count = pieces[0].shape[0]
        block_size = math.gcd(key_count, 1024)

        def per_block(current, offset):
            key_part = tuple(
                (lax.dynamic_slice_in_dim(piece_arr, offset, block_size, 0) for piece_arr in pieces)
            )
            first_key = first_row + offset
            k_slot, k_level, _ = layout(
                lengths, first_key + jnp.arange(block_size, dtype=jnp.int32), group_len
            )
            allowed = (tok_slot[:, None] == k_slot[None, :]) & (
                k_level[None, :] <= tok_level[:, None]
            )
            current = advance(current, key_part, allowed, first_key)
            return (current, None)

        offsets = jnp.arange(key_count // block_size, dtype=jnp.int32) * block_size
        return lax.scan(per_block, running, offsets)[0]

    def scores_of(key_block, allowed):
        raw_scores = jnp.einsum(
            "qhd,khd->hqk",
            query_heads,
            key_block.reshape(-1, HEADS, head_dim),
            preferred_element_type=jnp.float32,
        )
        return jnp.where(allowed[None], raw_scores, MASKED)

    def stats_step(running, key_part, allowed, first_key):
        scores = scores_of(key_part[0], allowed)
        top_score, exp_total = running
        new_top = jnp.maximum(top_score, jnp.max(scores, axis=-1, keepdims=True))
        exp_total = exp_total * jnp.exp(top_score - new_top) + jnp.sum(
            jnp.exp(scores - new_top), axis=-1, keepdims=True
        )
        return (new_top, exp_total)

    kv_rows = (
        lax.all_gather(keys_low, "wide", axis=0, tiled=True),
        lax.all_gather(values_low, "wide", axis=0, tiled=True),
    )
    start_stats = (
        jnp.full((HEADS, tok_rows, 1), MASKED, jnp.float32),
        jnp.zeros((HEADS, tok_rows, 1), jnp.float32),
    )
    top_score, exp_total = blockwise(stats_step, start_stats, kv_rows, 0)
    log_total = top_score + jnp.log(exp_total)

    def value_step(running, key_part, allowed, first_key):
        attn_probs = jnp.exp(scores_of(key_part[0], allowed) - log_total).astype(jnp.bfloat16)
        return running + jnp.einsum(
            "hqk,khd->qhd",
            attn_probs,
            key_part[1].reshape(-1, HEADS, head_dim),
            preferred_element_type=jnp.float32,
        )

    attended = blockwise(
        value_step, jnp.zeros((tok_rows, HEADS, head_dim), jnp.float32), kv_rows, 0
    )
    attn_low = attended.reshape(tok_rows, model_width).astype(jnp.bfloat16)
    attn_proj = jnp.dot(attn_low, w_out, preferred_element_type=jnp.float32)
    x_one = x_zero + gate_one * attn_proj
    h_two_low = pre_norm(x_one, scale_two, shift_two).astype(jnp.bfloat16)
    hidden_pre = jnp.dot(h_two_low, w_up, preferred_element_type=jnp.float32)
    act_low = jax.nn.gelu(hidden_pre, approximate=True).astype(jnp.bfloat16)
    mlp_out = jnp.dot(act_low, w_down, preferred_element_type=jnp.float32)
    x_two = x_one + gate_two * mlp_out
    block_out = (x_two * live_rows).astype(jnp.bfloat16)
    logits = against(block_out, code_book)
    code_mass = jnp.sum(jax.nn.softmax(logits, axis=-1) * live_rows, axis=0)
    g_two = cotangent.astype(jnp.float32) * live_rows
    d_mlp = (gate_two * g_two).astype(jnp.bfloat16)
    d_gate_two = g_two * mlp_out
    dw_down = contract_rows(act_low, d_mlp)
    d_act = against(d_mlp, w_down)
    _, gelu_back = jax.vjp(lambda inputs: jax.nn.gelu(inputs, approximate=True), hidden_pre)
    d_hidden = gelu_back(d_act)[0].astype(jnp.bfloat16)
    dw_up = contract_rows(h_two_low, d_hidden)
    d_h_two = against(d_hidden, w_up)
    _, norm_back_two = jax.vjp(pre_norm, x_one, scale_two, shift_two)
    d_x_one, d_scale_two, d_shift_two = norm_back_two(d_h_two)
    d_x_one = d_x_one + g_two
    d_attn = (gate_one * d_x_one).astype(jnp.bfloat16)
    d_gate_one = d_x_one * attn_proj
    dw_out = contract_rows(attn_low, d_attn)
    grad_flat = against(d_attn, w_out).astype(jnp.bfloat16)
    grad_heads = grad_flat.reshape(tok_rows, HEADS, head_dim)

    def delta_step(running, key_part, allowed, first_key):
        attn_probs = jnp.exp(scores_of(key_part[0], allowed) - log_total)
        d_probs = jnp.einsum(
            "qhd,khd->hqk",
            grad_heads,
            key_part[1].reshape(-1, HEADS, head_dim),
            preferred_element_type=jnp.float32,
        )
        return running + jnp.sum(attn_probs * d_probs, axis=-1, keepdims=True)

    row_delta = blockwise(delta_step, jnp.zeros((HEADS, tok_rows, 1), jnp.float32), kv_rows, 0)

    def grad_step(running, key_part, allowed, first_key):
        d_query, d_keys, d_values = running
        key_heads = key_part[0].reshape(-1, HEADS, head_dim)
        value_heads = key_part[1].reshape(-1, HEADS, head_dim)
        block_rows = key_part[0].shape[0]
        attn_probs = jnp.exp(scores_of(key_part[0], allowed) - log_total)
        d_probs = jnp.einsum(
            "qhd,khd->hqk", grad_heads, value_heads, preferred_element_type=jnp.float32
        )
        d_scores = (attn_probs * (d_probs - row_delta)).astype(jnp.bfloat16)
        d_query = d_query + jnp.einsum(
            "hqk,khd->qhd", d_scores, key_heads, preferred_element_type=jnp.float32
        )
        key_grad = jnp.einsum(
            "hqk,qhd->khd", d_scores, query_heads, preferred_element_type=jnp.float32
        )
        value_grad = jnp.einsum(
            "hqk,qhd->khd",
            attn_probs.astype(jnp.bfloat16),
            grad_heads,
            preferred_element_type=jnp.float32,
        )
        key_sum = lax.dynamic_slice_in_dim(d_keys, first_key, block_rows, 0) + key_grad.reshape(
            block_rows, model_width
        )
        value_sum = lax.dynamic_slice_in_dim(
            d_values, first_key, block_rows, 0
        ) + value_grad.reshape(block_rows, model_width)
        d_keys = lax.dynamic_update_slice_in_dim(d_keys, key_sum, first_key, 0)
        d_values = lax.dynamic_update_slice_in_dim(d_values, value_sum, first_key, 0)
        return (d_query, d_keys, d_values)

    grad_init = (
        jnp.zeros((tok_rows, HEADS, head_dim), jnp.float32),
        jnp.zeros((group_len, model_width), jnp.float32),
        jnp.zeros((group_len, model_width), jnp.float32),
    )
    d_query, d_keys, d_values = blockwise(grad_step, grad_init, kv_rows, 0)
    d_keys_own, d_values_own = (
        lax.psum_scatter(
            d_keys.astype(jnp.bfloat16), "wide", scatter_dimension=0, tiled=True
        ).astype(jnp.float32),
        lax.psum_scatter(
            d_values.astype(jnp.bfloat16), "wide", scatter_dimension=0, tiled=True
        ).astype(jnp.float32),
    )
    d_projected, d_gain = heads_back(
        (d_query.reshape(tok_rows, model_width), d_keys_own, d_values_own)
    )
    d_projected_low = d_projected.astype(jnp.bfloat16)
    dw_qkv = contract_rows(h_one_low, d_projected_low)
    d_h_one = against(d_projected_low, w_qkv)
    _, norm_back_one = jax.vjp(pre_norm, x_zero, scale_one, shift_one)
    d_x_zero, d_scale_one, d_shift_one = norm_back_one(d_h_one)
    d_x_zero = d_x_zero + d_x_one
    d_token_ada = jnp.concatenate(
        [d_gate_one, d_gate_two, d_scale_one, d_scale_two, d_shift_one, d_shift_two], axis=1
    )
    d_ada_all = contract_rows(one_hot, d_token_ada, HIGHEST_PRECISION)
    d_smooth = lax.dot_general(
        embed_w, d_x_zero, (((1,), (1,)), ((), ())), precision=HIGHEST_PRECISION
    )
    d_embed = lax.dot_general(
        smooth, d_x_zero, (((1,), (0,)), ((), ())), precision=HIGHEST_PRECISION
    )
    d_vectors = jnp.concatenate(
        [
            jnp.sum(d_ada_all, axis=0).reshape(6, model_width),
            jnp.sum(d_x_zero, axis=0)[None],
            d_gain[None],
        ],
        axis=0,
    )
    grad_share = d_smooth / (2.0 + left_ok + right_ok)
    rim_share = padded(grad_share, (("wide", 1),), 1)
    map_grad = 2.0 * grad_share + left_ok * rim_share[:, :-2] + right_ok * rim_share[:, 2:]
    d_embed_all, d_vectors_all, mass_all = lax.psum((d_embed, d_vectors, code_mass), ("dp", "wide"))
    histogram = mass_all * (code_book.shape[0] / tokens_all)
    ada_term = contract_rows(silu_cond.astype(jnp.float32), d_ada_all, HIGHEST_PRECISION)
    split_cols = (
        lax.psum_scatter(
            dw_qkv.astype(jnp.bfloat16), "wide", scatter_dimension=1, tiled=True
        ).astype(jnp.float32),
        lax.psum_scatter(
            dw_out.astype(jnp.bfloat16), "wide", scatter_dimension=1, tiled=True
        ).astype(jnp.float32),
        lax.psum_scatter(
            dw_up.astype(jnp.bfloat16), "wide", scatter_dimension=1, tiled=True
        ).astype(jnp.float32),
        lax.psum_scatter(
            dw_down.astype(jnp.bfloat16), "wide", scatter_dimension=1, tiled=True
        ).astype(jnp.float32),
        lax.psum_scatter(
            ada_term.astype(jnp.bfloat16), "wide", scatter_dimension=1, tiled=True
        ).astype(jnp.float32),
    )
    ada_cols = split_cols[4]
    owned_grads = (
        lax.psum_scatter(
            split_cols[0].astype(jnp.bfloat16), "dp", scatter_dimension=0, tiled=True
        ).astype(jnp.float32),
        lax.psum_scatter(
            split_cols[1].astype(jnp.bfloat16), "dp", scatter_dimension=0, tiled=True
        ).astype(jnp.float32),
        lax.psum_scatter(
            split_cols[2].astype(jnp.bfloat16), "dp", scatter_dimension=0, tiled=True
        ).astype(jnp.float32),
        lax.psum_scatter(
            split_cols[3].astype(jnp.bfloat16), "dp", scatter_dimension=0, tiled=True
        ).astype(jnp.float32),
        lax.psum_scatter(
            ada_cols.astype(jnp.bfloat16), "dp", scatter_dimension=0, tiled=True
        ).astype(jnp.float32),
    )
    root_tokens = math.sqrt(tokens_all)
    spreads = (
        model_width ** (-0.5),
        (model_width // 16) ** (-0.5),
        model_width ** (-0.5),
        w_up.shape[1] ** (-0.5),
        model_width ** (-0.5),
    )
    new_states = tuple(
        (
            nesterov(
                stacked, gradient, BASE_RATE * spread_w / (factor_g * root_tokens), WEIGHT_DECAY
            )
            for stacked, gradient, spread_w, factor_g in zip(
                states, owned_grads, spreads, GRAD_FACTORS
            )
        )
    )
    embed_new = nesterov(
        embed_state,
        d_embed_all,
        BASE_RATE * embed_w.shape[0] ** (-0.5) / (EMBED_FACTOR * root_tokens),
        0.0,
    )
    vector_new = nesterov(vector_state, d_vectors_all, VECTOR_RATE / root_tokens, 0.0)
    return (
        block_out,
        map_grad,
        histogram,
        new_states[0],
        new_states[0][1].astype(jnp.bfloat16),
        new_states[1],
        new_states[1][1].astype(jnp.bfloat16),
        new_states[2],
        new_states[2][1].astype(jnp.bfloat16),
        new_states[3],
        new_states[3][1].astype(jnp.bfloat16),
        new_states[4],
        new_states[4][1].astype(jnp.bfloat16),
        embed_new,
        vector_new,
        d_vectors_all[7],
    )


MESH_ID = pl.DeviceIdType.MESH
ANY = pl.BlockSpec(memory_space=pl.ANY)
VM = pl.BlockSpec(memory_space=pltpu.VMEM)
VMEM_BYTES = 56 * 1024 * 1024
SHORT_TOTAL = sum(side * side for side in SHORT_SIDES)
LONG_TOTAL = sum(side * side for side in LONG_SIDES)
GELU_SCALE = math.sqrt(2.0 / math.pi)
GELU_CUBE = 0.044715
LANES = 128
HALF_LANES = 64
BIG = 1e30


def nt(left_side, right_side):
    return lax.dot_general(
        left_side, right_side, (((1,), (1,)), ((), ())), preferred_element_type=jnp.float32
    )


def nn(left_side, right_side):
    return lax.dot_general(
        left_side, right_side, (((1,), (0,)), ((), ())), preferred_element_type=jnp.float32
    )


def entry_barrier(peers):
    barrier = pltpu.get_barrier_semaphore()
    for peer in peers:
        pl.semaphore_signal(barrier, inc=1, device_id=peer, device_id_type=MESH_ID)
    pl.semaphore_wait(barrier, len(peers))


def place():
    core, wide = lax.axis_index("dp"), lax.axis_index("wide")
    return core, wide // 4, wide % 4


def at_dev(core, z, yx):
    return (core, z * 4 + yx)


def lane_iota(shape):
    return lax.broadcasted_iota(jnp.int32, shape, len(shape) - 1)


def swap_halves(pair):
    return pltpu.roll(pair, HALF_LANES, 1)


def head_sums(values):
    width = values.shape[1]
    rows = lax.broadcasted_iota(jnp.int32, (width, width), 0) // HALF_LANES
    cols = lax.broadcasted_iota(jnp.int32, (width, width), 1) // HALF_LANES
    ones = (rows == cols).astype(jnp.float32)
    return lax.dot_general(
        values,
        ones,
        (((1,), (0,)), ((), ())),
        precision=HIGHEST_PRECISION,
        preferred_element_type=jnp.float32,
    )


ROWS = 256
CHUNK = 512


def key_limits(group_len, slots):
    short_total = sum(side * side for side in SHORT_SIDES)
    long_total = sum(side * side for side in LONG_SIDES)
    limits = [0] * (group_len // ROWS)
    for longs in range(1, slots + 1):
        for shorts in range(slots - longs + 1):
            total = longs * long_total + shorts * short_total
            if not group_len - short_total < total <= group_len:
                continue
            ends, position = [], 0
            for long_side, short_side in zip(LONG_SIDES, SHORT_SIDES):
                position += longs * long_side**2 + shorts * short_side**2
                ends.append(position)
            ends.append(group_len)
            for block in range(len(limits)):
                last = block * ROWS + ROWS - 1
                seen = min(end for end in ends if end > last)
                limits[block] = max(limits[block], -(-seen // LANES) * LANES)
    return limits


def same_limits(limits):
    groups = []
    for block, limit in enumerate(limits):
        if groups and groups[-1][2] == limit:
            groups[-1][1] = block + 1
        else:
            groups.append([block, block + 1, limit])
    return groups


def fold_lanes(values, combine):
    total = values[:, :LANES]
    for j in range(1, values.shape[1] // LANES):
        total = combine(total, values[:, j * LANES : (j + 1) * LANES])
    return total


def split_three(values):
    high = values.astype(jnp.bfloat16).astype(jnp.float32)
    rest = values - high
    mid = rest.astype(jnp.bfloat16).astype(jnp.float32)
    return high, mid, rest - mid


def lanes_three(lane, first, values, otherwise):
    high, mid, rest = split_three(values)
    return jnp.where(
        lane == first, high, jnp.where(lane == first + 1, mid, jnp.where(lane == first + 2, rest, otherwise))
    )


class Gather:
    KINDS = ("up", "down", "x", "y", "turn")

    def __init__(self, shards, fulls, sems, pieces):
        self.shards, self.fulls, self.pieces = shards, fulls, pieces
        self.send, self.recv, self.send_s, self.recv_s, self.local = sems
        self.core, self.z, self.yx = place()
        core, z, yx = self.core, self.z, self.yx
        self.up_dev, self.down_dev = at_dev(core, lax.min(z + 1, 3), yx), at_dev(core, lax.max(z - 1, 0), yx)
        self.x_dev, self.y_dev = at_dev(core, z, yx ^ 1), at_dev(core, z, yx ^ 2)
        self.sib = at_dev(1 - core, z, yx)
        self.ends = []

    @staticmethod
    def scratch(count):
        dma = pltpu.SemaphoreType.DMA
        return [dma((count, 5, 4)), dma((count, 4, 4)), dma((count, 4, 4)), dma((count, 4, 4)), dma((count,))]

    def spot(self, p, z_at, d, core=None):
        i, first, rows = self.pieces[p]
        core = self.core if core is None else core
        size = self.shards[i].shape[0]
        start = pl.multiple_of((z_at * 4 + (self.yx ^ d)) * size + first, 16)
        return self.fulls[i].at[core, pl.ds(start, rows)]

    def copy(self, p, kind, z_at, d, src=None):
        there = {0: 0, 1: 0, 2: 1, 3: 2, 4: 3}[kind]
        ref = self.spot(p, z_at, d)
        device = (self.up_dev, self.down_dev, self.x_dev, self.y_dev)[kind] if kind < 4 else (self.y_dev if d == 1 else self.x_dev)
        return pltpu.make_async_remote_copy(
            src_ref=ref if src is None else src,
            dst_ref=ref,
            send_sem=self.send.at[p, kind, z_at],
            recv_sem=self.recv.at[p, there, z_at],
            device_id=device,
            device_id_type=MESH_ID,
        )

    def go(self, condition, p, kind, z_at, d, src=None):
        def start():
            self.copy(p, kind, z_at, d, src).start()

        def end():
            self.copy(p, kind, z_at, d, src).wait_send()

        if condition is None:
            start()
            self.ends.append(end)
        else:
            pl.when(condition)(start)
            self.ends.append(lambda: pl.when(condition)(end))

    def across(self, p, d):
        for z_at in range(4):
            ref = self.spot(p, z_at, d)
            copy = pltpu.make_async_remote_copy(
                src_ref=ref,
                dst_ref=ref,
                send_sem=self.send_s.at[p, d, z_at],
                recv_sem=self.recv_s.at[p, d, z_at],
                device_id=self.sib,
                device_id_type=MESH_ID,
            )
            copy.start()
            self.ends.append(copy.wait_send)

    def arrive(self, p, kind, z_at, d):
        ref = self.spot(p, z_at, d)
        pltpu.make_async_copy(ref, ref, self.recv.at[p, kind, z_at]).wait()

    def own(self, p):
        i, first, rows = self.pieces[p]
        src = self.shards[i].at[pl.ds(first, rows)]
        z = self.z
        self.go(z < 3, p, 0, z, 0, src)
        self.go(z > 0, p, 1, z, 0, src)
        self.go(None, p, 2, z, 0, src)
        self.go(None, p, 3, z, 0, src)
        copy = pltpu.make_async_copy(src, self.spot(p, z, 0), self.local.at[p])
        copy.start()
        self.locals_ = getattr(self, "locals_", {})
        self.locals_[p] = copy

    def z_step(self, p, r):
        z = self.z
        for side in (-1, 1):
            there = (z - r >= 0) if side < 0 else (z + r <= 3)
            z_at = z + side * r

            def landed(z_at=z_at):
                self.arrive(p, 0, z_at, 0)

            pl.when(there)(landed)
            if side < 0:
                self.go(there & (z < 3), p, 0, z_at, 0)
            else:
                self.go(there & (z > 0), p, 1, z_at, 0)
            self.go(there, p, 2, z_at, 0)
            self.go(there, p, 3, z_at, 0)

    def plane_step(self, p, r):
        z = self.z
        for side in (-1, 1) if r else (0,):
            z_at = z + side * r
            there = None if not r else ((z - r >= 0) if side < 0 else (z + r <= 3))

            def landed(z_at=z_at):
                self.arrive(p, 1, z_at, 1)
                self.arrive(p, 2, z_at, 2)

            if there is None:
                landed()
            else:
                pl.when(there)(landed)
            low_z, high_z = z_at < 2, z_at >= 2
            self.go(low_z if there is None else there & low_z, p, 4, z_at, 1)
            self.go(high_z if there is None else there & high_z, p, 4, z_at, 2)

    def stage(self, p, s):
        if s == 0:
            self.own(p)
        elif s == 1:
            self.z_step(p, 1)
            self.plane_step(p, 0)
        elif s == 2:
            self.z_step(p, 2)
            self.plane_step(p, 1)
        elif s == 3:
            self.z_step(p, 3)
            self.locals_[p].wait()
            self.across(p, 0)
            self.plane_step(p, 2)
        elif s == 4:
            self.plane_step(p, 3)
            self.across(p, 1)
            self.across(p, 2)
        elif s == 5:
            for z_at in range(4):
                self.arrive(p, 3, z_at, 3)
            self.across(p, 3)

    STAGES = 6

    def steps(self):
        return len(self.pieces) + self.STAGES - 1

    def run(self, t):
        for s in range(self.STAGES):
            if 0 <= t - s < len(self.pieces):
                self.stage(t - s, s)

    def landed(self, which=None):
        for p in range(len(self.pieces)) if which is None else which:
            for d in range(4):
                for z_at in range(4):
                    ref = self.spot(p, z_at, d, 1 - self.core)
                    pltpu.make_async_copy(ref, ref, self.recv_s.at[p, d, z_at]).wait()

    def finish(self):
        for end in self.ends:
            end()


def pieces_of(shards, splits):
    pieces = []
    for i, (shard, split) in enumerate(zip(shards, splits)):
        rows = shard.shape[0] // split
        pieces += [(i, j * rows, rows) for j in range(split)]
    return pieces


class Exchange:
    def __init__(self, out, landed, sems):
        self.out, self.landed = out, landed
        self.send, self.recv = sems
        self.core, z, yx = place()
        self.wide = z * 4 + yx

    def copy(self, w):
        return pltpu.make_async_remote_copy(
            src_ref=self.out.at[w],
            dst_ref=self.landed.at[self.wide],
            send_sem=self.send.at[w],
            recv_sem=self.recv.at[self.wide],
            device_id=(self.core, w),
            device_id_type=MESH_ID,
        )

    def push(self, w):
        pl.when(w != self.wide)(lambda: self.copy(w).start())

        def keep():
            self.landed[w] = self.out[w]

        pl.when(w == self.wide)(keep)

    def wait(self, w):
        def landed():
            ref = self.landed.at[w]
            pltpu.make_async_copy(ref, ref, self.recv.at[w]).wait()

        pl.when(w != self.wide)(landed)

    def finish(self):
        for w in range(16):
            pl.when(w != self.wide)(lambda w=w: self.copy(w).wait_send())


def column_of(row):
    return jnp.broadcast_to(row, (LANES, row.shape[1])).T[:, 0:1]


def exact(left_side, right_side, contract=(1, 0)):
    return lax.dot_general(
        left_side,
        right_side,
        (((contract[0],), (contract[1],)), ((), ())),
        precision=HIGHEST_PRECISION,
        preferred_element_type=jnp.float32,
    )


def gelu(values):
    return 0.5 * values * (1.0 + jnp.tanh(GELU_SCALE * (values + GELU_CUBE * values * values * values)))


def gradient(grads, inputs, out, rows, shard):
    count = rows // shard

    def body(c, carry):
        cols = pl.ds(pl.multiple_of(c * rows, LANES), rows)
        total = nn(grads[0, :, cols].astype(jnp.float32).T.astype(jnp.bfloat16), inputs[0])
        total = total + nn(grads[1, :, cols].astype(jnp.float32).T.astype(jnp.bfloat16), inputs[1])
        first = lax.rem(c * count, 4)
        out[c * count // 4, pl.ds(first, count)] = total.astype(jnp.bfloat16).reshape(count, shard, -1)
        return carry

    return body


def front_kernel(groups, slots, *refs):
    (m_qkv, m_out, m_up, m_down, cond_ref, ada_any, map_ref, embed_ref, vec3_ref, len_ref, squares_ref, tri_ref, pick_ref, rule_ref, cot_ref) = refs[:15]
    (f_qkv, f_out, f_up, f_down, ada_ref, h_ref, kept_any, out32_any, q_any, k_any, kt_any, vt_any, low_ref) = refs[15:28]
    (x_ref, smooth_ref, flags_ref, hot_ref, silu_ref, proj_ref, one_ref, two_ref, pre_any, act_any, p_any) = refs[28:39]
    (w_ref, send_ref, got_ref, back_send, back_got, v_ref, s_ref, load_sem) = refs[39:47]
    (w_ada, silu_own, theirs, ours, ada_in, edge, edge_left, edge_right, wo_ref, wu_ref, dmlp, act_half) = refs[47:59]
    (kept_ref, out32_ref, q_ref, k_ref, kt_ref, vt_ref, pre_ref, act_ref, p_down) = refs[59:68]
    (c_qkv, c_out, c_up, c_down, s_qkv, s_out, s_up, s_down, cast_sem, store_sem) = refs[68:78]
    sems = refs[78:]
    first_flow = Gather([s_qkv], [f_qkv], sems[:5], pieces_of([s_qkv], FRONT_SPLITS[0]))
    flow = Gather([s_out, s_up, s_down], [f_out, f_up, f_down], sems[5:10], pieces_of([s_out, s_up, s_down], FRONT_SPLITS[1]))
    ada_send, ada_recv = sems[10:12]
    there = Exchange(send_ref, got_ref, sems[12:14])
    home = Exchange(back_send, back_got, sems[14:16])
    ada_sem, sib_s, sib_r, edge_s, edge_r, wo_sem, wu_sem = sems[16:23]
    core, z, yx = place()
    wide = z * 4 + yx
    sib = (1 - core, wide)
    tokens, width = x_ref.shape
    half = width // 2
    mid = tokens // 2
    two = 2 * tokens
    group_len = q_ref.shape[0]
    f32, low = jnp.float32, jnp.bfloat16
    vec_ref = vec3_ref.at[1]
    casts = []
    for i, (src, dst) in enumerate(((m_qkv, c_qkv), (m_out, c_out), (m_up, c_up), (m_down, c_down))):
        casts.append(pltpu.make_async_copy(src.at[1], dst, cast_sem.at[i]))
        casts[-1].start()
    stores = []

    def store(*pairs):
        for src, dst in pairs:
            stores.append(pltpu.make_async_copy(src, dst, store_sem.at[len(stores)]))
            stores[-1].start()

    casts[0].wait()
    s_qkv[...] = c_qkv[...].astype(low)
    entry_barrier([(core, wide ^ r) for r in range(1, 16)] + [sib])

    def to_sib(slot, src, dst):
        copy = pltpu.make_async_remote_copy(
            src_ref=src, dst_ref=dst, send_sem=sib_s.at[slot], recv_sem=sib_r.at[slot], device_id=sib, device_id_type=MESH_ID
        )
        copy.start()
        return copy

    next_tick = [0]

    def tick(n):
        for _ in range(n):
            if next_tick[0] < flow.steps():
                flow.run(next_tick[0])
                next_tick[0] += 1

    def tick_to(n):
        tick(max(0, n - next_tick[0]))

    first_flow.run(0)
    ada_copy = pltpu.make_async_copy(ada_any.at[1], w_ada, ada_sem)
    ada_copy.start()
    cond = cond_ref[...]
    silu = (cond / (1.0 + jnp.exp(-cond))).astype(low).astype(f32)
    silu_own[...] = jnp.zeros_like(silu_own)
    silu_own[0:slots, :] = silu
    their_half = pl.ds(pl.multiple_of((1 - core) * half, half), half)
    my_half = pl.ds(pl.multiple_of(core * half, half), half)
    silu_copy = to_sib(0, silu_own.at[:, their_half], silu_ref.at[core])
    silu_ref[core] = silu_own[:, my_half]
    spot = lane_iota((32, LANES))
    cells = map_ref[...]
    edge[...] = jnp.where(spot == 0, cells[:, 0:1], jnp.where(spot == 1, cells[:, tokens - 1 : tokens], 0.0))

    def edge_copy(slot, dst, shift):
        return pltpu.make_async_remote_copy(
            src_ref=edge,
            dst_ref=dst,
            send_sem=edge_s.at[slot],
            recv_sem=edge_r.at[slot],
            device_id=(core, lax.rem(wide + shift, 16)),
            device_id_type=MESH_ID,
        )

    edges = [edge_copy(0, edge_left, 1), edge_copy(1, edge_right, 15)]
    for copy in edges:
        copy.start()
    first_flow.run(1)

    for copy in casts[1:]:
        copy.wait()
    s_out[...] = c_out[...].astype(low)
    s_up[...] = c_up[...].T.astype(low)
    s_down[...] = c_down[...].astype(low)

    run_lane = lane_iota((1, LANES))
    run_slot = lax.rem(run_lane - HALF_LANES + slots * LANES, slots)
    lens = jnp.zeros((1, LANES), jnp.int32)
    for j in range(slots):
        lens = jnp.where(run_slot == j, len_ref[0:1, j : j + 1], lens)
    counts = jnp.where(lens == LONG_TOTAL, squares_ref[0:1, :], jnp.where(lens == SHORT_TOTAL, squares_ref[1:2, :], 0.0))
    unused = group_len - jnp.sum(counts, axis=1, keepdims=True)
    counts = jnp.where(run_lane == HALF_LANES + slots * LEVELS, unused, counts)
    ends = exact(jnp.broadcast_to(counts, (8, LANES)), tri_ref[...])[0:1, :]
    starts = ends - counts
    start_col, end_col = column_of(starts), column_of(ends)
    here = (wide * tokens + lane_iota((1, tokens))).astype(f32)
    left = 1.0 - jnp.sum(((here == start_col) & (here < end_col)).astype(f32), axis=0, keepdims=True)
    right = 1.0 - jnp.sum(((here == end_col - 1.0) & (here >= start_col)).astype(f32), axis=0, keepdims=True)
    flags_ref[...] = jnp.zeros_like(flags_ref)
    flags_ref[0:1, :] = left
    flags_ref[1:2, :] = right
    row_at = (wide * tokens + lax.broadcasted_iota(jnp.int32, (tokens, LANES), 0)).astype(f32)
    my_runs = ((row_at >= starts) & (row_at < ends)).astype(low)
    hot = nn(my_runs, pick_ref[...])[:, 0:8]
    hot_ref[...] = hot

    ada_copy.wait()
    w_low = w_ada[...].astype(low)
    silu_copy.wait_recv()
    theirs[...] = nn(silu_ref[1 - core].astype(low), w_low)
    part_copy = to_sib(1, theirs, ours)
    mine = nn(silu_ref[core].astype(low), w_low)
    first_flow.run(2)

    for copy in edges:
        copy.wait_recv()
    column = lane_iota((32, tokens))
    before = jnp.where(column == 0, edge_left[:, 1:2], jnp.roll(cells, 1, axis=1))
    after = jnp.where(column == tokens - 1, edge_right[:, 0:1], jnp.roll(cells, -1, axis=1))
    smooth = smooth_map(cells, left, right, before, after)
    smooth_ref[...] = smooth
    x = exact(smooth, embed_ref[1], (0, 0)) + vec_ref[6:7, :]
    x_ref[...] = x
    part_copy.wait_recv()
    ada_in[...] = mine + ours[...]
    ada_copies = []
    for r in range(1, 16):
        copy = pltpu.make_async_remote_copy(
            src_ref=ada_in,
            dst_ref=ada_ref.at[wide],
            send_sem=ada_send.at[r],
            recv_sem=ada_recv.at[r],
            device_id=(core, wide ^ r),
            device_id_type=MESH_ID,
        )
        copy.start()
        ada_copies.append(copy)
    ada_ref[wide] = ada_in[...]

    def standard(values):
        centred = values - jnp.mean(values, axis=1, keepdims=True)
        return centred * lax.rsqrt(jnp.mean(centred * centred, axis=1, keepdims=True) + NORM_EPS)

    unit = standard(x)
    first_flow.run(3)
    for copy in ada_copies:
        copy.wait_recv()
    ada = jnp.concatenate([ada_ref[w] for w in range(16)], axis=1)

    def of_tokens(block):
        return exact(hot, ada[:, block * width : (block + 1) * width] + vec_ref[block : block + 1, :])

    h_ref[...] = (unit * (1.0 + of_tokens(2)) + of_tokens(4)).astype(low)
    for i, t in enumerate(range(4, first_flow.steps())):
        first_flow.run(t)
        tick(FRONT_TICKS[0][min(i, 3)])
    first_flow.landed()

    group = 256
    loads = []

    def load(j):
        g = lax.rem(z + 1 + j, 4)
        out = []
        for c in range(2):
            for part in range(3):
                rows = pl.ds(pl.multiple_of(g * group + part * width, group), group)
                out.append(pltpu.make_async_copy(f_qkv.at[c, rows], w_ref.at[j, c, part], load_sem.at[j, c, part]))
        return out

    for j in range(4):
        loads.append(load(j))
        for copy in loads[-1]:
            copy.start()
    lane = lane_iota((tokens, LANES))
    lane_mid = lane_iota((mid, LANES))
    for j in range(4):
        g = lax.rem(z + 1 + j, 4)
        first = pl.multiple_of(g * group, group)
        for copy in loads[j]:
            copy.wait()

        def project(part):
            return nt(h_ref[:, :half], w_ref[j, 0, part]) + nt(h_ref[:, half:], w_ref[j, 1, part])

        q_all, k_all, v_all = (project(part) for part in range(3))
        for pair in range(group // LANES):
            cols = slice(pair * LANES, (pair + 1) * LANES)
            at = g * (group // LANES) + pair
            kept_ref[at] = q_all[:, cols]
            kept_ref[at + width // LANES] = k_all[:, cols]
        q_all = q_all * lax.rsqrt(head_sums(q_all * q_all) + NORM_EPS)
        q_all = q_all * (8.0 * (1.0 + vec_ref[7:8, pl.ds(first, group)]))
        k_all = k_all * lax.rsqrt(head_sums(k_all * k_all) + NORM_EPS)
        for pair in range(group // LANES):
            cols = slice(pair * LANES, (pair + 1) * LANES)
            q, k, v = q_all[:, cols], k_all[:, cols], v_all[:, cols]
            head = g * (group // HALF_LANES) + 2 * pair
            send_ref[head, 0:tokens, :] = jnp.where(lane < HALF_LANES, q, swap_halves(k)).astype(low)
            send_ref[head + 1, 0:tokens, :] = jnp.where(lane < HALF_LANES, swap_halves(q), k).astype(low)
            v_a, v_b = v[:mid], v[mid:]
            send_ref[head, tokens:, :] = jnp.where(lane_mid < HALF_LANES, v_a, swap_halves(v_b)).astype(low)
            send_ref[head + 1, tokens:, :] = jnp.where(lane_mid < HALF_LANES, swap_halves(v_a), v_b).astype(low)
        for e in range(4):
            there.push(g * 4 + e)
        tick(FRONT_TICKS[1][j])

    lane_two = lane_iota((two, LANES))

    def unpack(pair, carry):
        for e in range(2):
            there.wait(2 * pair + e)
        first = pl.multiple_of(pair * two, two)
        qk = jnp.concatenate([got_ref[2 * pair + e, 0:tokens, :].astype(f32) for e in range(2)], axis=0)
        spot = (first + lax.broadcasted_iota(jnp.int32, (two, LANES), 0)).astype(f32)
        runs = ((spot >= starts) & (spot < ends)).astype(f32)
        barred = nn(runs.astype(low), rule_ref[...])
        rows = pl.ds(first, two)
        q_ref[rows, :] = jnp.where(lane_two < HALF_LANES, qk, barred).astype(low)
        tail = jnp.where(lane_two >= LANES - 3, 1.0, runs)
        keys = jnp.where(lane_two < HALF_LANES, swap_halves(qk), tail)
        k_ref[rows, :] = keys.astype(low)
        kt_ref[:, rows] = keys.T.astype(low)
        ones = ((lane_mid >= HALF_LANES) & (lane_mid < HALF_LANES + 3)).astype(f32)
        pieces = []
        for e in range(2):
            v = got_ref[2 * pair + e, tokens:, :].astype(f32)
            pieces.append(jnp.where(lane_mid < HALF_LANES, v, ones))
            pieces.append(jnp.where(lane_mid < HALF_LANES, swap_halves(v), ones))
        values = jnp.concatenate(pieces, axis=0)
        v_ref[rows, :] = values.astype(low)
        vt_ref[:, rows] = values.T.astype(low)
        return carry

    lane_q = lane_iota((ROWS, LANES))

    def query_block(limit, b, carry):
        rows = pl.ds(pl.multiple_of(b * ROWS, ROWS), ROWS)
        q = q_ref[rows, :]

        def score(c, top):
            cols = pl.ds(pl.multiple_of(c * CHUNK, CHUNK), CHUNK)
            s = nn(q, kt_ref[:, cols])
            s_ref[:, cols] = s
            return jnp.maximum(top, fold_lanes(s, jnp.maximum))

        whole, left = limit // CHUNK, limit % CHUNK
        top = lax.fori_loop(0, whole, score, jnp.full((ROWS, LANES), -3e38, f32))
        if left:
            tail = slice(whole * CHUNK, limit)
            s = nn(q, kt_ref[:, tail])
            s_ref[:, tail] = s
            top = jnp.maximum(top, fold_lanes(s, jnp.maximum))
        peak = jnp.max(top, axis=1, keepdims=True)

        def weigh(cols, carry):
            total, acc = carry
            p = jnp.exp(s_ref[:, cols] - peak)
            return total + fold_lanes(p, jnp.add), acc + nn(p.astype(low), v_ref[cols, :])

        zero = jnp.zeros((ROWS, LANES), f32)
        total, acc = lax.fori_loop(
            0,
            whole,
            lambda c, carry: weigh(pl.ds(pl.multiple_of(c * CHUNK, CHUNK), CHUNK), carry),
            (zero, zero),
        )
        if left:
            total, acc = weigh(slice(whole * CHUNK, limit), (total, acc))
        total = jnp.sum(total, axis=1, keepdims=True)
        out32_ref[rows, :] = acc / total
        log_total = peak + jnp.log(total)
        q_ref[rows, :] = lanes_three(lane_q, LANES - 3, -log_total, q.astype(f32)).astype(low)
        return carry

    def give_back(w, carry):
        rows = pl.multiple_of(w * tokens, tokens)
        a = out32_ref[pl.ds(rows, mid), :]
        b = out32_ref[pl.ds(pl.multiple_of(rows + mid, mid), mid), :]
        back_send[w] = jnp.where(lane_mid < HALF_LANES, a, swap_halves(b)).astype(low)
        home.push(w)
        return carry

    store((kept_ref, kept_any))
    for i in range(4):
        lax.fori_loop(2 * i, 2 * i + 2, unpack, 0)
        tick(FRONT_TICKS[2][i])
    store((k_ref, k_any), (kt_ref, kt_any), (vt_ref, vt_any))
    plane = 4 * tokens // ROWS
    for p in range(4):
        for first, last, limit in groups:
            begin, end = max(first, p * plane), min(last, (p + 1) * plane)
            for b in range(begin, end):
                lax.fori_loop(b, b + 1, functools.partial(query_block, limit), 0)
                tick(FRONT_TICKS[3][b])
        lax.fori_loop(4 * p, 4 * p + 4, give_back, 0)
    store((q_ref, q_any), (out32_ref, out32_any))
    splits = FRONT_SPLITS[1]
    tick_to(splits[0] + 5)
    flow.landed(range(splits[0]))
    wo_copy = pltpu.make_async_copy(f_out, wo_ref, wo_sem)
    wo_copy.start()
    for pair in range(8):
        home.wait(2 * pair)
        home.wait(2 * pair + 1)
        cols = slice(pair * LANES, (pair + 1) * LANES)
        even, odd = back_got[2 * pair].astype(f32), back_got[2 * pair + 1].astype(f32)
        low_ref[0:mid, cols] = jnp.where(lane_mid < HALF_LANES, even, swap_halves(odd)).astype(low)
        low_ref[mid:, cols] = jnp.where(lane_mid < HALF_LANES, swap_halves(even), odd).astype(low)

    wo_copy.wait()
    proj = nt(low_ref[:, :half], wo_ref[0]) + nt(low_ref[:, half:], wo_ref[1])
    proj_ref[...] = proj
    x_one = x_ref[...] + of_tokens(0) * proj
    one_ref[...] = x_one
    two_ref[...] = (standard(x_one) * (1.0 + of_tokens(3)) + of_tokens(5)).astype(low)
    tick_to(splits[0] + splits[1] + 5)
    flow.landed(range(splits[0], splits[0] + splits[1]))
    step = 512
    hidden = pre_ref.shape[1]

    def load_up(c):
        rows = pl.ds(pl.multiple_of(c * step, step), step)
        slot = lax.rem(c, 2)
        return pltpu.make_async_copy(f_up.at[:, rows], wu_ref.at[slot], wu_sem.at[slot])

    load_up(0).start()

    def up_step(c, carry):
        pl.when(c + 1 < hidden // step)(lambda: load_up(c + 1).start())
        load_up(c).wait()
        w = wu_ref.at[lax.rem(c, 2)]
        pre = nt(two_ref[:, :half], w[0]) + nt(two_ref[:, half:], w[1])
        cols = pl.ds(pl.multiple_of(c * step, step), step)
        pre_ref[:, cols] = pre
        act_ref[:, cols] = gelu(pre).astype(low)
        return carry

    live = jnp.sum(hot, axis=1, keepdims=True)
    dmlp[core] = (of_tokens(1) * (cot_ref[...].astype(f32) * live)).astype(low)
    pair_copies = [to_sib(2, dmlp.at[core], dmlp.at[core])]
    hid_half = hidden // 2
    hid_theirs = pl.ds(pl.multiple_of((1 - core) * hid_half, hid_half), hid_half)
    hid_mine = pl.ds(pl.multiple_of(core * hid_half, hid_half), hid_half)
    for i in range(2):
        lax.fori_loop(4 * i, 4 * i + 4, up_step, 0)
        tick(FRONT_TICKS[4][i])
    store((pre_ref, pre_any), (act_ref, act_any))
    pair_copies.append(to_sib(3, act_ref.at[:, hid_theirs], act_half.at[core]))
    act_half[core] = act_ref[:, hid_mine]
    tick(FRONT_TICKS[4][2])
    for copy in pair_copies:
        copy.wait_recv()
    lax.fori_loop(0, width // LANES, gradient(dmlp, act_half, p_down, LANES, width // 16), 0)
    store((p_down, p_any))
    tick(flow.steps())
    flow.landed(range(splits[0] + splits[1], sum(splits)))
    first_flow.finish()
    flow.finish()
    there.finish()
    home.finish()
    for copy in ada_copies + edges + pair_copies + [silu_copy, part_copy]:
        copy.wait_send()
    for copy in stores:
        copy.wait()


def front(states, condition, ada_state, cells, embed_state, vector_state, lengths, tables, cotangent, groups):
    width = condition.shape[1]
    tokens = cells.shape[1]
    slots = lengths.shape[1]
    group_len = 16 * tokens
    hidden = 16 * states[2].shape[2]
    f32, low = jnp.float32, jnp.bfloat16
    dma = pltpu.SemaphoreType.DMA
    shape = jax.ShapeDtypeStruct
    ada_width = ada_state.shape[2]
    shards = [s.shape[1:] if i != 2 else s.shape[:0:-1] for i, s in enumerate(states)]
    fulls = [shape((2, 16 * s[0], s[1]), low) for s in shards]
    outs = fulls + [
        shape((16, 8, ada_width), f32),
        shape((tokens, width), low),
        shape((2 * width // LANES, tokens, LANES), f32),
        shape((group_len, LANES), f32),
        shape((group_len, LANES), low),
        shape((group_len, LANES), low),
        shape((LANES, group_len), low),
        shape((LANES, group_len), low),
        shape((tokens, width), low),
        shape((tokens, width), f32),
        shape(cells.shape, f32),
        shape((8, tokens), f32),
        shape((tokens, 8), f32),
        shape((2, 8, width // 2), f32),
        shape((tokens, width), f32),
        shape((tokens, width), f32),
        shape((tokens, width), low),
        shape((tokens, hidden), f32),
        shape((tokens, hidden), low),
        shape((4, 4, width // 16, hidden // 2), low),
    ]
    packed, mid = tokens * 3 // 2, tokens // 2
    scratch = [
        pltpu.VMEM((4, 2, 3, 256, width // 2), low),
        pltpu.VMEM((16, packed, LANES), low),
        pltpu.VMEM((16, packed, LANES), low),
        pltpu.VMEM((16, mid, LANES), low),
        pltpu.VMEM((16, mid, LANES), low),
        pltpu.VMEM((group_len, LANES), low),
        pltpu.VMEM((ROWS, group_len), f32),
        dma((4, 2, 3)),
        pltpu.VMEM(ada_state.shape[1:], f32),
        pltpu.VMEM((8, width), f32),
        pltpu.VMEM((8, ada_width), f32),
        pltpu.VMEM((8, ada_width), f32),
        pltpu.VMEM((8, ada_width), f32),
        pltpu.VMEM((32, LANES), f32),
        pltpu.VMEM((32, LANES), f32),
        pltpu.VMEM((32, LANES), f32),
        pltpu.VMEM((2, width, width // 2), low),
        pltpu.VMEM((2, 2, 512, width // 2), low),
        pltpu.VMEM((2, tokens, width), low),
        pltpu.VMEM((2, tokens, hidden // 2), low),
    ]
    scratch += [pltpu.VMEM(o.shape, o.dtype) for o in outs[6:12] + outs[21:24]]
    scratch += [pltpu.VMEM(s.shape[1:], f32) for s in states] + [pltpu.VMEM(s, low) for s in shards]
    scratch += [dma((4,)), dma((10,))]
    scratch += Gather.scratch(sum(FRONT_SPLITS[0])) + Gather.scratch(sum(FRONT_SPLITS[1])) + [dma((16,)) for _ in range(6)]
    scratch += [dma, dma((4,)), dma((4,)), dma((2,)), dma((2,)), dma, dma((2,))]
    return pl.pallas_call(
        functools.partial(front_kernel, groups, slots),
        out_shape=outs,
        in_specs=[ANY] * 4 + [VM, ANY] + [VM] * 9,
        out_specs=[ANY] * 4 + [VM] * 2 + [ANY] * 6 + [VM] * 9 + [ANY] * 3,
        scratch_shapes=scratch,
        compiler_params=pltpu.CompilerParams(
            collective_id=0, has_side_effects=True, vmem_limit_bytes=VMEM_BYTES
        ),
    )(*states, condition, ada_state, cells, embed_state, vector_state, lengths, *tables, cotangent)


class Scatter:
    STAGES = 6

    def __init__(self, parts, outs, bufs, sems, pieces):
        self.parts, self.outs, self.bufs, self.pieces = parts, outs, bufs, pieces
        self.send, self.recv = sems
        self.parts_left = {}
        core, z, yx = place()
        self.z, self.yx = z, yx
        self.x_dev, self.y_dev = at_dev(core, z, yx ^ 1), at_dev(core, z, yx ^ 2)
        self.up_dev, self.down_dev = at_dev(core, lax.min(z + 1, 3), yx), at_dev(core, lax.max(z - 1, 0), yx)
        self.ends = []

    @staticmethod
    def scratch(shapes, count):
        low = jnp.bfloat16
        out = []
        for rows, cols in shapes:
            out += [pltpu.VMEM((depth, rows, cols), low) for depth in (2, 2, 4, 4, 3, 3)]
        dma = pltpu.SemaphoreType.DMA
        return out + [dma((count, 8)), dma((count, 8))]

    def push(self, p, slot, src, dst, device):
        copy = pltpu.make_async_remote_copy(
            src_ref=src,
            dst_ref=dst,
            send_sem=self.send.at[p, slot],
            recv_sem=self.recv.at[p, slot],
            device_id=device,
            device_id_type=MESH_ID,
        )
        copy.start()
        return copy

    def arrive(self, p, slot, ref):
        pltpu.make_async_copy(ref, ref, self.recv.at[p, slot]).wait()

    def stage(self, p, s):
        i, first, rows = self.pieces[p]
        rows = pl.ds(first, rows)
        part = self.parts[i]
        names = ("turn_x", "turn_y", "rx", "ry", "up", "down")
        buf = dict(zip(names, self.bufs[6 * i : 6 * i + 6]))
        z, yx = self.z, self.yx
        f32, low = jnp.float32, jnp.bfloat16
        lo2, hi2 = pl.ds(0, 2), pl.ds(2, 2)

        def view(name, which):
            return buf[name].at[which, rows]

        def wide(ref):
            return ref[...].astype(f32)

        def hop(condition, slot, name, which, device):
            ref = view(name, which)

            def start():
                self.push(p, slot, ref, ref, device)

            def end():
                pltpu.make_async_copy(ref, ref, self.send.at[p, slot]).wait()

            pl.when(condition)(start)
            self.ends.append(lambda: pl.when(condition)(end))

        if s == 0:
            copies = [
                self.push(p, 0, part.at[lo2, yx ^ 3, rows], view("turn_x", lo2), self.x_dev),
                self.push(p, 1, part.at[hi2, yx ^ 3, rows], view("turn_y", lo2), self.y_dev),
                self.push(p, 2, part.at[lo2, yx ^ 1, rows], view("rx", lo2), self.x_dev),
                self.push(p, 3, part.at[hi2, yx ^ 2, rows], view("ry", hi2), self.y_dev),
            ]
            self.parts_left[p] = [copy.wait_send for copy in copies]
        elif s == 1:
            turn = view("turn_x", lo2)
            self.arrive(p, 0, turn)
            turn[...] = (wide(part.at[lo2, yx ^ 2, rows]) + wide(turn)).astype(low)
            self.ends.append(self.push(p, 4, turn, view("ry", lo2), self.y_dev).wait_send)
            turn = view("turn_y", lo2)
            self.arrive(p, 1, turn)
            turn[...] = (wide(part.at[hi2, yx ^ 1, rows]) + wide(turn)).astype(low)
            self.ends.append(self.push(p, 5, turn, view("rx", hi2), self.x_dev).wait_send)
        elif s == 2:
            self.arrive(p, 2, view("rx", lo2))
            self.arrive(p, 3, view("ry", hi2))
            self.arrive(p, 4, view("ry", lo2))
            self.arrive(p, 5, view("rx", hi2))
            self.outs[i][rows] = wide(part.at[z, yx, rows]) + wide(view("rx", z)) + wide(view("ry", z))
            for z_at in range(4):
                total = wide(part.at[z_at, yx, rows]) + wide(view("rx", z_at)) + wide(view("ry", z_at))
                view("rx", z_at)[...] = total.astype(low)

            def first_up():
                view("up", pl.ds(0, 3))[...] = view("rx", pl.ds(1, 3))[...]

            def first_down():
                view("down", pl.ds(0, 3))[...] = view("rx", pl.ds(0, 3))[...]

            pl.when(z == 0)(first_up)
            hop(z == 0, 6, "up", pl.ds(0, 3), self.up_dev)
            pl.when(z == 3)(first_down)
            hop(z == 3, 7, "down", pl.ds(0, 3), self.down_dev)
        elif s in (3, 4):
            at = s - 2
            count = 3 - at

            def add_up():
                self.arrive(p, 6, view("up", pl.ds(at - 1, count + 1)))
                ref = view("up", pl.ds(at, count))
                ref[...] = (wide(ref) + wide(view("rx", pl.ds(at + 1, count)))).astype(low)

            def add_down():
                self.arrive(p, 7, view("down", pl.ds(0, count + 1)))
                ref = view("down", pl.ds(0, count))
                ref[...] = (wide(ref) + wide(view("rx", pl.ds(0, count)))).astype(low)

            pl.when(z == at)(add_up)
            hop(z == at, 6, "up", pl.ds(at, count), self.up_dev)
            pl.when(z == 3 - at)(add_down)
            hop(z == 3 - at, 7, "down", pl.ds(0, count), self.down_dev)
        else:
            out = self.outs[i].at[rows]

            def end_low():
                self.arrive(p, 7, view("down", pl.ds(0, 1)))
                out[...] += wide(view("down", 0))

            def end_high():
                self.arrive(p, 6, view("up", pl.ds(2, 1)))
                out[...] += wide(view("up", 2))

            def end_inner(at):
                out[...] += wide(view("up", at - 1)) + wide(view("down", at))

            pl.when(z == 0)(end_low)
            pl.when(z == 1)(lambda: end_inner(1))
            pl.when(z == 2)(lambda: end_inner(2))
            pl.when(z == 3)(end_high)

    def steps(self):
        return len(self.pieces) + self.STAGES - 1

    def run(self, t):
        for s in reversed(range(self.STAGES)):
            if 0 <= t - s < len(self.pieces):
                self.stage(t - s, s)

    def sent(self, p):
        for end in self.parts_left.pop(p, ()):
            end()

    def finish(self):
        for p in list(self.parts_left):
            self.sent(p)
        for end in self.ends:
            end()


COMMON_ROWS = 48
FRONT_SPLITS = ((2,), (1, 4, 4))
FRONT_TICKS = ((1, 1, 1, 0), (0, 1, 0, 1), (0, 1, 0, 1), (0, 0, 0, 0, 0, 1, 0, 0, 1, 0, 0, 1), (1, 1, 1))
BACK_SPLITS = ((4, 4, 1), (3,))
BACK_TICKS = ((1, 1, 1, 1), (1, 0), (0, 0, 1, 0), (0, 0, 0, 0, 0, 1, 0, 0, 1, 0, 0, 1), (1, 1, 1), (1, 1))


def standard_of(values):
    centred = values - jnp.mean(values, axis=1, keepdims=True)
    rstd = lax.rsqrt(jnp.mean(centred * centred, axis=1, keepdims=True) + NORM_EPS)
    return centred * rstd, rstd


def standard_back(unit, rstd, d_unit):
    along = jnp.mean(d_unit * unit, axis=1, keepdims=True)
    return rstd * (d_unit - jnp.mean(d_unit, axis=1, keepdims=True) - unit * along)


def gelu_slope(values):
    square = values * values
    inner = jnp.tanh(GELU_SCALE * (values + GELU_CUBE * values * square))
    slope = GELU_SCALE * (1.0 + 3.0 * GELU_CUBE * square)
    return 0.5 * (1.0 + inner) + 0.5 * values * (1.0 - inner * inner) * slope


def back_kernel(groups, splits, *refs):
    (
        cot_ref, hot_ref, ada_in, vec3_ref, x_ref, one_ref, proj_ref, h_any, two_any, low_any, act_any, pre_any,
        w_any, wo_any, wu_any, wd_any, book_any, out32_any, q_any, k_any, kt_any, vt_any, kept_any,
        smooth_ref, embed_ref, ok_ref, p_any,
    ) = refs[:27]
    (o_down, o_up, o_out, o_qkv, ada_both, common_all, bias_all, map_ref, block_ref) = refs[27:36]
    (
        send_ref, got_ref, back_send, back_got, g_ref, gt_ref, qt_ref, dq_ref, dkt_ref, dvt_ref,
        w_buf, dhid, h_both, dh_ref, ada_ref, com_ref, ada_land, com_land, ada_sum, com_sum, ada_sib, com_sib,
        bias_own, com_own, edge, edge_left, edge_right,
        dmlp, two_half, low_half, dattn, mlp_ref, dx_one, act_buf, pre_buf, d_att, p_up, p_out, p_down, q_ref, k_ref, kt_ref, vt_ref, early_sem,
    ) = refs[36:80]
    rest = refs[80:]
    flow_bufs, rest = rest[:18], rest[18:]
    flow_sems, rest = rest[:2], rest[2:]
    last_bufs, rest = rest[:6], rest[6:]
    last_sems, rest = rest[:2], rest[2:]
    (
        ex_s, ex_r, home_s, home_r, w_sem, sib_s, sib_r, small_s, small_r, spread_s, spread_r, edge_s, edge_r,
        hid_s, hid_r, half_sem, kept_sem, free_sem,
    ) = rest
    core, z, yx = place()
    wide = z * 4 + yx
    sib = (1 - core, wide)
    f32, low = jnp.float32, jnp.bfloat16
    tokens, width = x_ref.shape
    half = width // 2
    hidden = dhid.shape[2]
    mid = tokens // 2
    two = 2 * tokens
    step = 512
    vec_ref = vec3_ref.at[1]
    dproj = dhid.at[:, :, pl.ds(0, 3 * width)]
    p_qkv = p_up.at[:, :, pl.ds(0, tokens)]
    flow = Scatter([p_down, p_up, p_out], [o_down, o_up, o_out], flow_bufs, flow_sems, splits[0])
    last = Scatter([p_qkv], [o_qkv], last_bufs, last_sems, splits[1])
    there = Exchange(back_send, back_got, (ex_s, ex_r))
    home = Exchange(send_ref, got_ref, (home_s, home_r))
    early = [
        pltpu.make_async_copy(src, dst, early_sem.at[i])
        for i, (src, dst) in enumerate(
            [(p_any, p_down), (q_any, q_ref), (k_any, k_ref), (kt_any, kt_ref), (vt_any, vt_ref)]
        )
    ]
    for copy in early:
        copy.start()
    entry_barrier([(core, wide ^ r) for r in range(1, 16)] + [sib])

    def to_sib(slot, src, dst):
        copy = pltpu.make_async_remote_copy(
            src_ref=src, dst_ref=dst, send_sem=sib_s.at[slot], recv_sem=sib_r.at[slot], device_id=sib, device_id_type=MESH_ID
        )
        copy.start()
        return copy

    next_tick = [0]

    def tick(n):
        for _ in range(n):
            if next_tick[0] < flow.steps():
                flow.run(next_tick[0])
                next_tick[0] += 1

    lane = lane_iota((two, LANES))
    lane_tok = lane_iota((tokens, LANES))
    lane_mid = lane_iota((mid, LANES))

    def load_chunk(c):
        slot = lax.rem(c, 2)
        cols = pl.ds(pl.multiple_of(c * step, step), step)
        down_cols = pl.ds(pl.multiple_of(lax.rem(c, hidden // 2 // step) * step, step), step)
        down = wd_any.at[c // (hidden // 2 // step)]
        pairs = [
            (down.at[pl.ds(0, half), down_cols], w_buf.at[slot, 0]),
            (down.at[pl.ds(half, half), down_cols], w_buf.at[slot, 1]),
            (wu_any.at[0, cols], w_buf.at[slot, 2]),
            (wu_any.at[1, cols], w_buf.at[slot, 3]),
            (act_any.at[:, cols], act_buf.at[slot]),
            (pre_any.at[:, cols], pre_buf.at[slot]),
        ]
        return [pltpu.make_async_copy(src, dst, w_sem.at[slot, i]) for i, (src, dst) in enumerate(pairs)]

    def start_chunk(c):
        for copy in load_chunk(c):
            copy.start()

    start_chunk(0)
    out32_copy = pltpu.make_async_copy(out32_any, dq_ref, kept_sem)
    out32_copy.start()
    theirs = pl.ds(pl.multiple_of((1 - core) * half, half), half)
    mine = pl.ds(pl.multiple_of(core * half, half), half)
    ada = jnp.concatenate([ada_in[w] for w in range(16)], axis=1)
    hot = hot_ref[...]

    def of_tokens(block):
        return exact(hot, ada[:, block * width : (block + 1) * width] + vec_ref[block : block + 1, :])

    live = jnp.sum(hot, axis=1, keepdims=True)
    gate_two = of_tokens(1)
    dmlp[...] = (gate_two * (cot_ref[...].astype(f32) * live)).astype(low)
    sib_copies = [
        to_sib(2, two_any.at[:, theirs], two_half.at[core]),
        to_sib(3, low_any.at[:, theirs], low_half.at[core]),
        to_sib(4, h_any.at[:, theirs], h_both.at[core]),
    ]
    half_copies = [
        pltpu.make_async_copy(src, dst.at[core], half_sem.at[i])
        for i, (src, dst) in enumerate(
            [
                (two_any.at[:, mine], two_half),
                (low_any.at[:, mine], low_half),
                (h_any.at[:, mine], h_both),
            ]
        )
    ]
    for copy in half_copies:
        copy.start()
    mlp_ref[...] = jnp.zeros_like(mlp_ref)
    dh_ref[...] = jnp.zeros_like(dh_ref)

    def hid_copy(c):
        cols = pl.ds(pl.multiple_of(c * step, step), step)
        return pltpu.make_async_remote_copy(
            src_ref=dhid.at[core, :, cols],
            dst_ref=dhid.at[core, :, cols],
            send_sem=hid_s.at[c],
            recv_sem=hid_r.at[c],
            device_id=sib,
            device_id_type=MESH_ID,
        )

    def hidden_step(c, carry):
        pl.when(c + 1 < hidden // step)(lambda: start_chunk(c + 1))
        for copy in load_chunk(c):
            copy.wait()
        slot = lax.rem(c, 2)
        w = w_buf.at[slot]
        d_act = nn(dmlp[:, :half], w[0]) + nn(dmlp[:, half:], w[1])
        d_hid = (d_act * gelu_slope(pre_buf[slot])).astype(low)
        dhid[core, :, pl.ds(pl.multiple_of(c * step, step), step)] = d_hid
        hid_copy(c).start()
        act = act_buf[slot]
        mlp_ref[:, :half] += nt(act, w[0])
        mlp_ref[:, half:] += nt(act, w[1])
        dh_ref[:, :half] += nn(d_hid, w[2])
        dh_ref[:, half:] += nn(d_hid, w[3])
        return carry

    chunks = hidden // step
    early[0].wait()
    for i in range(4):
        tick(BACK_TICKS[0][i])
        lax.fori_loop(2 * i, 2 * i + 2, hidden_step, 0)

    wo_copies = [
        pltpu.make_async_copy(wo_any.at[c, pl.ds(r * half, half)], w_buf.at[0, 2 * c + r], w_sem.at[0, 2 * c + r])
        for c in range(2)
        for r in range(2)
    ]
    for copy in wo_copies:
        copy.start()
    unit, rstd = standard_of(one_ref[...])
    g_two = cot_ref[...].astype(f32) * live
    d_one = standard_back(unit, rstd, dh_ref[...] * (1.0 + of_tokens(3))) + g_two
    dx_one[...] = d_one
    dattn[core] = (of_tokens(0) * d_one).astype(low)
    sib_copies.append(to_sib(5, dattn.at[core], dattn.at[core]))
    for copy in wo_copies:
        copy.wait()
    for c in range(2):
        part = nn(dattn[core, :, :half], w_buf[0, 2 * c]) + nn(dattn[core, :, half:], w_buf[0, 2 * c + 1])
        d_att[:, c * half : (c + 1) * half] = part.astype(low)

    def pack(pair, carry):
        cols = pl.ds(pl.multiple_of(pair * LANES, LANES), LANES)
        a, b = d_att[0:mid, cols].astype(f32), d_att[mid:, cols].astype(f32)
        back_send[2 * pair] = jnp.where(lane_mid < HALF_LANES, a, swap_halves(b)).astype(low)
        back_send[2 * pair + 1] = jnp.where(lane_mid < HALF_LANES, swap_halves(a), b).astype(low)
        there.push(2 * pair)
        there.push(2 * pair + 1)
        return carry

    lax.fori_loop(0, 8, pack, 0)

    def per_slot(values):
        return exact(hot, values, (0, 0))

    ada_ref[:, 3 * width : 4 * width] = per_slot(dh_ref[...] * unit)
    ada_ref[:, 5 * width : 6 * width] = per_slot(dh_ref[...])
    ada_ref[:, 0:width] = per_slot(d_one * proj_ref[...])
    ada_ref[:, width : 2 * width] = per_slot(g_two * mlp_ref[...])
    block_ref[...] = (live * (one_ref[...] + gate_two * mlp_ref[...])).astype(low)
    for c in range(chunks):
        hid_copy(c).wait_recv()
    half_copies[0].wait()
    sib_copies[0].wait_recv()
    lax.fori_loop(0, hidden // 256, gradient(dhid, two_half, p_up, 256, hidden // 16), 0)
    for c in range(chunks):
        hid_copy(c).wait_send()
    pl.semaphore_signal(free_sem, inc=1, device_id=sib, device_id_type=MESH_ID)
    tick(BACK_TICKS[1][0])
    half_copies[1].wait()
    sib_copies[1].wait_recv()
    sib_copies[3].wait_recv()
    lax.fori_loop(0, width // LANES, gradient(dattn, low_half, p_out, LANES, width // 16), 0)
    tick(BACK_TICKS[1][1])
    dkt_ref[...] = jnp.zeros_like(dkt_ref)
    dvt_ref[...] = jnp.zeros_like(dvt_ref)

    def unpack(pair, carry):
        there.wait(2 * pair)
        there.wait(2 * pair + 1)
        rows = pl.ds(pl.multiple_of(pair * two, two), two)
        pieces = []
        for e in range(2):
            g = back_got[2 * pair + e].astype(f32)
            pieces += [g, swap_halves(g)]
        grad = jnp.where(lane < HALF_LANES, jnp.concatenate(pieces, axis=0), 0.0)
        delta = jnp.sum(grad * dq_ref[rows, :], axis=1, keepdims=True)
        grad = lanes_three(lane, HALF_LANES, -delta, grad)
        g_ref[rows, :] = grad.astype(low)
        gt_ref[:, rows] = grad.T[:HALF_LANES].astype(low)
        qt_ref[:, rows] = q_ref[rows, :].astype(f32).T[:HALF_LANES].astype(low)
        return carry

    out32_copy.wait()
    for copy in early[1:]:
        copy.wait()
    for i in range(4):
        lax.fori_loop(2 * i, 2 * i + 2, unpack, 0)
        tick(BACK_TICKS[2][i])

    def query_block(limit, b, carry):
        rows = pl.ds(pl.multiple_of(b * ROWS, ROWS), ROWS)
        q, g = q_ref[rows, :], g_ref[rows, :]
        qt, gt = qt_ref[:, rows], gt_ref[:, rows]

        def chunk(cols, acc):
            p = jnp.exp(nn(q, kt_ref[:, cols]))
            ds = (p * nn(g, vt_ref[:, cols])).astype(low)
            dvt_ref[:, cols] += nn(gt, p.astype(low))
            dkt_ref[:, cols] += nn(qt, ds)
            return acc + nn(ds, k_ref[cols, :])

        whole, left = limit // CHUNK, limit % CHUNK
        acc = lax.fori_loop(
            0,
            whole,
            lambda c, acc: chunk(pl.ds(pl.multiple_of(c * CHUNK, CHUNK), CHUNK), acc),
            jnp.zeros((ROWS, LANES), f32),
        )
        if left:
            acc = chunk(slice(whole * CHUNK, limit), acc)
        dq_ref[rows, :] = acc
        return carry

    for first, stop, limit in groups:
        for b in range(first, stop):
            lax.fori_loop(b, b + 1, functools.partial(query_block, limit), 0)
            tick(BACK_TICKS[3][b])

    def send_out(pair, carry):
        rows = pl.ds(pl.multiple_of(pair * two, two), two)
        dkv = jnp.concatenate([dkt_ref[:, rows], dvt_ref[:, rows]], axis=0).T
        qk = jnp.where(lane < HALF_LANES, dq_ref[rows, :], swap_halves(dkv)).astype(low)
        for e in range(2):
            send_ref[2 * pair + e, 0:tokens, :] = qk[e * tokens : (e + 1) * tokens]
            a = dkv[e * tokens : e * tokens + mid]
            b = dkv[e * tokens + mid : (e + 1) * tokens]
            send_ref[2 * pair + e, tokens:, :] = jnp.where(lane_mid < HALF_LANES, swap_halves(a), b).astype(low)
            home.push(2 * pair + e)
        return carry

    lax.fori_loop(0, 8, send_out, 0)

    kept_copy = pltpu.make_async_copy(kept_any, dq_ref, kept_sem)
    kept_copy.start()
    tick(BACK_TICKS[4][0])
    com_ref[...] = jnp.zeros_like(com_ref)

    def load_codes(c):
        slot = lax.rem(c, 2)
        rows = pl.ds(pl.multiple_of(lax.rem(c, chunks) * step, step), step)
        return [
            pltpu.make_async_copy(book_any.at[rows, pl.ds(r * half, half)], w_buf.at[slot, r], w_sem.at[slot, r])
            for r in range(2)
        ]

    def start_codes(c):
        for copy in load_codes(c):
            copy.start()

    start_codes(0)

    def logits_of(c):
        pl.when(c + 1 < 2 * chunks)(lambda: start_codes(c + 1))
        for copy in load_codes(c):
            copy.wait()
        w = w_buf.at[lax.rem(c, 2)]
        return nt(block_ref[:, :half], w[0]) + nt(block_ref[:, half:], w[1])

    def sum_codes(c, carry):
        top, total = carry
        logits = logits_of(c)
        new_top = jnp.maximum(top, jnp.max(logits, axis=1, keepdims=True))
        return new_top, total * jnp.exp(top - new_top) + jnp.sum(jnp.exp(logits - new_top), axis=1, keepdims=True)

    start = (jnp.full((tokens, 1), -3e38, f32), jnp.zeros((tokens, 1), f32))
    top, total = lax.fori_loop(0, chunks, sum_codes, start)
    share_of = live / total
    tick(BACK_TICKS[4][1])
    for c in range(chunks):
        mass = jnp.sum(jnp.exp(logits_of(chunks + c) - top) * share_of, axis=0, keepdims=True)
        com_ref[34 + c // 2 : 35 + c // 2, (c % 2) * step : (c % 2 + 1) * step] = mass
    slabs = 3 * width // step

    def load_w(j):
        rows = pl.ds(j * step, step)
        return [pltpu.make_async_copy(w_any.at[c, rows], w_buf.at[j % 2, c], w_sem.at[j % 2, c]) for c in range(2)]

    for j in range(2):
        for copy in load_w(j):
            copy.start()
    kept_copy.wait()
    tick(BACK_TICKS[4][2])

    def unnormalize(values, grad):
        inverse = lax.rsqrt(head_sums(values * values) + NORM_EPS)
        unit = values * inverse
        return inverse * (grad - unit * head_sums(unit * grad)), unit

    def heads_back(pair, carry):
        home.wait(2 * pair)
        home.wait(2 * pair + 1)
        cols = pl.ds(pl.multiple_of(pair * LANES, LANES), LANES)
        key_cols = pl.ds(pl.multiple_of(pair * LANES + width, LANES), LANES)
        val_cols = pl.ds(pl.multiple_of(pair * LANES + 2 * width, LANES), LANES)
        even = got_ref[2 * pair].astype(f32)
        odd = got_ref[2 * pair + 1].astype(f32)
        even_qk, odd_qk = even[:tokens], odd[:tokens]
        d_query = jnp.where(lane_tok < HALF_LANES, even_qk, swap_halves(odd_qk))
        d_key = jnp.where(lane_tok < HALF_LANES, swap_halves(even_qk), odd_qk)
        even_v, odd_v = even[tokens:], odd[tokens:]
        dproj[core, 0:mid, val_cols] = jnp.where(lane_mid < HALF_LANES, even_v, swap_halves(odd_v)).astype(low)
        dproj[core, mid:, val_cols] = jnp.where(lane_mid < HALF_LANES, swap_halves(even_v), odd_v).astype(low)
        scaled = d_query * (8.0 * (1.0 + vec_ref[7:8, cols]))
        d_q, unit = unnormalize(dq_ref[pl.ds(pl.multiple_of(pair * tokens, tokens), tokens), :], scaled)
        com_ref[33:34, cols] = jnp.sum(d_query * unit, axis=0, keepdims=True) * 8.0
        dproj[core, :, cols] = d_q.astype(low)
        dproj[core, :, key_cols] = unnormalize(dq_ref[pl.ds(pl.multiple_of((pair + 8) * tokens, tokens), tokens), :], d_key)[0].astype(low)
        return carry

    for i in range(2):
        lax.fori_loop(4 * i, 4 * i + 4, heads_back, 0)
        tick(BACK_TICKS[5][i])
    pl.semaphore_wait(free_sem, 1)
    d_copy = to_sib(6, dproj.at[core], dproj.at[core])

    for j in range(slabs):
        for copy in load_w(j):
            copy.wait()
        for c in range(2):
            part = nn(dproj[core, :, j * step : (j + 1) * step], w_buf[j % 2, c])
            cols = slice(c * half, (c + 1) * half)
            dh_ref[:, cols] = part if j == 0 else dh_ref[:, cols] + part
        if j + 2 < slabs:
            for copy in load_w(j + 2):
                copy.start()
    half_copies[2].wait()
    sib_copies[2].wait_recv()
    d_copy.wait_recv()

    def weight_grad(c, carry):
        cols = pl.ds(pl.multiple_of(c * two, two), two)
        total = nn(dproj[0, :, cols].astype(f32).T.astype(low), h_both[0])
        total = total + nn(dproj[1, :, cols].astype(f32).T.astype(low), h_both[1])
        p_qkv[c // 2, pl.ds(2 * (c % 2), 2)] = total.astype(low).reshape(2, tokens, half)
        return carry

    assert next_tick[0] >= len(splits[0]) + 2
    for p in range(len(splits[0])):
        flow.sent(p)
    lax.fori_loop(0, 8, weight_grad, 0)
    last.run(0)
    tick(flow.steps())

    unit, rstd = standard_of(x_ref[...])
    d_h = dh_ref[...]
    ada_ref[:, 2 * width : 3 * width] = per_slot(d_h * unit)
    ada_ref[:, 4 * width : 5 * width] = per_slot(d_h)
    d_x = standard_back(unit, rstd, d_h * (1.0 + of_tokens(2))) + dx_one[...]
    last.run(1)
    com_ref[0:32, :] = lax.dot_general(
        smooth_ref[...], d_x, (((1,), (0,)), ((), ())), precision=HIGHEST_PRECISION, preferred_element_type=f32
    )
    com_ref[32:33, :] = jnp.sum(d_x, axis=0, keepdims=True)
    small = []
    quarter = COMMON_ROWS // 2

    def common_part(ref, w):
        rows = pl.ds(pl.multiple_of((w // 8) * quarter, 8), quarter)
        return ref.at[rows, pl.ds(pl.multiple_of((w % 8) * LANES, LANES), LANES)]

    ada_width = 6 * width // 16

    def ada_part(ref, w):
        return ref.at[:, pl.ds(pl.multiple_of(w * ada_width, LANES), ada_width)]

    def spread(sem_s, sem_r, r, slot, src, dst):
        copy = pltpu.make_async_remote_copy(
            src_ref=src,
            dst_ref=dst,
            send_sem=sem_s.at[slot, r],
            recv_sem=sem_r.at[slot, r],
            device_id=(core, wide ^ r),
            device_id_type=MESH_ID,
        )
        copy.start()
        return copy

    for r in range(1, 16):
        small.append(spread(small_s, small_r, r, 0, ada_part(ada_ref, wide ^ r), ada_land.at[r]))
        small.append(spread(small_s, small_r, r, 1, common_part(com_ref, wide ^ r), com_land.at[r]))
    d_smooth = lax.dot_general(
        embed_ref[1], d_x, (((1,), (1,)), ((), ())), precision=HIGHEST_PRECISION, preferred_element_type=f32
    )
    left, right = ok_ref[0:1, :], ok_ref[1:2, :]
    share = d_smooth / (2.0 + left + right)
    spot = lane_iota((32, LANES))
    edge[...] = jnp.where(spot == 0, share[:, 0:1], jnp.where(spot == 1, share[:, tokens - 1 : tokens], 0.0))

    def edge_copy(slot, dst, shift):
        return pltpu.make_async_remote_copy(
            src_ref=edge,
            dst_ref=dst,
            send_sem=edge_s.at[slot],
            recv_sem=edge_r.at[slot],
            device_id=(core, lax.rem(wide + shift, 16)),
            device_id_type=MESH_ID,
        )

    to_right, to_left = edge_copy(0, edge_left, 1), edge_copy(1, edge_right, 15)
    last.run(2)
    ada_total, com_total = ada_part(ada_ref, wide)[...], common_part(com_ref, wide)[...]
    for copy in small:
        copy.wait_recv()
    for r in range(1, 16):
        ada_total = ada_total + ada_land[r]
        com_total = com_total + com_land[r]
    ada_sum[...] = ada_total
    com_sum[...] = com_total
    swaps = [to_sib(7, ada_sum, ada_sib), to_sib(8, com_sum, com_sib)]
    last.run(3)
    for copy in swaps:
        copy.wait_recv()
    ada_both[core] = ada_sum[...]
    ada_both[1 - core] = ada_sib[...]
    bias = jnp.sum(ada_sum[...] + ada_sib[...], axis=0, keepdims=True)
    bias_own[...] = jnp.broadcast_to(bias, bias_own.shape)
    com_own[...] = com_sum[...] + com_sib[...]
    ada_part(bias_all, wide)[...] = bias_own[...]
    common_part(common_all, wide)[...] = com_own[...]
    back = []
    for r in range(1, 16):
        back.append(spread(spread_s, spread_r, r, 0, bias_own, ada_part(bias_all, wide)))
        back.append(spread(spread_s, spread_r, r, 1, com_own, common_part(common_all, wide)))
    for i in range(4, last.steps()):
        last.run(i)
    to_right.start()
    to_left.start()
    to_right.wait_recv()
    to_left.wait_recv()
    column = lane_iota((32, tokens))
    before = jnp.where(column == 0, edge_left[:, 1:2], jnp.roll(share, 1, axis=1))
    after = jnp.where(column == tokens - 1, edge_right[:, 0:1], jnp.roll(share, -1, axis=1))
    map_ref[...] = 2.0 * share + left * before + right * after
    for copy in back:
        copy.wait_recv()
    for copy in small + swaps + back + sib_copies + [d_copy, to_right, to_left]:
        copy.wait_send()
    flow.finish()
    last.finish()
    there.finish()
    home.finish()


def back(args, groups, splits, call_id):
    x_zero, act = args[4], args[10]
    tokens, width = x_zero.shape
    hidden = act.shape[1]
    group_len = 16 * tokens
    half, mid, packed = width // 2, tokens // 2, tokens * 3 // 2
    f32, low = jnp.float32, jnp.bfloat16
    dma = pltpu.SemaphoreType.DMA
    shape = jax.ShapeDtypeStruct
    sizes = [(width // 16, hidden // 2), (hidden // 16, half), (width // 16, half), (3 * width // 16, half)]
    first = pieces_of([shape(s, f32) for s in sizes[:3]], splits[0])
    second = pieces_of([shape(sizes[3], f32)], splits[1])
    ada_width, quarter = 6 * width // 16, COMMON_ROWS // 2
    outs = [shape(s, f32) for s in sizes] + [
        shape((2, 8, ada_width), f32),
        shape((COMMON_ROWS, width), f32),
        shape((8, 6 * width), f32),
        shape((32, tokens), f32),
        shape((tokens, width), low),
    ]
    vm = pltpu.VMEM
    scratch = [
        vm((16, packed, LANES), low),
        vm((16, packed, LANES), low),
        vm((16, mid, LANES), low),
        vm((16, mid, LANES), low),
        vm((group_len, LANES), low),
        vm((HALF_LANES, group_len), low),
        vm((HALF_LANES, group_len), low),
        vm((group_len, LANES), f32),
        vm((HALF_LANES, group_len), f32),
        vm((HALF_LANES, group_len), f32),
        vm((2, 4, 512, half), low),
        vm((2, tokens, hidden), low),
        vm((2, tokens, half), low),
        vm((tokens, width), f32),
        vm((8, 6 * width), f32),
        vm((COMMON_ROWS, width), f32),
        vm((16, 8, ada_width), f32),
        vm((16, quarter, LANES), f32),
        vm((8, ada_width), f32),
        vm((quarter, LANES), f32),
        vm((8, ada_width), f32),
        vm((quarter, LANES), f32),
        vm((8, ada_width), f32),
        vm((quarter, LANES), f32),
        vm((32, LANES), f32),
        vm((32, LANES), f32),
        vm((32, LANES), f32),
        vm((tokens, width), low),
        vm((2, tokens, half), low),
        vm((2, tokens, half), low),
        vm((2, tokens, width), low),
        vm((tokens, width), f32),
        vm((tokens, width), f32),
        vm((2, tokens, 512), low),
        vm((2, tokens, 512), f32),
        vm((tokens, width), low),
    ] + [vm((4, 4) + s, low) for s in (sizes[1], sizes[2], sizes[0])]
    scratch += [vm((group_len, LANES), low)] * 2 + [vm((LANES, group_len), low)] * 2 + [dma((5,))]
    scratch += Scatter.scratch(sizes[:3], len(first)) + Scatter.scratch(sizes[3:], len(second))
    scratch += [dma((16,)) for _ in range(4)] + [dma((2, 6)), dma((16,)), dma((16,))]
    scratch += [dma((2, 16)) for _ in range(4)] + [dma((2,)), dma((2,))]
    scratch += [dma((8,)), dma((8,)), dma((4,)), dma, pltpu.SemaphoreType.REGULAR]
    return pl.pallas_call(
        functools.partial(back_kernel, groups, (first, second)),
        out_shape=outs,
        in_specs=[VM] * 7 + [ANY] * 16 + [VM] * 3 + [ANY],
        out_specs=[VM] * 9,
        scratch_shapes=scratch,
        compiler_params=pltpu.CompilerParams(
            collective_id=call_id, has_side_effects=True, vmem_limit_bytes=63 * 1024 * 1024
        ),
    )(*args)


def nesterov_rows(moment, weight, average, gradient, step_rate, decay_rate):
    step_grad = gradient + decay_rate * weight
    new_moment = MOMENTUM * moment + step_rate * step_grad
    new_weight = weight - (step_rate * step_grad + MOMENTUM * new_moment)
    retain = min(0.999, (1.0 + STEP) / (10.0 + STEP))
    return new_moment, new_weight, retain * average + (1.0 - retain) * new_weight


def update_kernel(rates, mass_scale, *refs):
    states = refs[:5]
    (embed_ref, vector_ref, s_down, s_up, s_out, s_qkv, d_ada, silu_ref, common_ref, bias_ref) = refs[5:15]
    news, copies = refs[15:20], refs[20:25]
    (embed_new, vector_new, mass_out, gain_out) = refs[25:29]
    held, lows = refs[29:34], refs[34:39]
    load_sem, store_sem, low_sem = refs[39:]
    width = vector_ref.shape[2]

    def grad_of(i):
        if i == 4:
            return exact(silu_ref[...], d_ada[...], (0, 0))
        return (s_qkv, s_out, None, s_down)[i][...] if i != 2 else s_up[...].T

    order = (3, 2, 4, 0, 1)
    loads = {i: pltpu.make_async_copy(states[i], held[i], load_sem.at[i]) for i in order}
    for i in order:
        loads[i].start()
    rows = embed_ref.shape[1]
    parts = nesterov_rows(embed_ref[0], embed_ref[1], embed_ref[2], common_ref[0:rows, :], rates[5], 0.0)
    for j in range(3):
        embed_new[j] = parts[j]
    for block in range(8):
        if block < 6:
            grad = bias_ref[0:1, block * width : (block + 1) * width]
        else:
            grad = common_ref[rows + block - 6 : rows + block - 5, :]
        here = slice(block, block + 1)
        parts = nesterov_rows(vector_ref[0, here], vector_ref[1, here], vector_ref[2, here], grad, rates[6], 0.0)
        for j in range(3):
            vector_new[j, here] = parts[j]
    per_row = width // LANES
    for r in range(per_row):
        cols = slice(r * LANES, (r + 1) * LANES)
        gain_out[r : r + 1, :] = common_ref[rows + 1 : rows + 2, cols]
        for a in range(mass_out.shape[0] // per_row):
            at = a * per_row + r
            mass_out[at : at + 1, :] = common_ref[rows + 2 + a : rows + 3 + a, cols] * mass_scale
    stores = []
    for i in order:
        loads[i].wait()
        parts = nesterov_rows(held[i][0], held[i][1], held[i][2], grad_of(i), rates[i], WEIGHT_DECAY)
        for j in range(3):
            held[i][j] = parts[j]
        lows[i][...] = parts[1].astype(jnp.bfloat16)
        stores.append(pltpu.make_async_copy(held[i], news[i], store_sem.at[i]))
        stores.append(pltpu.make_async_copy(lows[i], copies[i], low_sem.at[i]))
        for copy in stores[-2:]:
            copy.start()
    for copy in stores:
        copy.wait()


def update(states, embed_state, vector_state, grads, rates, codes, mass_scale):
    f32, low = jnp.float32, jnp.bfloat16
    shape = jax.ShapeDtypeStruct
    dma = pltpu.SemaphoreType.DMA
    width = vector_state.shape[2]
    outs = [shape(s.shape, f32) for s in states] + [shape(s.shape[1:], low) for s in states]
    outs += [shape(embed_state.shape, f32), shape(vector_state.shape, f32)]
    outs += [shape((codes // LANES, LANES), f32), shape((width // LANES, LANES), f32)]
    return pl.pallas_call(
        functools.partial(update_kernel, rates, mass_scale),
        out_shape=outs,
        in_specs=[ANY] * 5 + [VM] * 10,
        out_specs=[ANY] * 10 + [VM] * 4,
        scratch_shapes=[pltpu.VMEM(s.shape, f32) for s in states]
        + [pltpu.VMEM(s.shape[1:], low) for s in states]
        + [dma((5,)), dma((5,)), dma((5,))],
        compiler_params=pltpu.CompilerParams(vmem_limit_bytes=VMEM_BYTES),
    )(*states, embed_state, vector_state, *grads)


def run_tables(slots):
    squares = np.zeros((8, LANES), np.float32)
    pick = np.zeros((LANES, LANES), np.float32)
    for run in range(slots * LEVELS):
        squares[0, HALF_LANES + run] = LONG_SIDES[run // slots] ** 2
        squares[1, HALF_LANES + run] = SHORT_SIDES[run // slots] ** 2
        pick[HALF_LANES + run, run % slots] = 1.0
    tri = np.triu(np.ones((LANES, LANES), np.float32))
    low = jnp.bfloat16
    return [jnp.asarray(squares), jnp.asarray(tri), jnp.asarray(pick, low), jnp.asarray(attention_rule(slots), low)]


def attention_rule(slots):
    runs = slots * LEVELS + 1
    rule = np.zeros((LANES, LANES), np.float32)
    for a in range(runs):
        for b in range(runs):
            slot_a, level_a = (slots, 0) if a == runs - 1 else (a % slots, a // slots)
            slot_b, level_b = (slots, 0) if b == runs - 1 else (b % slots, b // slots)
            if slot_a != slot_b or level_b > level_a:
                rule[HALF_LANES + a, HALF_LANES + b] = -BIG
    return rule


def fast_shards(
    feature_map,
    condition,
    item_lengths,
    cotangent,
    code_book,
    qkv_state,
    out_state,
    up_state,
    down_state,
    ada_state,
    embed_state,
    vector_state,
):
    tok_rows, model_width = cotangent.shape
    low = jnp.bfloat16
    group_len = tok_rows * lax.axis_size("wide")
    tokens_all = lax.axis_size("dp") * group_len
    lengths = item_lengths[0]
    slot_count = lengths.shape[0]

    flip = lambda values: jnp.swapaxes(values, -1, -2)
    flipped = [flip(qkv_state), flip(out_state), up_state, flip(down_state)]
    groups = same_limits(key_limits(group_len, slot_count))
    (
        w_qkv, w_out, w_up, w_down, ada_gathered, h_one_low, kept_qk, out32, q_own, k_own, kt_own, vt_own, attn_low,
        x_zero, smooth, flags, one_hot_wide, silu_rows, attn_proj, x_one, h_two_low, hidden_pre, act_low, p_down,
    ) = front(
        flipped,
        condition,
        ada_state,
        feature_map,
        embed_state,
        vector_state,
        item_lengths,
        run_tables(slot_count),
        cotangent,
        groups,
    )
    s_down, s_up, s_out, s_qkv, d_ada_both, common_sum, bias_sum, map_grad, block_out = back(
        [cotangent, one_hot_wide, ada_gathered, vector_state, x_zero, x_one, attn_proj, h_one_low, h_two_low, attn_low]
        + [act_low, hidden_pre, w_qkv, w_out, w_up, w_down, code_book, out32, q_own, k_own, kt_own, vt_own]
        + [kept_qk.reshape(-1, LANES), smooth, embed_state, flags, p_down],
        groups,
        BACK_SPLITS,
        1,
    )
    root_tokens = math.sqrt(tokens_all)
    spreads = (
        model_width ** (-0.5),
        (model_width // 16) ** (-0.5),
        model_width ** (-0.5),
        w_up.shape[1] ** (-0.5),
        model_width ** (-0.5),
    )
    rates = [BASE_RATE * spread_w / (factor_g * root_tokens) for spread_w, factor_g in zip(spreads, GRAD_FACTORS)]
    rates.append(BASE_RATE * embed_state.shape[1] ** (-0.5) / (EMBED_FACTOR * root_tokens))
    rates.append(VECTOR_RATE / root_tokens)
    codes = code_book.shape[0]
    results = update(
        flipped + [ada_state],
        embed_state,
        vector_state,
        [s_down, s_up, s_out, s_qkv, d_ada_both.reshape(16, -1), silu_rows.reshape(16, -1), common_sum, bias_sum],
        tuple(rates),
        codes,
        codes / tokens_all,
    )
    outputs = [block_out, map_grad, results[12].reshape(-1)]
    for i in range(5):
        new, copied = results[i], results[5 + i]
        outputs += [flip(new), flip(copied)] if i in (0, 1, 3) else [new, copied]
    return tuple(outputs + [results[10], results[11], results[13].reshape(-1)])


def solution(mesh):
    body = fast_shards if dict(mesh.shape) == {"dp": 2, "wide": 16} else shards
    in_specs = (
        P(None, ("dp", "wide")),
        P("dp", None),
        P("dp", None),
        P(("dp", "wide"), None),
        P(),
        P(None, "dp", "wide"),
        P(None, "dp", "wide"),
        P(None, "dp", "wide"),
        P(None, "dp", "wide"),
        P(None, "dp", "wide"),
        P(),
        P(),
    )
    out_specs = (
        P(("dp", "wide"), None),
        P(None, ("dp", "wide")),
        P(),
        P(None, "dp", "wide"),
        P("dp", "wide"),
        P(None, "dp", "wide"),
        P("dp", "wide"),
        P(None, "dp", "wide"),
        P("dp", "wide"),
        P(None, "dp", "wide"),
        P("dp", "wide"),
        P(None, "dp", "wide"),
        P("dp", "wide"),
        P(),
        P(),
        P(),
    )
    return jax.shard_map(body, mesh=mesh, in_specs=in_specs, out_specs=out_specs, check_vma=False)
```

```python
import functools
import math

import jax
import jax.numpy as jnp
import numpy as np
from jax import lax
from jax.experimental import pallas as pl
from jax.experimental.pallas import tpu as pltpu
from jax.sharding import PartitionSpec as P

HEADS = 16
LEVELS = 10
STEP = 7


SHORT_SIDES = (1, 2, 3, 4, 5, 6, 8, 10, 13, 16)
LONG_SIDES = (1, 2, 3, 4, 6, 9, 13, 18, 24, 32)
MASKED = -1e30
NORM_EPS = 1e-06
MOMENTUM = 0.9
WEIGHT_DECAY = 0.05
BASE_RATE = 0.37
VECTOR_RATE = 0.22
GRAD_FACTORS = (0.15, 0.1, 0.3, 0.35, 0.3)
EMBED_FACTOR = 0.6
HIGHEST_PRECISION = lax.Precision.HIGHEST


def padded(cells, sides, width):
    for axis, dim in sides:
        count = lax.axis_size(axis)
        ends = count - 1
        head = lax.slice_in_dim(cells, 0, width, axis=dim)
        tail = lax.slice_in_dim(cells, cells.shape[dim] - width, cells.shape[dim], axis=dim)
        cells = jnp.concatenate(
            [
                lax.ppermute(tail, axis, [(i, (i + 1) % count) for i in range(ends)]),
                cells,
                lax.ppermute(head, axis, [((i + 1) % count, i) for i in range(ends)]),
            ],
            axis=dim,
        )
    return cells


def layout(lengths, positions, group_len):
    short_sq = jnp.array([side * side for side in SHORT_SIDES[:LEVELS]], jnp.int32)
    long_sq = jnp.array([side * side for side in LONG_SIDES[:LEVELS]], jnp.int32)
    short_total = sum((side * side for side in SHORT_SIDES[:LEVELS]))
    long_total = sum((side * side for side in LONG_SIDES[:LEVELS]))
    slot_count = lengths.shape[0]
    counts = jnp.where(
        lengths[None, :] == long_total,
        long_sq[:, None],
        jnp.where(lengths[None, :] == short_total, short_sq[:, None], 0),
    )
    unused = group_len - jnp.sum(lengths)
    ordered = jnp.concatenate([counts.reshape(-1), unused[None]])
    boundary = jnp.cumsum(ordered)
    segment = jnp.sum((boundary[None, :] <= positions[:, None]).astype(jnp.int32), axis=1)
    segment = jnp.minimum(segment, ordered.shape[0] - 1)
    unused_id = slot_count * LEVELS
    tok_level = jnp.where(segment >= unused_id, 0, segment // slot_count)
    tok_slot = jnp.where(segment >= unused_id, slot_count, segment % slot_count)
    return (tok_slot, tok_level, segment)


def pre_norm(inputs, scaling, offset_add):
    row_mean = jnp.mean(inputs, axis=-1, keepdims=True)
    centred = inputs - row_mean
    spread = jnp.mean(centred * centred, axis=-1, keepdims=True)
    return centred * lax.rsqrt(spread + NORM_EPS) * (1.0 + scaling) + offset_add


def unit_heads(inputs):
    shaped = inputs.reshape(inputs.shape[0], HEADS, -1)
    shaped = shaped * lax.rsqrt(jnp.sum(shaped * shaped, axis=-1, keepdims=True) + NORM_EPS)
    return shaped.reshape(inputs.shape)


def split_heads(projected, q_gain):
    queries, key_part, value_part = jnp.split(projected, 3, axis=1)
    head_scale = math.sqrt(queries.shape[1] // HEADS)
    return (unit_heads(queries) * (head_scale * (1.0 + q_gain)), unit_heads(key_part), value_part)


def smooth_map(values, left_ok, right_ok, before, following):
    return (left_ok * before + 2.0 * values + right_ok * following) / (2.0 + left_ok + right_ok)


def nesterov(stacked, gradient, step_rate, decay_rate):
    moment, weight, average = (stacked[0], stacked[1], stacked[2])
    step_grad = gradient + decay_rate * weight
    new_moment = MOMENTUM * moment + step_rate * step_grad
    new_weight = weight - (step_rate * step_grad + MOMENTUM * new_moment)
    retain = min(0.999, (1.0 + STEP) / (10.0 + STEP))
    new_average = retain * average + (1.0 - retain) * new_weight
    return jnp.stack([new_moment, new_weight, new_average])


def contract_rows(left_side, right_side, precision=None):
    return lax.dot_general(
        left_side,
        right_side,
        (((0,), (0,)), ((), ())),
        precision=precision,
        preferred_element_type=jnp.float32,
    )


def against(left_side, right_side):
    return lax.dot_general(
        left_side, right_side, (((1,), (1,)), ((), ())), preferred_element_type=jnp.float32
    )


def shards(
    feature_map,
    condition,
    item_lengths,
    cotangent,
    code_book,
    qkv_state,
    out_state,
    up_state,
    down_state,
    ada_state,
    embed_state,
    vector_state,
):
    tok_rows = cotangent.shape[0]
    model_width = cotangent.shape[1]
    head_dim = model_width // HEADS
    wide_count = lax.axis_size("wide")
    group_len = tok_rows * wide_count
    tokens_all = lax.axis_size("dp") * group_len
    lengths = item_lengths[0]
    slot_count = lengths.shape[0]
    positions = lax.axis_index("wide") * tok_rows + jnp.arange(tok_rows, dtype=jnp.int32)
    tok_slot, tok_level, segment = layout(lengths, positions, group_len)
    live_rows = (tok_slot < slot_count).astype(jnp.float32)[:, None]
    left_ok = ((layout(lengths, positions - 1, group_len)[2] == segment) & (positions > 0)).astype(
        jnp.float32
    )
    right_ok = (
        (layout(lengths, positions + 1, group_len)[2] == segment) & (positions < group_len - 1)
    ).astype(jnp.float32)
    rimmed = padded(feature_map, (("wide", 1),), 1)
    smooth = smooth_map(feature_map, left_ok, right_ok, rimmed[:, :-2], rimmed[:, 2:])
    states = (qkv_state, out_state, up_state, down_state, ada_state)
    masters = tuple((stacked[1].astype(jnp.bfloat16) for stacked in states))
    columns = (
        lax.all_gather(masters[0], "wide", axis=1, tiled=True),
        lax.all_gather(masters[1], "wide", axis=1, tiled=True),
        lax.all_gather(masters[2], "wide", axis=1, tiled=True),
        lax.all_gather(masters[3], "wide", axis=1, tiled=True),
    )
    ada_piece = lax.all_gather(masters[4], "wide", axis=1, tiled=True)
    w_qkv, w_out, w_up, w_down, w_ada = (
        lax.all_gather(columns[0], "dp", axis=0, tiled=True),
        lax.all_gather(columns[1], "dp", axis=0, tiled=True),
        lax.all_gather(columns[2], "dp", axis=0, tiled=True),
        lax.all_gather(columns[3], "dp", axis=0, tiled=True),
        lax.all_gather(ada_piece, "dp", axis=0, tiled=True),
    )
    embed_w = embed_state[1]
    vectors = vector_state[1]
    x_zero = (
        lax.dot_general(smooth, embed_w, (((0,), (0,)), ((), ())), precision=HIGHEST_PRECISION)
        + vectors[6]
    )
    silu_cond = jax.nn.silu(condition).astype(jnp.bfloat16)
    ada_product = jnp.dot(silu_cond, w_ada, preferred_element_type=jnp.float32)
    ada_all = ada_product + vectors[:6].reshape(-1)
    one_hot = (tok_slot[:, None] == jnp.arange(slot_count, dtype=jnp.int32)[None, :]).astype(
        jnp.float32
    )
    token_ada = jnp.dot(one_hot, ada_all, precision=HIGHEST_PRECISION)
    gate_one, gate_two, scale_one, scale_two, shift_one, shift_two = jnp.split(token_ada, 6, axis=1)
    h_one_low = pre_norm(x_zero, scale_one, shift_one).astype(jnp.bfloat16)
    projected = jnp.dot(h_one_low, w_qkv, preferred_element_type=jnp.float32)
    (q_unit, k_unit, v_full), heads_back = jax.vjp(split_heads, projected, vectors[7])
    queries = q_unit.astype(jnp.bfloat16)
    keys_low = k_unit.astype(jnp.bfloat16)
    values_low = v_full.astype(jnp.bfloat16)
    query_heads = queries.reshape(tok_rows, HEADS, head_dim)

    def blockwise(advance, running, pieces, first_row):
        key_count = pieces[0].shape[0]
        block_size = math.gcd(key_count, 1024)

        def per_block(current, offset):
            key_part = tuple(
                (lax.dynamic_slice_in_dim(piece_arr, offset, block_size, 0) for piece_arr in pieces)
            )
            first_key = first_row + offset
            k_slot, k_level, _ = layout(
                lengths, first_key + jnp.arange(block_size, dtype=jnp.int32), group_len
            )
            allowed = (tok_slot[:, None] == k_slot[None, :]) & (
                k_level[None, :] <= tok_level[:, None]
            )
            current = advance(current, key_part, allowed, first_key)
            return (current, None)

        offsets = jnp.arange(key_count // block_size, dtype=jnp.int32) * block_size
        return lax.scan(per_block, running, offsets)[0]

    def scores_of(key_block, allowed):
        raw_scores = jnp.einsum(
            "qhd,khd->hqk",
            query_heads,
            key_block.reshape(-1, HEADS, head_dim),
            preferred_element_type=jnp.float32,
        )
        return jnp.where(allowed[None], raw_scores, MASKED)

    def stats_step(running, key_part, allowed, first_key):
        scores = scores_of(key_part[0], allowed)
        top_score, exp_total = running
        new_top = jnp.maximum(top_score, jnp.max(scores, axis=-1, keepdims=True))
        exp_total = exp_total * jnp.exp(top_score - new_top) + jnp.sum(
            jnp.exp(scores - new_top), axis=-1, keepdims=True
        )
        return (new_top, exp_total)

    kv_rows = (
        lax.all_gather(keys_low, "wide", axis=0, tiled=True),
        lax.all_gather(values_low, "wide", axis=0, tiled=True),
    )
    start_stats = (
        jnp.full((HEADS, tok_rows, 1), MASKED, jnp.float32),
        jnp.zeros((HEADS, tok_rows, 1), jnp.float32),
    )
    top_score, exp_total = blockwise(stats_step, start_stats, kv_rows, 0)
    log_total = top_score + jnp.log(exp_total)

    def value_step(running, key_part, allowed, first_key):
        attn_probs = jnp.exp(scores_of(key_part[0], allowed) - log_total).astype(jnp.bfloat16)
        return running + jnp.einsum(
            "hqk,khd->qhd",
            attn_probs,
            key_part[1].reshape(-1, HEADS, head_dim),
            preferred_element_type=jnp.float32,
        )

    attended = blockwise(
        value_step, jnp.zeros((tok_rows, HEADS, head_dim), jnp.float32), kv_rows, 0
    )
    attn_low = attended.reshape(tok_rows, model_width).astype(jnp.bfloat16)
    attn_proj = jnp.dot(attn_low, w_out, preferred_element_type=jnp.float32)
    x_one = x_zero + gate_one * attn_proj
    h_two_low = pre_norm(x_one, scale_two, shift_two).astype(jnp.bfloat16)
    hidden_pre = jnp.dot(h_two_low, w_up, preferred_element_type=jnp.float32)
    act_low = jax.nn.gelu(hidden_pre, approximate=True).astype(jnp.bfloat16)
    mlp_out = jnp.dot(act_low, w_down, preferred_element_type=jnp.float32)
    x_two = x_one + gate_two * mlp_out
    block_out = (x_two * live_rows).astype(jnp.bfloat16)
    logits = against(block_out, code_book)
    code_mass = jnp.sum(jax.nn.softmax(logits, axis=-1) * live_rows, axis=0)
    g_two = cotangent.astype(jnp.float32) * live_rows
    d_mlp = (gate_two * g_two).astype(jnp.bfloat16)
    d_gate_two = g_two * mlp_out
    dw_down = contract_rows(act_low, d_mlp)
    d_act = against(d_mlp, w_down)
    _, gelu_back = jax.vjp(lambda inputs: jax.nn.gelu(inputs, approximate=True), hidden_pre)
    d_hidden = gelu_back(d_act)[0].astype(jnp.bfloat16)
    dw_up = contract_rows(h_two_low, d_hidden)
    d_h_two = against(d_hidden, w_up)
    _, norm_back_two = jax.vjp(pre_norm, x_one, scale_two, shift_two)
    d_x_one, d_scale_two, d_shift_two = norm_back_two(d_h_two)
    d_x_one = d_x_one + g_two
    d_attn = (gate_one * d_x_one).astype(jnp.bfloat16)
    d_gate_one = d_x_one * attn_proj
    dw_out = contract_rows(attn_low, d_attn)
    grad_flat = against(d_attn, w_out).astype(jnp.bfloat16)
    grad_heads = grad_flat.reshape(tok_rows, HEADS, head_dim)

    def delta_step(running, key_part, allowed, first_key):
        attn_probs = jnp.exp(scores_of(key_part[0], allowed) - log_total)
        d_probs = jnp.einsum(
            "qhd,khd->hqk",
            grad_heads,
            key_part[1].reshape(-1, HEADS, head_dim),
            preferred_element_type=jnp.float32,
        )
        return running + jnp.sum(attn_probs * d_probs, axis=-1, keepdims=True)

    row_delta = blockwise(delta_step, jnp.zeros((HEADS, tok_rows, 1), jnp.float32), kv_rows, 0)

    def grad_step(running, key_part, allowed, first_key):
        d_query, d_keys, d_values = running
        key_heads = key_part[0].reshape(-1, HEADS, head_dim)
        value_heads = key_part[1].reshape(-1, HEADS, head_dim)
        block_rows = key_part[0].shape[0]
        attn_probs = jnp.exp(scores_of(key_part[0], allowed) - log_total)
        d_probs = jnp.einsum(
            "qhd,khd->hqk", grad_heads, value_heads, preferred_element_type=jnp.float32
        )
        d_scores = (attn_probs * (d_probs - row_delta)).astype(jnp.bfloat16)
        d_query = d_query + jnp.einsum(
            "hqk,khd->qhd", d_scores, key_heads, preferred_element_type=jnp.float32
        )
        key_grad = jnp.einsum(
            "hqk,qhd->khd", d_scores, query_heads, preferred_element_type=jnp.float32
        )
        value_grad = jnp.einsum(
            "hqk,qhd->khd",
            attn_probs.astype(jnp.bfloat16),
            grad_heads,
            preferred_element_type=jnp.float32,
        )
        key_sum = lax.dynamic_slice_in_dim(d_keys, first_key, block_rows, 0) + key_grad.reshape(
            block_rows, model_width
        )
        value_sum = lax.dynamic_slice_in_dim(
            d_values, first_key, block_rows, 0
        ) + value_grad.reshape(block_rows, model_width)
        d_keys = lax.dynamic_update_slice_in_dim(d_keys, key_sum, first_key, 0)
        d_values = lax.dynamic_update_slice_in_dim(d_values, value_sum, first_key, 0)
        return (d_query, d_keys, d_values)

    grad_init = (
        jnp.zeros((tok_rows, HEADS, head_dim), jnp.float32),
        jnp.zeros((group_len, model_width), jnp.float32),
        jnp.zeros((group_len, model_width), jnp.float32),
    )
    d_query, d_keys, d_values = blockwise(grad_step, grad_init, kv_rows, 0)
    d_keys_own, d_values_own = (
        lax.psum_scatter(
            d_keys.astype(jnp.bfloat16), "wide", scatter_dimension=0, tiled=True
        ).astype(jnp.float32),
        lax.psum_scatter(
            d_values.astype(jnp.bfloat16), "wide", scatter_dimension=0, tiled=True
        ).astype(jnp.float32),
    )
    d_projected, d_gain = heads_back(
        (d_query.reshape(tok_rows, model_width), d_keys_own, d_values_own)
    )
    d_projected_low = d_projected.astype(jnp.bfloat16)
    dw_qkv = contract_rows(h_one_low, d_projected_low)
    d_h_one = against(d_projected_low, w_qkv)
    _, norm_back_one = jax.vjp(pre_norm, x_zero, scale_one, shift_one)
    d_x_zero, d_scale_one, d_shift_one = norm_back_one(d_h_one)
    d_x_zero = d_x_zero + d_x_one
    d_token_ada = jnp.concatenate(
        [d_gate_one, d_gate_two, d_scale_one, d_scale_two, d_shift_one, d_shift_two], axis=1
    )
    d_ada_all = contract_rows(one_hot, d_token_ada, HIGHEST_PRECISION)
    d_smooth = lax.dot_general(
        embed_w, d_x_zero, (((1,), (1,)), ((), ())), precision=HIGHEST_PRECISION
    )
    d_embed = lax.dot_general(
        smooth, d_x_zero, (((1,), (0,)), ((), ())), precision=HIGHEST_PRECISION
    )
    d_vectors = jnp.concatenate(
        [
            jnp.sum(d_ada_all, axis=0).reshape(6, model_width),
            jnp.sum(d_x_zero, axis=0)[None],
            d_gain[None],
        ],
        axis=0,
    )
    grad_share = d_smooth / (2.0 + left_ok + right_ok)
    rim_share = padded(grad_share, (("wide", 1),), 1)
    map_grad = 2.0 * grad_share + left_ok * rim_share[:, :-2] + right_ok * rim_share[:, 2:]
    d_embed_all, d_vectors_all, mass_all = lax.psum((d_embed, d_vectors, code_mass), ("dp", "wide"))
    histogram = mass_all * (code_book.shape[0] / tokens_all)
    ada_term = contract_rows(silu_cond.astype(jnp.float32), d_ada_all, HIGHEST_PRECISION)
    split_cols = (
        lax.psum_scatter(
            dw_qkv.astype(jnp.bfloat16), "wide", scatter_dimension=1, tiled=True
        ).astype(jnp.float32),
        lax.psum_scatter(
            dw_out.astype(jnp.bfloat16), "wide", scatter_dimension=1, tiled=True
        ).astype(jnp.float32),
        lax.psum_scatter(
            dw_up.astype(jnp.bfloat16), "wide", scatter_dimension=1, tiled=True
        ).astype(jnp.float32),
        lax.psum_scatter(
            dw_down.astype(jnp.bfloat16), "wide", scatter_dimension=1, tiled=True
        ).astype(jnp.float32),
        lax.psum_scatter(
            ada_term.astype(jnp.bfloat16), "wide", scatter_dimension=1, tiled=True
        ).astype(jnp.float32),
    )
    ada_cols = split_cols[4]
    owned_grads = (
        lax.psum_scatter(
            split_cols[0].astype(jnp.bfloat16), "dp", scatter_dimension=0, tiled=True
        ).astype(jnp.float32),
        lax.psum_scatter(
            split_cols[1].astype(jnp.bfloat16), "dp", scatter_dimension=0, tiled=True
        ).astype(jnp.float32),
        lax.psum_scatter(
            split_cols[2].astype(jnp.bfloat16), "dp", scatter_dimension=0, tiled=True
        ).astype(jnp.float32),
        lax.psum_scatter(
            split_cols[3].astype(jnp.bfloat16), "dp", scatter_dimension=0, tiled=True
        ).astype(jnp.float32),
        lax.psum_scatter(
            ada_cols.astype(jnp.bfloat16), "dp", scatter_dimension=0, tiled=True
        ).astype(jnp.float32),
    )
    root_tokens = math.sqrt(tokens_all)
    spreads = (
        model_width ** (-0.5),
        (model_width // 16) ** (-0.5),
        model_width ** (-0.5),
        w_up.shape[1] ** (-0.5),
        model_width ** (-0.5),
    )
    new_states = tuple(
        (
            nesterov(
                stacked, gradient, BASE_RATE * spread_w / (factor_g * root_tokens), WEIGHT_DECAY
            )
            for stacked, gradient, spread_w, factor_g in zip(
                states, owned_grads, spreads, GRAD_FACTORS
            )
        )
    )
    embed_new = nesterov(
        embed_state,
        d_embed_all,
        BASE_RATE * embed_w.shape[0] ** (-0.5) / (EMBED_FACTOR * root_tokens),
        0.0,
    )
    vector_new = nesterov(vector_state, d_vectors_all, VECTOR_RATE / root_tokens, 0.0)
    return (
        block_out,
        map_grad,
        histogram,
        new_states[0],
        new_states[0][1].astype(jnp.bfloat16),
        new_states[1],
        new_states[1][1].astype(jnp.bfloat16),
        new_states[2],
        new_states[2][1].astype(jnp.bfloat16),
        new_states[3],
        new_states[3][1].astype(jnp.bfloat16),
        new_states[4],
        new_states[4][1].astype(jnp.bfloat16),
        embed_new,
        vector_new,
        d_vectors_all[7],
    )


MESH_ID = pl.DeviceIdType.MESH
ANY = pl.BlockSpec(memory_space=pl.ANY)
VM = pl.BlockSpec(memory_space=pltpu.VMEM)
VMEM_BYTES = 56 * 1024 * 1024
SHORT_TOTAL = sum(side * side for side in SHORT_SIDES)
LONG_TOTAL = sum(side * side for side in LONG_SIDES)
GELU_SCALE = math.sqrt(2.0 / math.pi)
GELU_CUBE = 0.044715
LANES = 128
HALF_LANES = 64
BIG = 1e30


def nt(left_side, right_side):
    return lax.dot_general(
        left_side, right_side, (((1,), (1,)), ((), ())), preferred_element_type=jnp.float32
    )


def nn(left_side, right_side):
    return lax.dot_general(
        left_side, right_side, (((1,), (0,)), ((), ())), preferred_element_type=jnp.float32
    )


def entry_barrier(peers):
    barrier = pltpu.get_barrier_semaphore()
    for peer in peers:
        pl.semaphore_signal(barrier, inc=1, device_id=peer, device_id_type=MESH_ID)
    pl.semaphore_wait(barrier, len(peers))


def place():
    core, wide = lax.axis_index("dp"), lax.axis_index("wide")
    return core, wide // 4, wide % 4


def at_dev(core, z, yx):
    return (core, z * 4 + yx)


def lane_iota(shape):
    return lax.broadcasted_iota(jnp.int32, shape, len(shape) - 1)


def swap_halves(pair):
    return pltpu.roll(pair, HALF_LANES, 1)


def head_sums(values):
    width = values.shape[1]
    rows = lax.broadcasted_iota(jnp.int32, (width, width), 0) // HALF_LANES
    cols = lax.broadcasted_iota(jnp.int32, (width, width), 1) // HALF_LANES
    ones = (rows == cols).astype(jnp.float32)
    return lax.dot_general(
        values,
        ones,
        (((1,), (0,)), ((), ())),
        precision=HIGHEST_PRECISION,
        preferred_element_type=jnp.float32,
    )


ROWS = 256
CHUNK = 512


def key_limits(group_len, slots):
    short_total = sum(side * side for side in SHORT_SIDES)
    long_total = sum(side * side for side in LONG_SIDES)
    limits = [0] * (group_len // ROWS)
    for longs in range(1, slots + 1):
        for shorts in range(slots - longs + 1):
            total = longs * long_total + shorts * short_total
            if not group_len - short_total < total <= group_len:
                continue
            ends, position = [], 0
            for long_side, short_side in zip(LONG_SIDES, SHORT_SIDES):
                position += longs * long_side**2 + shorts * short_side**2
                ends.append(position)
            ends.append(group_len)
            for block in range(len(limits)):
                last = block * ROWS + ROWS - 1
                seen = min(end for end in ends if end > last)
                limits[block] = max(limits[block], -(-seen // LANES) * LANES)
    return limits


def same_limits(limits):
    groups = []
    for block, limit in enumerate(limits):
        if groups and groups[-1][2] == limit:
            groups[-1][1] = block + 1
        else:
            groups.append([block, block + 1, limit])
    return groups


def fold_lanes(values, combine):
    total = values[:, :LANES]
    for j in range(1, values.shape[1] // LANES):
        total = combine(total, values[:, j * LANES : (j + 1) * LANES])
    return total


def split_three(values):
    high = values.astype(jnp.bfloat16).astype(jnp.float32)
    rest = values - high
    mid = rest.astype(jnp.bfloat16).astype(jnp.float32)
    return high, mid, rest - mid


def lanes_three(lane, first, values, otherwise):
    high, mid, rest = split_three(values)
    return jnp.where(
        lane == first, high, jnp.where(lane == first + 1, mid, jnp.where(lane == first + 2, rest, otherwise))
    )


class Gather:
    KINDS = ("up", "down", "x", "y", "turn")

    def __init__(self, shards, fulls, sems, pieces):
        self.shards, self.fulls, self.pieces = shards, fulls, pieces
        self.send, self.recv, self.send_s, self.recv_s, self.local = sems
        self.core, self.z, self.yx = place()
        core, z, yx = self.core, self.z, self.yx
        self.up_dev, self.down_dev = at_dev(core, lax.min(z + 1, 3), yx), at_dev(core, lax.max(z - 1, 0), yx)
        self.x_dev, self.y_dev = at_dev(core, z, yx ^ 1), at_dev(core, z, yx ^ 2)
        self.sib = at_dev(1 - core, z, yx)
        self.ends = []

    @staticmethod
    def scratch(count):
        dma = pltpu.SemaphoreType.DMA
        return [dma((count, 5, 4)), dma((count, 4, 4)), dma((count, 4, 4)), dma((count, 4, 4)), dma((count,))]

    def spot(self, p, z_at, d, core=None):
        i, first, rows = self.pieces[p]
        core = self.core if core is None else core
        size = self.shards[i].shape[0]
        start = pl.multiple_of((z_at * 4 + (self.yx ^ d)) * size + first, 16)
        return self.fulls[i].at[core, pl.ds(start, rows)]

    def copy(self, p, kind, z_at, d, src=None):
        there = {0: 0, 1: 0, 2: 1, 3: 2, 4: 3}[kind]
        ref = self.spot(p, z_at, d)
        device = (self.up_dev, self.down_dev, self.x_dev, self.y_dev)[kind] if kind < 4 else (self.y_dev if d == 1 else self.x_dev)
        return pltpu.make_async_remote_copy(
            src_ref=ref if src is None else src,
            dst_ref=ref,
            send_sem=self.send.at[p, kind, z_at],
            recv_sem=self.recv.at[p, there, z_at],
            device_id=device,
            device_id_type=MESH_ID,
        )

    def go(self, condition, p, kind, z_at, d, src=None):
        def start():
            self.copy(p, kind, z_at, d, src).start()

        def end():
            self.copy(p, kind, z_at, d, src).wait_send()

        if condition is None:
            start()
            self.ends.append(end)
        else:
            pl.when(condition)(start)
            self.ends.append(lambda: pl.when(condition)(end))

    def across(self, p, d):
        for z_at in range(4):
            ref = self.spot(p, z_at, d)
            copy = pltpu.make_async_remote_copy(
                src_ref=ref,
                dst_ref=ref,
                send_sem=self.send_s.at[p, d, z_at],
                recv_sem=self.recv_s.at[p, d, z_at],
                device_id=self.sib,
                device_id_type=MESH_ID,
            )
            copy.start()
            self.ends.append(copy.wait_send)

    def arrive(self, p, kind, z_at, d):
        ref = self.spot(p, z_at, d)
        pltpu.make_async_copy(ref, ref, self.recv.at[p, kind, z_at]).wait()

    def own(self, p):
        i, first, rows = self.pieces[p]
        src = self.shards[i].at[pl.ds(first, rows)]
        z = self.z
        self.go(z < 3, p, 0, z, 0, src)
        self.go(z > 0, p, 1, z, 0, src)
        self.go(None, p, 2, z, 0, src)
        self.go(None, p, 3, z, 0, src)
        copy = pltpu.make_async_copy(src, self.spot(p, z, 0), self.local.at[p])
        copy.start()
        self.locals_ = getattr(self, "locals_", {})
        self.locals_[p] = copy

    def z_step(self, p, r):
        z = self.z
        for side in (-1, 1):
            there = (z - r >= 0) if side < 0 else (z + r <= 3)
            z_at = z + side * r

            def landed(z_at=z_at):
                self.arrive(p, 0, z_at, 0)

            pl.when(there)(landed)
            if side < 0:
                self.go(there & (z < 3), p, 0, z_at, 0)
            else:
                self.go(there & (z > 0), p, 1, z_at, 0)
            self.go(there, p, 2, z_at, 0)
            self.go(there, p, 3, z_at, 0)

    def plane_step(self, p, r):
        z = self.z
        for side in (-1, 1) if r else (0,):
            z_at = z + side * r
            there = None if not r else ((z - r >= 0) if side < 0 else (z + r <= 3))

            def landed(z_at=z_at):
                self.arrive(p, 1, z_at, 1)
                self.arrive(p, 2, z_at, 2)

            if there is None:
                landed()
            else:
                pl.when(there)(landed)
            low_z, high_z = z_at < 2, z_at >= 2
            self.go(low_z if there is None else there & low_z, p, 4, z_at, 1)
            self.go(high_z if there is None else there & high_z, p, 4, z_at, 2)

    def stage(self, p, s):
        if s == 0:
            self.own(p)
        elif s == 1:
            self.z_step(p, 1)
            self.plane_step(p, 0)
        elif s == 2:
            self.z_step(p, 2)
            self.plane_step(p, 1)
        elif s == 3:
            self.z_step(p, 3)
            self.locals_[p].wait()
            self.across(p, 0)
            self.plane_step(p, 2)
        elif s == 4:
            self.plane_step(p, 3)
            self.across(p, 1)
            self.across(p, 2)
        elif s == 5:
            for z_at in range(4):
                self.arrive(p, 3, z_at, 3)
            self.across(p, 3)

    STAGES = 6

    def steps(self):
        return len(self.pieces) + self.STAGES - 1

    def run(self, t):
        for s in range(self.STAGES):
            if 0 <= t - s < len(self.pieces):
                self.stage(t - s, s)

    def landed(self, which=None):
        for p in range(len(self.pieces)) if which is None else which:
            for d in range(4):
                for z_at in range(4):
                    ref = self.spot(p, z_at, d, 1 - self.core)
                    pltpu.make_async_copy(ref, ref, self.recv_s.at[p, d, z_at]).wait()

    def finish(self):
        for end in self.ends:
            end()


def pieces_of(shards, splits):
    pieces = []
    for i, (shard, split) in enumerate(zip(shards, splits)):
        rows = shard.shape[0] // split
        pieces += [(i, j * rows, rows) for j in range(split)]
    return pieces


class Exchange:
    def __init__(self, out, landed, sems):
        self.out, self.landed = out, landed
        self.send, self.recv = sems
        self.core, z, yx = place()
        self.wide = z * 4 + yx

    def copy(self, w):
        return pltpu.make_async_remote_copy(
            src_ref=self.out.at[w],
            dst_ref=self.landed.at[self.wide],
            send_sem=self.send.at[w],
            recv_sem=self.recv.at[self.wide],
            device_id=(self.core, w),
            device_id_type=MESH_ID,
        )

    def push(self, w):
        pl.when(w != self.wide)(lambda: self.copy(w).start())

        def keep():
            self.landed[w] = self.out[w]

        pl.when(w == self.wide)(keep)

    def wait(self, w):
        def landed():
            ref = self.landed.at[w]
            pltpu.make_async_copy(ref, ref, self.recv.at[w]).wait()

        pl.when(w != self.wide)(landed)

    def finish(self):
        for w in range(16):
            pl.when(w != self.wide)(lambda w=w: self.copy(w).wait_send())


def column_of(row):
    return jnp.broadcast_to(row, (LANES, row.shape[1])).T[:, 0:1]


def exact(left_side, right_side, contract=(1, 0)):
    return lax.dot_general(
        left_side,
        right_side,
        (((contract[0],), (contract[1],)), ((), ())),
        precision=HIGHEST_PRECISION,
        preferred_element_type=jnp.float32,
    )


def gelu(values):
    return 0.5 * values * (1.0 + jnp.tanh(GELU_SCALE * (values + GELU_CUBE * values * values * values)))


def gradient(grads, inputs, out, rows, shard):
    count = rows // shard

    def body(c, carry):
        cols = pl.ds(pl.multiple_of(c * rows, LANES), rows)
        total = nn(grads[0, :, cols].astype(jnp.float32).T.astype(jnp.bfloat16), inputs[0])
        total = total + nn(grads[1, :, cols].astype(jnp.float32).T.astype(jnp.bfloat16), inputs[1])
        first = lax.rem(c * count, 4)
        out[c * count // 4, pl.ds(first, count)] = total.astype(jnp.bfloat16).reshape(count, shard, -1)
        return carry

    return body


def front_kernel(groups, slots, *refs):
    (m_qkv, m_out, m_up, m_down, cond_ref, ada_any, map_ref, embed_ref, vec3_ref, len_ref, squares_ref, tri_ref, pick_ref, rule_ref, cot_ref) = refs[:15]
    (f_qkv, f_out, f_up, f_down, ada_ref, h_ref, kept_any, out32_any, q_any, k_any, kt_any, vt_any, low_ref) = refs[15:28]
    (x_ref, smooth_ref, flags_ref, hot_ref, silu_ref, proj_ref, one_ref, two_ref, pre_any, act_any, p_any) = refs[28:39]
    (w_ref, send_ref, got_ref, back_send, back_got, v_ref, s_ref, load_sem) = refs[39:47]
    (w_ada, silu_own, theirs, ours, ada_in, edge, edge_left, edge_right, wo_ref, wu_ref, dmlp, act_half) = refs[47:59]
    (kept_ref, out32_ref, q_ref, k_ref, kt_ref, vt_ref, pre_ref, act_ref, p_down) = refs[59:68]
    (c_qkv, c_out, c_up, c_down, s_qkv, s_out, s_up, s_down, cast_sem, store_sem) = refs[68:78]
    sems = refs[78:]
    first_flow = Gather([s_qkv], [f_qkv], sems[:5], pieces_of([s_qkv], FRONT_SPLITS[0]))
    shards = [s_out, s_up, s_down]
    flow = Gather(shards, [f_out, f_up, f_down], sems[5:10], pieces_of(shards, FRONT_SPLITS[1]))
    ada_send, ada_recv = sems[10:12]
    there = Exchange(send_ref, got_ref, sems[12:14])
    home = Exchange(back_send, back_got, sems[14:16])
    ada_sem, sib_s, sib_r, edge_s, edge_r, wo_sem, wu_sem = sems[16:23]
    core, z, yx = place()
    wide = z * 4 + yx
    sib = (1 - core, wide)
    tokens, width = x_ref.shape
    half = width // 2
    mid = tokens // 2
    two = 2 * tokens
    group_len = q_ref.shape[0]
    f32, low = jnp.float32, jnp.bfloat16
    vec_ref = vec3_ref.at[1]
    casts = []
    for i, (src, dst) in enumerate(((m_qkv, c_qkv), (m_out, c_out), (m_up, c_up), (m_down, c_down))):
        casts.append(pltpu.make_async_copy(src.at[1], dst, cast_sem.at[i]))
        casts[-1].start()
    stores = []

    def store(*pairs):
        for src, dst in pairs:
            stores.append(pltpu.make_async_copy(src, dst, store_sem.at[len(stores)]))
            stores[-1].start()

    casts[0].wait()
    s_qkv[...] = c_qkv[...].astype(low)
    entry_barrier([(core, wide ^ r) for r in range(1, 16)] + [sib])

    def to_sib(slot, src, dst):
        copy = pltpu.make_async_remote_copy(
            src_ref=src, dst_ref=dst, send_sem=sib_s.at[slot], recv_sem=sib_r.at[slot], device_id=sib, device_id_type=MESH_ID
        )
        copy.start()
        return copy

    next_tick = [0]

    def tick(n):
        for _ in range(n):
            if next_tick[0] < flow.steps():
                flow.run(next_tick[0])
                next_tick[0] += 1

    def tick_to(n):
        tick(max(0, n - next_tick[0]))

    first_flow.run(0)
    ada_copy = pltpu.make_async_copy(ada_any.at[1], w_ada, ada_sem)
    ada_copy.start()
    cond = cond_ref[...]
    silu = (cond / (1.0 + jnp.exp(-cond))).astype(low).astype(f32)
    silu_own[...] = jnp.zeros_like(silu_own)
    silu_own[0:slots, :] = silu
    their_half = pl.ds(pl.multiple_of((1 - core) * half, half), half)
    my_half = pl.ds(pl.multiple_of(core * half, half), half)
    silu_copy = to_sib(0, silu_own.at[:, their_half], silu_ref.at[core])
    silu_ref[core] = silu_own[:, my_half]
    spot = lane_iota((32, LANES))
    cells = map_ref[...]
    edge[...] = jnp.where(spot == 0, cells[:, 0:1], jnp.where(spot == 1, cells[:, tokens - 1 : tokens], 0.0))

    def edge_copy(slot, dst, shift):
        return pltpu.make_async_remote_copy(
            src_ref=edge,
            dst_ref=dst,
            send_sem=edge_s.at[slot],
            recv_sem=edge_r.at[slot],
            device_id=(core, lax.rem(wide + shift, 16)),
            device_id_type=MESH_ID,
        )

    edges = [edge_copy(0, edge_left, 1), edge_copy(1, edge_right, 15)]
    for copy in edges:
        copy.start()
    first_flow.run(1)

    for copy in casts[1:]:
        copy.wait()
    s_out[...] = c_out[...].astype(low)
    s_up[...] = c_up[...].T.astype(low)
    s_down[...] = c_down[...].astype(low)

    run_lane = lane_iota((1, LANES))
    run_slot = lax.rem(run_lane - HALF_LANES + slots * LANES, slots)
    lens = jnp.zeros((1, LANES), jnp.int32)
    for j in range(slots):
        lens = jnp.where(run_slot == j, len_ref[0:1, j : j + 1], lens)
    counts = jnp.where(lens == LONG_TOTAL, squares_ref[0:1, :], jnp.where(lens == SHORT_TOTAL, squares_ref[1:2, :], 0.0))
    unused = group_len - jnp.sum(counts, axis=1, keepdims=True)
    counts = jnp.where(run_lane == HALF_LANES + slots * LEVELS, unused, counts)
    ends = exact(jnp.broadcast_to(counts, (8, LANES)), tri_ref[...])[0:1, :]
    starts = ends - counts
    start_col, end_col = column_of(starts), column_of(ends)
    here = (wide * tokens + lane_iota((1, tokens))).astype(f32)
    left = 1.0 - jnp.sum(((here == start_col) & (here < end_col)).astype(f32), axis=0, keepdims=True)
    right = 1.0 - jnp.sum(((here == end_col - 1.0) & (here >= start_col)).astype(f32), axis=0, keepdims=True)
    flags_ref[...] = jnp.zeros_like(flags_ref)
    flags_ref[0:1, :] = left
    flags_ref[1:2, :] = right
    row_at = (wide * tokens + lax.broadcasted_iota(jnp.int32, (tokens, LANES), 0)).astype(f32)
    my_runs = ((row_at >= starts) & (row_at < ends)).astype(low)
    hot = nn(my_runs, pick_ref[...])[:, 0:8]
    hot_ref[...] = hot

    ada_copy.wait()
    w_low = w_ada[...].astype(low)
    silu_copy.wait_recv()
    theirs[...] = nn(silu_ref[1 - core].astype(low), w_low)
    part_copy = to_sib(1, theirs, ours)
    mine = nn(silu_ref[core].astype(low), w_low)
    first_flow.run(2)

    for copy in edges:
        copy.wait_recv()
    column = lane_iota((32, tokens))
    before = jnp.where(column == 0, edge_left[:, 1:2], jnp.roll(cells, 1, axis=1))
    after = jnp.where(column == tokens - 1, edge_right[:, 0:1], jnp.roll(cells, -1, axis=1))
    smooth = smooth_map(cells, left, right, before, after)
    smooth_ref[...] = smooth
    x = exact(smooth, embed_ref[1], (0, 0)) + vec_ref[6:7, :]
    x_ref[...] = x
    part_copy.wait_recv()
    ada_in[...] = mine + ours[...]
    ada_copies = []
    for r in range(1, 16):
        copy = pltpu.make_async_remote_copy(
            src_ref=ada_in,
            dst_ref=ada_ref.at[wide],
            send_sem=ada_send.at[r],
            recv_sem=ada_recv.at[r],
            device_id=(core, wide ^ r),
            device_id_type=MESH_ID,
        )
        copy.start()
        ada_copies.append(copy)
    ada_ref[wide] = ada_in[...]

    def standard(values):
        centred = values - jnp.mean(values, axis=1, keepdims=True)
        return centred * lax.rsqrt(jnp.mean(centred * centred, axis=1, keepdims=True) + NORM_EPS)

    unit = standard(x)
    first_flow.run(3)
    for copy in ada_copies:
        copy.wait_recv()
    ada = jnp.concatenate([ada_ref[w] for w in range(16)], axis=1)

    def of_tokens(block):
        return exact(hot, ada[:, block * width : (block + 1) * width] + vec_ref[block : block + 1, :])

    h_ref[...] = (unit * (1.0 + of_tokens(2)) + of_tokens(4)).astype(low)
    for i, t in enumerate(range(4, first_flow.steps())):
        first_flow.run(t)
        tick(FRONT_TICKS[0][min(i, 3)])
    first_flow.landed()

    group = 256
    loads = []

    def load(j):
        g = lax.rem(z + 1 + j, 4)
        out = []
        for c in range(2):
            for part in range(3):
                rows = pl.ds(pl.multiple_of(g * group + part * width, group), group)
                out.append(pltpu.make_async_copy(f_qkv.at[c, rows], w_ref.at[j, c, part], load_sem.at[j, c, part]))
        return out

    for j in range(4):
        loads.append(load(j))
        for copy in loads[-1]:
            copy.start()
    lane = lane_iota((tokens, LANES))
    lane_mid = lane_iota((mid, LANES))
    for j in range(4):
        g = lax.rem(z + 1 + j, 4)
        first = pl.multiple_of(g * group, group)
        for copy in loads[j]:
            copy.wait()

        def project(part):
            return nt(h_ref[:, :half], w_ref[j, 0, part]) + nt(h_ref[:, half:], w_ref[j, 1, part])

        q_all, k_all, v_all = (project(part) for part in range(3))
        for pair in range(group // LANES):
            cols = slice(pair * LANES, (pair + 1) * LANES)
            at = g * (group // LANES) + pair
            kept_ref[at] = q_all[:, cols]
            kept_ref[at + width // LANES] = k_all[:, cols]
        q_all = q_all * lax.rsqrt(head_sums(q_all * q_all) + NORM_EPS)
        q_all = q_all * (8.0 * (1.0 + vec_ref[7:8, pl.ds(first, group)]))
        k_all = k_all * lax.rsqrt(head_sums(k_all * k_all) + NORM_EPS)
        for pair in range(group // LANES):
            cols = slice(pair * LANES, (pair + 1) * LANES)
            q, k, v = q_all[:, cols], k_all[:, cols], v_all[:, cols]
            head = g * (group // HALF_LANES) + 2 * pair
            send_ref[head, 0:tokens, :] = jnp.where(lane < HALF_LANES, q, swap_halves(k)).astype(low)
            send_ref[head + 1, 0:tokens, :] = jnp.where(lane < HALF_LANES, swap_halves(q), k).astype(low)
            v_a, v_b = v[:mid], v[mid:]
            send_ref[head, tokens:, :] = jnp.where(lane_mid < HALF_LANES, v_a, swap_halves(v_b)).astype(low)
            send_ref[head + 1, tokens:, :] = jnp.where(lane_mid < HALF_LANES, swap_halves(v_a), v_b).astype(low)
        for e in range(4):
            there.push(g * 4 + e)
        tick(FRONT_TICKS[1][j])

    lane_two = lane_iota((two, LANES))

    def unpack(pair, carry):
        for e in range(2):
            there.wait(2 * pair + e)
        first = pl.multiple_of(pair * two, two)
        qk = jnp.concatenate([got_ref[2 * pair + e, 0:tokens, :].astype(f32) for e in range(2)], axis=0)
        spot = (first + lax.broadcasted_iota(jnp.int32, (two, LANES), 0)).astype(f32)
        runs = ((spot >= starts) & (spot < ends)).astype(f32)
        barred = nn(runs.astype(low), rule_ref[...])
        rows = pl.ds(first, two)
        q_ref[rows, :] = jnp.where(lane_two < HALF_LANES, qk, barred).astype(low)
        tail = jnp.where(lane_two >= LANES - 3, 1.0, runs)
        keys = jnp.where(lane_two < HALF_LANES, swap_halves(qk), tail)
        k_ref[rows, :] = keys.astype(low)
        kt_ref[:, rows] = keys.T.astype(low)
        ones = ((lane_mid >= HALF_LANES) & (lane_mid < HALF_LANES + 3)).astype(f32)
        pieces = []
        for e in range(2):
            v = got_ref[2 * pair + e, tokens:, :].astype(f32)
            pieces.append(jnp.where(lane_mid < HALF_LANES, v, ones))
            pieces.append(jnp.where(lane_mid < HALF_LANES, swap_halves(v), ones))
        values = jnp.concatenate(pieces, axis=0)
        v_ref[rows, :] = values.astype(low)
        vt_ref[:, rows] = values.T.astype(low)
        return carry

    lane_q = lane_iota((ROWS, LANES))

    def query_block(limit, b, carry):
        rows = pl.ds(pl.multiple_of(b * ROWS, ROWS), ROWS)
        q = q_ref[rows, :]

        def score(c, top):
            cols = pl.ds(pl.multiple_of(c * CHUNK, CHUNK), CHUNK)
            s = nn(q, kt_ref[:, cols])
            s_ref[:, cols] = s
            return jnp.maximum(top, fold_lanes(s, jnp.maximum))

        whole, left = limit // CHUNK, limit % CHUNK
        top = lax.fori_loop(0, whole, score, jnp.full((ROWS, LANES), -3e38, f32))
        if left:
            tail = slice(whole * CHUNK, limit)
            s = nn(q, kt_ref[:, tail])
            s_ref[:, tail] = s
            top = jnp.maximum(top, fold_lanes(s, jnp.maximum))
        peak = jnp.max(top, axis=1, keepdims=True)

        def weigh(cols, carry):
            total, acc = carry
            p = jnp.exp(s_ref[:, cols] - peak)
            return total + fold_lanes(p, jnp.add), acc + nn(p.astype(low), v_ref[cols, :])

        zero = jnp.zeros((ROWS, LANES), f32)
        total, acc = lax.fori_loop(
            0,
            whole,
            lambda c, carry: weigh(pl.ds(pl.multiple_of(c * CHUNK, CHUNK), CHUNK), carry),
            (zero, zero),
        )
        if left:
            total, acc = weigh(slice(whole * CHUNK, limit), (total, acc))
        total = jnp.sum(total, axis=1, keepdims=True)
        out32_ref[rows, :] = acc / total
        log_total = peak + jnp.log(total)
        q_ref[rows, :] = lanes_three(lane_q, LANES - 3, -log_total, q.astype(f32)).astype(low)
        return carry

    def give_back(w, carry):
        rows = pl.multiple_of(w * tokens, tokens)
        a = out32_ref[pl.ds(rows, mid), :]
        b = out32_ref[pl.ds(pl.multiple_of(rows + mid, mid), mid), :]
        back_send[w] = jnp.where(lane_mid < HALF_LANES, a, swap_halves(b)).astype(low)
        home.push(w)
        return carry

    store((kept_ref, kept_any))
    for i in range(4):
        lax.fori_loop(2 * i, 2 * i + 2, unpack, 0)
        tick(FRONT_TICKS[2][i])
    store((k_ref, k_any), (kt_ref, kt_any), (vt_ref, vt_any))
    plane = 4 * tokens // ROWS
    for p in range(4):
        for first, last, limit in groups:
            begin, end = max(first, p * plane), min(last, (p + 1) * plane)
            for b in range(begin, end):
                lax.fori_loop(b, b + 1, functools.partial(query_block, limit), 0)
                tick(FRONT_TICKS[3][b])
        lax.fori_loop(4 * p, 4 * p + 4, give_back, 0)
    store((q_ref, q_any), (out32_ref, out32_any))
    splits = FRONT_SPLITS[1]
    tick_to(splits[0] + 5)
    flow.landed(range(splits[0]))
    wo_copy = pltpu.make_async_copy(f_out, wo_ref, wo_sem)
    wo_copy.start()
    for pair in range(8):
        home.wait(2 * pair)
        home.wait(2 * pair + 1)
        cols = slice(pair * LANES, (pair + 1) * LANES)
        even, odd = back_got[2 * pair].astype(f32), back_got[2 * pair + 1].astype(f32)
        low_ref[0:mid, cols] = jnp.where(lane_mid < HALF_LANES, even, swap_halves(odd)).astype(low)
        low_ref[mid:, cols] = jnp.where(lane_mid < HALF_LANES, swap_halves(even), odd).astype(low)

    wo_copy.wait()
    proj = nt(low_ref[:, :half], wo_ref[0]) + nt(low_ref[:, half:], wo_ref[1])
    proj_ref[...] = proj
    x_one = x_ref[...] + of_tokens(0) * proj
    one_ref[...] = x_one
    two_ref[...] = (standard(x_one) * (1.0 + of_tokens(3)) + of_tokens(5)).astype(low)
    ups = range(splits[0], splits[0] + splits[1])
    tick_to(ups[-1] + 6)
    flow.landed(ups)
    step = 512
    hidden = pre_ref.shape[1]

    def load_up(c):
        rows = pl.ds(pl.multiple_of(c * step, step), step)
        slot = lax.rem(c, 2)
        return pltpu.make_async_copy(f_up.at[:, rows], wu_ref.at[slot], wu_sem.at[slot])

    load_up(0).start()

    def up_step(c, carry):
        pl.when(c + 1 < hidden // step)(lambda: load_up(c + 1).start())
        load_up(c).wait()
        w = wu_ref.at[lax.rem(c, 2)]
        pre = nt(two_ref[:, :half], w[0]) + nt(two_ref[:, half:], w[1])
        cols = pl.ds(pl.multiple_of(c * step, step), step)
        pre_ref[:, cols] = pre
        act_ref[:, cols] = gelu(pre).astype(low)
        return carry

    live = jnp.sum(hot, axis=1, keepdims=True)
    dmlp[core] = (of_tokens(1) * (cot_ref[...].astype(f32) * live)).astype(low)
    pair_copies = [to_sib(2, dmlp.at[core], dmlp.at[core])]
    hid_half = hidden // 2
    hid_theirs = pl.ds(pl.multiple_of((1 - core) * hid_half, hid_half), hid_half)
    hid_mine = pl.ds(pl.multiple_of(core * hid_half, hid_half), hid_half)
    for i in range(2):
        lax.fori_loop(4 * i, 4 * i + 4, up_step, 0)
        tick(FRONT_TICKS[4][i])
    store((pre_ref, pre_any), (act_ref, act_any))
    pair_copies.append(to_sib(3, act_ref.at[:, hid_theirs], act_half.at[core]))
    act_half[core] = act_ref[:, hid_mine]
    tick(FRONT_TICKS[4][2])
    for copy in pair_copies:
        copy.wait_recv()
    lax.fori_loop(0, width // LANES, gradient(dmlp, act_half, p_down, LANES, width // 16), 0)
    store((p_down, p_any))
    tick(flow.steps())
    flow.landed(range(ups[-1] + 1, sum(splits)))
    first_flow.finish()
    flow.finish()
    there.finish()
    home.finish()
    for copy in ada_copies + edges + pair_copies + [silu_copy, part_copy]:
        copy.wait_send()
    for copy in stores:
        copy.wait()


def front(states, condition, ada_state, cells, embed_state, vector_state, lengths, tables, cotangent, groups):
    width = condition.shape[1]
    tokens = cells.shape[1]
    slots = lengths.shape[1]
    group_len = 16 * tokens
    hidden = 16 * states[2].shape[2]
    f32, low = jnp.float32, jnp.bfloat16
    dma = pltpu.SemaphoreType.DMA
    shape = jax.ShapeDtypeStruct
    ada_width = ada_state.shape[2]
    shards = [s.shape[1:] if i != 2 else s.shape[:0:-1] for i, s in enumerate(states)]
    fulls = [shape((2, 16 * s[0], s[1]), low) for s in shards]
    outs = fulls + [
        shape((16, 8, ada_width), f32),
        shape((tokens, width), low),
        shape((2 * width // LANES, tokens, LANES), f32),
        shape((group_len, LANES), f32),
        shape((group_len, LANES), low),
        shape((group_len, LANES), low),
        shape((LANES, group_len), low),
        shape((LANES, group_len), low),
        shape((tokens, width), low),
        shape((tokens, width), f32),
        shape(cells.shape, f32),
        shape((8, tokens), f32),
        shape((tokens, 8), f32),
        shape((2, 8, width // 2), f32),
        shape((tokens, width), f32),
        shape((tokens, width), f32),
        shape((tokens, width), low),
        shape((tokens, hidden), f32),
        shape((tokens, hidden), low),
        shape((4, 4, width // 16, hidden // 2), low),
    ]
    packed, mid = tokens * 3 // 2, tokens // 2
    scratch = [
        pltpu.VMEM((4, 2, 3, 256, width // 2), low),
        pltpu.VMEM((16, packed, LANES), low),
        pltpu.VMEM((16, packed, LANES), low),
        pltpu.VMEM((16, mid, LANES), low),
        pltpu.VMEM((16, mid, LANES), low),
        pltpu.VMEM((group_len, LANES), low),
        pltpu.VMEM((ROWS, group_len), f32),
        dma((4, 2, 3)),
        pltpu.VMEM(ada_state.shape[1:], f32),
        pltpu.VMEM((8, width), f32),
        pltpu.VMEM((8, ada_width), f32),
        pltpu.VMEM((8, ada_width), f32),
        pltpu.VMEM((8, ada_width), f32),
        pltpu.VMEM((32, LANES), f32),
        pltpu.VMEM((32, LANES), f32),
        pltpu.VMEM((32, LANES), f32),
        pltpu.VMEM((2, width, width // 2), low),
        pltpu.VMEM((2, 2, 512, width // 2), low),
        pltpu.VMEM((2, tokens, width), low),
        pltpu.VMEM((2, tokens, hidden // 2), low),
    ]
    scratch += [pltpu.VMEM(o.shape, o.dtype) for o in outs[6:12] + outs[21:24]]
    scratch += [pltpu.VMEM(s.shape[1:], f32) for s in states] + [pltpu.VMEM(s, low) for s in shards]
    scratch += [dma((4,)), dma((10,))]
    scratch += Gather.scratch(sum(FRONT_SPLITS[0])) + Gather.scratch(sum(FRONT_SPLITS[1])) + [dma((16,)) for _ in range(6)]
    scratch += [dma, dma((4,)), dma((4,)), dma((2,)), dma((2,)), dma, dma((2,))]
    return pl.pallas_call(
        functools.partial(front_kernel, groups, slots),
        out_shape=outs,
        in_specs=[ANY] * 4 + [VM, ANY] + [VM] * 9,
        out_specs=[ANY] * 4 + [VM] * 2 + [ANY] * 6 + [VM] * 9 + [ANY] * 3,
        scratch_shapes=scratch,
        compiler_params=pltpu.CompilerParams(
            collective_id=0, has_side_effects=True, vmem_limit_bytes=VMEM_BYTES
        ),
    )(*states, condition, ada_state, cells, embed_state, vector_state, lengths, *tables, cotangent)


class Scatter:
    STAGES = 6

    def __init__(self, parts, outs, bufs, sems, pieces):
        self.parts, self.outs, self.bufs, self.pieces = parts, outs, bufs, pieces
        self.send, self.recv = sems
        self.parts_left = {}
        core, z, yx = place()
        self.z, self.yx = z, yx
        self.x_dev, self.y_dev = at_dev(core, z, yx ^ 1), at_dev(core, z, yx ^ 2)
        self.up_dev, self.down_dev = at_dev(core, lax.min(z + 1, 3), yx), at_dev(core, lax.max(z - 1, 0), yx)
        self.ends = []

    @staticmethod
    def scratch(shapes, count):
        out = []
        for rows, cols in shapes:
            out += [pltpu.VMEM((depth, rows, cols), jnp.bfloat16) for depth in (2, 2, 4, 4, 3, 3)]
        dma = pltpu.SemaphoreType.DMA
        return out + [dma((count, 8)), dma((count, 8))]

    def push(self, p, slot, src, dst, device):
        copy = pltpu.make_async_remote_copy(
            src_ref=src,
            dst_ref=dst,
            send_sem=self.send.at[p, slot],
            recv_sem=self.recv.at[p, slot],
            device_id=device,
            device_id_type=MESH_ID,
        )
        copy.start()
        return copy

    def arrive(self, p, slot, ref):
        pltpu.make_async_copy(ref, ref, self.recv.at[p, slot]).wait()

    def stage(self, p, s):
        i, first, rows = self.pieces[p]
        rows = pl.ds(first, rows)
        part = self.parts[i]
        names = ("turn_x", "turn_y", "rx", "ry", "up", "down")
        buf = dict(zip(names, self.bufs[6 * i : 6 * i + 6]))
        z, yx = self.z, self.yx
        f32, low = jnp.float32, jnp.bfloat16
        lo2, hi2 = pl.ds(0, 2), pl.ds(2, 2)

        def view(name, which):
            return buf[name].at[which, rows]

        def wide(ref):
            return ref[...].astype(f32)

        def hop(condition, slot, name, which, device):
            ref = view(name, which)

            def start():
                self.push(p, slot, ref, ref, device)

            def end():
                pltpu.make_async_copy(ref, ref, self.send.at[p, slot]).wait()

            pl.when(condition)(start)
            self.ends.append(lambda: pl.when(condition)(end))

        if s == 0:
            copies = [
                self.push(p, 0, part.at[lo2, yx ^ 3, rows], view("turn_x", lo2), self.x_dev),
                self.push(p, 1, part.at[hi2, yx ^ 3, rows], view("turn_y", lo2), self.y_dev),
                self.push(p, 2, part.at[lo2, yx ^ 1, rows], view("rx", lo2), self.x_dev),
                self.push(p, 3, part.at[hi2, yx ^ 2, rows], view("ry", hi2), self.y_dev),
            ]
            self.parts_left[p] = [copy.wait_send for copy in copies]
        elif s == 1:
            turn = view("turn_x", lo2)
            self.arrive(p, 0, turn)
            turn[...] = (wide(part.at[lo2, yx ^ 2, rows]) + wide(turn)).astype(low)
            self.ends.append(self.push(p, 4, turn, view("ry", lo2), self.y_dev).wait_send)
            turn = view("turn_y", lo2)
            self.arrive(p, 1, turn)
            turn[...] = (wide(part.at[hi2, yx ^ 1, rows]) + wide(turn)).astype(low)
            self.ends.append(self.push(p, 5, turn, view("rx", hi2), self.x_dev).wait_send)
        elif s == 2:
            self.arrive(p, 2, view("rx", lo2))
            self.arrive(p, 3, view("ry", hi2))
            self.arrive(p, 4, view("ry", lo2))
            self.arrive(p, 5, view("rx", hi2))
            self.outs[i][rows] = wide(part.at[z, yx, rows]) + wide(view("rx", z)) + wide(view("ry", z))
            for z_at in range(4):
                total = wide(part.at[z_at, yx, rows]) + wide(view("rx", z_at)) + wide(view("ry", z_at))
                view("rx", z_at)[...] = total.astype(low)

            def first_up():
                view("up", pl.ds(0, 3))[...] = view("rx", pl.ds(1, 3))[...]

            def first_down():
                view("down", pl.ds(0, 3))[...] = view("rx", pl.ds(0, 3))[...]

            pl.when(z == 0)(first_up)
            hop(z == 0, 6, "up", pl.ds(0, 3), self.up_dev)
            pl.when(z == 3)(first_down)
            hop(z == 3, 7, "down", pl.ds(0, 3), self.down_dev)
        elif s in (3, 4):
            at = s - 2
            count = 3 - at

            def add_up():
                self.arrive(p, 6, view("up", pl.ds(at - 1, count + 1)))
                ref = view("up", pl.ds(at, count))
                ref[...] = (wide(ref) + wide(view("rx", pl.ds(at + 1, count)))).astype(low)

            def add_down():
                self.arrive(p, 7, view("down", pl.ds(0, count + 1)))
                ref = view("down", pl.ds(0, count))
                ref[...] = (wide(ref) + wide(view("rx", pl.ds(0, count)))).astype(low)

            pl.when(z == at)(add_up)
            hop(z == at, 6, "up", pl.ds(at, count), self.up_dev)
            pl.when(z == 3 - at)(add_down)
            hop(z == 3 - at, 7, "down", pl.ds(0, count), self.down_dev)
        else:
            out = self.outs[i].at[rows]

            def end_low():
                self.arrive(p, 7, view("down", pl.ds(0, 1)))
                out[...] += wide(view("down", 0))

            def end_high():
                self.arrive(p, 6, view("up", pl.ds(2, 1)))
                out[...] += wide(view("up", 2))

            def end_inner(at):
                out[...] += wide(view("up", at - 1)) + wide(view("down", at))

            pl.when(z == 0)(end_low)
            pl.when(z == 1)(lambda: end_inner(1))
            pl.when(z == 2)(lambda: end_inner(2))
            pl.when(z == 3)(end_high)

    def steps(self):
        return len(self.pieces) + self.STAGES - 1

    def run(self, t):
        for s in reversed(range(self.STAGES)):
            if 0 <= t - s < len(self.pieces):
                self.stage(t - s, s)

    def sent(self, p):
        for end in self.parts_left.pop(p, ()):
            end()

    def finish(self):
        for p in list(self.parts_left):
            self.sent(p)
        for end in self.ends:
            end()


COMMON_ROWS = 48
FRONT_SPLITS = ((2,), (1, 4, 4))
FRONT_TICKS = ((1, 1, 1, 0), (0, 1, 0, 1), (0, 0, 0, 1), (0, 0, 0, 0, 0, 1, 0, 0, 1, 0, 0, 1), (1, 1, 1))
BACK_SPLITS = ((4, 4, 1), (3,))
BACK_TICKS = ((1, 0, 1, 1), (1, 0), (0, 0, 0, 1), (0, 1, 1, 0), (1, 1, 1), (1, 1))


def standard_of(values):
    centred = values - jnp.mean(values, axis=1, keepdims=True)
    rstd = lax.rsqrt(jnp.mean(centred * centred, axis=1, keepdims=True) + NORM_EPS)
    return centred * rstd, rstd


def standard_back(unit, rstd, d_unit):
    along = jnp.mean(d_unit * unit, axis=1, keepdims=True)
    return rstd * (d_unit - jnp.mean(d_unit, axis=1, keepdims=True) - unit * along)


def gelu_slope(values):
    square = values * values
    inner = jnp.tanh(GELU_SCALE * (values + GELU_CUBE * values * square))
    slope = GELU_SCALE * (1.0 + 3.0 * GELU_CUBE * square)
    return 0.5 * (1.0 + inner) + 0.5 * values * (1.0 - inner * inner) * slope


def back_kernel(groups, splits, *refs):
    (
        cot_ref, hot_ref, ada_in, vec3_ref, x_ref, one_ref, proj_ref, h_any, two_any, low_any, act_any, pre_any,
        w_any, wo_any, wu_any, wd_any, book_any, out32_any, q_any, k_any, kt_any, vt_any, kept_any,
        smooth_ref, embed_ref, ok_ref, p_any,
    ) = refs[:27]
    (o_down, o_up, o_out, o_qkv, ada_both, common_all, bias_all, map_ref, block_ref) = refs[27:36]
    (
        send_ref, got_ref, back_send, back_got, g_ref, gt_ref, qt_ref, dq_ref, dkt_ref, dvt_ref,
        w_buf, dhid, h_both, dh_ref, ada_ref, com_ref, ada_land, com_land, ada_sum, com_sum, ada_sib, com_sib,
        bias_own, com_own, edge, edge_left, edge_right,
        dmlp, two_half, low_half, dattn, mlp_ref, dx_one, act_buf, pre_buf, d_att, p_up, p_out, p_down, q_ref, k_ref, kt_ref, vt_ref, early_sem, att_send, att_got, dq_s, dq_r,
    ) = refs[36:84]
    rest = refs[84:]
    flow_bufs, rest = rest[:18], rest[18:]
    flow_sems, rest = rest[:2], rest[2:]
    last_bufs, rest = rest[:6], rest[6:]
    last_sems, rest = rest[:2], rest[2:]
    (
        ex_s, ex_r, home_s, home_r, w_sem, sib_s, sib_r, small_s, small_r, spread_s, spread_r, edge_s, edge_r,
        hid_s, hid_r, half_sem, kept_sem, free_sem,
    ) = rest
    core, z, yx = place()
    wide = z * 4 + yx
    sib = (1 - core, wide)
    f32, low = jnp.float32, jnp.bfloat16
    tokens, width = x_ref.shape
    half = width // 2
    hidden = dhid.shape[2]
    mid = tokens // 2
    two = 2 * tokens
    step = 512
    vec_ref = vec3_ref.at[1]
    dproj = dhid.at[:, :, pl.ds(0, 3 * width)]
    p_qkv = p_up.at[:, :, pl.ds(0, tokens)]
    flow = Scatter([p_down, p_up, p_out], [o_down, o_up, o_out], flow_bufs, flow_sems, splits[0])
    last = Scatter([p_qkv], [o_qkv], last_bufs, last_sems, splits[1])
    there = Exchange(att_send, att_got, (ex_s, ex_r))
    home = Exchange(send_ref, got_ref, (home_s, home_r))
    back = Exchange(back_send, back_got, (dq_s, dq_r))
    early = [
        pltpu.make_async_copy(src, dst, early_sem.at[i])
        for i, (src, dst) in enumerate(
            [(p_any, p_down), (q_any, q_ref), (k_any, k_ref), (kt_any, kt_ref), (vt_any, vt_ref)]
        )
    ]
    for copy in early:
        copy.start()
    entry_barrier([(core, wide ^ r) for r in range(1, 16)] + [sib])

    def to_sib(slot, src, dst):
        copy = pltpu.make_async_remote_copy(
            src_ref=src, dst_ref=dst, send_sem=sib_s.at[slot], recv_sem=sib_r.at[slot], device_id=sib, device_id_type=MESH_ID
        )
        copy.start()
        return copy

    next_tick = [0]

    def tick(n):
        for _ in range(n):
            if next_tick[0] < flow.steps():
                flow.run(next_tick[0])
                next_tick[0] += 1

    lane = lane_iota((two, LANES))
    lane_tok = lane_iota((tokens, LANES))
    lane_mid = lane_iota((mid, LANES))

    def load_chunk(c):
        slot = lax.rem(c, 2)
        cols = pl.ds(pl.multiple_of(c * step, step), step)
        down_cols = pl.ds(pl.multiple_of(lax.rem(c, hidden // 2 // step) * step, step), step)
        down = wd_any.at[c // (hidden // 2 // step)]
        pairs = [
            (down.at[pl.ds(0, half), down_cols], w_buf.at[slot, 0]),
            (down.at[pl.ds(half, half), down_cols], w_buf.at[slot, 1]),
            (wu_any.at[0, cols], w_buf.at[slot, 2]),
            (wu_any.at[1, cols], w_buf.at[slot, 3]),
            (act_any.at[:, cols], act_buf.at[slot]),
            (pre_any.at[:, cols], pre_buf.at[slot]),
        ]
        return [pltpu.make_async_copy(src, dst, w_sem.at[slot, i]) for i, (src, dst) in enumerate(pairs)]

    def start_chunk(c):
        for copy in load_chunk(c):
            copy.start()

    start_chunk(0)
    out32_copy = pltpu.make_async_copy(out32_any, dq_ref, kept_sem)
    out32_copy.start()
    theirs = pl.ds(pl.multiple_of((1 - core) * half, half), half)
    mine = pl.ds(pl.multiple_of(core * half, half), half)
    ada = jnp.concatenate([ada_in[w] for w in range(16)], axis=1)
    hot = hot_ref[...]

    def of_tokens(block):
        return exact(hot, ada[:, block * width : (block + 1) * width] + vec_ref[block : block + 1, :])

    live = jnp.sum(hot, axis=1, keepdims=True)
    gate_two = of_tokens(1)
    dmlp[...] = (gate_two * (cot_ref[...].astype(f32) * live)).astype(low)
    sib_copies = [
        to_sib(2, two_any.at[:, theirs], two_half.at[core]),
        to_sib(3, low_any.at[:, theirs], low_half.at[core]),
        to_sib(4, h_any.at[:, theirs], h_both.at[core]),
    ]
    half_copies = [
        pltpu.make_async_copy(src, dst.at[core], half_sem.at[i])
        for i, (src, dst) in enumerate(
            [
                (two_any.at[:, mine], two_half),
                (low_any.at[:, mine], low_half),
                (h_any.at[:, mine], h_both),
            ]
        )
    ]
    for copy in half_copies:
        copy.start()
    mlp_ref[...] = jnp.zeros_like(mlp_ref)
    dh_ref[...] = jnp.zeros_like(dh_ref)

    def hid_copy(c):
        cols = pl.ds(pl.multiple_of(c * step, step), step)
        return pltpu.make_async_remote_copy(
            src_ref=dhid.at[core, :, cols],
            dst_ref=dhid.at[core, :, cols],
            send_sem=hid_s.at[c],
            recv_sem=hid_r.at[c],
            device_id=sib,
            device_id_type=MESH_ID,
        )

    def hidden_step(c, carry):
        pl.when(c + 1 < hidden // step)(lambda: start_chunk(c + 1))
        for copy in load_chunk(c):
            copy.wait()
        slot = lax.rem(c, 2)
        w = w_buf.at[slot]
        d_act = nn(dmlp[:, :half], w[0]) + nn(dmlp[:, half:], w[1])
        d_hid = (d_act * gelu_slope(pre_buf[slot])).astype(low)
        dhid[core, :, pl.ds(pl.multiple_of(c * step, step), step)] = d_hid
        hid_copy(c).start()
        act = act_buf[slot]
        mlp_ref[:, :half] += nt(act, w[0])
        mlp_ref[:, half:] += nt(act, w[1])
        dh_ref[:, :half] += nn(d_hid, w[2])
        dh_ref[:, half:] += nn(d_hid, w[3])
        return carry

    chunks = hidden // step
    early[0].wait()
    for i in range(4):
        tick(BACK_TICKS[0][i])
        lax.fori_loop(2 * i, 2 * i + 2, hidden_step, 0)

    wo_copies = [
        pltpu.make_async_copy(wo_any.at[c, pl.ds(r * half, half)], w_buf.at[0, 2 * c + r], w_sem.at[0, 2 * c + r])
        for c in range(2)
        for r in range(2)
    ]
    for copy in wo_copies:
        copy.start()
    unit, rstd = standard_of(one_ref[...])
    g_two = cot_ref[...].astype(f32) * live
    d_one = standard_back(unit, rstd, dh_ref[...] * (1.0 + of_tokens(3))) + g_two
    dx_one[...] = d_one
    dattn[core] = (of_tokens(0) * d_one).astype(low)
    sib_copies.append(to_sib(5, dattn.at[core], dattn.at[core]))
    for copy in wo_copies:
        copy.wait()
    for c in range(2):
        part = nn(dattn[core, :, :half], w_buf[0, 2 * c]) + nn(dattn[core, :, half:], w_buf[0, 2 * c + 1])
        d_att[:, c * half : (c + 1) * half] = part.astype(low)

    def pack(pair, carry):
        cols = pl.ds(pl.multiple_of(pair * LANES, LANES), LANES)
        a, b = d_att[0:mid, cols].astype(f32), d_att[mid:, cols].astype(f32)
        att_send[2 * pair] = jnp.where(lane_mid < HALF_LANES, a, swap_halves(b)).astype(low)
        att_send[2 * pair + 1] = jnp.where(lane_mid < HALF_LANES, swap_halves(a), b).astype(low)
        there.push(2 * pair)
        there.push(2 * pair + 1)
        return carry

    lax.fori_loop(0, 8, pack, 0)

    def per_slot(values):
        return exact(hot, values, (0, 0))

    ada_ref[:, 3 * width : 4 * width] = per_slot(dh_ref[...] * unit)
    ada_ref[:, 5 * width : 6 * width] = per_slot(dh_ref[...])
    ada_ref[:, 0:width] = per_slot(d_one * proj_ref[...])
    ada_ref[:, width : 2 * width] = per_slot(g_two * mlp_ref[...])
    block_ref[...] = (live * (one_ref[...] + gate_two * mlp_ref[...])).astype(low)
    for c in range(chunks):
        hid_copy(c).wait_recv()
    half_copies[0].wait()
    sib_copies[0].wait_recv()
    lax.fori_loop(0, hidden // 256, gradient(dhid, two_half, p_up, 256, hidden // 16), 0)
    for c in range(chunks):
        hid_copy(c).wait_send()
    pl.semaphore_signal(free_sem, inc=1, device_id=sib, device_id_type=MESH_ID)
    tick(BACK_TICKS[1][0])
    half_copies[1].wait()
    sib_copies[1].wait_recv()
    sib_copies[3].wait_recv()
    lax.fori_loop(0, width // LANES, gradient(dattn, low_half, p_out, LANES, width // 16), 0)
    tick(BACK_TICKS[1][1])
    dkt_ref[...] = jnp.zeros_like(dkt_ref)
    dvt_ref[...] = jnp.zeros_like(dvt_ref)

    def unpack(pair, carry):
        there.wait(2 * pair)
        there.wait(2 * pair + 1)
        rows = pl.ds(pl.multiple_of(pair * two, two), two)
        pieces = []
        for e in range(2):
            g = att_got[2 * pair + e].astype(f32)
            pieces += [g, swap_halves(g)]
        grad = jnp.where(lane < HALF_LANES, jnp.concatenate(pieces, axis=0), 0.0)
        delta = jnp.sum(grad * dq_ref[rows, :], axis=1, keepdims=True)
        grad = lanes_three(lane, HALF_LANES, -delta, grad)
        g_ref[rows, :] = grad.astype(low)
        gt_ref[:, rows] = grad.T[:HALF_LANES].astype(low)
        qt_ref[:, rows] = q_ref[rows, :].astype(f32).T[:HALF_LANES].astype(low)
        return carry

    out32_copy.wait()
    for copy in early[1:]:
        copy.wait()
    for i in range(4):
        lax.fori_loop(2 * i, 2 * i + 2, unpack, 0)
        tick(BACK_TICKS[2][i])

    def query_block(first, size, b, carry):
        rows = pl.ds(pl.multiple_of(b * ROWS, ROWS), ROWS)
        cols = slice(first, first + size)
        q, g = q_ref[rows, :], g_ref[rows, :]
        p = jnp.exp(nn(q, kt_ref[:, cols]))
        ds = (p * nn(g, vt_ref[:, cols])).astype(low)
        dvt_ref[:, cols] += nn(gt_ref[:, rows], p.astype(low))
        dkt_ref[:, cols] += nn(qt_ref[:, rows], ds)
        part = nn(ds, k_ref[cols, :])
        if first == 0:
            dq_ref[rows, :] = part
        else:
            dq_ref[rows, :] += part
        return carry

    def send_keys(pair, carry):
        rows = pl.ds(pl.multiple_of(pair * two, two), two)
        dkv = jnp.concatenate([dkt_ref[:, rows], dvt_ref[:, rows]], axis=0).T.astype(low)
        for e in range(2):
            send_ref[2 * pair + e] = dkv[e * tokens : (e + 1) * tokens]
            home.push(2 * pair + e)
        return carry

    def send_queries(w, carry):
        rows = pl.multiple_of(w * tokens, tokens)
        a = dq_ref[pl.ds(rows, mid), :]
        b = dq_ref[pl.ds(pl.multiple_of(rows + mid, mid), mid), :]
        back_send[w] = jnp.where(lane_mid < HALF_LANES, a, swap_halves(b)).astype(low)
        back.push(w)
        return carry

    plane = 4 * tokens
    sent = 0
    for c in range(4):
        for first, stop, limit in groups:
            if limit > c * plane:
                size = min(plane, limit - c * plane)
                lax.fori_loop(first, stop, functools.partial(query_block, c * plane, size), 0)
        lax.fori_loop(2 * c, 2 * c + 2, send_keys, 0)
        while sent < 4 and all(
            limit <= (c + 1) * plane
            for first, stop, limit in groups
            if first * ROWS < (sent + 1) * plane and stop * ROWS > sent * plane
        ):
            lax.fori_loop(4 * sent, 4 * sent + 4, send_queries, 0)
            sent += 1
        tick(BACK_TICKS[3][c])

    kept_copy = pltpu.make_async_copy(kept_any, dq_ref, kept_sem)
    kept_copy.start()
    tick(BACK_TICKS[4][0])
    com_ref[...] = jnp.zeros_like(com_ref)

    def load_codes(c):
        slot = lax.rem(c, 2)
        rows = pl.ds(pl.multiple_of(lax.rem(c, chunks) * step, step), step)
        return [
            pltpu.make_async_copy(book_any.at[rows, pl.ds(r * half, half)], w_buf.at[slot, r], w_sem.at[slot, r])
            for r in range(2)
        ]

    def start_codes(c):
        for copy in load_codes(c):
            copy.start()

    start_codes(0)

    def logits_of(c):
        pl.when(c + 1 < 2 * chunks)(lambda: start_codes(c + 1))
        for copy in load_codes(c):
            copy.wait()
        w = w_buf.at[lax.rem(c, 2)]
        return nt(block_ref[:, :half], w[0]) + nt(block_ref[:, half:], w[1])

    def sum_codes(c, carry):
        top, total = carry
        logits = logits_of(c)
        new_top = jnp.maximum(top, jnp.max(logits, axis=1, keepdims=True))
        return new_top, total * jnp.exp(top - new_top) + jnp.sum(jnp.exp(logits - new_top), axis=1, keepdims=True)

    start = (jnp.full((tokens, 1), -3e38, f32), jnp.zeros((tokens, 1), f32))
    top, total = lax.fori_loop(0, chunks, sum_codes, start)
    share_of = live / total
    tick(BACK_TICKS[4][1])
    for c in range(chunks):
        mass = jnp.sum(jnp.exp(logits_of(chunks + c) - top) * share_of, axis=0, keepdims=True)
        com_ref[34 + c // 2 : 35 + c // 2, (c % 2) * step : (c % 2 + 1) * step] = mass
    slabs = 3 * width // step

    def load_w(j):
        rows = pl.ds(j * step, step)
        return [pltpu.make_async_copy(w_any.at[c, rows], w_buf.at[j % 2, c], w_sem.at[j % 2, c]) for c in range(2)]

    for j in range(2):
        for copy in load_w(j):
            copy.start()
    kept_copy.wait()
    tick(BACK_TICKS[4][2])

    def unnormalize(values, grad):
        inverse = lax.rsqrt(head_sums(values * values) + NORM_EPS)
        unit = values * inverse
        return inverse * (grad - unit * head_sums(unit * grad)), unit

    def heads_back(pair, carry):
        for e in range(2):
            home.wait(2 * pair + e)
            back.wait(2 * pair + e)
        cols = pl.ds(pl.multiple_of(pair * LANES, LANES), LANES)
        key_cols = pl.ds(pl.multiple_of(pair * LANES + width, LANES), LANES)
        val_cols = pl.ds(pl.multiple_of(pair * LANES + 2 * width, LANES), LANES)
        even, odd = got_ref[2 * pair].astype(f32), got_ref[2 * pair + 1].astype(f32)
        d_key = jnp.where(lane_tok < HALF_LANES, even, swap_halves(odd))
        dproj[core, :, val_cols] = jnp.where(lane_tok < HALF_LANES, swap_halves(even), odd).astype(low)
        even, odd = back_got[2 * pair].astype(f32), back_got[2 * pair + 1].astype(f32)
        d_query = jnp.concatenate(
            [
                jnp.where(lane_mid < HALF_LANES, even, swap_halves(odd)),
                jnp.where(lane_mid < HALF_LANES, swap_halves(even), odd),
            ],
            axis=0,
        )
        scaled = d_query * (8.0 * (1.0 + vec_ref[7:8, cols]))
        d_q, unit = unnormalize(dq_ref[pl.ds(pl.multiple_of(pair * tokens, tokens), tokens), :], scaled)
        com_ref[33:34, cols] = jnp.sum(d_query * unit, axis=0, keepdims=True) * 8.0
        dproj[core, :, cols] = d_q.astype(low)
        dproj[core, :, key_cols] = unnormalize(dq_ref[pl.ds(pl.multiple_of((pair + 8) * tokens, tokens), tokens), :], d_key)[0].astype(low)
        return carry

    for i in range(2):
        lax.fori_loop(4 * i, 4 * i + 4, heads_back, 0)
        tick(BACK_TICKS[5][i])
    pl.semaphore_wait(free_sem, 1)
    d_copy = to_sib(6, dproj.at[core], dproj.at[core])

    for j in range(slabs):
        for copy in load_w(j):
            copy.wait()
        for c in range(2):
            part = nn(dproj[core, :, j * step : (j + 1) * step], w_buf[j % 2, c])
            cols = slice(c * half, (c + 1) * half)
            dh_ref[:, cols] = part if j == 0 else dh_ref[:, cols] + part
        if j + 2 < slabs:
            for copy in load_w(j + 2):
                copy.start()
    half_copies[2].wait()
    sib_copies[2].wait_recv()
    d_copy.wait_recv()

    def weight_grad(c, carry):
        cols = pl.ds(pl.multiple_of(c * two, two), two)
        total = nn(dproj[0, :, cols].astype(f32).T.astype(low), h_both[0])
        total = total + nn(dproj[1, :, cols].astype(f32).T.astype(low), h_both[1])
        p_qkv[c // 2, pl.ds(2 * (c % 2), 2)] = total.astype(low).reshape(2, tokens, half)
        return carry

    assert next_tick[0] >= len(splits[0]) + 3
    for p in range(len(splits[0])):
        flow.sent(p)
    lax.fori_loop(0, 8, weight_grad, 0)
    last.run(0)
    tick(flow.steps())

    unit, rstd = standard_of(x_ref[...])
    d_h = dh_ref[...]
    ada_ref[:, 2 * width : 3 * width] = per_slot(d_h * unit)
    ada_ref[:, 4 * width : 5 * width] = per_slot(d_h)
    d_x = standard_back(unit, rstd, d_h * (1.0 + of_tokens(2))) + dx_one[...]
    last.run(1)
    com_ref[0:32, :] = lax.dot_general(
        smooth_ref[...], d_x, (((1,), (0,)), ((), ())), precision=HIGHEST_PRECISION, preferred_element_type=f32
    )
    com_ref[32:33, :] = jnp.sum(d_x, axis=0, keepdims=True)
    small = []
    quarter = COMMON_ROWS // 2

    def common_part(ref, w):
        rows = pl.ds(pl.multiple_of((w // 8) * quarter, 8), quarter)
        return ref.at[rows, pl.ds(pl.multiple_of((w % 8) * LANES, LANES), LANES)]

    ada_width = 6 * width // 16

    def ada_part(ref, w):
        return ref.at[:, pl.ds(pl.multiple_of(w * ada_width, LANES), ada_width)]

    def spread(sem_s, sem_r, r, slot, src, dst):
        copy = pltpu.make_async_remote_copy(
            src_ref=src,
            dst_ref=dst,
            send_sem=sem_s.at[slot, r],
            recv_sem=sem_r.at[slot, r],
            device_id=(core, wide ^ r),
            device_id_type=MESH_ID,
        )
        copy.start()
        return copy

    for r in range(1, 16):
        small.append(spread(small_s, small_r, r, 0, ada_part(ada_ref, wide ^ r), ada_land.at[r]))
        small.append(spread(small_s, small_r, r, 1, common_part(com_ref, wide ^ r), com_land.at[r]))
    d_smooth = lax.dot_general(
        embed_ref[1], d_x, (((1,), (1,)), ((), ())), precision=HIGHEST_PRECISION, preferred_element_type=f32
    )
    left, right = ok_ref[0:1, :], ok_ref[1:2, :]
    share = d_smooth / (2.0 + left + right)
    spot = lane_iota((32, LANES))
    edge[...] = jnp.where(spot == 0, share[:, 0:1], jnp.where(spot == 1, share[:, tokens - 1 : tokens], 0.0))

    def edge_copy(slot, dst, shift):
        return pltpu.make_async_remote_copy(
            src_ref=edge,
            dst_ref=dst,
            send_sem=edge_s.at[slot],
            recv_sem=edge_r.at[slot],
            device_id=(core, lax.rem(wide + shift, 16)),
            device_id_type=MESH_ID,
        )

    to_right, to_left = edge_copy(0, edge_left, 1), edge_copy(1, edge_right, 15)
    to_right.start()
    to_left.start()
    last.run(2)
    ada_total, com_total = ada_part(ada_ref, wide)[...], common_part(com_ref, wide)[...]
    for copy in small:
        copy.wait_recv()
    for r in range(1, 16):
        ada_total = ada_total + ada_land[r]
        com_total = com_total + com_land[r]
    ada_sum[...] = ada_total
    com_sum[...] = com_total
    swaps = [to_sib(7, ada_sum, ada_sib), to_sib(8, com_sum, com_sib)]
    last.run(3)
    for copy in swaps:
        copy.wait_recv()
    ada_both[core] = ada_sum[...]
    ada_both[1 - core] = ada_sib[...]
    bias = jnp.sum(ada_sum[...] + ada_sib[...], axis=0, keepdims=True)
    bias_own[...] = jnp.broadcast_to(bias, bias_own.shape)
    com_own[...] = com_sum[...] + com_sib[...]
    ada_part(bias_all, wide)[...] = bias_own[...]
    common_part(common_all, wide)[...] = com_own[...]
    spreads = []
    for r in range(1, 16):
        spreads.append(spread(spread_s, spread_r, r, 0, bias_own, ada_part(bias_all, wide)))
        spreads.append(spread(spread_s, spread_r, r, 1, com_own, common_part(common_all, wide)))
    for i in range(4, last.steps()):
        last.run(i)
    to_right.wait_recv()
    to_left.wait_recv()
    column = lane_iota((32, tokens))
    before = jnp.where(column == 0, edge_left[:, 1:2], jnp.roll(share, 1, axis=1))
    after = jnp.where(column == tokens - 1, edge_right[:, 0:1], jnp.roll(share, -1, axis=1))
    map_ref[...] = 2.0 * share + left * before + right * after
    for copy in spreads:
        copy.wait_recv()
    for copy in small + swaps + spreads + sib_copies + [d_copy, to_right, to_left]:
        copy.wait_send()
    flow.finish()
    last.finish()
    there.finish()
    home.finish()
    back.finish()


def back(args, groups, splits, call_id):
    x_zero, act = args[4], args[10]
    tokens, width = x_zero.shape
    hidden = act.shape[1]
    group_len = 16 * tokens
    half, mid = width // 2, tokens // 2
    f32, low = jnp.float32, jnp.bfloat16
    dma = pltpu.SemaphoreType.DMA
    shape = jax.ShapeDtypeStruct
    sizes = [(width // 16, hidden // 2), (hidden // 16, half), (width // 16, half), (3 * width // 16, half)]
    first = pieces_of([shape(s, f32) for s in sizes[:3]], splits[0])
    second = pieces_of([shape(sizes[3], f32)], splits[1])
    ada_width, quarter = 6 * width // 16, COMMON_ROWS // 2
    outs = [shape(s, f32) for s in sizes] + [
        shape((2, 8, ada_width), f32),
        shape((COMMON_ROWS, width), f32),
        shape((8, 6 * width), f32),
        shape((32, tokens), f32),
        shape((tokens, width), low),
    ]
    vm = pltpu.VMEM
    scratch = [
        vm((16, tokens, LANES), low),
        vm((16, tokens, LANES), low),
        vm((16, mid, LANES), low),
        vm((16, mid, LANES), low),
        vm((group_len, LANES), low),
        vm((HALF_LANES, group_len), low),
        vm((HALF_LANES, group_len), low),
        vm((group_len, LANES), f32),
        vm((HALF_LANES, group_len), f32),
        vm((HALF_LANES, group_len), f32),
        vm((2, 4, 512, half), low),
        vm((2, tokens, hidden), low),
        vm((2, tokens, half), low),
        vm((tokens, width), f32),
        vm((8, 6 * width), f32),
        vm((COMMON_ROWS, width), f32),
        vm((16, 8, ada_width), f32),
        vm((16, quarter, LANES), f32),
        vm((8, ada_width), f32),
        vm((quarter, LANES), f32),
        vm((8, ada_width), f32),
        vm((quarter, LANES), f32),
        vm((8, ada_width), f32),
        vm((quarter, LANES), f32),
        vm((32, LANES), f32),
        vm((32, LANES), f32),
        vm((32, LANES), f32),
        vm((tokens, width), low),
        vm((2, tokens, half), low),
        vm((2, tokens, half), low),
        vm((2, tokens, width), low),
        vm((tokens, width), f32),
        vm((tokens, width), f32),
        vm((2, tokens, 512), low),
        vm((2, tokens, 512), f32),
        vm((tokens, width), low),
    ] + [vm((4, 4) + s, low) for s in (sizes[1], sizes[2], sizes[0])]
    scratch += [vm((group_len, LANES), low)] * 2 + [vm((LANES, group_len), low)] * 2 + [dma((5,))]
    scratch += [vm((16, mid, LANES), low)] * 2 + [dma((16,))] * 2
    scratch += Scatter.scratch(sizes[:3], len(first)) + Scatter.scratch(sizes[3:], len(second))
    scratch += [dma((16,)) for _ in range(4)] + [dma((2, 6)), dma((16,)), dma((16,))]
    scratch += [dma((2, 16)) for _ in range(4)] + [dma((2,)), dma((2,))]
    scratch += [dma((8,)), dma((8,)), dma((4,)), dma, pltpu.SemaphoreType.REGULAR]
    return pl.pallas_call(
        functools.partial(back_kernel, groups, (first, second)),
        out_shape=outs,
        in_specs=[VM] * 7 + [ANY] * 16 + [VM] * 3 + [ANY],
        out_specs=[VM] * 9,
        scratch_shapes=scratch,
        compiler_params=pltpu.CompilerParams(
            collective_id=call_id, has_side_effects=True, vmem_limit_bytes=63 * 1024 * 1024
        ),
    )(*args)


def nesterov_rows(moment, weight, average, gradient, step_rate, decay_rate):
    step_grad = gradient + decay_rate * weight
    new_moment = MOMENTUM * moment + step_rate * step_grad
    new_weight = weight - (step_rate * step_grad + MOMENTUM * new_moment)
    retain = min(0.999, (1.0 + STEP) / (10.0 + STEP))
    return new_moment, new_weight, retain * average + (1.0 - retain) * new_weight


def update_kernel(rates, mass_scale, *refs):
    states = refs[:5]
    (embed_ref, vector_ref, s_down, s_up, s_out, s_qkv, d_ada, silu_ref, common_ref, bias_ref) = refs[5:15]
    passed, news, copies, passed_out = refs[15:17], refs[17:22], refs[22:27], refs[27:29]
    for src, dst in zip(passed, passed_out):
        dst[...] = src[...]
    (embed_new, vector_new, mass_out, gain_out) = refs[29:33]
    held, lows = refs[33:38], refs[38:43]
    load_sem, store_sem, low_sem = refs[43:]
    width = vector_ref.shape[2]

    def grad_of(i):
        if i == 4:
            return exact(silu_ref[...], d_ada[...], (0, 0))
        return (s_qkv, s_out, None, s_down)[i][...] if i != 2 else s_up[...].T

    order = (3, 2, 4, 0, 1)
    loads = {i: pltpu.make_async_copy(states[i], held[i], load_sem.at[i]) for i in order}
    for i in order:
        loads[i].start()
    rows = embed_ref.shape[1]
    parts = nesterov_rows(embed_ref[0], embed_ref[1], embed_ref[2], common_ref[0:rows, :], rates[5], 0.0)
    for j in range(3):
        embed_new[j] = parts[j]
    for block in range(8):
        if block < 6:
            grad = bias_ref[0:1, block * width : (block + 1) * width]
        else:
            grad = common_ref[rows + block - 6 : rows + block - 5, :]
        here = slice(block, block + 1)
        parts = nesterov_rows(vector_ref[0, here], vector_ref[1, here], vector_ref[2, here], grad, rates[6], 0.0)
        for j in range(3):
            vector_new[j, here] = parts[j]
    per_row = width // LANES
    for r in range(per_row):
        cols = slice(r * LANES, (r + 1) * LANES)
        gain_out[r : r + 1, :] = common_ref[rows + 1 : rows + 2, cols]
        for a in range(mass_out.shape[0] // per_row):
            at = a * per_row + r
            mass_out[at : at + 1, :] = common_ref[rows + 2 + a : rows + 3 + a, cols] * mass_scale
    stores = []
    for i in order:
        loads[i].wait()
        parts = nesterov_rows(held[i][0], held[i][1], held[i][2], grad_of(i), rates[i], WEIGHT_DECAY)
        for j in range(3):
            held[i][j] = parts[j]
        lows[i][...] = parts[1].astype(jnp.bfloat16)
        stores.append(pltpu.make_async_copy(held[i], news[i], store_sem.at[i]))
        stores.append(pltpu.make_async_copy(lows[i], copies[i], low_sem.at[i]))
        for copy in stores[-2:]:
            copy.start()
    for copy in stores:
        copy.wait()


def update(states, embed_state, vector_state, grads, passed, rates, codes, mass_scale):
    f32, low = jnp.float32, jnp.bfloat16
    shape = jax.ShapeDtypeStruct
    dma = pltpu.SemaphoreType.DMA
    width = vector_state.shape[2]
    outs = [shape(s.shape, f32) for s in states] + [shape(s.shape[1:], low) for s in states]
    outs += [shape(p.shape, p.dtype) for p in passed]
    outs += [shape(embed_state.shape, f32), shape(vector_state.shape, f32)]
    outs += [shape((codes // LANES, LANES), f32), shape((width // LANES, LANES), f32)]
    return pl.pallas_call(
        functools.partial(update_kernel, rates, mass_scale),
        out_shape=outs,
        in_specs=[ANY] * 5 + [VM] * 12,
        out_specs=[ANY] * 10 + [VM] * 6,
        scratch_shapes=[pltpu.VMEM(s.shape, f32) for s in states]
        + [pltpu.VMEM(s.shape[1:], low) for s in states]
        + [dma((5,)), dma((5,)), dma((5,))],
        compiler_params=pltpu.CompilerParams(vmem_limit_bytes=VMEM_BYTES),
    )(*states, embed_state, vector_state, *grads, *passed)


def run_tables(slots):
    squares = np.zeros((8, LANES), np.float32)
    pick = np.zeros((LANES, LANES), np.float32)
    for run in range(slots * LEVELS):
        squares[0, HALF_LANES + run] = LONG_SIDES[run // slots] ** 2
        squares[1, HALF_LANES + run] = SHORT_SIDES[run // slots] ** 2
        pick[HALF_LANES + run, run % slots] = 1.0
    tri = np.triu(np.ones((LANES, LANES), np.float32))
    low = jnp.bfloat16
    return [jnp.asarray(squares), jnp.asarray(tri), jnp.asarray(pick, low), jnp.asarray(attention_rule(slots), low)]


def attention_rule(slots):
    runs = slots * LEVELS + 1
    rule = np.zeros((LANES, LANES), np.float32)
    for a in range(runs):
        for b in range(runs):
            slot_a, level_a = (slots, 0) if a == runs - 1 else (a % slots, a // slots)
            slot_b, level_b = (slots, 0) if b == runs - 1 else (b % slots, b // slots)
            if slot_a != slot_b or level_b > level_a:
                rule[HALF_LANES + a, HALF_LANES + b] = -BIG
    return rule


def fast_shards(
    feature_map,
    condition,
    item_lengths,
    cotangent,
    code_book,
    qkv_state,
    out_state,
    up_state,
    down_state,
    ada_state,
    embed_state,
    vector_state,
):
    tok_rows, model_width = cotangent.shape
    low = jnp.bfloat16
    group_len = tok_rows * lax.axis_size("wide")
    tokens_all = lax.axis_size("dp") * group_len
    lengths = item_lengths[0]
    slot_count = lengths.shape[0]

    flip = lambda values: jnp.swapaxes(values, -1, -2)
    flipped = [flip(qkv_state), flip(out_state), up_state, flip(down_state)]
    groups = same_limits(key_limits(group_len, slot_count))
    (
        w_qkv, w_out, w_up, w_down, ada_gathered, h_one_low, kept_qk, out32, q_own, k_own, kt_own, vt_own, attn_low,
        x_zero, smooth, flags, one_hot_wide, silu_rows, attn_proj, x_one, h_two_low, hidden_pre, act_low, p_down,
    ) = front(
        flipped,
        condition,
        ada_state,
        feature_map,
        embed_state,
        vector_state,
        item_lengths,
        run_tables(slot_count),
        cotangent,
        groups,
    )
    s_down, s_up, s_out, s_qkv, d_ada_both, common_sum, bias_sum, map_grad, block_out = back(
        [cotangent, one_hot_wide, ada_gathered, vector_state, x_zero, x_one, attn_proj, h_one_low, h_two_low, attn_low]
        + [act_low, hidden_pre, w_qkv, w_out, w_up, w_down, code_book, out32, q_own, k_own, kt_own, vt_own]
        + [kept_qk.reshape(-1, LANES), smooth, embed_state, flags, p_down],
        groups,
        BACK_SPLITS,
        1,
    )
    root_tokens = math.sqrt(tokens_all)
    spreads = (
        model_width ** (-0.5),
        (model_width // 16) ** (-0.5),
        model_width ** (-0.5),
        w_up.shape[1] ** (-0.5),
        model_width ** (-0.5),
    )
    rates = [BASE_RATE * spread_w / (factor_g * root_tokens) for spread_w, factor_g in zip(spreads, GRAD_FACTORS)]
    rates.append(BASE_RATE * embed_state.shape[1] ** (-0.5) / (EMBED_FACTOR * root_tokens))
    rates.append(VECTOR_RATE / root_tokens)
    codes = code_book.shape[0]
    results = update(
        flipped + [ada_state],
        embed_state,
        vector_state,
        [s_down, s_up, s_out, s_qkv, d_ada_both.reshape(16, -1), silu_rows.reshape(16, -1), common_sum, bias_sum],
        [block_out, map_grad],
        tuple(rates),
        codes,
        codes / tokens_all,
    )
    outputs = [results[10], results[11], results[14].reshape(-1)]
    for i in range(5):
        new, copied = results[i], results[5 + i]
        outputs += [flip(new), flip(copied)] if i in (0, 1, 3) else [new, copied]
    return tuple(outputs + [results[12], results[13], results[15].reshape(-1)])


def solution(mesh):
    body = fast_shards if dict(mesh.shape) == {"dp": 2, "wide": 16} else shards
    in_specs = (
        P(None, ("dp", "wide")),
        P("dp", None),
        P("dp", None),
        P(("dp", "wide"), None),
        P(),
        P(None, "dp", "wide"),
        P(None, "dp", "wide"),
        P(None, "dp", "wide"),
        P(None, "dp", "wide"),
        P(None, "dp", "wide"),
        P(),
        P(),
    )
    out_specs = (
        P(("dp", "wide"), None),
        P(None, ("dp", "wide")),
        P(),
        P(None, "dp", "wide"),
        P("dp", "wide"),
        P(None, "dp", "wide"),
        P("dp", "wide"),
        P(None, "dp", "wide"),
        P("dp", "wide"),
        P(None, "dp", "wide"),
        P("dp", "wide"),
        P(None, "dp", "wide"),
        P("dp", "wide"),
        P(),
        P(),
        P(),
    )
    return jax.shard_map(body, mesh=mesh, in_specs=in_specs, out_specs=out_specs, check_vma=False)
```

```python
import functools
import math

import jax
import jax.numpy as jnp
import numpy as np
from jax import lax
from jax.experimental import pallas as pl
from jax.experimental.pallas import tpu as pltpu
from jax.sharding import PartitionSpec as P

HEADS = 16
LEVELS = 10
STEP = 7


SHORT_SIDES = (1, 2, 3, 4, 5, 6, 8, 10, 13, 16)
LONG_SIDES = (1, 2, 3, 4, 6, 9, 13, 18, 24, 32)
MASKED = -1e30
NORM_EPS = 1e-06
MOMENTUM = 0.9
WEIGHT_DECAY = 0.05
BASE_RATE = 0.37
VECTOR_RATE = 0.22
GRAD_FACTORS = (0.15, 0.1, 0.3, 0.35, 0.3)
EMBED_FACTOR = 0.6
HIGHEST_PRECISION = lax.Precision.HIGHEST


def padded(cells, sides, width):
    for axis, dim in sides:
        count = lax.axis_size(axis)
        ends = count - 1
        head = lax.slice_in_dim(cells, 0, width, axis=dim)
        tail = lax.slice_in_dim(cells, cells.shape[dim] - width, cells.shape[dim], axis=dim)
        cells = jnp.concatenate(
            [
                lax.ppermute(tail, axis, [(i, (i + 1) % count) for i in range(ends)]),
                cells,
                lax.ppermute(head, axis, [((i + 1) % count, i) for i in range(ends)]),
            ],
            axis=dim,
        )
    return cells


def layout(lengths, positions, group_len):
    short_sq = jnp.array([side * side for side in SHORT_SIDES[:LEVELS]], jnp.int32)
    long_sq = jnp.array([side * side for side in LONG_SIDES[:LEVELS]], jnp.int32)
    short_total = sum((side * side for side in SHORT_SIDES[:LEVELS]))
    long_total = sum((side * side for side in LONG_SIDES[:LEVELS]))
    slot_count = lengths.shape[0]
    counts = jnp.where(
        lengths[None, :] == long_total,
        long_sq[:, None],
        jnp.where(lengths[None, :] == short_total, short_sq[:, None], 0),
    )
    unused = group_len - jnp.sum(lengths)
    ordered = jnp.concatenate([counts.reshape(-1), unused[None]])
    boundary = jnp.cumsum(ordered)
    segment = jnp.sum((boundary[None, :] <= positions[:, None]).astype(jnp.int32), axis=1)
    segment = jnp.minimum(segment, ordered.shape[0] - 1)
    unused_id = slot_count * LEVELS
    tok_level = jnp.where(segment >= unused_id, 0, segment // slot_count)
    tok_slot = jnp.where(segment >= unused_id, slot_count, segment % slot_count)
    return (tok_slot, tok_level, segment)


def pre_norm(inputs, scaling, offset_add):
    row_mean = jnp.mean(inputs, axis=-1, keepdims=True)
    centred = inputs - row_mean
    spread = jnp.mean(centred * centred, axis=-1, keepdims=True)
    return centred * lax.rsqrt(spread + NORM_EPS) * (1.0 + scaling) + offset_add


def unit_heads(inputs):
    shaped = inputs.reshape(inputs.shape[0], HEADS, -1)
    shaped = shaped * lax.rsqrt(jnp.sum(shaped * shaped, axis=-1, keepdims=True) + NORM_EPS)
    return shaped.reshape(inputs.shape)


def split_heads(projected, q_gain):
    queries, key_part, value_part = jnp.split(projected, 3, axis=1)
    head_scale = math.sqrt(queries.shape[1] // HEADS)
    return (unit_heads(queries) * (head_scale * (1.0 + q_gain)), unit_heads(key_part), value_part)


def smooth_map(values, left_ok, right_ok, before, following):
    return (left_ok * before + 2.0 * values + right_ok * following) / (2.0 + left_ok + right_ok)


def nesterov(stacked, gradient, step_rate, decay_rate):
    moment, weight, average = (stacked[0], stacked[1], stacked[2])
    step_grad = gradient + decay_rate * weight
    new_moment = MOMENTUM * moment + step_rate * step_grad
    new_weight = weight - (step_rate * step_grad + MOMENTUM * new_moment)
    retain = min(0.999, (1.0 + STEP) / (10.0 + STEP))
    new_average = retain * average + (1.0 - retain) * new_weight
    return jnp.stack([new_moment, new_weight, new_average])


def contract_rows(left_side, right_side, precision=None):
    return lax.dot_general(
        left_side,
        right_side,
        (((0,), (0,)), ((), ())),
        precision=precision,
        preferred_element_type=jnp.float32,
    )


def against(left_side, right_side):
    return lax.dot_general(
        left_side, right_side, (((1,), (1,)), ((), ())), preferred_element_type=jnp.float32
    )


def shards(
    feature_map,
    condition,
    item_lengths,
    cotangent,
    code_book,
    qkv_state,
    out_state,
    up_state,
    down_state,
    ada_state,
    embed_state,
    vector_state,
):
    tok_rows = cotangent.shape[0]
    model_width = cotangent.shape[1]
    head_dim = model_width // HEADS
    wide_count = lax.axis_size("wide")
    group_len = tok_rows * wide_count
    tokens_all = lax.axis_size("dp") * group_len
    lengths = item_lengths[0]
    slot_count = lengths.shape[0]
    positions = lax.axis_index("wide") * tok_rows + jnp.arange(tok_rows, dtype=jnp.int32)
    tok_slot, tok_level, segment = layout(lengths, positions, group_len)
    live_rows = (tok_slot < slot_count).astype(jnp.float32)[:, None]
    left_ok = ((layout(lengths, positions - 1, group_len)[2] == segment) & (positions > 0)).astype(
        jnp.float32
    )
    right_ok = (
        (layout(lengths, positions + 1, group_len)[2] == segment) & (positions < group_len - 1)
    ).astype(jnp.float32)
    rimmed = padded(feature_map, (("wide", 1),), 1)
    smooth = smooth_map(feature_map, left_ok, right_ok, rimmed[:, :-2], rimmed[:, 2:])
    states = (qkv_state, out_state, up_state, down_state, ada_state)
    masters = tuple((stacked[1].astype(jnp.bfloat16) for stacked in states))
    columns = (
        lax.all_gather(masters[0], "wide", axis=1, tiled=True),
        lax.all_gather(masters[1], "wide", axis=1, tiled=True),
        lax.all_gather(masters[2], "wide", axis=1, tiled=True),
        lax.all_gather(masters[3], "wide", axis=1, tiled=True),
    )
    ada_piece = lax.all_gather(masters[4], "wide", axis=1, tiled=True)
    w_qkv, w_out, w_up, w_down, w_ada = (
        lax.all_gather(columns[0], "dp", axis=0, tiled=True),
        lax.all_gather(columns[1], "dp", axis=0, tiled=True),
        lax.all_gather(columns[2], "dp", axis=0, tiled=True),
        lax.all_gather(columns[3], "dp", axis=0, tiled=True),
        lax.all_gather(ada_piece, "dp", axis=0, tiled=True),
    )
    embed_w = embed_state[1]
    vectors = vector_state[1]
    x_zero = (
        lax.dot_general(smooth, embed_w, (((0,), (0,)), ((), ())), precision=HIGHEST_PRECISION)
        + vectors[6]
    )
    silu_cond = jax.nn.silu(condition).astype(jnp.bfloat16)
    ada_product = jnp.dot(silu_cond, w_ada, preferred_element_type=jnp.float32)
    ada_all = ada_product + vectors[:6].reshape(-1)
    one_hot = (tok_slot[:, None] == jnp.arange(slot_count, dtype=jnp.int32)[None, :]).astype(
        jnp.float32
    )
    token_ada = jnp.dot(one_hot, ada_all, precision=HIGHEST_PRECISION)
    gate_one, gate_two, scale_one, scale_two, shift_one, shift_two = jnp.split(token_ada, 6, axis=1)
    h_one_low = pre_norm(x_zero, scale_one, shift_one).astype(jnp.bfloat16)
    projected = jnp.dot(h_one_low, w_qkv, preferred_element_type=jnp.float32)
    (q_unit, k_unit, v_full), heads_back = jax.vjp(split_heads, projected, vectors[7])
    queries = q_unit.astype(jnp.bfloat16)
    keys_low = k_unit.astype(jnp.bfloat16)
    values_low = v_full.astype(jnp.bfloat16)
    query_heads = queries.reshape(tok_rows, HEADS, head_dim)

    def blockwise(advance, running, pieces, first_row):
        key_count = pieces[0].shape[0]
        block_size = math.gcd(key_count, 1024)

        def per_block(current, offset):
            key_part = tuple(
                (lax.dynamic_slice_in_dim(piece_arr, offset, block_size, 0) for piece_arr in pieces)
            )
            first_key = first_row + offset
            k_slot, k_level, _ = layout(
                lengths, first_key + jnp.arange(block_size, dtype=jnp.int32), group_len
            )
            allowed = (tok_slot[:, None] == k_slot[None, :]) & (
                k_level[None, :] <= tok_level[:, None]
            )
            current = advance(current, key_part, allowed, first_key)
            return (current, None)

        offsets = jnp.arange(key_count // block_size, dtype=jnp.int32) * block_size
        return lax.scan(per_block, running, offsets)[0]

    def scores_of(key_block, allowed):
        raw_scores = jnp.einsum(
            "qhd,khd->hqk",
            query_heads,
            key_block.reshape(-1, HEADS, head_dim),
            preferred_element_type=jnp.float32,
        )
        return jnp.where(allowed[None], raw_scores, MASKED)

    def stats_step(running, key_part, allowed, first_key):
        scores = scores_of(key_part[0], allowed)
        top_score, exp_total = running
        new_top = jnp.maximum(top_score, jnp.max(scores, axis=-1, keepdims=True))
        exp_total = exp_total * jnp.exp(top_score - new_top) + jnp.sum(
            jnp.exp(scores - new_top), axis=-1, keepdims=True
        )
        return (new_top, exp_total)

    kv_rows = (
        lax.all_gather(keys_low, "wide", axis=0, tiled=True),
        lax.all_gather(values_low, "wide", axis=0, tiled=True),
    )
    start_stats = (
        jnp.full((HEADS, tok_rows, 1), MASKED, jnp.float32),
        jnp.zeros((HEADS, tok_rows, 1), jnp.float32),
    )
    top_score, exp_total = blockwise(stats_step, start_stats, kv_rows, 0)
    log_total = top_score + jnp.log(exp_total)

    def value_step(running, key_part, allowed, first_key):
        attn_probs = jnp.exp(scores_of(key_part[0], allowed) - log_total).astype(jnp.bfloat16)
        return running + jnp.einsum(
            "hqk,khd->qhd",
            attn_probs,
            key_part[1].reshape(-1, HEADS, head_dim),
            preferred_element_type=jnp.float32,
        )

    attended = blockwise(
        value_step, jnp.zeros((tok_rows, HEADS, head_dim), jnp.float32), kv_rows, 0
    )
    attn_low = attended.reshape(tok_rows, model_width).astype(jnp.bfloat16)
    attn_proj = jnp.dot(attn_low, w_out, preferred_element_type=jnp.float32)
    x_one = x_zero + gate_one * attn_proj
    h_two_low = pre_norm(x_one, scale_two, shift_two).astype(jnp.bfloat16)
    hidden_pre = jnp.dot(h_two_low, w_up, preferred_element_type=jnp.float32)
    act_low = jax.nn.gelu(hidden_pre, approximate=True).astype(jnp.bfloat16)
    mlp_out = jnp.dot(act_low, w_down, preferred_element_type=jnp.float32)
    x_two = x_one + gate_two * mlp_out
    block_out = (x_two * live_rows).astype(jnp.bfloat16)
    logits = against(block_out, code_book)
    code_mass = jnp.sum(jax.nn.softmax(logits, axis=-1) * live_rows, axis=0)
    g_two = cotangent.astype(jnp.float32) * live_rows
    d_mlp = (gate_two * g_two).astype(jnp.bfloat16)
    d_gate_two = g_two * mlp_out
    dw_down = contract_rows(act_low, d_mlp)
    d_act = against(d_mlp, w_down)
    _, gelu_back = jax.vjp(lambda inputs: jax.nn.gelu(inputs, approximate=True), hidden_pre)
    d_hidden = gelu_back(d_act)[0].astype(jnp.bfloat16)
    dw_up = contract_rows(h_two_low, d_hidden)
    d_h_two = against(d_hidden, w_up)
    _, norm_back_two = jax.vjp(pre_norm, x_one, scale_two, shift_two)
    d_x_one, d_scale_two, d_shift_two = norm_back_two(d_h_two)
    d_x_one = d_x_one + g_two
    d_attn = (gate_one * d_x_one).astype(jnp.bfloat16)
    d_gate_one = d_x_one * attn_proj
    dw_out = contract_rows(attn_low, d_attn)
    grad_flat = against(d_attn, w_out).astype(jnp.bfloat16)
    grad_heads = grad_flat.reshape(tok_rows, HEADS, head_dim)

    def delta_step(running, key_part, allowed, first_key):
        attn_probs = jnp.exp(scores_of(key_part[0], allowed) - log_total)
        d_probs = jnp.einsum(
            "qhd,khd->hqk",
            grad_heads,
            key_part[1].reshape(-1, HEADS, head_dim),
            preferred_element_type=jnp.float32,
        )
        return running + jnp.sum(attn_probs * d_probs, axis=-1, keepdims=True)

    row_delta = blockwise(delta_step, jnp.zeros((HEADS, tok_rows, 1), jnp.float32), kv_rows, 0)

    def grad_step(running, key_part, allowed, first_key):
        d_query, d_keys, d_values = running
        key_heads = key_part[0].reshape(-1, HEADS, head_dim)
        value_heads = key_part[1].reshape(-1, HEADS, head_dim)
        block_rows = key_part[0].shape[0]
        attn_probs = jnp.exp(scores_of(key_part[0], allowed) - log_total)
        d_probs = jnp.einsum(
            "qhd,khd->hqk", grad_heads, value_heads, preferred_element_type=jnp.float32
        )
        d_scores = (attn_probs * (d_probs - row_delta)).astype(jnp.bfloat16)
        d_query = d_query + jnp.einsum(
            "hqk,khd->qhd", d_scores, key_heads, preferred_element_type=jnp.float32
        )
        key_grad = jnp.einsum(
            "hqk,qhd->khd", d_scores, query_heads, preferred_element_type=jnp.float32
        )
        value_grad = jnp.einsum(
            "hqk,qhd->khd",
            attn_probs.astype(jnp.bfloat16),
            grad_heads,
            preferred_element_type=jnp.float32,
        )
        key_sum = lax.dynamic_slice_in_dim(d_keys, first_key, block_rows, 0) + key_grad.reshape(
            block_rows, model_width
        )
        value_sum = lax.dynamic_slice_in_dim(
            d_values, first_key, block_rows, 0
        ) + value_grad.reshape(block_rows, model_width)
        d_keys = lax.dynamic_update_slice_in_dim(d_keys, key_sum, first_key, 0)
        d_values = lax.dynamic_update_slice_in_dim(d_values, value_sum, first_key, 0)
        return (d_query, d_keys, d_values)

    grad_init = (
        jnp.zeros((tok_rows, HEADS, head_dim), jnp.float32),
        jnp.zeros((group_len, model_width), jnp.float32),
        jnp.zeros((group_len, model_width), jnp.float32),
    )
    d_query, d_keys, d_values = blockwise(grad_step, grad_init, kv_rows, 0)
    d_keys_own, d_values_own = (
        lax.psum_scatter(
            d_keys.astype(jnp.bfloat16), "wide", scatter_dimension=0, tiled=True
        ).astype(jnp.float32),
        lax.psum_scatter(
            d_values.astype(jnp.bfloat16), "wide", scatter_dimension=0, tiled=True
        ).astype(jnp.float32),
    )
    d_projected, d_gain = heads_back(
        (d_query.reshape(tok_rows, model_width), d_keys_own, d_values_own)
    )
    d_projected_low = d_projected.astype(jnp.bfloat16)
    dw_qkv = contract_rows(h_one_low, d_projected_low)
    d_h_one = against(d_projected_low, w_qkv)
    _, norm_back_one = jax.vjp(pre_norm, x_zero, scale_one, shift_one)
    d_x_zero, d_scale_one, d_shift_one = norm_back_one(d_h_one)
    d_x_zero = d_x_zero + d_x_one
    d_token_ada = jnp.concatenate(
        [d_gate_one, d_gate_two, d_scale_one, d_scale_two, d_shift_one, d_shift_two], axis=1
    )
    d_ada_all = contract_rows(one_hot, d_token_ada, HIGHEST_PRECISION)
    d_smooth = lax.dot_general(
        embed_w, d_x_zero, (((1,), (1,)), ((), ())), precision=HIGHEST_PRECISION
    )
    d_embed = lax.dot_general(
        smooth, d_x_zero, (((1,), (0,)), ((), ())), precision=HIGHEST_PRECISION
    )
    d_vectors = jnp.concatenate(
        [
            jnp.sum(d_ada_all, axis=0).reshape(6, model_width),
            jnp.sum(d_x_zero, axis=0)[None],
            d_gain[None],
        ],
        axis=0,
    )
    grad_share = d_smooth / (2.0 + left_ok + right_ok)
    rim_share = padded(grad_share, (("wide", 1),), 1)
    map_grad = 2.0 * grad_share + left_ok * rim_share[:, :-2] + right_ok * rim_share[:, 2:]
    d_embed_all, d_vectors_all, mass_all = lax.psum((d_embed, d_vectors, code_mass), ("dp", "wide"))
    histogram = mass_all * (code_book.shape[0] / tokens_all)
    ada_term = contract_rows(silu_cond.astype(jnp.float32), d_ada_all, HIGHEST_PRECISION)
    split_cols = (
        lax.psum_scatter(
            dw_qkv.astype(jnp.bfloat16), "wide", scatter_dimension=1, tiled=True
        ).astype(jnp.float32),
        lax.psum_scatter(
            dw_out.astype(jnp.bfloat16), "wide", scatter_dimension=1, tiled=True
        ).astype(jnp.float32),
        lax.psum_scatter(
            dw_up.astype(jnp.bfloat16), "wide", scatter_dimension=1, tiled=True
        ).astype(jnp.float32),
        lax.psum_scatter(
            dw_down.astype(jnp.bfloat16), "wide", scatter_dimension=1, tiled=True
        ).astype(jnp.float32),
        lax.psum_scatter(
            ada_term.astype(jnp.bfloat16), "wide", scatter_dimension=1, tiled=True
        ).astype(jnp.float32),
    )
    ada_cols = split_cols[4]
    owned_grads = (
        lax.psum_scatter(
            split_cols[0].astype(jnp.bfloat16), "dp", scatter_dimension=0, tiled=True
        ).astype(jnp.float32),
        lax.psum_scatter(
            split_cols[1].astype(jnp.bfloat16), "dp", scatter_dimension=0, tiled=True
        ).astype(jnp.float32),
        lax.psum_scatter(
            split_cols[2].astype(jnp.bfloat16), "dp", scatter_dimension=0, tiled=True
        ).astype(jnp.float32),
        lax.psum_scatter(
            split_cols[3].astype(jnp.bfloat16), "dp", scatter_dimension=0, tiled=True
        ).astype(jnp.float32),
        lax.psum_scatter(
            ada_cols.astype(jnp.bfloat16), "dp", scatter_dimension=0, tiled=True
        ).astype(jnp.float32),
    )
    root_tokens = math.sqrt(tokens_all)
    spreads = (
        model_width ** (-0.5),
        (model_width // 16) ** (-0.5),
        model_width ** (-0.5),
        w_up.shape[1] ** (-0.5),
        model_width ** (-0.5),
    )
    new_states = tuple(
        (
            nesterov(
                stacked, gradient, BASE_RATE * spread_w / (factor_g * root_tokens), WEIGHT_DECAY
            )
            for stacked, gradient, spread_w, factor_g in zip(
                states, owned_grads, spreads, GRAD_FACTORS
            )
        )
    )
    embed_new = nesterov(
        embed_state,
        d_embed_all,
        BASE_RATE * embed_w.shape[0] ** (-0.5) / (EMBED_FACTOR * root_tokens),
        0.0,
    )
    vector_new = nesterov(vector_state, d_vectors_all, VECTOR_RATE / root_tokens, 0.0)
    return (
        block_out,
        map_grad,
        histogram,
        new_states[0],
        new_states[0][1].astype(jnp.bfloat16),
        new_states[1],
        new_states[1][1].astype(jnp.bfloat16),
        new_states[2],
        new_states[2][1].astype(jnp.bfloat16),
        new_states[3],
        new_states[3][1].astype(jnp.bfloat16),
        new_states[4],
        new_states[4][1].astype(jnp.bfloat16),
        embed_new,
        vector_new,
        d_vectors_all[7],
    )


MESH_ID = pl.DeviceIdType.MESH
ANY = pl.BlockSpec(memory_space=pl.ANY)
VM = pl.BlockSpec(memory_space=pltpu.VMEM)
VMEM_BYTES = 56 * 1024 * 1024
SHORT_TOTAL = sum(side * side for side in SHORT_SIDES)
LONG_TOTAL = sum(side * side for side in LONG_SIDES)
GELU_SCALE = math.sqrt(2.0 / math.pi)
GELU_CUBE = 0.044715
LANES = 128
HALF_LANES = 64
BIG = 1e30


def nt(left_side, right_side):
    return lax.dot_general(
        left_side, right_side, (((1,), (1,)), ((), ())), preferred_element_type=jnp.float32
    )


def nn(left_side, right_side):
    return lax.dot_general(
        left_side, right_side, (((1,), (0,)), ((), ())), preferred_element_type=jnp.float32
    )


def entry_barrier(peers):
    barrier = pltpu.get_barrier_semaphore()
    for peer in peers:
        pl.semaphore_signal(barrier, inc=1, device_id=peer, device_id_type=MESH_ID)
    pl.semaphore_wait(barrier, len(peers))


def place():
    core, wide = lax.axis_index("dp"), lax.axis_index("wide")
    return core, wide // 4, wide % 4


def at_dev(core, z, yx):
    return (core, z * 4 + yx)


def lane_iota(shape):
    return lax.broadcasted_iota(jnp.int32, shape, len(shape) - 1)


def swap_halves(pair):
    return pltpu.roll(pair, HALF_LANES, 1)


def head_sums(values):
    width = values.shape[1]
    rows = lax.broadcasted_iota(jnp.int32, (width, width), 0) // HALF_LANES
    cols = lax.broadcasted_iota(jnp.int32, (width, width), 1) // HALF_LANES
    ones = (rows == cols).astype(jnp.float32)
    return lax.dot_general(
        values,
        ones,
        (((1,), (0,)), ((), ())),
        precision=HIGHEST_PRECISION,
        preferred_element_type=jnp.float32,
    )


ROWS = 256
CHUNK = 512


def key_limits(group_len, slots):
    short_total = sum(side * side for side in SHORT_SIDES)
    long_total = sum(side * side for side in LONG_SIDES)
    limits = [0] * (group_len // ROWS)
    for longs in range(1, slots + 1):
        for shorts in range(slots - longs + 1):
            total = longs * long_total + shorts * short_total
            if not group_len - short_total < total <= group_len:
                continue
            ends, position = [], 0
            for long_side, short_side in zip(LONG_SIDES, SHORT_SIDES):
                position += longs * long_side**2 + shorts * short_side**2
                ends.append(position)
            ends.append(group_len)
            for block in range(len(limits)):
                last = block * ROWS + ROWS - 1
                seen = min(end for end in ends if end > last)
                limits[block] = max(limits[block], -(-seen // LANES) * LANES)
    return limits


def same_limits(limits):
    groups = []
    for block, limit in enumerate(limits):
        if groups and groups[-1][2] == limit:
            groups[-1][1] = block + 1
        else:
            groups.append([block, block + 1, limit])
    return groups


def fold_lanes(values, combine):
    total = values[:, :LANES]
    for j in range(1, values.shape[1] // LANES):
        total = combine(total, values[:, j * LANES : (j + 1) * LANES])
    return total


def split_three(values):
    high = values.astype(jnp.bfloat16).astype(jnp.float32)
    rest = values - high
    mid = rest.astype(jnp.bfloat16).astype(jnp.float32)
    return high, mid, rest - mid


def lanes_three(lane, first, values, otherwise):
    high, mid, rest = split_three(values)
    return jnp.where(
        lane == first, high, jnp.where(lane == first + 1, mid, jnp.where(lane == first + 2, rest, otherwise))
    )


class Gather:
    KINDS = ("up", "down", "x", "y", "turn")

    def __init__(self, shards, fulls, sems, pieces):
        self.shards, self.fulls, self.pieces = shards, fulls, pieces
        self.send, self.recv, self.send_s, self.recv_s, self.local = sems
        self.core, self.z, self.yx = place()
        core, z, yx = self.core, self.z, self.yx
        self.up_dev, self.down_dev = at_dev(core, lax.min(z + 1, 3), yx), at_dev(core, lax.max(z - 1, 0), yx)
        self.x_dev, self.y_dev = at_dev(core, z, yx ^ 1), at_dev(core, z, yx ^ 2)
        self.sib = at_dev(1 - core, z, yx)
        self.ends = []

    @staticmethod
    def scratch(count):
        dma = pltpu.SemaphoreType.DMA
        return [dma((count, 5, 4)), dma((count, 4, 4)), dma((count, 4, 4)), dma((count, 4, 4)), dma((count,))]

    def spot(self, p, z_at, d, core=None):
        i, first, rows = self.pieces[p]
        core = self.core if core is None else core
        size = self.shards[i].shape[0]
        start = pl.multiple_of((z_at * 4 + (self.yx ^ d)) * size + first, 16)
        return self.fulls[i].at[core, pl.ds(start, rows)]

    def copy(self, p, kind, z_at, d, src=None):
        there = {0: 0, 1: 0, 2: 1, 3: 2, 4: 3}[kind]
        ref = self.spot(p, z_at, d)
        device = (self.up_dev, self.down_dev, self.x_dev, self.y_dev)[kind] if kind < 4 else (self.y_dev if d == 1 else self.x_dev)
        return pltpu.make_async_remote_copy(
            src_ref=ref if src is None else src,
            dst_ref=ref,
            send_sem=self.send.at[p, kind, z_at],
            recv_sem=self.recv.at[p, there, z_at],
            device_id=device,
            device_id_type=MESH_ID,
        )

    def go(self, condition, p, kind, z_at, d, src=None):
        def start():
            self.copy(p, kind, z_at, d, src).start()

        def end():
            self.copy(p, kind, z_at, d, src).wait_send()

        if condition is None:
            start()
            self.ends.append(end)
        else:
            pl.when(condition)(start)
            self.ends.append(lambda: pl.when(condition)(end))

    def across(self, p, d):
        for z_at in range(4):
            ref = self.spot(p, z_at, d)
            copy = pltpu.make_async_remote_copy(
                src_ref=ref,
                dst_ref=ref,
                send_sem=self.send_s.at[p, d, z_at],
                recv_sem=self.recv_s.at[p, d, z_at],
                device_id=self.sib,
                device_id_type=MESH_ID,
            )
            copy.start()
            self.ends.append(copy.wait_send)

    def arrive(self, p, kind, z_at, d):
        ref = self.spot(p, z_at, d)
        pltpu.make_async_copy(ref, ref, self.recv.at[p, kind, z_at]).wait()

    def own(self, p):
        i, first, rows = self.pieces[p]
        src = self.shards[i].at[pl.ds(first, rows)]
        z = self.z
        self.go(z < 3, p, 0, z, 0, src)
        self.go(z > 0, p, 1, z, 0, src)
        self.go(None, p, 2, z, 0, src)
        self.go(None, p, 3, z, 0, src)
        copy = pltpu.make_async_copy(src, self.spot(p, z, 0), self.local.at[p])
        copy.start()
        self.locals_ = getattr(self, "locals_", {})
        self.locals_[p] = copy

    def z_step(self, p, r):
        z = self.z
        for side in (-1, 1):
            there = (z - r >= 0) if side < 0 else (z + r <= 3)
            z_at = z + side * r

            def landed(z_at=z_at):
                self.arrive(p, 0, z_at, 0)

            pl.when(there)(landed)
            if side < 0:
                self.go(there & (z < 3), p, 0, z_at, 0)
            else:
                self.go(there & (z > 0), p, 1, z_at, 0)
            self.go(there, p, 2, z_at, 0)
            self.go(there, p, 3, z_at, 0)

    def plane_step(self, p, r):
        z = self.z
        for side in (-1, 1) if r else (0,):
            z_at = z + side * r
            there = None if not r else ((z - r >= 0) if side < 0 else (z + r <= 3))

            def landed(z_at=z_at):
                self.arrive(p, 1, z_at, 1)
                self.arrive(p, 2, z_at, 2)

            if there is None:
                landed()
            else:
                pl.when(there)(landed)
            low_z, high_z = z_at < 2, z_at >= 2
            self.go(low_z if there is None else there & low_z, p, 4, z_at, 1)
            self.go(high_z if there is None else there & high_z, p, 4, z_at, 2)

    def stage(self, p, s):
        if s == 0:
            self.own(p)
        elif s == 1:
            self.z_step(p, 1)
            self.plane_step(p, 0)
        elif s == 2:
            self.z_step(p, 2)
            self.plane_step(p, 1)
        elif s == 3:
            self.z_step(p, 3)
            self.locals_[p].wait()
            self.across(p, 0)
            self.plane_step(p, 2)
        elif s == 4:
            self.plane_step(p, 3)
            self.across(p, 1)
            self.across(p, 2)
        elif s == 5:
            for z_at in range(4):
                self.arrive(p, 3, z_at, 3)
            self.across(p, 3)

    STAGES = 6

    def steps(self):
        return len(self.pieces) + self.STAGES - 1

    def run(self, t):
        for s in range(self.STAGES):
            if 0 <= t - s < len(self.pieces):
                self.stage(t - s, s)

    def landed(self, which=None):
        for p in range(len(self.pieces)) if which is None else which:
            for d in range(4):
                for z_at in range(4):
                    ref = self.spot(p, z_at, d, 1 - self.core)
                    pltpu.make_async_copy(ref, ref, self.recv_s.at[p, d, z_at]).wait()

    def finish(self):
        for end in self.ends:
            end()


def pieces_of(shards, splits):
    pieces = []
    for i, (shard, split) in enumerate(zip(shards, splits)):
        rows = shard.shape[0] // split
        pieces += [(i, j * rows, rows) for j in range(split)]
    return pieces


class Exchange:
    def __init__(self, out, landed, sems):
        self.out, self.landed = out, landed
        self.send, self.recv = sems
        self.core, z, yx = place()
        self.wide = z * 4 + yx

    def copy(self, w):
        return pltpu.make_async_remote_copy(
            src_ref=self.out.at[w],
            dst_ref=self.landed.at[self.wide],
            send_sem=self.send.at[w],
            recv_sem=self.recv.at[self.wide],
            device_id=(self.core, w),
            device_id_type=MESH_ID,
        )

    def push(self, w):
        pl.when(w != self.wide)(lambda: self.copy(w).start())

        def keep():
            self.landed[w] = self.out[w]

        pl.when(w == self.wide)(keep)

    def wait(self, w):
        def landed():
            ref = self.landed.at[w]
            pltpu.make_async_copy(ref, ref, self.recv.at[w]).wait()

        pl.when(w != self.wide)(landed)

    def finish(self):
        for w in range(16):
            pl.when(w != self.wide)(lambda w=w: self.copy(w).wait_send())


def column_of(row):
    return jnp.broadcast_to(row, (LANES, row.shape[1])).T[:, 0:1]


def exact(left_side, right_side, contract=(1, 0)):
    return lax.dot_general(
        left_side,
        right_side,
        (((contract[0],), (contract[1],)), ((), ())),
        precision=HIGHEST_PRECISION,
        preferred_element_type=jnp.float32,
    )


def gelu(values):
    return 0.5 * values * (1.0 + jnp.tanh(GELU_SCALE * (values + GELU_CUBE * values * values * values)))


def gradient(grads, inputs, out, rows, shard):
    count = rows // shard

    def body(c, carry):
        cols = pl.ds(pl.multiple_of(c * rows, LANES), rows)
        total = nn(grads[0, :, cols].astype(jnp.float32).T.astype(jnp.bfloat16), inputs[0])
        total = total + nn(grads[1, :, cols].astype(jnp.float32).T.astype(jnp.bfloat16), inputs[1])
        first = lax.rem(c * count, 4)
        out[c * count // 4, pl.ds(first, count)] = total.astype(jnp.bfloat16).reshape(count, shard, -1)
        return carry

    return body


def front_kernel(groups, slots, *refs):
    (m_qkv, m_out, m_up, m_down, cond_ref, ada_any, map_ref, embed_ref, vec3_ref, len_ref, squares_ref, tri_ref, pick_ref, rule_ref, cot_ref) = refs[:15]
    (f_qkv, f_out, f_up, f_down, ada_ref, h_ref, kept_any, out32_any, q_any, k_any, kt_any, vt_any, low_ref) = refs[15:28]
    (x_ref, smooth_ref, flags_ref, hot_ref, silu_ref, proj_ref, one_ref, two_ref, pre_any, act_any, p_any) = refs[28:39]
    (w_ref, send_ref, got_ref, back_send, back_got, v_ref, s_ref, load_sem) = refs[39:47]
    (w_ada, silu_own, theirs, ours, ada_in, edge, edge_left, edge_right, wo_ref, wu_ref, dmlp, act_half) = refs[47:59]
    (kept_ref, out32_ref, q_ref, k_ref, kt_ref, vt_ref, pre_ref, act_ref, p_down) = refs[59:68]
    (c_qkv, c_out, c_up, c_down, s_qkv, s_out, s_up, s_down, cast_sem, store_sem) = refs[68:78]
    sems = refs[78:]
    first_flow = Gather([s_qkv], [f_qkv], sems[:5], pieces_of([s_qkv], FRONT_SPLITS[0]))
    shards = [s_out, s_up, s_down]
    flow = Gather(shards, [f_out, f_up, f_down], sems[5:10], pieces_of(shards, FRONT_SPLITS[1]))
    ada_send, ada_recv = sems[10:12]
    there = Exchange(send_ref, got_ref, sems[12:14])
    home = Exchange(back_send, back_got, sems[14:16])
    ada_sem, sib_s, sib_r, edge_s, edge_r, wo_sem, wu_sem = sems[16:23]
    core, z, yx = place()
    wide = z * 4 + yx
    sib = (1 - core, wide)
    tokens, width = x_ref.shape
    half = width // 2
    mid = tokens // 2
    two = 2 * tokens
    group_len = q_ref.shape[0]
    f32, low = jnp.float32, jnp.bfloat16
    vec_ref = vec3_ref.at[1]
    casts = []
    for i, (src, dst) in enumerate(((m_qkv, c_qkv), (m_out, c_out), (m_up, c_up), (m_down, c_down))):
        casts.append(pltpu.make_async_copy(src.at[1], dst, cast_sem.at[i]))
        casts[-1].start()
    stores = []

    def store(*pairs):
        for src, dst in pairs:
            stores.append(pltpu.make_async_copy(src, dst, store_sem.at[len(stores)]))
            stores[-1].start()

    casts[0].wait()
    s_qkv[...] = c_qkv[...].astype(low)
    entry_barrier([(core, wide ^ r) for r in range(1, 16)] + [sib])

    def to_sib(slot, src, dst):
        copy = pltpu.make_async_remote_copy(
            src_ref=src, dst_ref=dst, send_sem=sib_s.at[slot], recv_sem=sib_r.at[slot], device_id=sib, device_id_type=MESH_ID
        )
        copy.start()
        return copy

    next_tick = [0]

    def tick(n):
        for _ in range(n):
            if next_tick[0] < flow.steps():
                flow.run(next_tick[0])
                next_tick[0] += 1

    def tick_to(n):
        tick(max(0, n - next_tick[0]))

    first_flow.run(0)
    ada_copy = pltpu.make_async_copy(ada_any.at[1], w_ada, ada_sem)
    ada_copy.start()
    cond = cond_ref[...]
    silu = (cond / (1.0 + jnp.exp(-cond))).astype(low).astype(f32)
    silu_own[...] = jnp.zeros_like(silu_own)
    silu_own[0:slots, :] = silu
    their_half = pl.ds(pl.multiple_of((1 - core) * half, half), half)
    my_half = pl.ds(pl.multiple_of(core * half, half), half)
    silu_copy = to_sib(0, silu_own.at[:, their_half], silu_ref.at[core])
    silu_ref[core] = silu_own[:, my_half]
    spot = lane_iota((32, LANES))
    cells = map_ref[...]
    edge[...] = jnp.where(spot == 0, cells[:, 0:1], jnp.where(spot == 1, cells[:, tokens - 1 : tokens], 0.0))

    def edge_copy(slot, dst, shift):
        return pltpu.make_async_remote_copy(
            src_ref=edge,
            dst_ref=dst,
            send_sem=edge_s.at[slot],
            recv_sem=edge_r.at[slot],
            device_id=(core, lax.rem(wide + shift, 16)),
            device_id_type=MESH_ID,
        )

    edges = [edge_copy(0, edge_left, 1), edge_copy(1, edge_right, 15)]
    for copy in edges:
        copy.start()
    first_flow.run(1)

    for copy in casts[1:]:
        copy.wait()
    s_out[...] = c_out[...].astype(low)
    s_up[...] = c_up[...].T.astype(low)
    s_down[...] = c_down[...].astype(low)

    run_lane = lane_iota((1, LANES))
    run_slot = lax.rem(run_lane - HALF_LANES + slots * LANES, slots)
    lens = jnp.zeros((1, LANES), jnp.int32)
    for j in range(slots):
        lens = jnp.where(run_slot == j, len_ref[0:1, j : j + 1], lens)
    counts = jnp.where(lens == LONG_TOTAL, squares_ref[0:1, :], jnp.where(lens == SHORT_TOTAL, squares_ref[1:2, :], 0.0))
    unused = group_len - jnp.sum(counts, axis=1, keepdims=True)
    counts = jnp.where(run_lane == HALF_LANES + slots * LEVELS, unused, counts)
    ends = exact(jnp.broadcast_to(counts, (8, LANES)), tri_ref[...])[0:1, :]
    starts = ends - counts
    start_col, end_col = column_of(starts), column_of(ends)
    here = (wide * tokens + lane_iota((1, tokens))).astype(f32)
    left = 1.0 - jnp.sum(((here == start_col) & (here < end_col)).astype(f32), axis=0, keepdims=True)
    right = 1.0 - jnp.sum(((here == end_col - 1.0) & (here >= start_col)).astype(f32), axis=0, keepdims=True)
    flags_ref[...] = jnp.zeros_like(flags_ref)
    flags_ref[0:1, :] = left
    flags_ref[1:2, :] = right
    row_at = (wide * tokens + lax.broadcasted_iota(jnp.int32, (tokens, LANES), 0)).astype(f32)
    my_runs = ((row_at >= starts) & (row_at < ends)).astype(low)
    hot = nn(my_runs, pick_ref[...])[:, 0:8]
    hot_ref[...] = hot

    ada_copy.wait()
    w_low = w_ada[...].astype(low)
    silu_copy.wait_recv()
    theirs[...] = nn(silu_ref[1 - core].astype(low), w_low)
    part_copy = to_sib(1, theirs, ours)
    mine = nn(silu_ref[core].astype(low), w_low)
    first_flow.run(2)

    for copy in edges:
        copy.wait_recv()
    column = lane_iota((32, tokens))
    before = jnp.where(column == 0, edge_left[:, 1:2], jnp.roll(cells, 1, axis=1))
    after = jnp.where(column == tokens - 1, edge_right[:, 0:1], jnp.roll(cells, -1, axis=1))
    smooth = smooth_map(cells, left, right, before, after)
    smooth_ref[...] = smooth
    x = exact(smooth, embed_ref[1], (0, 0)) + vec_ref[6:7, :]
    x_ref[...] = x
    part_copy.wait_recv()
    ada_in[...] = mine + ours[...]
    ada_copies = []
    for r in range(1, 16):
        copy = pltpu.make_async_remote_copy(
            src_ref=ada_in,
            dst_ref=ada_ref.at[wide],
            send_sem=ada_send.at[r],
            recv_sem=ada_recv.at[r],
            device_id=(core, wide ^ r),
            device_id_type=MESH_ID,
        )
        copy.start()
        ada_copies.append(copy)
    ada_ref[wide] = ada_in[...]

    def standard(values):
        centred = values - jnp.mean(values, axis=1, keepdims=True)
        return centred * lax.rsqrt(jnp.mean(centred * centred, axis=1, keepdims=True) + NORM_EPS)

    unit = standard(x)
    first_flow.run(3)
    for copy in ada_copies:
        copy.wait_recv()
    ada = jnp.concatenate([ada_ref[w] for w in range(16)], axis=1)

    def of_tokens(block):
        return exact(hot, ada[:, block * width : (block + 1) * width] + vec_ref[block : block + 1, :])

    h_ref[...] = (unit * (1.0 + of_tokens(2)) + of_tokens(4)).astype(low)
    for i, t in enumerate(range(4, first_flow.steps())):
        first_flow.run(t)
        tick(FRONT_TICKS[0][min(i, 3)])
    first_flow.landed()

    group = 256
    loads = []

    def load(j):
        g = lax.rem(z + 1 + j, 4)
        out = []
        for c in range(2):
            for part in range(3):
                rows = pl.ds(pl.multiple_of(g * group + part * width, group), group)
                out.append(pltpu.make_async_copy(f_qkv.at[c, rows], w_ref.at[j, c, part], load_sem.at[j, c, part]))
        return out

    for j in range(4):
        loads.append(load(j))
        for copy in loads[-1]:
            copy.start()
    lane = lane_iota((tokens, LANES))
    lane_mid = lane_iota((mid, LANES))
    for j in range(4):
        g = lax.rem(z + 1 + j, 4)
        first = pl.multiple_of(g * group, group)
        for copy in loads[j]:
            copy.wait()

        def project(part):
            return nt(h_ref[:, :half], w_ref[j, 0, part]) + nt(h_ref[:, half:], w_ref[j, 1, part])

        q_all, k_all, v_all = (project(part) for part in range(3))
        for pair in range(group // LANES):
            cols = slice(pair * LANES, (pair + 1) * LANES)
            at = g * (group // LANES) + pair
            kept_ref[at] = q_all[:, cols]
            kept_ref[at + width // LANES] = k_all[:, cols]
        q_all = q_all * lax.rsqrt(head_sums(q_all * q_all) + NORM_EPS)
        q_all = q_all * (8.0 * (1.0 + vec_ref[7:8, pl.ds(first, group)]))
        k_all = k_all * lax.rsqrt(head_sums(k_all * k_all) + NORM_EPS)
        for pair in range(group // LANES):
            cols = slice(pair * LANES, (pair + 1) * LANES)
            q, k, v = q_all[:, cols], k_all[:, cols], v_all[:, cols]
            head = g * (group // HALF_LANES) + 2 * pair
            send_ref[head, 0:tokens, :] = jnp.where(lane < HALF_LANES, q, swap_halves(k)).astype(low)
            send_ref[head + 1, 0:tokens, :] = jnp.where(lane < HALF_LANES, swap_halves(q), k).astype(low)
            v_a, v_b = v[:mid], v[mid:]
            send_ref[head, tokens:, :] = jnp.where(lane_mid < HALF_LANES, v_a, swap_halves(v_b)).astype(low)
            send_ref[head + 1, tokens:, :] = jnp.where(lane_mid < HALF_LANES, swap_halves(v_a), v_b).astype(low)
        for e in range(4):
            there.push(g * 4 + e)
        tick(FRONT_TICKS[1][j])

    lane_two = lane_iota((two, LANES))

    def unpack(pair, carry):
        for e in range(2):
            there.wait(2 * pair + e)
        first = pl.multiple_of(pair * two, two)
        qk = jnp.concatenate([got_ref[2 * pair + e, 0:tokens, :].astype(f32) for e in range(2)], axis=0)
        spot = (first + lax.broadcasted_iota(jnp.int32, (two, LANES), 0)).astype(f32)
        runs = ((spot >= starts) & (spot < ends)).astype(f32)
        barred = nn(runs.astype(low), rule_ref[...])
        rows = pl.ds(first, two)
        q_ref[rows, :] = jnp.where(lane_two < HALF_LANES, qk, barred).astype(low)
        tail = jnp.where(lane_two >= LANES - 3, 1.0, runs)
        keys = jnp.where(lane_two < HALF_LANES, swap_halves(qk), tail)
        k_ref[rows, :] = keys.astype(low)
        kt_ref[:, rows] = keys.T.astype(low)
        ones = ((lane_mid >= HALF_LANES) & (lane_mid < HALF_LANES + 3)).astype(f32)
        pieces = []
        for e in range(2):
            v = got_ref[2 * pair + e, tokens:, :].astype(f32)
            pieces.append(jnp.where(lane_mid < HALF_LANES, v, ones))
            pieces.append(jnp.where(lane_mid < HALF_LANES, swap_halves(v), ones))
        values = jnp.concatenate(pieces, axis=0)
        v_ref[rows, :] = values.astype(low)
        vt_ref[:, rows] = values.T.astype(low)
        return carry

    lane_q = lane_iota((ROWS, LANES))

    def query_block(limit, b, carry):
        rows = pl.ds(pl.multiple_of(b * ROWS, ROWS), ROWS)
        q = q_ref[rows, :]

        def score(c, top):
            cols = pl.ds(pl.multiple_of(c * CHUNK, CHUNK), CHUNK)
            s = nn(q, kt_ref[:, cols])
            s_ref[:, cols] = s
            return jnp.maximum(top, fold_lanes(s, jnp.maximum))

        whole, left = limit // CHUNK, limit % CHUNK
        top = lax.fori_loop(0, whole, score, jnp.full((ROWS, LANES), -3e38, f32))
        if left:
            tail = slice(whole * CHUNK, limit)
            s = nn(q, kt_ref[:, tail])
            s_ref[:, tail] = s
            top = jnp.maximum(top, fold_lanes(s, jnp.maximum))
        peak = jnp.max(top, axis=1, keepdims=True)

        def weigh(cols, carry):
            total, acc = carry
            p = jnp.exp(s_ref[:, cols] - peak)
            return total + fold_lanes(p, jnp.add), acc + nn(p.astype(low), v_ref[cols, :])

        zero = jnp.zeros((ROWS, LANES), f32)
        total, acc = lax.fori_loop(
            0,
            whole,
            lambda c, carry: weigh(pl.ds(pl.multiple_of(c * CHUNK, CHUNK), CHUNK), carry),
            (zero, zero),
        )
        if left:
            total, acc = weigh(slice(whole * CHUNK, limit), (total, acc))
        total = jnp.sum(total, axis=1, keepdims=True)
        out32_ref[rows, :] = acc / total
        log_total = peak + jnp.log(total)
        q_ref[rows, :] = lanes_three(lane_q, LANES - 3, -log_total, q.astype(f32)).astype(low)
        return carry

    def give_back(w, carry):
        rows = pl.multiple_of(w * tokens, tokens)
        a = out32_ref[pl.ds(rows, mid), :]
        b = out32_ref[pl.ds(pl.multiple_of(rows + mid, mid), mid), :]
        back_send[w] = jnp.where(lane_mid < HALF_LANES, a, swap_halves(b)).astype(low)
        home.push(w)
        return carry

    store((kept_ref, kept_any))
    for i in range(4):
        lax.fori_loop(2 * i, 2 * i + 2, unpack, 0)
        tick(FRONT_TICKS[2][i])
    store((k_ref, k_any), (kt_ref, kt_any), (vt_ref, vt_any))
    plane = 4 * tokens // ROWS
    for p in range(4):
        for first, last, limit in groups:
            begin, end = max(first, p * plane), min(last, (p + 1) * plane)
            for b in range(begin, end):
                lax.fori_loop(b, b + 1, functools.partial(query_block, limit), 0)
                tick(FRONT_TICKS[3][b])
        lax.fori_loop(4 * p, 4 * p + 4, give_back, 0)
    store((q_ref, q_any), (out32_ref, out32_any))
    splits = FRONT_SPLITS[1]
    tick_to(splits[0] + 5)
    flow.landed(range(splits[0]))
    wo_copy = pltpu.make_async_copy(f_out, wo_ref, wo_sem)
    wo_copy.start()
    for pair in range(8):
        home.wait(2 * pair)
        home.wait(2 * pair + 1)
        cols = slice(pair * LANES, (pair + 1) * LANES)
        even, odd = back_got[2 * pair].astype(f32), back_got[2 * pair + 1].astype(f32)
        low_ref[0:mid, cols] = jnp.where(lane_mid < HALF_LANES, even, swap_halves(odd)).astype(low)
        low_ref[mid:, cols] = jnp.where(lane_mid < HALF_LANES, swap_halves(even), odd).astype(low)

    wo_copy.wait()
    proj = nt(low_ref[:, :half], wo_ref[0]) + nt(low_ref[:, half:], wo_ref[1])
    proj_ref[...] = proj
    x_one = x_ref[...] + of_tokens(0) * proj
    one_ref[...] = x_one
    two_ref[...] = (standard(x_one) * (1.0 + of_tokens(3)) + of_tokens(5)).astype(low)
    ups = range(splits[0], splits[0] + splits[1])
    tick_to(ups[-1] + 6)
    flow.landed(ups)
    step = 512
    hidden = pre_ref.shape[1]

    def load_up(c):
        rows = pl.ds(pl.multiple_of(c * step, step), step)
        slot = lax.rem(c, 2)
        return pltpu.make_async_copy(f_up.at[:, rows], wu_ref.at[slot], wu_sem.at[slot])

    load_up(0).start()

    def up_step(c, carry):
        pl.when(c + 1 < hidden // step)(lambda: load_up(c + 1).start())
        load_up(c).wait()
        w = wu_ref.at[lax.rem(c, 2)]
        pre = nt(two_ref[:, :half], w[0]) + nt(two_ref[:, half:], w[1])
        cols = pl.ds(pl.multiple_of(c * step, step), step)
        pre_ref[:, cols] = pre
        act_ref[:, cols] = gelu(pre).astype(low)
        return carry

    live = jnp.sum(hot, axis=1, keepdims=True)
    dmlp[core] = (of_tokens(1) * (cot_ref[...].astype(f32) * live)).astype(low)
    pair_copies = [to_sib(2, dmlp.at[core], dmlp.at[core])]
    hid_half = hidden // 2
    hid_theirs = pl.ds(pl.multiple_of((1 - core) * hid_half, hid_half), hid_half)
    hid_mine = pl.ds(pl.multiple_of(core * hid_half, hid_half), hid_half)
    for i in range(2):
        lax.fori_loop(4 * i, 4 * i + 4, up_step, 0)
        tick(FRONT_TICKS[4][i])
    store((pre_ref, pre_any), (act_ref, act_any))
    pair_copies.append(to_sib(3, act_ref.at[:, hid_theirs], act_half.at[core]))
    act_half[core] = act_ref[:, hid_mine]
    tick(FRONT_TICKS[4][2])
    for copy in pair_copies:
        copy.wait_recv()
    lax.fori_loop(0, width // LANES, gradient(dmlp, act_half, p_down, LANES, width // 16), 0)
    store((p_down, p_any))
    tick(flow.steps())
    flow.landed(range(ups[-1] + 1, sum(splits)))
    first_flow.finish()
    flow.finish()
    there.finish()
    home.finish()
    for copy in ada_copies + edges + pair_copies + [silu_copy, part_copy]:
        copy.wait_send()
    for copy in stores:
        copy.wait()


def front(states, condition, ada_state, cells, embed_state, vector_state, lengths, tables, cotangent, groups):
    width = condition.shape[1]
    tokens = cells.shape[1]
    slots = lengths.shape[1]
    group_len = 16 * tokens
    hidden = 16 * states[2].shape[2]
    f32, low = jnp.float32, jnp.bfloat16
    dma = pltpu.SemaphoreType.DMA
    shape = jax.ShapeDtypeStruct
    ada_width = ada_state.shape[2]
    shards = [s.shape[1:] if i != 2 else s.shape[:0:-1] for i, s in enumerate(states)]
    fulls = [shape((2, 16 * s[0], s[1]), low) for s in shards]
    outs = fulls + [
        shape((16, 8, ada_width), f32),
        shape((tokens, width), low),
        shape((2 * width // LANES, tokens, LANES), f32),
        shape((group_len, LANES), f32),
        shape((group_len, LANES), low),
        shape((group_len, LANES), low),
        shape((LANES, group_len), low),
        shape((LANES, group_len), low),
        shape((tokens, width), low),
        shape((tokens, width), f32),
        shape(cells.shape, f32),
        shape((8, tokens), f32),
        shape((tokens, 8), f32),
        shape((2, 8, width // 2), f32),
        shape((tokens, width), f32),
        shape((tokens, width), f32),
        shape((tokens, width), low),
        shape((tokens, hidden), f32),
        shape((tokens, hidden), low),
        shape((4, 4, width // 16, hidden // 2), low),
    ]
    packed, mid = tokens * 3 // 2, tokens // 2
    scratch = [
        pltpu.VMEM((4, 2, 3, 256, width // 2), low),
        pltpu.VMEM((16, packed, LANES), low),
        pltpu.VMEM((16, packed, LANES), low),
        pltpu.VMEM((16, mid, LANES), low),
        pltpu.VMEM((16, mid, LANES), low),
        pltpu.VMEM((group_len, LANES), low),
        pltpu.VMEM((ROWS, group_len), f32),
        dma((4, 2, 3)),
        pltpu.VMEM(ada_state.shape[1:], f32),
        pltpu.VMEM((8, width), f32),
        pltpu.VMEM((8, ada_width), f32),
        pltpu.VMEM((8, ada_width), f32),
        pltpu.VMEM((8, ada_width), f32),
        pltpu.VMEM((32, LANES), f32),
        pltpu.VMEM((32, LANES), f32),
        pltpu.VMEM((32, LANES), f32),
        pltpu.VMEM((2, width, width // 2), low),
        pltpu.VMEM((2, 2, 512, width // 2), low),
        pltpu.VMEM((2, tokens, width), low),
        pltpu.VMEM((2, tokens, hidden // 2), low),
    ]
    scratch += [pltpu.VMEM(o.shape, o.dtype) for o in outs[6:12] + outs[21:24]]
    scratch += [pltpu.VMEM(s.shape[1:], f32) for s in states] + [pltpu.VMEM(s, low) for s in shards]
    scratch += [dma((4,)), dma((10,))]
    scratch += Gather.scratch(sum(FRONT_SPLITS[0])) + Gather.scratch(sum(FRONT_SPLITS[1])) + [dma((16,)) for _ in range(6)]
    scratch += [dma, dma((4,)), dma((4,)), dma((2,)), dma((2,)), dma, dma((2,))]
    return pl.pallas_call(
        functools.partial(front_kernel, groups, slots),
        out_shape=outs,
        in_specs=[ANY] * 4 + [VM, ANY] + [VM] * 9,
        out_specs=[ANY] * 4 + [VM] * 2 + [ANY] * 6 + [VM] * 9 + [ANY] * 3,
        scratch_shapes=scratch,
        compiler_params=pltpu.CompilerParams(
            collective_id=0, has_side_effects=True, vmem_limit_bytes=VMEM_BYTES
        ),
    )(*states, condition, ada_state, cells, embed_state, vector_state, lengths, *tables, cotangent)


class Scatter:
    STAGES = 6

    def __init__(self, parts, outs, bufs, sems, pieces):
        self.parts, self.outs, self.bufs, self.pieces = parts, outs, bufs, pieces
        self.send, self.recv = sems
        self.parts_left = {}
        core, z, yx = place()
        self.z, self.yx = z, yx
        self.x_dev, self.y_dev = at_dev(core, z, yx ^ 1), at_dev(core, z, yx ^ 2)
        self.up_dev, self.down_dev = at_dev(core, lax.min(z + 1, 3), yx), at_dev(core, lax.max(z - 1, 0), yx)
        self.ends = []

    @staticmethod
    def scratch(shapes, count):
        out = []
        for rows, cols in shapes:
            out += [pltpu.VMEM((depth, rows, cols), jnp.bfloat16) for depth in (2, 2, 4, 4, 3, 3)]
        dma = pltpu.SemaphoreType.DMA
        return out + [dma((count, 8)), dma((count, 8))]

    def push(self, p, slot, src, dst, device):
        copy = pltpu.make_async_remote_copy(
            src_ref=src,
            dst_ref=dst,
            send_sem=self.send.at[p, slot],
            recv_sem=self.recv.at[p, slot],
            device_id=device,
            device_id_type=MESH_ID,
        )
        copy.start()
        return copy

    def arrive(self, p, slot, ref):
        pltpu.make_async_copy(ref, ref, self.recv.at[p, slot]).wait()

    def stage(self, p, s):
        i, first, rows = self.pieces[p]
        rows = pl.ds(first, rows)
        part = self.parts[i]
        names = ("turn_x", "turn_y", "rx", "ry", "up", "down")
        buf = dict(zip(names, self.bufs[6 * i : 6 * i + 6]))
        z, yx = self.z, self.yx
        f32, low = jnp.float32, jnp.bfloat16
        lo2, hi2 = pl.ds(0, 2), pl.ds(2, 2)

        def view(name, which):
            return buf[name].at[which, rows]

        def wide(ref):
            return ref[...].astype(f32)

        def hop(condition, slot, name, which, device):
            ref = view(name, which)

            def start():
                self.push(p, slot, ref, ref, device)

            def end():
                pltpu.make_async_copy(ref, ref, self.send.at[p, slot]).wait()

            pl.when(condition)(start)
            self.ends.append(lambda: pl.when(condition)(end))

        if s == 0:
            copies = [
                self.push(p, 0, part.at[lo2, yx ^ 3, rows], view("turn_x", lo2), self.x_dev),
                self.push(p, 1, part.at[hi2, yx ^ 3, rows], view("turn_y", lo2), self.y_dev),
                self.push(p, 2, part.at[lo2, yx ^ 1, rows], view("rx", lo2), self.x_dev),
                self.push(p, 3, part.at[hi2, yx ^ 2, rows], view("ry", hi2), self.y_dev),
            ]
            self.parts_left[p] = [copy.wait_send for copy in copies]
        elif s == 1:
            turn = view("turn_x", lo2)
            self.arrive(p, 0, turn)
            turn[...] = (wide(part.at[lo2, yx ^ 2, rows]) + wide(turn)).astype(low)
            self.ends.append(self.push(p, 4, turn, view("ry", lo2), self.y_dev).wait_send)
            turn = view("turn_y", lo2)
            self.arrive(p, 1, turn)
            turn[...] = (wide(part.at[hi2, yx ^ 1, rows]) + wide(turn)).astype(low)
            self.ends.append(self.push(p, 5, turn, view("rx", hi2), self.x_dev).wait_send)
        elif s == 2:
            self.arrive(p, 2, view("rx", lo2))
            self.arrive(p, 3, view("ry", hi2))
            self.arrive(p, 4, view("ry", lo2))
            self.arrive(p, 5, view("rx", hi2))
            self.outs[i][rows] = wide(part.at[z, yx, rows]) + wide(view("rx", z)) + wide(view("ry", z))
            for z_at in range(4):
                total = wide(part.at[z_at, yx, rows]) + wide(view("rx", z_at)) + wide(view("ry", z_at))
                view("rx", z_at)[...] = total.astype(low)

            def first_up():
                view("up", pl.ds(0, 3))[...] = view("rx", pl.ds(1, 3))[...]

            def first_down():
                view("down", pl.ds(0, 3))[...] = view("rx", pl.ds(0, 3))[...]

            pl.when(z == 0)(first_up)
            hop(z == 0, 6, "up", pl.ds(0, 3), self.up_dev)
            pl.when(z == 3)(first_down)
            hop(z == 3, 7, "down", pl.ds(0, 3), self.down_dev)
        elif s in (3, 4):
            at = s - 2
            count = 3 - at

            def add_up():
                self.arrive(p, 6, view("up", pl.ds(at - 1, count + 1)))
                ref = view("up", pl.ds(at, count))
                ref[...] = (wide(ref) + wide(view("rx", pl.ds(at + 1, count)))).astype(low)

            def add_down():
                self.arrive(p, 7, view("down", pl.ds(0, count + 1)))
                ref = view("down", pl.ds(0, count))
                ref[...] = (wide(ref) + wide(view("rx", pl.ds(0, count)))).astype(low)

            pl.when(z == at)(add_up)
            hop(z == at, 6, "up", pl.ds(at, count), self.up_dev)
            pl.when(z == 3 - at)(add_down)
            hop(z == 3 - at, 7, "down", pl.ds(0, count), self.down_dev)
        else:
            out = self.outs[i].at[rows]

            def end_low():
                self.arrive(p, 7, view("down", pl.ds(0, 1)))
                out[...] += wide(view("down", 0))

            def end_high():
                self.arrive(p, 6, view("up", pl.ds(2, 1)))
                out[...] += wide(view("up", 2))

            def end_inner(at):
                out[...] += wide(view("up", at - 1)) + wide(view("down", at))

            pl.when(z == 0)(end_low)
            pl.when(z == 1)(lambda: end_inner(1))
            pl.when(z == 2)(lambda: end_inner(2))
            pl.when(z == 3)(end_high)

    def steps(self):
        return len(self.pieces) + self.STAGES - 1

    def run(self, t):
        for s in reversed(range(self.STAGES)):
            if 0 <= t - s < len(self.pieces):
                self.stage(t - s, s)

    def sent(self, p):
        for end in self.parts_left.pop(p, ()):
            end()

    def finish(self):
        for p in list(self.parts_left):
            self.sent(p)
        for end in self.ends:
            end()


COMMON_ROWS = 48
FRONT_SPLITS = ((2,), (1, 4, 4))
FRONT_TICKS = ((1, 1, 1, 0), (0, 1, 0, 1), (0, 0, 0, 1), (0, 0, 0, 0, 0, 0, 1, 0, 0, 1, 0, 1), (1, 1, 1))
BACK_SPLITS = ((4, 4, 1), (3,))
BACK_TICKS = ((1, 0, 1, 1), (1, 0), (0, 0, 0, 1), (1, 0, 1, 0), (1, 1, 1), (1, 1))


def standard_of(values):
    centred = values - jnp.mean(values, axis=1, keepdims=True)
    rstd = lax.rsqrt(jnp.mean(centred * centred, axis=1, keepdims=True) + NORM_EPS)
    return centred * rstd, rstd


def standard_back(unit, rstd, d_unit):
    along = jnp.mean(d_unit * unit, axis=1, keepdims=True)
    return rstd * (d_unit - jnp.mean(d_unit, axis=1, keepdims=True) - unit * along)


def gelu_slope(values):
    square = values * values
    inner = jnp.tanh(GELU_SCALE * (values + GELU_CUBE * values * square))
    slope = GELU_SCALE * (1.0 + 3.0 * GELU_CUBE * square)
    return 0.5 * (1.0 + inner) + 0.5 * values * (1.0 - inner * inner) * slope


def back_kernel(groups, splits, *refs):
    (
        cot_ref, hot_ref, ada_in, vec3_ref, x_ref, one_ref, proj_ref, h_any, two_any, low_any, act_any, pre_any,
        w_any, wo_any, wu_any, wd_any, book_any, out32_any, q_any, k_any, kt_any, vt_any, kept_any,
        smooth_ref, embed_ref, ok_ref, p_any,
    ) = refs[:27]
    (o_down, o_up, o_out, o_qkv, ada_both, common_all, bias_all, map_ref, block_ref) = refs[27:36]
    (
        send_ref, got_ref, back_send, back_got, g_ref, gt_ref, qt_ref, dq_ref, dkt_ref, dvt_ref,
        w_buf, dhid, h_both, dh_ref, ada_ref, com_ref, ada_land, com_land, ada_sum, com_sum, ada_sib, com_sib,
        bias_own, com_own, edge, edge_left, edge_right,
        dmlp, two_half, low_half, dattn, mlp_ref, dx_one, act_buf, pre_buf, d_att, p_up, p_out, p_down, q_ref, k_ref, kt_ref, vt_ref, early_sem, att_send, att_got, dq_s, dq_r,
    ) = refs[36:84]
    rest = refs[84:]
    flow_bufs, rest = rest[:18], rest[18:]
    flow_sems, rest = rest[:2], rest[2:]
    last_bufs, rest = rest[:6], rest[6:]
    last_sems, rest = rest[:2], rest[2:]
    (
        ex_s, ex_r, home_s, home_r, w_sem, sib_s, sib_r, small_s, small_r, spread_s, spread_r, edge_s, edge_r,
        hid_s, hid_r, half_sem, kept_sem, free_sem,
    ) = rest
    core, z, yx = place()
    wide = z * 4 + yx
    sib = (1 - core, wide)
    f32, low = jnp.float32, jnp.bfloat16
    tokens, width = x_ref.shape
    half = width // 2
    hidden = dhid.shape[2]
    mid = tokens // 2
    two = 2 * tokens
    step = 512
    vec_ref = vec3_ref.at[1]
    dproj = dhid.at[:, :, pl.ds(0, 3 * width)]
    p_qkv = p_up.at[:, :, pl.ds(0, tokens)]
    flow = Scatter([p_down, p_up, p_out], [o_down, o_up, o_out], flow_bufs, flow_sems, splits[0])
    last = Scatter([p_qkv], [o_qkv], last_bufs, last_sems, splits[1])
    there = Exchange(att_send, att_got, (ex_s, ex_r))
    home = Exchange(send_ref, got_ref, (home_s, home_r))
    back = Exchange(back_send, back_got, (dq_s, dq_r))
    early = [
        pltpu.make_async_copy(src, dst, early_sem.at[i])
        for i, (src, dst) in enumerate(
            [(p_any, p_down), (q_any, q_ref), (k_any, k_ref), (kt_any, kt_ref), (vt_any, vt_ref)]
        )
    ]
    for copy in early:
        copy.start()
    entry_barrier([(core, wide ^ r) for r in range(1, 16)] + [sib])

    def to_sib(slot, src, dst):
        copy = pltpu.make_async_remote_copy(
            src_ref=src, dst_ref=dst, send_sem=sib_s.at[slot], recv_sem=sib_r.at[slot], device_id=sib, device_id_type=MESH_ID
        )
        copy.start()
        return copy

    next_tick = [0]

    def tick(n):
        for _ in range(n):
            if next_tick[0] < flow.steps():
                flow.run(next_tick[0])
                next_tick[0] += 1

    lane = lane_iota((two, LANES))
    lane_tok = lane_iota((tokens, LANES))
    lane_mid = lane_iota((mid, LANES))

    def load_chunk(c):
        slot = lax.rem(c, 2)
        cols = pl.ds(pl.multiple_of(c * step, step), step)
        down_cols = pl.ds(pl.multiple_of(lax.rem(c, hidden // 2 // step) * step, step), step)
        down = wd_any.at[c // (hidden // 2 // step)]
        pairs = [
            (down.at[pl.ds(0, half), down_cols], w_buf.at[slot, 0]),
            (down.at[pl.ds(half, half), down_cols], w_buf.at[slot, 1]),
            (wu_any.at[0, cols], w_buf.at[slot, 2]),
            (wu_any.at[1, cols], w_buf.at[slot, 3]),
            (act_any.at[:, cols], act_buf.at[slot]),
            (pre_any.at[:, cols], pre_buf.at[slot]),
        ]
        return [pltpu.make_async_copy(src, dst, w_sem.at[slot, i]) for i, (src, dst) in enumerate(pairs)]

    def start_chunk(c):
        for copy in load_chunk(c):
            copy.start()

    start_chunk(0)
    out32_copy = pltpu.make_async_copy(out32_any, dq_ref, kept_sem)
    out32_copy.start()
    theirs = pl.ds(pl.multiple_of((1 - core) * half, half), half)
    mine = pl.ds(pl.multiple_of(core * half, half), half)
    ada = jnp.concatenate([ada_in[w] for w in range(16)], axis=1)
    hot = hot_ref[...]

    def of_tokens(block):
        return exact(hot, ada[:, block * width : (block + 1) * width] + vec_ref[block : block + 1, :])

    live = jnp.sum(hot, axis=1, keepdims=True)
    gate_two = of_tokens(1)
    dmlp[...] = (gate_two * (cot_ref[...].astype(f32) * live)).astype(low)
    sib_copies = [
        to_sib(2, two_any.at[:, theirs], two_half.at[core]),
        to_sib(3, low_any.at[:, theirs], low_half.at[core]),
        to_sib(4, h_any.at[:, theirs], h_both.at[core]),
    ]
    half_copies = [
        pltpu.make_async_copy(src, dst.at[core], half_sem.at[i])
        for i, (src, dst) in enumerate(
            [
                (two_any.at[:, mine], two_half),
                (low_any.at[:, mine], low_half),
                (h_any.at[:, mine], h_both),
            ]
        )
    ]
    for copy in half_copies:
        copy.start()
    mlp_ref[...] = jnp.zeros_like(mlp_ref)
    dh_ref[...] = jnp.zeros_like(dh_ref)

    def hid_copy(c):
        cols = pl.ds(pl.multiple_of(c * step, step), step)
        return pltpu.make_async_remote_copy(
            src_ref=dhid.at[core, :, cols],
            dst_ref=dhid.at[core, :, cols],
            send_sem=hid_s.at[c],
            recv_sem=hid_r.at[c],
            device_id=sib,
            device_id_type=MESH_ID,
        )

    def hidden_step(c, carry):
        pl.when(c + 1 < hidden // step)(lambda: start_chunk(c + 1))
        for copy in load_chunk(c):
            copy.wait()
        slot = lax.rem(c, 2)
        w = w_buf.at[slot]
        d_act = nn(dmlp[:, :half], w[0]) + nn(dmlp[:, half:], w[1])
        d_hid = (d_act * gelu_slope(pre_buf[slot])).astype(low)
        dhid[core, :, pl.ds(pl.multiple_of(c * step, step), step)] = d_hid
        hid_copy(c).start()
        act = act_buf[slot]
        mlp_ref[:, :half] += nt(act, w[0])
        mlp_ref[:, half:] += nt(act, w[1])
        dh_ref[:, :half] += nn(d_hid, w[2])
        dh_ref[:, half:] += nn(d_hid, w[3])
        return carry

    chunks = hidden // step
    early[0].wait()
    for i in range(4):
        tick(BACK_TICKS[0][i])
        lax.fori_loop(2 * i, 2 * i + 2, hidden_step, 0)

    wo_copies = [
        pltpu.make_async_copy(wo_any.at[c, pl.ds(r * half, half)], w_buf.at[0, 2 * c + r], w_sem.at[0, 2 * c + r])
        for c in range(2)
        for r in range(2)
    ]
    for copy in wo_copies:
        copy.start()
    unit, rstd = standard_of(one_ref[...])
    g_two = cot_ref[...].astype(f32) * live
    d_one = standard_back(unit, rstd, dh_ref[...] * (1.0 + of_tokens(3))) + g_two
    dx_one[...] = d_one
    dattn[core] = (of_tokens(0) * d_one).astype(low)
    sib_copies.append(to_sib(5, dattn.at[core], dattn.at[core]))
    for copy in wo_copies:
        copy.wait()
    for c in range(2):
        part = nn(dattn[core, :, :half], w_buf[0, 2 * c]) + nn(dattn[core, :, half:], w_buf[0, 2 * c + 1])
        d_att[:, c * half : (c + 1) * half] = part.astype(low)

    def pack(pair, carry):
        cols = pl.ds(pl.multiple_of(pair * LANES, LANES), LANES)
        a, b = d_att[0:mid, cols].astype(f32), d_att[mid:, cols].astype(f32)
        att_send[2 * pair] = jnp.where(lane_mid < HALF_LANES, a, swap_halves(b)).astype(low)
        att_send[2 * pair + 1] = jnp.where(lane_mid < HALF_LANES, swap_halves(a), b).astype(low)
        there.push(2 * pair)
        there.push(2 * pair + 1)
        return carry

    lax.fori_loop(0, 8, pack, 0)

    def per_slot(values):
        return exact(hot, values, (0, 0))

    ada_ref[:, 3 * width : 4 * width] = per_slot(dh_ref[...] * unit)
    ada_ref[:, 5 * width : 6 * width] = per_slot(dh_ref[...])
    ada_ref[:, 0:width] = per_slot(d_one * proj_ref[...])
    ada_ref[:, width : 2 * width] = per_slot(g_two * mlp_ref[...])
    block_ref[...] = (live * (one_ref[...] + gate_two * mlp_ref[...])).astype(low)
    for c in range(chunks):
        hid_copy(c).wait_recv()
    half_copies[0].wait()
    sib_copies[0].wait_recv()
    lax.fori_loop(0, hidden // 256, gradient(dhid, two_half, p_up, 256, hidden // 16), 0)
    for c in range(chunks):
        hid_copy(c).wait_send()
    pl.semaphore_signal(free_sem, inc=1, device_id=sib, device_id_type=MESH_ID)
    tick(BACK_TICKS[1][0])
    half_copies[1].wait()
    sib_copies[1].wait_recv()
    sib_copies[3].wait_recv()
    lax.fori_loop(0, width // LANES, gradient(dattn, low_half, p_out, LANES, width // 16), 0)
    tick(BACK_TICKS[1][1])
    dkt_ref[...] = jnp.zeros_like(dkt_ref)
    dvt_ref[...] = jnp.zeros_like(dvt_ref)

    def unpack(pair, carry):
        there.wait(2 * pair)
        there.wait(2 * pair + 1)
        rows = pl.ds(pl.multiple_of(pair * two, two), two)
        pieces = []
        for e in range(2):
            g = att_got[2 * pair + e].astype(f32)
            pieces += [g, swap_halves(g)]
        grad = jnp.where(lane < HALF_LANES, jnp.concatenate(pieces, axis=0), 0.0)
        delta = jnp.sum(grad * dq_ref[rows, :], axis=1, keepdims=True)
        grad = lanes_three(lane, HALF_LANES, -delta, grad)
        g_ref[rows, :] = grad.astype(low)
        gt_ref[:, rows] = grad.T[:HALF_LANES].astype(low)
        qt_ref[:, rows] = q_ref[rows, :].astype(f32).T[:HALF_LANES].astype(low)
        return carry

    out32_copy.wait()
    for copy in early[1:]:
        copy.wait()
    for i in range(4):
        lax.fori_loop(2 * i, 2 * i + 2, unpack, 0)
        tick(BACK_TICKS[2][i])

    def query_block(first, size, b, carry):
        rows = pl.ds(pl.multiple_of(b * ROWS, ROWS), ROWS)
        cols = slice(first, first + size)
        q, g = q_ref[rows, :], g_ref[rows, :]
        p = jnp.exp(nn(q, kt_ref[:, cols]))
        ds = (p * nn(g, vt_ref[:, cols])).astype(low)
        dvt_ref[:, cols] += nn(gt_ref[:, rows], p.astype(low))
        dkt_ref[:, cols] += nn(qt_ref[:, rows], ds)
        part = nn(ds, k_ref[cols, :])
        if first == 0:
            dq_ref[rows, :] = part
        else:
            dq_ref[rows, :] += part
        return carry

    def send_keys(pair, carry):
        rows = pl.ds(pl.multiple_of(pair * two, two), two)
        dkv = jnp.concatenate([dkt_ref[:, rows], dvt_ref[:, rows]], axis=0).T.astype(low)
        for e in range(2):
            send_ref[2 * pair + e] = dkv[e * tokens : (e + 1) * tokens]
            home.push(2 * pair + e)
        return carry

    def send_queries(w, carry):
        rows = pl.multiple_of(w * tokens, tokens)
        a = dq_ref[pl.ds(rows, mid), :]
        b = dq_ref[pl.ds(pl.multiple_of(rows + mid, mid), mid), :]
        back_send[w] = jnp.where(lane_mid < HALF_LANES, a, swap_halves(b)).astype(low)
        back.push(w)
        return carry

    plane = 4 * tokens
    sent = 0
    for c in range(4):
        for first, stop, limit in groups:
            if limit > c * plane:
                size = min(plane, limit - c * plane)
                lax.fori_loop(first, stop, functools.partial(query_block, c * plane, size), 0)
        lax.fori_loop(2 * c, 2 * c + 2, send_keys, 0)
        while sent < 4 and all(
            limit <= (c + 1) * plane
            for first, stop, limit in groups
            if first * ROWS < (sent + 1) * plane and stop * ROWS > sent * plane
        ):
            lax.fori_loop(4 * sent, 4 * sent + 4, send_queries, 0)
            sent += 1
        tick(BACK_TICKS[3][c])

    kept_copy = pltpu.make_async_copy(kept_any, dq_ref, kept_sem)
    kept_copy.start()
    tick(BACK_TICKS[4][0])
    com_ref[...] = jnp.zeros_like(com_ref)

    def load_codes(c):
        slot = lax.rem(c, 2)
        rows = pl.ds(pl.multiple_of(lax.rem(c, chunks) * step, step), step)
        return [
            pltpu.make_async_copy(book_any.at[rows, pl.ds(r * half, half)], w_buf.at[slot, r], w_sem.at[slot, r])
            for r in range(2)
        ]

    def start_codes(c):
        for copy in load_codes(c):
            copy.start()

    start_codes(0)

    def logits_of(c):
        pl.when(c + 1 < 2 * chunks)(lambda: start_codes(c + 1))
        for copy in load_codes(c):
            copy.wait()
        w = w_buf.at[lax.rem(c, 2)]
        return nt(block_ref[:, :half], w[0]) + nt(block_ref[:, half:], w[1])

    def sum_codes(c, carry):
        top, total = carry
        logits = logits_of(c)
        new_top = jnp.maximum(top, jnp.max(logits, axis=1, keepdims=True))
        return new_top, total * jnp.exp(top - new_top) + jnp.sum(jnp.exp(logits - new_top), axis=1, keepdims=True)

    start = (jnp.full((tokens, 1), -3e38, f32), jnp.zeros((tokens, 1), f32))
    top, total = lax.fori_loop(0, chunks, sum_codes, start)
    share_of = live / total
    tick(BACK_TICKS[4][1])
    for c in range(chunks):
        mass = jnp.sum(jnp.exp(logits_of(chunks + c) - top) * share_of, axis=0, keepdims=True)
        com_ref[34 + c // 2 : 35 + c // 2, (c % 2) * step : (c % 2 + 1) * step] = mass
    slabs = 3 * width // step

    def load_w(j):
        rows = pl.ds(j * step, step)
        return [pltpu.make_async_copy(w_any.at[c, rows], w_buf.at[j % 2, c], w_sem.at[j % 2, c]) for c in range(2)]

    for j in range(2):
        for copy in load_w(j):
            copy.start()
    kept_copy.wait()
    tick(BACK_TICKS[4][2])

    def unnormalize(values, grad):
        inverse = lax.rsqrt(head_sums(values * values) + NORM_EPS)
        unit = values * inverse
        return inverse * (grad - unit * head_sums(unit * grad)), unit

    def heads_back(pair, carry):
        for e in range(2):
            home.wait(2 * pair + e)
            back.wait(2 * pair + e)
        cols = pl.ds(pl.multiple_of(pair * LANES, LANES), LANES)
        key_cols = pl.ds(pl.multiple_of(pair * LANES + width, LANES), LANES)
        val_cols = pl.ds(pl.multiple_of(pair * LANES + 2 * width, LANES), LANES)
        even, odd = got_ref[2 * pair].astype(f32), got_ref[2 * pair + 1].astype(f32)
        d_key = jnp.where(lane_tok < HALF_LANES, even, swap_halves(odd))
        dproj[core, :, val_cols] = jnp.where(lane_tok < HALF_LANES, swap_halves(even), odd).astype(low)
        even, odd = back_got[2 * pair].astype(f32), back_got[2 * pair + 1].astype(f32)
        d_query = jnp.concatenate(
            [
                jnp.where(lane_mid < HALF_LANES, even, swap_halves(odd)),
                jnp.where(lane_mid < HALF_LANES, swap_halves(even), odd),
            ],
            axis=0,
        )
        scaled = d_query * (8.0 * (1.0 + vec_ref[7:8, cols]))
        d_q, unit = unnormalize(dq_ref[pl.ds(pl.multiple_of(pair * tokens, tokens), tokens), :], scaled)
        com_ref[33:34, cols] = jnp.sum(d_query * unit, axis=0, keepdims=True) * 8.0
        dproj[core, :, cols] = d_q.astype(low)
        dproj[core, :, key_cols] = unnormalize(dq_ref[pl.ds(pl.multiple_of((pair + 8) * tokens, tokens), tokens), :], d_key)[0].astype(low)
        return carry

    for i in range(2):
        lax.fori_loop(4 * i, 4 * i + 4, heads_back, 0)
        tick(BACK_TICKS[5][i])
    pl.semaphore_wait(free_sem, 1)
    d_copy = to_sib(6, dproj.at[core], dproj.at[core])

    for j in range(slabs):
        for copy in load_w(j):
            copy.wait()
        for c in range(2):
            part = nn(dproj[core, :, j * step : (j + 1) * step], w_buf[j % 2, c])
            cols = slice(c * half, (c + 1) * half)
            dh_ref[:, cols] = part if j == 0 else dh_ref[:, cols] + part
        if j + 2 < slabs:
            for copy in load_w(j + 2):
                copy.start()
    half_copies[2].wait()
    sib_copies[2].wait_recv()
    d_copy.wait_recv()

    def weight_grad(c, carry):
        cols = pl.ds(pl.multiple_of(c * two, two), two)
        total = nn(dproj[0, :, cols].astype(f32).T.astype(low), h_both[0])
        total = total + nn(dproj[1, :, cols].astype(f32).T.astype(low), h_both[1])
        p_qkv[c // 2, pl.ds(2 * (c % 2), 2)] = total.astype(low).reshape(2, tokens, half)
        return carry

    assert next_tick[0] >= len(splits[0]) + 3
    for p in range(len(splits[0])):
        flow.sent(p)
    lax.fori_loop(0, 8, weight_grad, 0)
    last.run(0)
    tick(flow.steps())

    unit, rstd = standard_of(x_ref[...])
    d_h = dh_ref[...]
    ada_ref[:, 2 * width : 3 * width] = per_slot(d_h * unit)
    ada_ref[:, 4 * width : 5 * width] = per_slot(d_h)
    d_x = standard_back(unit, rstd, d_h * (1.0 + of_tokens(2))) + dx_one[...]
    last.run(1)
    com_ref[0:32, :] = lax.dot_general(
        smooth_ref[...], d_x, (((1,), (0,)), ((), ())), precision=HIGHEST_PRECISION, preferred_element_type=f32
    )
    com_ref[32:33, :] = jnp.sum(d_x, axis=0, keepdims=True)
    small = []
    quarter = COMMON_ROWS // 2

    def common_part(ref, w):
        rows = pl.ds(pl.multiple_of((w // 8) * quarter, 8), quarter)
        return ref.at[rows, pl.ds(pl.multiple_of((w % 8) * LANES, LANES), LANES)]

    ada_width = 6 * width // 16

    def ada_part(ref, w):
        return ref.at[:, pl.ds(pl.multiple_of(w * ada_width, LANES), ada_width)]

    def spread(sem_s, sem_r, r, slot, src, dst):
        copy = pltpu.make_async_remote_copy(
            src_ref=src,
            dst_ref=dst,
            send_sem=sem_s.at[slot, r],
            recv_sem=sem_r.at[slot, r],
            device_id=(core, wide ^ r),
            device_id_type=MESH_ID,
        )
        copy.start()
        return copy

    for r in range(1, 16):
        small.append(spread(small_s, small_r, r, 0, ada_part(ada_ref, wide ^ r), ada_land.at[r]))
        small.append(spread(small_s, small_r, r, 1, common_part(com_ref, wide ^ r), com_land.at[r]))
    d_smooth = lax.dot_general(
        embed_ref[1], d_x, (((1,), (1,)), ((), ())), precision=HIGHEST_PRECISION, preferred_element_type=f32
    )
    left, right = ok_ref[0:1, :], ok_ref[1:2, :]
    share = d_smooth / (2.0 + left + right)
    spot = lane_iota((32, LANES))
    edge[...] = jnp.where(spot == 0, share[:, 0:1], jnp.where(spot == 1, share[:, tokens - 1 : tokens], 0.0))

    def edge_copy(slot, dst, shift):
        return pltpu.make_async_remote_copy(
            src_ref=edge,
            dst_ref=dst,
            send_sem=edge_s.at[slot],
            recv_sem=edge_r.at[slot],
            device_id=(core, lax.rem(wide + shift, 16)),
            device_id_type=MESH_ID,
        )

    to_right, to_left = edge_copy(0, edge_left, 1), edge_copy(1, edge_right, 15)
    to_right.start()
    to_left.start()
    last.run(2)
    ada_total, com_total = ada_part(ada_ref, wide)[...], common_part(com_ref, wide)[...]
    for copy in small:
        copy.wait_recv()
    for r in range(1, 16):
        ada_total = ada_total + ada_land[r]
        com_total = com_total + com_land[r]
    ada_sum[...] = ada_total
    com_sum[...] = com_total
    swaps = [to_sib(7, ada_sum, ada_sib), to_sib(8, com_sum, com_sib)]
    last.run(3)
    for copy in swaps:
        copy.wait_recv()
    ada_both[core] = ada_sum[...]
    ada_both[1 - core] = ada_sib[...]
    bias = jnp.sum(ada_sum[...] + ada_sib[...], axis=0, keepdims=True)
    bias_own[...] = jnp.broadcast_to(bias, bias_own.shape)
    com_own[...] = com_sum[...] + com_sib[...]
    ada_part(bias_all, wide)[...] = bias_own[...]
    common_part(common_all, wide)[...] = com_own[...]
    spreads = []
    for r in range(1, 16):
        spreads.append(spread(spread_s, spread_r, r, 0, bias_own, ada_part(bias_all, wide)))
        spreads.append(spread(spread_s, spread_r, r, 1, com_own, common_part(common_all, wide)))
    for i in range(4, last.steps()):
        last.run(i)
    to_right.wait_recv()
    to_left.wait_recv()
    column = lane_iota((32, tokens))
    before = jnp.where(column == 0, edge_left[:, 1:2], jnp.roll(share, 1, axis=1))
    after = jnp.where(column == tokens - 1, edge_right[:, 0:1], jnp.roll(share, -1, axis=1))
    map_ref[...] = 2.0 * share + left * before + right * after
    for copy in spreads:
        copy.wait_recv()
    for copy in small + swaps + spreads + sib_copies + [d_copy, to_right, to_left]:
        copy.wait_send()
    flow.finish()
    last.finish()
    there.finish()
    home.finish()
    back.finish()


def back(args, groups, splits, call_id):
    x_zero, act = args[4], args[10]
    tokens, width = x_zero.shape
    hidden = act.shape[1]
    group_len = 16 * tokens
    half, mid = width // 2, tokens // 2
    f32, low = jnp.float32, jnp.bfloat16
    dma = pltpu.SemaphoreType.DMA
    shape = jax.ShapeDtypeStruct
    sizes = [(width // 16, hidden // 2), (hidden // 16, half), (width // 16, half), (3 * width // 16, half)]
    first = pieces_of([shape(s, f32) for s in sizes[:3]], splits[0])
    second = pieces_of([shape(sizes[3], f32)], splits[1])
    ada_width, quarter = 6 * width // 16, COMMON_ROWS // 2
    outs = [shape(s, f32) for s in sizes] + [
        shape((2, 8, ada_width), f32),
        shape((COMMON_ROWS, width), f32),
        shape((8, 6 * width), f32),
        shape((32, tokens), f32),
        shape((tokens, width), low),
    ]
    vm = pltpu.VMEM
    scratch = [
        vm((16, tokens, LANES), low),
        vm((16, tokens, LANES), low),
        vm((16, mid, LANES), low),
        vm((16, mid, LANES), low),
        vm((group_len, LANES), low),
        vm((HALF_LANES, group_len), low),
        vm((HALF_LANES, group_len), low),
        vm((group_len, LANES), f32),
        vm((HALF_LANES, group_len), f32),
        vm((HALF_LANES, group_len), f32),
        vm((2, 4, 512, half), low),
        vm((2, tokens, hidden), low),
        vm((2, tokens, half), low),
        vm((tokens, width), f32),
        vm((8, 6 * width), f32),
        vm((COMMON_ROWS, width), f32),
        vm((16, 8, ada_width), f32),
        vm((16, quarter, LANES), f32),
        vm((8, ada_width), f32),
        vm((quarter, LANES), f32),
        vm((8, ada_width), f32),
        vm((quarter, LANES), f32),
        vm((8, ada_width), f32),
        vm((quarter, LANES), f32),
        vm((32, LANES), f32),
        vm((32, LANES), f32),
        vm((32, LANES), f32),
        vm((tokens, width), low),
        vm((2, tokens, half), low),
        vm((2, tokens, half), low),
        vm((2, tokens, width), low),
        vm((tokens, width), f32),
        vm((tokens, width), f32),
        vm((2, tokens, 512), low),
        vm((2, tokens, 512), f32),
        vm((tokens, width), low),
    ] + [vm((4, 4) + s, low) for s in (sizes[1], sizes[2], sizes[0])]
    scratch += [vm((group_len, LANES), low)] * 2 + [vm((LANES, group_len), low)] * 2 + [dma((5,))]
    scratch += [vm((16, mid, LANES), low)] * 2 + [dma((16,))] * 2
    scratch += Scatter.scratch(sizes[:3], len(first)) + Scatter.scratch(sizes[3:], len(second))
    scratch += [dma((16,)) for _ in range(4)] + [dma((2, 6)), dma((16,)), dma((16,))]
    scratch += [dma((2, 16)) for _ in range(4)] + [dma((2,)), dma((2,))]
    scratch += [dma((8,)), dma((8,)), dma((4,)), dma, pltpu.SemaphoreType.REGULAR]
    return pl.pallas_call(
        functools.partial(back_kernel, groups, (first, second)),
        out_shape=outs,
        in_specs=[VM] * 7 + [ANY] * 16 + [VM] * 3 + [ANY],
        out_specs=[VM] * 9,
        scratch_shapes=scratch,
        compiler_params=pltpu.CompilerParams(
            collective_id=call_id, has_side_effects=True, vmem_limit_bytes=63 * 1024 * 1024
        ),
    )(*args)


def nesterov_rows(moment, weight, average, gradient, step_rate, decay_rate):
    step_grad = gradient + decay_rate * weight
    new_moment = MOMENTUM * moment + step_rate * step_grad
    new_weight = weight - (step_rate * step_grad + MOMENTUM * new_moment)
    retain = min(0.999, (1.0 + STEP) / (10.0 + STEP))
    return new_moment, new_weight, retain * average + (1.0 - retain) * new_weight


def update_kernel(rates, mass_scale, *refs):
    states = refs[:5]
    (embed_ref, vector_ref, s_down, s_up, s_out, s_qkv, d_ada, silu_ref, common_ref, bias_ref) = refs[5:15]
    passed, news, copies, passed_out = refs[15:17], refs[17:22], refs[22:27], refs[27:29]
    for src, dst in zip(passed, passed_out):
        dst[...] = src[...]
    (embed_new, vector_new, mass_out, gain_out) = refs[29:33]
    held, lows = refs[33:38], refs[38:43]
    load_sem, store_sem, low_sem = refs[43:]
    width = vector_ref.shape[2]

    def grad_of(i):
        if i == 4:
            return exact(silu_ref[...], d_ada[...], (0, 0))
        return (s_qkv, s_out, None, s_down)[i][...] if i != 2 else s_up[...].T

    order = (3, 2, 4, 0, 1)
    loads = {i: pltpu.make_async_copy(states[i], held[i], load_sem.at[i]) for i in order}
    for i in order:
        loads[i].start()
    rows = embed_ref.shape[1]
    parts = nesterov_rows(embed_ref[0], embed_ref[1], embed_ref[2], common_ref[0:rows, :], rates[5], 0.0)
    for j in range(3):
        embed_new[j] = parts[j]
    for block in range(8):
        if block < 6:
            grad = bias_ref[0:1, block * width : (block + 1) * width]
        else:
            grad = common_ref[rows + block - 6 : rows + block - 5, :]
        here = slice(block, block + 1)
        parts = nesterov_rows(vector_ref[0, here], vector_ref[1, here], vector_ref[2, here], grad, rates[6], 0.0)
        for j in range(3):
            vector_new[j, here] = parts[j]
    per_row = width // LANES
    for r in range(per_row):
        cols = slice(r * LANES, (r + 1) * LANES)
        gain_out[r : r + 1, :] = common_ref[rows + 1 : rows + 2, cols]
        for a in range(mass_out.shape[0] // per_row):
            at = a * per_row + r
            mass_out[at : at + 1, :] = common_ref[rows + 2 + a : rows + 3 + a, cols] * mass_scale
    stores = []
    for i in order:
        loads[i].wait()
        parts = nesterov_rows(held[i][0], held[i][1], held[i][2], grad_of(i), rates[i], WEIGHT_DECAY)
        for j in range(3):
            held[i][j] = parts[j]
        lows[i][...] = parts[1].astype(jnp.bfloat16)
        stores.append(pltpu.make_async_copy(held[i], news[i], store_sem.at[i]))
        stores.append(pltpu.make_async_copy(lows[i], copies[i], low_sem.at[i]))
        for copy in stores[-2:]:
            copy.start()
    for copy in stores:
        copy.wait()


def update(states, embed_state, vector_state, grads, passed, rates, codes, mass_scale):
    f32, low = jnp.float32, jnp.bfloat16
    shape = jax.ShapeDtypeStruct
    dma = pltpu.SemaphoreType.DMA
    width = vector_state.shape[2]
    outs = [shape(s.shape, f32) for s in states] + [shape(s.shape[1:], low) for s in states]
    outs += [shape(p.shape, p.dtype) for p in passed]
    outs += [shape(embed_state.shape, f32), shape(vector_state.shape, f32)]
    outs += [shape((codes // LANES, LANES), f32), shape((width // LANES, LANES), f32)]
    return pl.pallas_call(
        functools.partial(update_kernel, rates, mass_scale),
        out_shape=outs,
        in_specs=[ANY] * 5 + [VM] * 12,
        out_specs=[ANY] * 10 + [VM] * 6,
        scratch_shapes=[pltpu.VMEM(s.shape, f32) for s in states]
        + [pltpu.VMEM(s.shape[1:], low) for s in states]
        + [dma((5,)), dma((5,)), dma((5,))],
        compiler_params=pltpu.CompilerParams(vmem_limit_bytes=VMEM_BYTES),
    )(*states, embed_state, vector_state, *grads, *passed)


def run_tables(slots):
    squares = np.zeros((8, LANES), np.float32)
    pick = np.zeros((LANES, LANES), np.float32)
    for run in range(slots * LEVELS):
        squares[0, HALF_LANES + run] = LONG_SIDES[run // slots] ** 2
        squares[1, HALF_LANES + run] = SHORT_SIDES[run // slots] ** 2
        pick[HALF_LANES + run, run % slots] = 1.0
    tri = np.triu(np.ones((LANES, LANES), np.float32))
    low = jnp.bfloat16
    return [jnp.asarray(squares), jnp.asarray(tri), jnp.asarray(pick, low), jnp.asarray(attention_rule(slots), low)]


def attention_rule(slots):
    runs = slots * LEVELS + 1
    rule = np.zeros((LANES, LANES), np.float32)
    for a in range(runs):
        for b in range(runs):
            slot_a, level_a = (slots, 0) if a == runs - 1 else (a % slots, a // slots)
            slot_b, level_b = (slots, 0) if b == runs - 1 else (b % slots, b // slots)
            if slot_a != slot_b or level_b > level_a:
                rule[HALF_LANES + a, HALF_LANES + b] = -BIG
    return rule


def fast_shards(
    feature_map,
    condition,
    item_lengths,
    cotangent,
    code_book,
    qkv_state,
    out_state,
    up_state,
    down_state,
    ada_state,
    embed_state,
    vector_state,
):
    tok_rows, model_width = cotangent.shape
    low = jnp.bfloat16
    group_len = tok_rows * lax.axis_size("wide")
    tokens_all = lax.axis_size("dp") * group_len
    lengths = item_lengths[0]
    slot_count = lengths.shape[0]

    flip = lambda values: jnp.swapaxes(values, -1, -2)
    flipped = [flip(qkv_state), flip(out_state), up_state, flip(down_state)]
    groups = same_limits(key_limits(group_len, slot_count))
    (
        w_qkv, w_out, w_up, w_down, ada_gathered, h_one_low, kept_qk, out32, q_own, k_own, kt_own, vt_own, attn_low,
        x_zero, smooth, flags, one_hot_wide, silu_rows, attn_proj, x_one, h_two_low, hidden_pre, act_low, p_down,
    ) = front(
        flipped,
        condition,
        ada_state,
        feature_map,
        embed_state,
        vector_state,
        item_lengths,
        run_tables(slot_count),
        cotangent,
        groups,
    )
    s_down, s_up, s_out, s_qkv, d_ada_both, common_sum, bias_sum, map_grad, block_out = back(
        [cotangent, one_hot_wide, ada_gathered, vector_state, x_zero, x_one, attn_proj, h_one_low, h_two_low, attn_low]
        + [act_low, hidden_pre, w_qkv, w_out, w_up, w_down, code_book, out32, q_own, k_own, kt_own, vt_own]
        + [kept_qk.reshape(-1, LANES), smooth, embed_state, flags, p_down],
        groups,
        BACK_SPLITS,
        1,
    )
    root_tokens = math.sqrt(tokens_all)
    spreads = (
        model_width ** (-0.5),
        (model_width // 16) ** (-0.5),
        model_width ** (-0.5),
        w_up.shape[1] ** (-0.5),
        model_width ** (-0.5),
    )
    rates = [BASE_RATE * spread_w / (factor_g * root_tokens) for spread_w, factor_g in zip(spreads, GRAD_FACTORS)]
    rates.append(BASE_RATE * embed_state.shape[1] ** (-0.5) / (EMBED_FACTOR * root_tokens))
    rates.append(VECTOR_RATE / root_tokens)
    codes = code_book.shape[0]
    results = update(
        flipped + [ada_state],
        embed_state,
        vector_state,
        [s_down, s_up, s_out, s_qkv, d_ada_both.reshape(16, -1), silu_rows.reshape(16, -1), common_sum, bias_sum],
        [block_out, map_grad],
        tuple(rates),
        codes,
        codes / tokens_all,
    )
    outputs = [results[10], results[11], results[14].reshape(-1)]
    for i in range(5):
        new, copied = results[i], results[5 + i]
        outputs += [flip(new), flip(copied)] if i in (0, 1, 3) else [new, copied]
    return tuple(outputs + [results[12], results[13], results[15].reshape(-1)])


def solution(mesh):
    body = fast_shards if dict(mesh.shape) == {"dp": 2, "wide": 16} else shards
    in_specs = (
        P(None, ("dp", "wide")),
        P("dp", None),
        P("dp", None),
        P(("dp", "wide"), None),
        P(),
        P(None, "dp", "wide"),
        P(None, "dp", "wide"),
        P(None, "dp", "wide"),
        P(None, "dp", "wide"),
        P(None, "dp", "wide"),
        P(),
        P(),
    )
    out_specs = (
        P(("dp", "wide"), None),
        P(None, ("dp", "wide")),
        P(),
        P(None, "dp", "wide"),
        P("dp", "wide"),
        P(None, "dp", "wide"),
        P("dp", "wide"),
        P(None, "dp", "wide"),
        P("dp", "wide"),
        P(None, "dp", "wide"),
        P("dp", "wide"),
        P(None, "dp", "wide"),
        P("dp", "wide"),
        P(),
        P(),
        P(),
    )
    return jax.shard_map(body, mesh=mesh, in_specs=in_specs, out_specs=out_specs, check_vma=False)
```
